32 devices in a mesh: groups: 2 (over y), col: 16 (over z, x, core).
Axes of the slice: x: 2, y: 2, z: 4, core: 2. Of those that a mesh axis runs over, the one named last changes fastest.
Arguments:
- features: bfloat16 [16, 128, 768], P('groups', 'col'), parts along dimension 0, may hold values from -6 to 6
- column_table: bfloat16 [128, 768], P('col'), may hold values from -3 to 3
- dw_kernel: bfloat16 [7, 7, 768], replicated, may hold values from -0.875 to 0.875
- norm_gain: float32 [768], replicated, may hold values from 0.5 to 2
- expand_weight: bfloat16 [768, 3072], replicated, may hold values from -0.21875 to 0.21875
- reduce_weight: bfloat16 [3072, 768], replicated, may hold values from -0.109375 to 0.109375
- layer_scale: float32 [768], replicated, may hold values from 0.2 to 1
Outputs:
- disagreement: bfloat16 [16, 128, 768], P('groups', 'col'), parts along dimension 0
- grad_expand: float32 [1536, 3072], P(('groups', 'col')), parts along dimension 0
- grad_reduce: float32 [6144, 768], P(('groups', 'col')), parts along dimension 0
- grad_kernel: float32 [14, 7, 768], P('groups'), parts along dimension 0
- grad_gain: float32 [1536], P('groups'), parts along dimension 0
- grad_scale: float32 [1536], P('groups'), parts along dimension 0
The draws below stay inside these ranges and needn't reach their ends.
There are 2 independent parts, one for each index of `groups`. The reference program is written for one: setup_inputs(seed, part) draws one part's arguments, and reference() takes and returns one part's arrays. A program takes and returns all parts, laid end to end along the dimension named above; an argument that names none is the same for every part. Nothing has to cross between parts.
All inputs are finite; a program needn't handle non-finite values.
Results may differ from the reference program's by a relative error of at most 0.0096.
The reference program's roundings to bfloat16 on the way (of `normed`, `hidden`, `residual`, `dbranch` and `dpre`) count: a program that leaves them out, or rounds other values in their place, can miss the bound.
Values may be sent and summed in bfloat16 or wider, within the bound.
No kernel may reach another device: no remote copies, remote signals or barrier semaphores. Data moves between devices by JAX's collectives and lax.ppermute only.
A program may use at most 128 MiB of HBM per device.

```python
import math
import jax
import jax.numpy as jnp
from jax import lax

C = 768
HID = 3072
ROWS = 8
WIDTH = 128


def with_spikes(drawn, rng, source, target, blocks, factor):
    def block_of(position):
        return (jnp.arange(drawn.shape[position]) // (drawn.shape[position] // blocks)).reshape((-1,) + (1,) * (drawn.ndim - 1 - position))

    near = jax.random.permutation(rng, blocks)[block_of(target)]
    far = (block_of(target) + blocks // 2) % blocks
    return jnp.where((block_of(source) == near) | (block_of(source) == far), factor * drawn, drawn)


def shard_levels(stream_key, extent, cuts, smallest, top_value):
    gain, own = 1.0, jax.random.fold_in(stream_key, 6)
    for dim, shards_of in cuts:
        draws = jnp.exp(jax.random.uniform(jax.random.fold_in(own, dim), (shards_of,), jnp.float32, smallest / len(cuts), top_value / len(cuts)))
        gain = gain * jnp.repeat(draws, extent[dim] // shards_of).reshape([-1 if axis == dim else 1 for axis in range(len(extent))])
    return gain


def noise(rng, extent, deviation, limit, shards=(), held_as=jnp.bfloat16):
    loudness = shard_levels(rng, extent, shards, -0.22, 0.18) if shards else 1.0
    values = jax.random.normal(rng, extent, jnp.float32) * deviation * loudness
    return jnp.minimum(jnp.maximum(values, -limit), limit).astype(held_as)


def noise_with(stream_key, extent, width, limit, shards, heavy, kind=jnp.bfloat16):
    values = width * jax.random.normal(stream_key, extent, jnp.float32)
    if shards:
        values = values * shard_levels(stream_key, extent, shards, -0.22, 0.18)
    return jnp.clip(with_spikes(values, jax.random.fold_in(stream_key, 3), *heavy), -limit, limit).astype(kind)


def setup_inputs(seed: int = 0, part: int = 0) -> dict:
    splits = jax.random.split(jax.random.key(seed), 8)
    part_keys = jax.random.split(jax.random.fold_in(splits[7], part), 8)
    return {
        "features": noise_with(part_keys[0], (ROWS, WIDTH, C), 1.0, 6.0, ((1, 16),), (1, 2, 16, 2.0)),
        "column_table": noise(splits[1], (WIDTH, C), 0.5, 3.0, ((0, 16),)),
        "dw_kernel": noise(splits[2], (7, 7, C), 49 ** -0.5, 0.875),
        "norm_gain": jnp.clip(jnp.exp(jax.random.uniform(splits[3], (C,), jnp.float32, math.log(0.5), math.log(2.0))), 0.5, 2.0),
        "expand_weight": noise(splits[4], (C, HID), C ** -0.5, 0.21875),
        "reduce_weight": noise(splits[5], (HID, C), HID ** -0.5, 0.109375),
        "layer_scale": jnp.clip(jnp.exp(jax.random.uniform(splits[6], (C,), jnp.float32, math.log(0.2), math.log(1.0))), 0.2, 1.0),
    }


def gelu_parts(pre):
    normal_cdf = 0.5 * (1.0 + jax.scipy.special.erf(pre * 0.7071067811865476))
    density = jnp.exp(-0.5 * pre * pre) * 0.3989422804014327
    return (pre * normal_cdf, normal_cdf + pre * density)

def forward(view, kernel_f, norm_gain, expand_weight, reduce_weight, layer_scale):
    row_count, col_count, channels = view.shape
    padded = jnp.pad(view.astype(jnp.float32), ((3, 3), (3, 3), (0, 0)))
    conv = jnp.zeros((row_count, col_count, channels), jnp.float32)
    for row_off in range(7):
        for col_off in range(7):
            conv = conv + kernel_f[row_off, col_off] * padded[row_off:row_off + row_count, col_off:col_off + col_count]
    mean_val = lax.optimization_barrier(jnp.mean(conv, axis=-1, keepdims=True))
    centred = conv - mean_val
    variance = lax.optimization_barrier(jnp.mean(centred * centred, axis=-1, keepdims=True))
    inverse = lax.rsqrt(variance + 1e-06)
    nhat = centred * inverse
    normed = (nhat * norm_gain).astype(jnp.bfloat16).reshape(-1, channels)
    pre = jnp.dot(normed, expand_weight, preferred_element_type=jnp.float32)
    activated, gelu_slope = gelu_parts(pre)
    hidden = activated.astype(jnp.bfloat16)
    branch = jnp.dot(hidden, reduce_weight, preferred_element_type=jnp.float32)
    output = (view.astype(jnp.float32) + layer_scale * branch.reshape(view.shape)).astype(jnp.bfloat16)
    return (output, (padded, nhat, inverse, normed, gelu_slope, hidden, branch))

def backward(out_grad, saved, norm_gain, expand_weight, reduce_weight, layer_scale):
    padded, nhat, inverse, normed, gelu_slope, hidden, branch = saved
    row_count, col_count, channels = out_grad.shape
    flat_grad = out_grad.reshape(-1, channels)
    grad_scale = lax.optimization_barrier(jnp.sum(branch * flat_grad, axis=0))
    dbranch = (layer_scale * flat_grad).astype(jnp.bfloat16)
    grad_reduce = jnp.dot(hidden.T, dbranch, preferred_element_type=jnp.float32)
    dhidden = jnp.dot(dbranch, reduce_weight.T, preferred_element_type=jnp.float32)
    dpre = (dhidden * gelu_slope).astype(jnp.bfloat16)
    grad_expand = jnp.dot(normed.T, dpre, preferred_element_type=jnp.float32)
    dnormed = jnp.dot(dpre, expand_weight.T, preferred_element_type=jnp.float32).reshape(out_grad.shape)
    grad_gain = lax.optimization_barrier(jnp.sum(dnormed * nhat, axis=(0, 1)))
    scaled = dnormed * norm_gain
    dconv = inverse * (scaled - lax.optimization_barrier(jnp.mean(scaled, axis=-1, keepdims=True)) - nhat * lax.optimization_barrier(jnp.mean(scaled * nhat, axis=-1, keepdims=True)))
    kernel_rows = []
    for row_off in range(7):
        kernel_cols = []
        for col_off in range(7):
            window = padded[row_off:row_off + row_count, col_off:col_off + col_count]
            kernel_cols.append(lax.optimization_barrier(jnp.sum(window * dconv, axis=(0, 1))))
        kernel_rows.append(jnp.stack(kernel_cols))
    grad_kernel = jnp.stack(kernel_rows)
    return (grad_expand, grad_reduce, grad_kernel, grad_gain, grad_scale)

def reference(features, column_table, dw_kernel, norm_gain, expand_weight, reduce_weight, layer_scale):
    table_f = column_table.astype(jnp.float32)
    view_a = (features.astype(jnp.float32) + table_f).astype(jnp.bfloat16)
    view_b = (features[:, ::-1].astype(jnp.float32) + table_f).astype(jnp.bfloat16)
    kernel_f = dw_kernel.astype(jnp.float32)
    out_a, saved_a = forward(view_a, kernel_f, norm_gain, expand_weight, reduce_weight, layer_scale)
    out_b, saved_b = forward(view_b, kernel_f, norm_gain, expand_weight, reduce_weight, layer_scale)
    difference = out_a.astype(jnp.float32) - out_b[:, ::-1].astype(jnp.float32)
    disagreement = difference.astype(jnp.bfloat16)
    residual = (difference * (1.0 / math.sqrt(ROWS * WIDTH))).astype(jnp.bfloat16)
    residual = lax.optimization_barrier(residual)
    grad_a = residual.astype(jnp.float32)
    grad_b = -residual[:, ::-1].astype(jnp.float32)
    parts_a = backward(grad_a, saved_a, norm_gain, expand_weight, reduce_weight, layer_scale)
    parts_b = backward(grad_b, saved_b, norm_gain, expand_weight, reduce_weight, layer_scale)
    return (disagreement, parts_a[0] + parts_b[0], parts_a[1] + parts_b[1], parts_a[2] + parts_b[2], parts_a[3] + parts_b[3], parts_a[4] + parts_b[4])
```

```python
import math

import jax
import jax.numpy as jnp
from jax import lax
from jax.sharding import PartitionSpec as P

BF16 = jnp.bfloat16
F32 = jnp.float32


def gelu_parts(pre):
    normal_cdf = 0.5 * (1.0 + lax.erf(pre * 0.7071067811865476))
    density = jnp.exp(-0.5 * pre * pre) * 0.3989422804014327
    return (pre * normal_cdf, normal_cdf + pre * density)


def dot(lhs, rhs, contract):
    return lax.dot_general(lhs, rhs, (contract, ((), ())), preferred_element_type=F32)


def on_device(
    features, column_table, dw_kernel, norm_gain, expand_weight, reduce_weight, layer_scale
):
    rows, cols, channels = features.shape
    hid = expand_weight.shape[1]
    count = lax.axis_size("col")
    bits = count.bit_length() - 1
    line = 1 << ((bits + 1) // 2)
    inner = count // line
    inner_bits = inner.bit_length() - 1
    me = lax.axis_index("col")
    my_line, my_inner = me // inner, me % inner
    units = hid // line
    total_cols = cols * count

    def along_line(block, step):
        route = [
            (z * inner + i, (z + step) % line * inner + i) for z in range(line) for i in range(inner)
        ]
        return lax.ppermute(block, "col", route)

    def swapped(block, bit):
        return lax.ppermute(block, "col", [(d, d ^ (1 << bit)) for d in range(count)])

    def gathered(block):
        return jnp.stack([block] + [along_line(block, step) for step in range(1, line)])

    def edge(lo):
        cut = slice(0, 3) if lo else slice(cols - 3, cols)
        return jnp.concatenate([features[:, cut], column_table[None, cut]])

    low = lax.ppermute(edge(False), "col", [(d, d + 1) for d in range(count - 1)])
    high = lax.ppermute(edge(True), "col", [(d + 1, d) for d in range(count - 1)])
    mid_m = lax.ppermute(column_table, "col", [(d, count - 1 - d) for d in range(count)])
    low_m = lax.ppermute(column_table[:3], "col", [(d, count - d) for d in range(1, count)])
    high_m = lax.ppermute(
        column_table[cols - 3 :], "col", [(d, count - 2 - d) for d in range(count - 1)]
    )
    wide = jnp.concatenate([low[:rows], features, high[:rows]], axis=1).astype(F32)
    table = jnp.concatenate([low[rows], column_table, high[rows]]).astype(F32)
    table_m = jnp.concatenate([low_m[::-1], mid_m[::-1], high_m[::-1]]).astype(F32)
    views = jnp.stack([wide + table, wide + table_m]).astype(BF16)
    kernel_f = dw_kernel.astype(F32)
    kernels = jnp.stack([kernel_f, kernel_f[:, ::-1]])
    padded = jnp.pad(views.astype(F32), ((0, 0), (3, 3), (0, 0), (0, 0)))
    conv = jnp.zeros((2, rows, cols, channels), F32)
    for i in range(7):
        for j in range(7):
            conv = conv + kernels[:, i, j][:, None, None] * padded[:, i : i + rows, j : j + cols]
    centred = conv - jnp.mean(conv, axis=-1, keepdims=True)
    inverse = lax.rsqrt(jnp.mean(centred * centred, axis=-1, keepdims=True) + 1e-06)
    nhat = centred * inverse
    normed = (nhat * norm_gain).astype(BF16).reshape(2, rows * cols, channels)
    normed_all = gathered(normed)
    flat = normed.reshape(-1, channels)
    pre = dot(flat, expand_weight, ((1,), (0,)))
    activated, slope = gelu_parts(pre)
    branch = dot(activated.astype(BF16), reduce_weight, ((1,), (0,))).reshape(conv.shape)
    own = views[:, :, 3 : 3 + cols].astype(F32)
    outputs = (own + layer_scale * branch).astype(BF16).astype(F32)
    difference = outputs[0] - outputs[1]
    disagreement = difference.astype(BF16)
    residual = (difference * (1.0 / math.sqrt(rows * total_cols))).astype(BF16).astype(F32)
    grad_scale = jnp.sum((branch[0] - branch[1]) * residual, axis=(0, 1))
    dbranch = (layer_scale * residual).astype(BF16).reshape(-1, channels)
    dbranch_all = gathered(dbranch)

    dhidden = dot(dbranch, reduce_weight, ((1,), (1,)))
    dpre = (jnp.concatenate([dhidden, -dhidden]) * slope).astype(BF16)
    dnormed = dot(dpre, expand_weight, ((1,), (1,))).reshape(conv.shape)
    grad_gain = jnp.sum(dnormed * nhat, axis=(0, 1, 2))
    scaled = dnormed * norm_gain
    dconv = inverse * (
        scaled
        - jnp.mean(scaled, axis=-1, keepdims=True)
        - nhat * jnp.mean(scaled * nhat, axis=-1, keepdims=True)
    )
    taps = []
    for i in range(7):
        for j in range(7):
            window = padded[:, i : i + rows]
            taps.append(
                jnp.sum(window[0, :, j : j + cols] * dconv[0], axis=(0, 1))
                + jnp.sum(window[1, :, 6 - j : 6 - j + cols] * dconv[1], axis=(0, 1))
            )
    small = jnp.stack(taps + [grad_gain, grad_scale]).astype(BF16)

    expand_own = lax.dynamic_slice_in_dim(expand_weight, my_line * units, units, 1)
    reduce_own = lax.dynamic_slice_in_dim(reduce_weight, my_line * units, units, 0)
    every = normed_all.reshape(-1, channels)
    pre_own = dot(every, expand_own, ((1,), (0,)))
    act_own, slope_own = gelu_parts(pre_own)
    act_own = act_own.astype(BF16).astype(F32).reshape(line, 2, -1, units)
    slope_own = slope_own.reshape(line, 2, -1, units)
    hidden_diff = (act_own[:, 0] - act_own[:, 1]).astype(BF16).reshape(-1, units)
    dbranch_flat = dbranch_all.reshape(-1, channels)
    dhidden_own = dot(dbranch_flat, reduce_own, ((1,), (1,))).reshape(line, -1, units)
    dpre_own = jnp.stack([dhidden_own * slope_own[:, 0], -dhidden_own * slope_own[:, 1]], axis=1)
    dpre_own = dpre_own.astype(BF16).reshape(-1, units)
    grad_expand = dot(every, dpre_own, ((0,), (0,)))
    grad_reduce = dot(hidden_diff, dbranch_flat, ((0,), (0,)))

    expand_rows = channels // count
    grad_expand = grad_expand.reshape(line, inner, expand_rows, units)
    grad_reduce = grad_reduce.reshape(inner, units // inner, channels)
    for bit in range(inner_bits):
        side = (my_inner >> bit) & 1
        left = inner >> (bit + 1)

        def halves(part, axis):
            shape = part.shape
            part = part.reshape(shape[:axis] + (left, 2) + shape[axis + 1 :])
            keep = lax.dynamic_index_in_dim(part, side, axis + 1, keepdims=False)
            send = lax.dynamic_index_in_dim(part, 1 - side, axis + 1, keepdims=False)
            return keep, send.astype(BF16)

        keep_e, send_e = halves(grad_expand, 1)
        keep_r, send_r = halves(grad_reduce, 0)
        grad_expand = keep_e + swapped(send_e, bit).astype(F32)
        grad_reduce = keep_r + swapped(send_r, bit).astype(F32)
        small = (small.astype(F32) + swapped(small, bit).astype(F32)).astype(BF16)
    grad_reduce = grad_reduce.reshape(units // inner, channels)
    grad_expand = grad_expand.reshape(line, expand_rows, units).astype(BF16)

    columns = jnp.zeros((line, expand_rows, units), BF16)
    sums = jnp.zeros((line,) + small.shape, BF16)
    for step in range(line):
        block = lax.dynamic_index_in_dim(grad_expand, (my_line + step) % line, 0, keepdims=False)
        source = (my_line - step) % line
        if step:
            block, part = along_line(block, step), along_line(small, step)
        else:
            part = small
        columns = lax.dynamic_update_index_in_dim(columns, block, source, 0)
        sums = lax.dynamic_update_index_in_dim(sums, part, source, 0)
    grad_expand = jnp.moveaxis(columns, 0, 1).reshape(expand_rows, hid).astype(F32)
    small = jnp.sum(sums.astype(F32), axis=0)
    grad_kernel = small[:49].reshape(7, 7, channels)
    return (disagreement, grad_expand, grad_reduce, grad_kernel, small[49], small[50])


def solution(mesh):
    in_specs = (P("groups", "col", None), P("col", None), P(), P(), P(), P(), P())
    out_specs = (
        P("groups", "col", None),
        P(("groups", "col"), None),
        P(("groups", "col"), None),
        P("groups", None, None),
        P("groups"),
        P("groups"),
    )
    return jax.shard_map(
        on_device, mesh=mesh, in_specs=in_specs, out_specs=out_specs, check_vma=False
    )
```

```python
import math

import jax
import jax.numpy as jnp
from jax import lax
from jax.sharding import PartitionSpec as P

BF16 = jnp.bfloat16
F32 = jnp.float32


def gelu_parts(pre):
    normal_cdf = 0.5 * (1.0 + lax.erf(pre * 0.7071067811865476))
    density = jnp.exp(-0.5 * pre * pre) * 0.3989422804014327
    return (pre * normal_cdf, normal_cdf + pre * density)


def dot(lhs, rhs, contract):
    return lax.dot_general(lhs, rhs, (contract, ((), ())), preferred_element_type=F32)


def on_device(
    features, column_table, dw_kernel, norm_gain, expand_weight, reduce_weight, layer_scale
):
    rows, cols, channels = features.shape
    hid = expand_weight.shape[1]
    count = lax.axis_size("col")
    bits = count.bit_length() - 1
    line = 1 << ((bits + 1) // 2)
    inner = count // line
    inner_bits = inner.bit_length() - 1
    me = lax.axis_index("col")
    my_line, my_inner = me // inner, me % inner
    units = hid // line
    total_cols = cols * count

    def swapped(block, bit):
        return lax.ppermute(block, "col", [(d, d ^ (1 << bit)) for d in range(count)])

    def gathered(block):
        lines = [[z * inner + i for z in range(line)] for i in range(inner)]
        return lax.all_gather(block, "col", axis_index_groups=lines)

    mirrored = lax.ppermute(column_table, "col", [(d, count - 1 - d) for d in range(count)])
    tables = jnp.stack([column_table, mirrored[::-1]]).astype(F32)[:, None]
    slab = (features.astype(F32) + tables).astype(BF16)
    low = lax.ppermute(slab[:, :, cols - 3 :], "col", [(d, d + 1) for d in range(count - 1)])
    high = lax.ppermute(slab[:, :, :3], "col", [(d + 1, d) for d in range(count - 1)])
    views = jnp.concatenate([low, slab, high], axis=2)
    kernel_f = dw_kernel.astype(F32)
    kernels = jnp.stack([kernel_f, kernel_f[:, ::-1]])
    padded = jnp.pad(views.astype(F32), ((0, 0), (3, 3), (0, 0), (0, 0)))
    conv = jnp.zeros((2, rows, cols, channels), F32)
    for i in range(7):
        for j in range(7):
            conv = conv + kernels[:, i, j][:, None, None] * padded[:, i : i + rows, j : j + cols]
    centred = conv - jnp.mean(conv, axis=-1, keepdims=True)
    inverse = lax.rsqrt(jnp.mean(centred * centred, axis=-1, keepdims=True) + 1e-06)
    nhat = centred * inverse
    normed = (nhat * norm_gain).astype(BF16).reshape(2, rows * cols, channels)
    normed_all = gathered(normed)
    flat = normed.reshape(-1, channels)
    pre = dot(flat, expand_weight, ((1,), (0,)))
    activated, slope = gelu_parts(pre)
    branch = dot(activated.astype(BF16), reduce_weight, ((1,), (0,))).reshape(conv.shape)
    own = views[:, :, 3 : 3 + cols].astype(F32)
    outputs = (own + layer_scale * branch).astype(BF16).astype(F32)
    difference = outputs[0] - outputs[1]
    disagreement = difference.astype(BF16)
    residual = (difference * (1.0 / math.sqrt(rows * total_cols))).astype(BF16).astype(F32)
    grad_scale = jnp.sum((branch[0] - branch[1]) * residual, axis=(0, 1))
    dbranch = (layer_scale * residual).astype(BF16).reshape(-1, channels)
    dbranch_all = gathered(dbranch)

    dhidden = dot(dbranch, reduce_weight, ((1,), (1,)))
    dpre = (jnp.concatenate([dhidden, -dhidden]) * slope).astype(BF16)
    dnormed = dot(dpre, expand_weight, ((1,), (1,))).reshape(conv.shape)
    grad_gain = jnp.sum(dnormed * nhat, axis=(0, 1, 2))
    scaled = dnormed * norm_gain
    dconv = inverse * (
        scaled
        - jnp.mean(scaled, axis=-1, keepdims=True)
        - nhat * jnp.mean(scaled * nhat, axis=-1, keepdims=True)
    )
    taps = []
    for i in range(7):
        for j in range(7):
            window = padded[:, i : i + rows]
            taps.append(
                jnp.sum(window[0, :, j : j + cols] * dconv[0], axis=(0, 1))
                + jnp.sum(window[1, :, 6 - j : 6 - j + cols] * dconv[1], axis=(0, 1))
            )
    small = jnp.stack(taps + [grad_gain, grad_scale]).astype(BF16)
    small = jnp.sum(gathered(small).astype(F32), axis=0).astype(BF16)

    expand_rows = channels // line
    every = normed_all.reshape(-1, channels)
    pre_all = dot(every, expand_weight, ((1,), (0,)))
    slope_all = gelu_parts(pre_all)[1].reshape(line, 2, -1, hid)
    expand_own = lax.dynamic_slice_in_dim(expand_weight, my_line * units, units, 1)
    pre_own = dot(every, expand_own, ((1,), (0,)))
    act_own = gelu_parts(pre_own)[0].astype(BF16).astype(F32).reshape(line, 2, -1, units)
    hidden_diff = (act_own[:, 0] - act_own[:, 1]).astype(BF16).reshape(-1, units)
    dbranch_flat = dbranch_all.reshape(-1, channels)
    dhidden_all = dot(dbranch_flat, reduce_weight, ((1,), (1,))).reshape(line, -1, hid)
    dpre_all = jnp.stack([dhidden_all * slope_all[:, 0], -dhidden_all * slope_all[:, 1]], axis=1)
    dpre_all = dpre_all.astype(BF16).reshape(-1, hid)
    every_own = lax.dynamic_slice_in_dim(every, my_line * expand_rows, expand_rows, 1)
    grad_expand = dot(every_own, dpre_all, ((0,), (0,)))
    grad_reduce = dot(hidden_diff, dbranch_flat, ((0,), (0,)))

    grad_expand = grad_expand.reshape(inner, expand_rows // inner, hid)
    grad_reduce = grad_reduce.reshape(inner, units // inner, channels)
    for bit in range(inner_bits):
        side = (my_inner >> bit) & 1

        def halves(part):
            part = part.reshape((inner >> (bit + 1), 2) + part.shape[1:])
            keep = lax.dynamic_index_in_dim(part, side, 1, keepdims=False)
            send = lax.dynamic_index_in_dim(part, 1 - side, 1, keepdims=False)
            return keep, send.astype(BF16)

        keep_e, send_e = halves(grad_expand)
        keep_r, send_r = halves(grad_reduce)
        grad_expand = keep_e + swapped(send_e, bit).astype(F32)
        grad_reduce = keep_r + swapped(send_r, bit).astype(F32)
        small = small.astype(F32) + swapped(small, bit).astype(F32)
        if bit < inner_bits - 1:
            small = small.astype(BF16)
    grad_reduce = grad_reduce.reshape(units // inner, channels)
    grad_expand = grad_expand.reshape(expand_rows // inner, hid)
    grad_kernel = small[:49].reshape(7, 7, channels)
    return (disagreement, grad_expand, grad_reduce, grad_kernel, small[49], small[50])


def solution(mesh):
    in_specs = (P("groups", "col", None), P("col", None), P(), P(), P(), P(), P())
    out_specs = (
        P("groups", "col", None),
        P(("groups", "col"), None),
        P(("groups", "col"), None),
        P("groups", None, None),
        P("groups"),
        P("groups"),
    )
    return jax.shard_map(
        on_device, mesh=mesh, in_specs=in_specs, out_specs=out_specs, check_vma=False
    )
```

```python
import math

import jax
import jax.numpy as jnp
from jax import lax
from jax.sharding import PartitionSpec as P

BF16 = jnp.bfloat16
F32 = jnp.float32


def gelu_parts(pre):
    normal_cdf = 0.5 * (1.0 + lax.erf(pre * 0.7071067811865476))
    density = jnp.exp(-0.5 * pre * pre) * 0.3989422804014327
    return (pre * normal_cdf, normal_cdf + pre * density)


def dot(lhs, rhs, contract):
    return lax.dot_general(lhs, rhs, (contract, ((), ())), preferred_element_type=F32)


def on_device(
    features, column_table, dw_kernel, norm_gain, expand_weight, reduce_weight, layer_scale
):
    rows, cols, channels = features.shape
    hid = expand_weight.shape[1]
    count = lax.axis_size("col")
    bits = count.bit_length() - 1
    line = 1 << ((bits + 1) // 2)
    inner = count // line
    inner_bits = inner.bit_length() - 1
    me = lax.axis_index("col")
    my_line, my_inner = me // inner, me % inner
    units = hid // line
    total_cols = cols * count

    def swapped(block, bit):
        return lax.ppermute(block, "col", [(d, d ^ (1 << bit)) for d in range(count)])

    def gathered(block):
        lines = [[z * inner + i for z in range(line)] for i in range(inner)]
        copies = jnp.broadcast_to(block[None], (line,) + block.shape)
        return lax.all_to_all(copies, "col", 0, 0, axis_index_groups=lines, tiled=True)

    mirrored = lax.ppermute(column_table, "col", [(d, count - 1 - d) for d in range(count)])
    tables = jnp.stack([column_table, mirrored[::-1]]).astype(F32)[:, None]
    slab = (features.astype(F32) + tables).astype(BF16)
    low = lax.ppermute(slab[:, :, cols - 3 :], "col", [(d, d + 1) for d in range(count - 1)])
    high = lax.ppermute(slab[:, :, :3], "col", [(d + 1, d) for d in range(count - 1)])
    views = jnp.concatenate([low, slab, high], axis=2)
    kernel_f = dw_kernel.astype(F32)
    kernels = jnp.stack([kernel_f, kernel_f[:, ::-1]])
    padded = jnp.pad(views.astype(F32), ((0, 0), (3, 3), (0, 0), (0, 0)))
    conv = jnp.zeros((2, rows, cols, channels), F32)
    for i in range(7):
        for j in range(7):
            conv = conv + kernels[:, i, j][:, None, None] * padded[:, i : i + rows, j : j + cols]
    centred = conv - jnp.mean(conv, axis=-1, keepdims=True)
    inverse = lax.rsqrt(jnp.mean(centred * centred, axis=-1, keepdims=True) + 1e-06)
    nhat = centred * inverse
    normed = (nhat * norm_gain).astype(BF16).reshape(2, rows * cols, channels)
    normed_all = gathered(normed)
    flat = normed.reshape(-1, channels)
    pre = dot(flat, expand_weight, ((1,), (0,)))
    activated, slope = gelu_parts(pre)
    branch = dot(activated.astype(BF16), reduce_weight, ((1,), (0,))).reshape(conv.shape)
    own = views[:, :, 3 : 3 + cols].astype(F32)
    outputs = (own + layer_scale * branch).astype(BF16).astype(F32)
    difference = outputs[0] - outputs[1]
    disagreement = difference.astype(BF16)
    residual = (difference * (1.0 / math.sqrt(rows * total_cols))).astype(BF16).astype(F32)
    grad_scale = jnp.sum((branch[0] - branch[1]) * residual, axis=(0, 1))
    dbranch = (layer_scale * residual).astype(BF16).reshape(-1, channels)
    dbranch_all = gathered(dbranch)

    dhidden = dot(dbranch, reduce_weight, ((1,), (1,)))
    dpre = (jnp.concatenate([dhidden, -dhidden]) * slope).astype(BF16)
    dnormed = dot(dpre, expand_weight, ((1,), (1,))).reshape(conv.shape)
    grad_gain = jnp.sum(dnormed * nhat, axis=(0, 1, 2))
    scaled = dnormed * norm_gain
    dconv = inverse * (
        scaled
        - jnp.mean(scaled, axis=-1, keepdims=True)
        - nhat * jnp.mean(scaled * nhat, axis=-1, keepdims=True)
    )
    taps = []
    for i in range(7):
        for j in range(7):
            window = padded[:, i : i + rows]
            taps.append(
                jnp.sum(window[0, :, j : j + cols] * dconv[0], axis=(0, 1))
                + jnp.sum(window[1, :, 6 - j : 6 - j + cols] * dconv[1], axis=(0, 1))
            )
    small = jnp.stack(taps + [grad_gain, grad_scale]).astype(BF16)
    small = jnp.sum(gathered(small).astype(F32), axis=0).astype(BF16)

    expand_rows = channels // line
    every = normed_all.reshape(-1, channels)
    pre_all = dot(every, expand_weight, ((1,), (0,)))
    slope_all = gelu_parts(pre_all)[1].reshape(line, 2, -1, hid)
    expand_own = lax.dynamic_slice_in_dim(expand_weight, my_line * units, units, 1)
    pre_own = dot(every, expand_own, ((1,), (0,)))
    act_own = gelu_parts(pre_own)[0].astype(BF16).astype(F32).reshape(line, 2, -1, units)
    hidden_diff = (act_own[:, 0] - act_own[:, 1]).astype(BF16).reshape(-1, units)
    dbranch_flat = dbranch_all.reshape(-1, channels)
    dhidden_all = dot(dbranch_flat, reduce_weight, ((1,), (1,))).reshape(line, -1, hid)
    dpre_all = jnp.stack([dhidden_all * slope_all[:, 0], -dhidden_all * slope_all[:, 1]], axis=1)
    dpre_all = dpre_all.astype(BF16).reshape(-1, hid)
    every_own = lax.dynamic_slice_in_dim(every, my_line * expand_rows, expand_rows, 1)
    grad_expand = dot(every_own, dpre_all, ((0,), (0,)))
    grad_reduce = dot(hidden_diff, dbranch_flat, ((0,), (0,)))

    grad_expand = grad_expand.reshape(inner, expand_rows // inner, hid)
    grad_reduce = grad_reduce.reshape(inner, units // inner, channels)
    for bit in range(inner_bits):
        side = (my_inner >> bit) & 1

        def halves(part):
            part = part.reshape((inner >> (bit + 1), 2) + part.shape[1:])
            keep = lax.dynamic_index_in_dim(part, side, 1, keepdims=False)
            send = lax.dynamic_index_in_dim(part, 1 - side, 1, keepdims=False)
            return keep, send.astype(BF16)

        keep_e, send_e = halves(grad_expand)
        keep_r, send_r = halves(grad_reduce)
        grad_expand = keep_e + swapped(send_e, bit).astype(F32)
        grad_reduce = keep_r + swapped(send_r, bit).astype(F32)
        small = small.astype(F32) + swapped(small, bit).astype(F32)
        if bit < inner_bits - 1:
            small = small.astype(BF16)
    grad_reduce = grad_reduce.reshape(units // inner, channels)
    grad_expand = grad_expand.reshape(expand_rows // inner, hid)
    grad_kernel = small[:49].reshape(7, 7, channels)
    return (disagreement, grad_expand, grad_reduce, grad_kernel, small[49], small[50])


def solution(mesh):
    in_specs = (P("groups", "col", None), P("col", None), P(), P(), P(), P(), P())
    out_specs = (
        P("groups", "col", None),
        P(("groups", "col"), None),
        P(("groups", "col"), None),
        P("groups", None, None),
        P("groups"),
        P("groups"),
    )
    return jax.shard_map(
        on_device, mesh=mesh, in_specs=in_specs, out_specs=out_specs, check_vma=False
    )
```

```python
import functools
import math

import jax
import jax.numpy as jnp
from jax import lax
from jax.experimental import pallas as pl
from jax.experimental.pallas import tpu as pltpu
from jax.sharding import PartitionSpec as P

BF16 = jnp.bfloat16
F32 = jnp.float32
LANES = 128
VMEM_LIMIT = 56 << 20


def phi_parts(pre):
    normal_cdf = 0.5 * (1.0 + lax.erf(pre * 0.7071067811865476))
    density = jnp.exp(-0.5 * pre * pre) * 0.3989422804014327
    return normal_cdf, density


def dot(lhs, rhs, contract):
    return lax.dot_general(lhs, rhs, (contract, ((), ())), preferred_element_type=F32)


def conv_body(feat, table, mirror, low, high, dw, gain, normed, nhat, inv, wide, taps, conv):
    rows, cols, channels = feat.shape
    own = feat[...].astype(F32)
    straight = table[...].astype(F32)
    turned = mirror[...].astype(F32)
    turned = jnp.concatenate([turned[c : c + 1] for c in reversed(range(cols))], axis=0)
    for v, add in enumerate((straight, turned)):
        wide[v, :, 3 : 3 + cols, :] = (own + add[None]).astype(BF16).astype(F32)
        wide[v, :, 0:3, :] = low[v].astype(F32)
        wide[v, :, 3 + cols : 6 + cols, :] = high[v].astype(F32)
    for i in range(7):
        taps[7 * i : 7 * i + 7, :] = dw[i].astype(F32)

    def tile(c, carry):
        lanes = pl.ds(pl.multiple_of(c * LANES, LANES), LANES)
        sums = [[jnp.zeros((cols, LANES), F32) for _ in range(rows)] for _ in range(2)]
        for j in range(7):
            for v in range(2):
                part = [wide[v, r, pl.ds(j, cols), lanes] for r in range(rows)]
                for i in range(7):
                    weight = taps[pl.ds(7 * i + (6 - j if v else j), 1), lanes]
                    for r in range(rows):
                        if 0 <= r + i - 3 < rows:
                            sums[v][r] = sums[v][r] + weight * part[r + i - 3]
        for v in range(2):
            for r in range(rows):
                conv[v, r, :, lanes] = sums[v][r]
        return carry

    lax.fori_loop(0, channels // LANES, tile, 0)
    for v in range(2):
        value = conv[v].reshape(rows * cols, channels)
        centred = value - jnp.mean(value, axis=-1, keepdims=True)
        inverse = lax.rsqrt(jnp.mean(centred * centred, axis=-1, keepdims=True) + 1e-06)
        value = centred * inverse
        nhat[v] = value
        inv[v] = jnp.broadcast_to(inverse, (rows * cols, LANES))
        normed[v] = (value * gain[...]).astype(BF16)


def conv_norm(features, table, mirror, low, high, dw, gain):
    rows, cols, channels = features.shape
    pixels = rows * cols
    return pl.pallas_call(
        conv_body,
        out_shape=(
            jax.ShapeDtypeStruct((2, pixels, channels), BF16),
            jax.ShapeDtypeStruct((2, pixels, channels), F32),
            jax.ShapeDtypeStruct((2, pixels, LANES), F32),
            jax.ShapeDtypeStruct((2, rows, 16, channels), F32),
        ),
        scratch_shapes=[
            pltpu.VMEM((49, channels), F32),
            pltpu.VMEM((2, rows, cols, channels), F32),
        ],
        compiler_params=pltpu.CompilerParams(vmem_limit_bytes=VMEM_LIMIT),
        name="conv_norm",
    )(features, table, mirror, low, high, dw, gain)


def forward_body(scale, normed, expand, reduce, wide, ls, slope, disagreement, dbranch, gscale, acc):
    step = pl.program_id(0)
    pixels, channels = normed.shape
    rows, cols, _ = disagreement.shape
    pre = dot(normed[...], expand[...], ((1,), (0,)))
    cdf, density = phi_parts(pre)
    slope[...] = cdf + pre * density
    part = dot((pre * cdf).astype(BF16), reduce[...], ((1,), (0,)))

    @pl.when(step == 0)
    def _():
        acc[...] = part

    @pl.when(step > 0)
    def _():
        acc[...] += part

    @pl.when(step == pl.num_programs(0) - 1)
    def _():
        half = pixels // 2
        outs = []
        for v in range(2):
            own = wide[v, :, 3 : 3 + cols, :].reshape(half, channels)
            branch = acc[v * half : (v + 1) * half, :]
            outs.append((own + ls[...] * branch).astype(BF16).astype(F32))
        difference = outs[0] - outs[1]
        disagreement[...] = difference.astype(BF16).reshape(rows, cols, channels)
        residual = (difference * scale).astype(BF16).astype(F32)
        gscale[...] = jnp.sum((acc[:half, :] - acc[half:, :]) * residual, axis=0, keepdims=True)
        dbranch[...] = (ls[...] * residual).astype(BF16)


def forward(scale, normed, expand, reduce, wide, ls, shape):
    pixels, channels = normed.shape
    hid = expand.shape[1]
    block = 512
    whole = lambda *dims: pl.BlockSpec(dims, lambda j: (0,) * len(dims))
    return pl.pallas_call(
        functools.partial(forward_body, scale),
        grid=(hid // block,),
        in_specs=[
            whole(pixels, channels),
            pl.BlockSpec((channels, block), lambda j: (0, j)),
            pl.BlockSpec((block, channels), lambda j: (j, 0)),
            whole(*wide.shape),
            whole(1, channels),
        ],
        out_specs=[
            pl.BlockSpec((pixels, block), lambda j: (0, j)),
            whole(*shape),
            whole(pixels // 2, channels),
            whole(1, channels),
        ],
        out_shape=(
            jax.ShapeDtypeStruct((pixels, hid), F32),
            jax.ShapeDtypeStruct(shape, BF16),
            jax.ShapeDtypeStruct((pixels // 2, channels), BF16),
            jax.ShapeDtypeStruct((1, channels), F32),
        ),
        scratch_shapes=[pltpu.VMEM((pixels, channels), F32)],
        compiler_params=pltpu.CompilerParams(vmem_limit_bytes=VMEM_LIMIT),
        name="forward",
    )(normed, expand, reduce, wide, ls)


def backward_body(dbranch, slope, expand, reduce, nhat, inv, gain, gscale, wide, small, acc):
    step = pl.program_id(0)
    half, channels = dbranch.shape
    _, rows, _, _ = wide.shape
    cols = half // rows
    dhidden = dot(dbranch[...], reduce[...], ((1,), (1,)))
    dpre = jnp.concatenate([dhidden * slope[:half, :], -dhidden * slope[half:, :]]).astype(BF16)
    part = dot(dpre, expand[...], ((1,), (1,)))

    @pl.when(step == 0)
    def _():
        acc[...] = part

    @pl.when(step > 0)
    def _():
        acc[...] += part

    @pl.when(step == pl.num_programs(0) - 1)
    def _():
        ggain = jnp.zeros((1, channels), F32)
        for v in range(2):
            here = slice(v * half, (v + 1) * half)
            dnormed = acc[here, :]
            ggain = ggain + jnp.sum(dnormed * nhat[v], axis=0, keepdims=True)
            scaled = dnormed * gain[...]
            gm = jnp.mean(scaled, axis=-1, keepdims=True)
            gn = jnp.mean(scaled * nhat[v], axis=-1, keepdims=True)
            acc[here, :] = inv[v][:, :1] * (scaled - gm - nhat[v] * gn)
        small[49:50, :] = ggain
        small[50:51, :] = gscale[...]

        def tile(c, carry):
            lanes = pl.ds(pl.multiple_of(c * LANES, LANES), LANES)
            dconv = [
                [acc[pl.ds(v * half + r * cols, cols), lanes] for r in range(rows)] for v in range(2)
            ]
            for j in range(7):
                part = [
                    [wide[v, r, pl.ds(6 - j if v else j, cols), lanes] for r in range(rows)]
                    for v in range(2)
                ]
                for i in range(7):
                    total = None
                    for v in range(2):
                        for r in range(rows):
                            if 0 <= r + i - 3 < rows:
                                term = part[v][r + i - 3] * dconv[v][r]
                                total = term if total is None else total + term
                    small[pl.ds(7 * i + j, 1), lanes] = jnp.sum(total, axis=0, keepdims=True)
            return carry

        lax.fori_loop(0, channels // LANES, tile, 0)
        small[51:, :] = jnp.zeros((small.shape[0] - 51, channels), F32)


def backward(dbranch, slope, expand, reduce, nhat, inv, gain, gscale, wide):
    half, channels = dbranch.shape
    hid = expand.shape[1]
    block = 512
    whole = lambda *dims: pl.BlockSpec(dims, lambda j: (0,) * len(dims))
    return pl.pallas_call(
        backward_body,
        grid=(hid // block,),
        in_specs=[
            whole(half, channels),
            pl.BlockSpec((2 * half, block), lambda j: (0, j)),
            pl.BlockSpec((channels, block), lambda j: (0, j)),
            pl.BlockSpec((block, channels), lambda j: (j, 0)),
            whole(*nhat.shape),
            whole(*inv.shape),
            whole(1, channels),
            whole(1, channels),
            whole(*wide.shape),
        ],
        out_specs=whole(64, channels),
        out_shape=jax.ShapeDtypeStruct((64, channels), F32),
        scratch_shapes=[pltpu.VMEM((2 * half, channels), F32)],
        compiler_params=pltpu.CompilerParams(vmem_limit_bytes=VMEM_LIMIT),
        name="backward",
    )(dbranch, slope, expand, reduce, nhat, inv, gain, gscale, wide)


def on_device(
    features, column_table, dw_kernel, norm_gain, expand_weight, reduce_weight, layer_scale
):
    rows, cols, channels = features.shape
    hid = expand_weight.shape[1]
    count = lax.axis_size("col")
    bits = count.bit_length() - 1
    line = 1 << ((bits + 1) // 2)
    inner = count // line
    inner_bits = inner.bit_length() - 1
    me = lax.axis_index("col")
    my_line, my_inner = me // inner, me % inner
    units = hid // line
    total_cols = cols * count
    gain = norm_gain.reshape(1, channels)
    ls = layer_scale.reshape(1, channels)

    def along_line(block, step):
        route = [
            (z * inner + i, (z + step) % line * inner + i) for z in range(line) for i in range(inner)
        ]
        return lax.ppermute(block, "col", route)

    def swapped(block, bit):
        return lax.ppermute(block, "col", [(d, d ^ (1 << bit)) for d in range(count)])

    def gathered(block):
        return jnp.stack([block] + [along_line(block, step) for step in range(1, line)])

    mirror = lax.ppermute(column_table, "col", [(d, count - 1 - d) for d in range(count)])
    def edge(here, there):
        pair = jnp.stack([column_table[here], mirror[there][::-1]]).astype(F32)
        return (features[:, here].astype(F32) + pair[:, None]).astype(BF16)

    low = lax.ppermute(
        edge(slice(cols - 3, cols), slice(0, 3)), "col", [(d, d + 1) for d in range(count - 1)]
    )
    high = lax.ppermute(
        edge(slice(0, 3), slice(cols - 3, cols)), "col", [(d + 1, d) for d in range(count - 1)]
    )
    normed, nhat, inv, wide = conv_norm(
        features, column_table, mirror, low, high, dw_kernel, gain
    )
    normed_all = gathered(normed)
    slope, disagreement, dbranch, gscale = forward(
        1.0 / math.sqrt(rows * total_cols),
        normed.reshape(-1, channels),
        expand_weight,
        reduce_weight,
        wide,
        ls,
        features.shape,
    )
    dbranch_all = gathered(dbranch)
    small = backward(dbranch, slope, expand_weight, reduce_weight, nhat, inv, gain, gscale, wide)
    for bit in range(inner_bits, count.bit_length() - 1):
        small = small.astype(BF16)
        small = small.astype(F32) + swapped(small, bit).astype(F32)
    small = small.astype(BF16)
    expand_rows = channels // line
    every = normed_all.reshape(-1, channels)
    pre_all = dot(every, expand_weight, ((1,), (0,)))
    cdf_all, density_all = phi_parts(pre_all)
    slope_all = (cdf_all + pre_all * density_all).reshape(line, 2, -1, hid)
    expand_own = lax.dynamic_slice_in_dim(expand_weight, my_line * units, units, 1)
    pre_own = dot(every, expand_own, ((1,), (0,)))
    act_own = (pre_own * phi_parts(pre_own)[0]).astype(BF16).astype(F32).reshape(line, 2, -1, units)
    hidden_diff = (act_own[:, 0] - act_own[:, 1]).astype(BF16).reshape(-1, units)
    dbranch_flat = dbranch_all.reshape(-1, channels)
    dhidden_all = dot(dbranch_flat, reduce_weight, ((1,), (1,))).reshape(line, -1, hid)
    dpre_all = jnp.stack([dhidden_all * slope_all[:, 0], -dhidden_all * slope_all[:, 1]], axis=1)
    dpre_all = dpre_all.astype(BF16).reshape(-1, hid)
    every_own = lax.dynamic_slice_in_dim(every, my_line * expand_rows, expand_rows, 1)
    grad_expand = dot(every_own, dpre_all, ((0,), (0,)))
    grad_reduce = dot(hidden_diff, dbranch_flat, ((0,), (0,)))

    grad_expand = grad_expand.reshape(inner, expand_rows // inner, hid)
    grad_reduce = grad_reduce.reshape(inner, units // inner, channels)
    for bit in range(inner_bits):
        side = (my_inner >> bit) & 1

        def halves(part):
            part = part.reshape((inner >> (bit + 1), 2) + part.shape[1:])
            keep = lax.dynamic_index_in_dim(part, side, 1, keepdims=False)
            send = lax.dynamic_index_in_dim(part, 1 - side, 1, keepdims=False)
            return keep, send.astype(BF16)

        keep_e, send_e = halves(grad_expand)
        keep_r, send_r = halves(grad_reduce)
        grad_expand = keep_e + swapped(send_e, bit).astype(F32)
        grad_reduce = keep_r + swapped(send_r, bit).astype(F32)
        small = small.astype(F32) + swapped(small, bit).astype(F32)
        if bit < inner_bits - 1:
            small = small.astype(BF16)
    grad_reduce = grad_reduce.reshape(units // inner, channels)
    grad_expand = grad_expand.reshape(expand_rows // inner, hid)
    grad_kernel = small[:49].reshape(7, 7, channels)
    return (disagreement, grad_expand, grad_reduce, grad_kernel, small[49], small[50])


def solution(mesh):
    in_specs = (P("groups", "col", None), P("col", None), P(), P(), P(), P(), P())
    out_specs = (
        P("groups", "col", None),
        P(("groups", "col"), None),
        P(("groups", "col"), None),
        P("groups", None, None),
        P("groups"),
        P("groups"),
    )
    return jax.shard_map(
        on_device, mesh=mesh, in_specs=in_specs, out_specs=out_specs, check_vma=False
    )
```

```python
import functools
import math

import jax
import jax.numpy as jnp
from jax import lax
from jax.experimental import pallas as pl
from jax.experimental.pallas import tpu as pltpu
from jax.sharding import PartitionSpec as P

BF16 = jnp.bfloat16
F32 = jnp.float32
LANES = 128
VMEM_LIMIT = 56 << 20


def phi_parts(pre):
    decay = jnp.exp(-0.5 * pre * pre)
    t = 1.0 / (1.0 + 0.23164189 * jnp.abs(pre))
    poly = 0.5307027145 * t - 0.7265760135
    poly = poly * t + 0.7107068705
    poly = poly * t - 0.142248368
    poly = poly * t + 0.127414796
    tail = poly * t * decay
    return jnp.where(pre < 0.0, tail, 1.0 - tail), decay * 0.3989422804014327


def params(flops, read):
    return dict(
        compiler_params=pltpu.CompilerParams(vmem_limit_bytes=VMEM_LIMIT),
        cost_estimate=pl.CostEstimate(flops=flops, bytes_accessed=read, transcendentals=0),
    )


def whole(*dims):
    return pl.BlockSpec(dims, lambda *_: (0,) * len(dims))


def dot(lhs, rhs, contract):
    return lax.dot_general(lhs, rhs, (contract, ((), ())), preferred_element_type=F32)


def conv_body(feat, table, mirror, low, high, dw, gain, normed, nhat, inv, wide, taps, conv):
    rows, cols, channels = feat.shape
    own = feat[...].astype(F32)
    straight = table[...].astype(F32)
    turned = mirror[...].astype(F32)
    turned = jnp.concatenate([turned[c : c + 1] for c in reversed(range(cols))], axis=0)
    for v, add in enumerate((straight, turned)):
        wide[v, :, 3 : 3 + cols, :] = (own + add[None]).astype(BF16).astype(F32)
        wide[v, :, 0:3, :] = low[v].astype(F32)
        wide[v, :, 3 + cols : 6 + cols, :] = high[v].astype(F32)
    for i in range(7):
        taps[7 * i : 7 * i + 7, :] = dw[i].astype(F32)

    def tile(c, carry):
        lanes = pl.ds(pl.multiple_of(c * LANES, LANES), LANES)
        sums = [[jnp.zeros((cols, LANES), F32) for _ in range(rows)] for _ in range(2)]
        for j in range(7):
            for v in range(2):
                part = [wide[v, r, pl.ds(j, cols), lanes] for r in range(rows)]
                for i in range(7):
                    weight = taps[pl.ds(7 * i + (6 - j if v else j), 1), lanes]
                    for r in range(rows):
                        if 0 <= r + i - 3 < rows:
                            sums[v][r] = sums[v][r] + weight * part[r + i - 3]
        for v in range(2):
            for r in range(rows):
                conv[v, r, :, lanes] = sums[v][r]
        return carry

    lax.fori_loop(0, channels // LANES, tile, 0)
    for v in range(2):
        value = conv[v].reshape(rows * cols, channels)
        centred = value - jnp.mean(value, axis=-1, keepdims=True)
        inverse = lax.rsqrt(jnp.mean(centred * centred, axis=-1, keepdims=True) + 1e-06)
        value = centred * inverse
        nhat[v] = value
        inv[v] = jnp.broadcast_to(inverse, (rows * cols, LANES))
        normed[v] = (value * gain[...].reshape(1, channels)).astype(BF16)


def conv_norm(features, table, mirror, low, high, dw, gain):
    rows, cols, channels = features.shape
    pixels = rows * cols
    return pl.pallas_call(
        conv_body,
        out_shape=(
            jax.ShapeDtypeStruct((2, pixels, channels), BF16),
            jax.ShapeDtypeStruct((2, pixels, channels), F32),
            jax.ShapeDtypeStruct((2, pixels, LANES), F32),
            jax.ShapeDtypeStruct((2, rows, 16, channels), F32),
        ),
        scratch_shapes=[
            pltpu.VMEM((49, channels), F32),
            pltpu.VMEM((2, rows, cols, channels), F32),
        ],
        name="conv_norm",
        **params(4 * 10**9, 10**7),
    )(features, table, mirror, low, high, dw, gain)


def forward_body(scale, normed, expand, reduce, wide, ls, slope, diff, disagreement, dbranch, gscale, acc):
    step = pl.program_id(0)
    pixels, channels = normed.shape
    rows, cols, _ = disagreement.shape
    pre = dot(normed[...], expand[...], ((1,), (0,)))
    cdf, density = phi_parts(pre)
    slope[...] = (cdf + pre * density).astype(BF16)
    hidden = (pre * cdf).astype(BF16)
    half = pixels // 2
    diff[...] = (hidden[:half].astype(F32) - hidden[half:].astype(F32)).astype(BF16)
    part = dot(hidden, reduce[...], ((1,), (0,)))

    @pl.when(step == 0)
    def _():
        acc[...] = part

    @pl.when(step > 0)
    def _():
        acc[...] += part

    @pl.when(step == pl.num_programs(0) - 1)
    def _():
        outs = []
        for v in range(2):
            own = wide[v, :, 3 : 3 + cols, :].reshape(half, channels)
            branch = acc[v * half : (v + 1) * half, :]
            outs.append((own + ls[...].reshape(1, channels) * branch).astype(BF16).astype(F32))
        difference = outs[0] - outs[1]
        disagreement[...] = difference.astype(BF16).reshape(rows, cols, channels)
        residual = (difference * scale).astype(BF16).astype(F32)
        gscale[...] = jnp.sum((acc[:half, :] - acc[half:, :]) * residual, axis=0, keepdims=True)
        dbranch[...] = (ls[...].reshape(1, channels) * residual).astype(BF16)


def forward(scale, normed, expand, reduce, wide, ls, shape):
    pixels, channels = normed.shape
    hid = expand.shape[1]
    block = 512
    return pl.pallas_call(
        functools.partial(forward_body, scale),
        grid=(hid // block,),
        in_specs=[
            whole(pixels, channels),
            pl.BlockSpec((channels, block), lambda j: (0, j)),
            pl.BlockSpec((block, channels), lambda j: (j, 0)),
            whole(*wide.shape),
            whole(channels),
        ],
        out_specs=[
            pl.BlockSpec((pixels, block), lambda j: (0, j)),
            pl.BlockSpec((pixels // 2, block), lambda j: (0, j)),
            whole(*shape),
            whole(pixels // 2, channels),
            whole(1, channels),
        ],
        out_shape=(
            jax.ShapeDtypeStruct((pixels, hid), BF16),
            jax.ShapeDtypeStruct((pixels // 2, hid), BF16),
            jax.ShapeDtypeStruct(shape, BF16),
            jax.ShapeDtypeStruct((pixels // 2, channels), BF16),
            jax.ShapeDtypeStruct((1, channels), F32),
        ),
        scratch_shapes=[pltpu.VMEM((pixels, channels), F32)],
        name="forward",
        **params(6 * 10**9, 2 * 10**7),
    )(normed, expand, reduce, wide, ls)


def backward_body(dbranch, slope, expand, reduce, nhat, inv, gain, gscale, wide, out, acc, small):
    step = pl.program_id(0)
    half, channels = dbranch.shape
    _, rows, _, _ = wide.shape
    cols = half // rows
    dhidden = dot(dbranch[...], reduce[...], ((1,), (1,)))
    dpre = jnp.concatenate(
        [dhidden * slope[:half, :].astype(F32), -dhidden * slope[half:, :].astype(F32)]
    ).astype(BF16)
    part = dot(dpre, expand[...], ((1,), (1,)))

    @pl.when(step == 0)
    def _():
        acc[...] = part

    @pl.when(step > 0)
    def _():
        acc[...] += part

    @pl.when(step == pl.num_programs(0) - 1)
    def _():
        ggain = jnp.zeros((1, channels), F32)
        for v in range(2):
            here = slice(v * half, (v + 1) * half)
            dnormed = acc[here, :]
            ggain = ggain + jnp.sum(dnormed * nhat[v], axis=0, keepdims=True)
            scaled = dnormed * gain[...].reshape(1, channels)
            gm = jnp.mean(scaled, axis=-1, keepdims=True)
            gn = jnp.mean(scaled * nhat[v], axis=-1, keepdims=True)
            acc[here, :] = inv[v][:, :1] * (scaled - gm - nhat[v] * gn)
        small[49:50, :] = ggain
        small[50:51, :] = gscale[...]

        def tile(c, carry):
            lanes = pl.ds(pl.multiple_of(c * LANES, LANES), LANES)
            dconv = [
                [acc[pl.ds(v * half + r * cols, cols), lanes] for r in range(rows)] for v in range(2)
            ]
            for j in range(7):
                part = [
                    [wide[v, r, pl.ds(6 - j if v else j, cols), lanes] for r in range(rows)]
                    for v in range(2)
                ]
                for i in range(7):
                    total = None
                    for v in range(2):
                        for r in range(rows):
                            if 0 <= r + i - 3 < rows:
                                term = part[v][r + i - 3] * dconv[v][r]
                                total = term if total is None else total + term
                    small[pl.ds(7 * i + j, 1), lanes] = jnp.sum(total, axis=0, keepdims=True)
            return carry

        lax.fori_loop(0, channels // LANES, tile, 0)
        small[51:, :] = jnp.zeros((small.shape[0] - 51, channels), F32)
        out[...] = small[...].astype(BF16)


def backward(dbranch, slope, expand, reduce, nhat, inv, gain, gscale, wide):
    half, channels = dbranch.shape
    hid = expand.shape[1]
    block = 512
    return pl.pallas_call(
        backward_body,
        grid=(hid // block,),
        in_specs=[
            whole(half, channels),
            pl.BlockSpec((2 * half, block), lambda j: (0, j)),
            pl.BlockSpec((channels, block), lambda j: (0, j)),
            pl.BlockSpec((block, channels), lambda j: (j, 0)),
            whole(*nhat.shape),
            whole(*inv.shape),
            whole(channels),
            whole(1, channels),
            whole(*wide.shape),
        ],
        out_specs=whole(64, channels),
        out_shape=jax.ShapeDtypeStruct((64, channels), BF16),
        scratch_shapes=[pltpu.VMEM((2 * half, channels), F32), pltpu.VMEM((64, channels), F32)],
        name="backward",
        **params(9 * 10**9, 3 * 10**7),
    )(dbranch, slope, expand, reduce, nhat, inv, gain, gscale, wide)


def remote_body(normed_1, normed_2, normed_3, expand, slope, diff):
    _, half, channels = normed_1.shape
    every = [ref[...].reshape(2 * half, channels) for ref in (normed_1, normed_2, normed_3)]
    for p in range(3):
        pre = dot(every[p], expand[...], ((1,), (0,)))
        cdf, density = phi_parts(pre)
        slope[p] = (cdf + pre * density).astype(BF16)
        hidden = (pre * cdf).astype(BF16).astype(F32)
        diff[p * half : (p + 1) * half, :] = (hidden[:half] - hidden[half:]).astype(BF16)


def remote_slopes(others, expand):
    _, half, channels = others[0].shape
    hid = expand.shape[1]
    block = 512
    return pl.pallas_call(
        remote_body,
        grid=(hid // block,),
        in_specs=[whole(2, half, channels)] * 3
        + [pl.BlockSpec((channels, block), lambda j: (0, j))],
        out_specs=[
            pl.BlockSpec((3, 2 * half, block), lambda j: (0, 0, j)),
            pl.BlockSpec((3 * half, block), lambda j: (0, j)),
        ],
        out_shape=(
            jax.ShapeDtypeStruct((3, 2 * half, hid), BF16),
            jax.ShapeDtypeStruct((3 * half, hid), BF16),
        ),
        name="remote_slopes",
        **params(7 * 10**9, 10**7),
    )(*others, expand)


def reduce_grad_body(where, d_0, d_1, d_23, diff_0, diff_rest, small, keep, send, total):
    half, channels = d_0.shape
    parts = keep.shape[0]
    rows = keep.shape[1]
    total[...] = dot(diff_0[...], d_0[...], ((0,), (0,)))
    rest = jnp.concatenate([d_1[...], d_23[: 2 * half, :]])
    total[...] += dot(diff_rest[...], rest, ((0,), (0,)))
    side = where[1]
    for x in range(parts):
        mine = pl.multiple_of((2 * x + side) * rows, 16)
        theirs = pl.multiple_of((2 * x + 1 - side) * rows, 16)
        keep[x] = total[pl.ds(mine, rows), :]
        send[x * rows : (x + 1) * rows, :] = total[pl.ds(theirs, rows), :].astype(BF16)
    send[parts * rows :, :] = small[...]


def reduce_grad(where, d_0, d_1, d_23, diff_0, diff_rest, small, line, inner):
    half, channels = d_0.shape
    units = diff_0.shape[1] // line
    rows = units // inner
    own = lambda height: pl.BlockSpec((height, units), lambda j, where: (0, where[0]))
    return pl.pallas_call(
        reduce_grad_body,
        grid_spec=pltpu.PrefetchScalarGridSpec(
            num_scalar_prefetch=1,
            grid=(1,),
            in_specs=[
                whole(*d_0.shape),
                whole(*d_1.shape),
                whole(*d_23.shape),
                own(half),
                own(3 * half),
                whole(*small.shape),
            ],
            out_specs=[
                whole(inner // 2, rows, channels),
                whole(units // 2 + small.shape[0], channels),
            ],
            scratch_shapes=[pltpu.VMEM((units, channels), F32)],
        ),
        out_shape=(
            jax.ShapeDtypeStruct((inner // 2, rows, channels), F32),
            jax.ShapeDtypeStruct((units // 2 + small.shape[0], channels), BF16),
        ),
        name="reduce_grad",
        **params(10**9, 4 * 10**6),
    )(where, d_0, d_1, d_23, diff_0, diff_rest, small)


def expand_grad_body(where, d_0, d_1, d_23, slope_0, slope_rest, reduce, normed, keep, send, dpre, total):
    half, channels = d_0.shape
    parts, rows, _ = keep.shape
    every = jnp.concatenate([d_0[...], d_1[...], d_23[: 2 * half, :]])
    dhidden = dot(every, reduce[...], ((1,), (1,)))
    for p in range(4):
        here = dhidden[p * half : (p + 1) * half]
        slope = (slope_rest[p - 1] if p else slope_0[...]).astype(F32)
        dpre[2 * p * half : (2 * p + 1) * half, :] = (here * slope[:half]).astype(BF16)
        dpre[(2 * p + 1) * half : (2 * p + 2) * half, :] = (-here * slope[half:]).astype(BF16)
    total[...] = dot(normed[...], dpre[...], ((0,), (0,)))
    side = where[1]
    for x in range(parts):
        mine = pl.multiple_of((2 * x + side) * rows, 16)
        theirs = pl.multiple_of((2 * x + 1 - side) * rows, 16)
        keep[x] = total[pl.ds(mine, rows), :]
        send[x] = total[pl.ds(theirs, rows), :].astype(BF16)


def expand_grad(where, d_0, d_1, d_23, slope_0, slope_rest, reduce, normed, inner):
    half, channels = d_0.shape
    hid = reduce.shape[0]
    block = 512
    own = normed.shape[1]
    rows = own // inner
    return pl.pallas_call(
        expand_grad_body,
        grid_spec=pltpu.PrefetchScalarGridSpec(
            num_scalar_prefetch=1,
            grid=(hid // block,),
            in_specs=[
                whole(*d_0.shape),
                whole(*d_1.shape),
                whole(*d_23.shape),
                pl.BlockSpec((2 * half, block), lambda j, where: (0, j)),
                pl.BlockSpec((3, 2 * half, block), lambda j, where: (0, 0, j)),
                pl.BlockSpec((block, channels), lambda j, where: (j, 0)),
                whole(*normed.shape),
            ],
            out_specs=[
                pl.BlockSpec((inner // 2, rows, block), lambda j, where: (0, 0, j)),
                pl.BlockSpec((inner // 2, rows, block), lambda j, where: (0, 0, j)),
            ],
            scratch_shapes=[
                pltpu.VMEM((8 * half, block), BF16),
                pltpu.VMEM((own, block), F32),
            ],
        ),
        out_shape=(
            jax.ShapeDtypeStruct((inner // 2, rows, hid), F32),
            jax.ShapeDtypeStruct((inner // 2, rows, hid), BF16),
        ),
        name="expand_grad",
        **params(4 * 10**9, 10**7),
    )(where, d_0, d_1, d_23, slope_0, slope_rest, reduce, normed)


def grads_plain(every, dbranch_all, expand_weight, reduce_weight, my_line, my_inner, line, inner):
    channels, hid = expand_weight.shape
    units, own = hid // line, channels // line
    every = every.reshape(-1, channels)
    pre = dot(every, expand_weight, ((1,), (0,)))
    cdf, density = phi_parts(pre)
    slope = (cdf + pre * density).reshape(line, 2, -1, hid)
    hidden = (pre * cdf).astype(BF16).astype(F32).reshape(line, 2, -1, hid)
    diff = (hidden[:, 0] - hidden[:, 1]).astype(BF16).reshape(-1, hid)
    diff = lax.dynamic_slice_in_dim(diff, my_line * units, units, 1)
    dhidden = dot(dbranch_all, reduce_weight, ((1,), (1,))).reshape(line, -1, hid)
    dpre = jnp.stack([dhidden * slope[:, 0], -dhidden * slope[:, 1]], axis=1)
    dpre = dpre.astype(BF16).reshape(-1, hid)
    normed_own = lax.dynamic_slice_in_dim(every, my_line * own, own, 1)
    expand = dot(normed_own, dpre, ((0,), (0,))).reshape(inner, own // inner, hid)
    reduce = dot(diff, dbranch_all, ((0,), (0,))).reshape(inner, units // inner, channels)
    return halves(expand, my_inner & 1), halves(reduce, my_inner & 1)


def halves(part, side):
    part = part.reshape((part.shape[0] // 2, 2) + part.shape[1:])
    keep = lax.dynamic_index_in_dim(part, side, 1, keepdims=False)
    send = lax.dynamic_index_in_dim(part, 1 - side, 1, keepdims=False)
    return keep, send.astype(BF16)


def on_device(
    features, column_table, dw_kernel, norm_gain, expand_weight, reduce_weight, layer_scale
):
    rows, cols, channels = features.shape
    hid = expand_weight.shape[1]
    count = lax.axis_size("col")
    bits = count.bit_length() - 1
    line = 1 << ((bits + 1) // 2)
    inner = count // line
    inner_bits = inner.bit_length() - 1
    line_bits = bits - inner_bits
    me = lax.axis_index("col")
    my_line, my_inner = me // inner, me % inner
    units, own = hid // line, channels // line
    total_cols = cols * count

    def swapped(block, mask):
        return lax.ppermute(block, "col", [(d, d ^ mask) for d in range(count)])

    mirror = lax.ppermute(column_table, "col", [(d, count - 1 - d) for d in range(count)])

    def edge(here, there):
        pair = jnp.stack([column_table[here], mirror[there][::-1]]).astype(F32)
        return (features[:, here].astype(F32) + pair[:, None]).astype(BF16)

    low = lax.ppermute(
        edge(slice(cols - 3, cols), slice(0, 3)), "col", [(d, d + 1) for d in range(count - 1)]
    )
    high = lax.ppermute(
        edge(slice(0, 3), slice(cols - 3, cols)), "col", [(d + 1, d) for d in range(count - 1)]
    )
    normed, nhat, inv, wide = conv_norm(
        features, column_table, mirror, low, high, dw_kernel, norm_gain
    )
    others = [swapped(normed, p * inner) for p in range(1, line)]
    slope, diff, disagreement, dbranch, gscale = forward(
        1.0 / math.sqrt(rows * total_cols),
        normed.reshape(-1, channels),
        expand_weight,
        reduce_weight,
        wide,
        layer_scale,
        features.shape,
    )
    small = backward(
        dbranch, slope, expand_weight, reduce_weight, nhat, inv, norm_gain, gscale, wide
    )
    held = dbranch
    for bit in range(line_bits - 1):
        fresh = swapped(held, inner << bit)
        held = jnp.concatenate([held, fresh])
    last = swapped(jnp.concatenate([held, small]), inner << (line_bits - 1))
    small = small.astype(F32) + last[held.shape[0] :].astype(F32)
    for bit in range(line_bits - 1):
        small = small.astype(BF16)
        small = small.astype(F32) + swapped(small, inner << bit).astype(F32)
    small = small.astype(BF16)

    if line == 4 and units % LANES == 0:
        where = jnp.stack([my_line, my_inner & 1]).astype(jnp.int32)
        slope_rest, diff_rest = remote_slopes(others, expand_weight)
        keep_r, send_r = reduce_grad(
            where, dbranch, fresh, last, diff, diff_rest, small, line, inner
        )
        normed_own = jnp.concatenate(
            [
                lax.dynamic_slice_in_dim(block.reshape(-1, channels), my_line * own, own, 1)
                for block in [normed] + others
            ]
        )
        keep_e, send_e = expand_grad(
            where, dbranch, fresh, last, slope, slope_rest, reduce_weight, normed_own, inner
        )
    else:
        (keep_e, send_e), (keep_r, send_r) = grads_plain(
            jnp.stack([normed] + others),
            jnp.concatenate([held, last[: held.shape[0]]]),
            expand_weight,
            reduce_weight,
            my_line,
            my_inner,
            line,
            inner,
        )
        send_r = jnp.concatenate([send_r.reshape(-1, channels), small])

    for bit in range(inner_bits):
        got_r, got_e = swapped(send_r, 1 << bit), swapped(send_e, 1 << bit)
        cut = got_r.shape[0] - small.shape[0]
        sum_r = keep_r + got_r[:cut].reshape(keep_r.shape).astype(F32)
        sum_e = keep_e + got_e.astype(F32)
        small = small.astype(F32) + got_r[cut:].astype(F32)
        if bit < inner_bits - 1:
            small = small.astype(BF16)
            side = (my_inner >> (bit + 1)) & 1
            keep_r, send_r = halves(sum_r, side)
            keep_e, send_e = halves(sum_e, side)
            send_r = jnp.concatenate([send_r.reshape(-1, channels), small])
    grad_kernel = small[:49].reshape(7, 7, channels)
    return (
        disagreement,
        sum_e.reshape(own // inner, hid),
        sum_r.reshape(units // inner, channels),
        grad_kernel,
        small[49],
        small[50],
    )


def solution(mesh):
    in_specs = (P("groups", "col", None), P("col", None), P(), P(), P(), P(), P())
    out_specs = (
        P("groups", "col", None),
        P(("groups", "col"), None),
        P(("groups", "col"), None),
        P("groups", None, None),
        P("groups"),
        P("groups"),
    )
    return jax.shard_map(
        on_device, mesh=mesh, in_specs=in_specs, out_specs=out_specs, check_vma=False
    )
```

```python
import functools
import math

import jax
import jax.numpy as jnp
from jax import lax
from jax.experimental import pallas as pl
from jax.experimental.pallas import tpu as pltpu
from jax.sharding import PartitionSpec as P

BF16 = jnp.bfloat16
F32 = jnp.float32
LANES = 128
VMEM_GRANT = 16 << 20
BLOCK = 512


def phi_parts(pre):
    decay = jnp.exp(-0.5 * pre * pre)
    t = 1.0 / (1.0 + 0.23164189 * jnp.abs(pre))
    poly = 0.5307027145 * t - 0.7265760135
    poly = poly * t + 0.7107068705
    poly = poly * t - 0.142248368
    poly = poly * t + 0.127414796
    tail = poly * t * decay
    return jnp.where(pre < 0.0, tail, 1.0 - tail), decay * 0.3989422804014327


def call(body, name, flops, out_shape, scratch, *operands, scalars=0):
    spaces = [pltpu.SMEM] * scalars + [pltpu.VMEM] * (len(operands) - scalars)
    return pl.pallas_call(
        body,
        in_specs=[pl.BlockSpec(memory_space=space) for space in spaces],
        out_specs=[pl.BlockSpec(memory_space=pltpu.VMEM) for _ in out_shape],
        out_shape=[jax.ShapeDtypeStruct(shape, dtype) for shape, dtype in out_shape],
        scratch_shapes=[pltpu.VMEM(shape, dtype) for shape, dtype in scratch],
        compiler_params=pltpu.CompilerParams(vmem_limit_bytes=VMEM_GRANT),
        cost_estimate=pl.CostEstimate(flops=flops, bytes_accessed=10**8, transcendentals=0),
        name=name,
    )(*operands)


def dot(lhs, rhs, contract):
    return lax.dot_general(lhs, rhs, (contract, ((), ())), preferred_element_type=F32)


def conv_body(feat, table, mirror, low, high, dw, gain, normed, nhat, inv, wide, taps, conv):
    rows, cols, channels = feat.shape
    own = feat[...].astype(F32)
    straight = table[...].astype(F32)
    turned = mirror[...].astype(F32)
    turned = jnp.concatenate([turned[c : c + 1] for c in reversed(range(cols))], axis=0)
    for v, add in enumerate((straight, turned)):
        wide[v, :, 3 : 3 + cols, :] = (own + add[None]).astype(BF16).astype(F32)
        wide[v, :, 0:3, :] = low[v].astype(F32)
        wide[v, :, 3 + cols : 6 + cols, :] = high[v].astype(F32)
    for i in range(7):
        taps[7 * i : 7 * i + 7, :] = dw[i].astype(F32)

    def tile(c, carry):
        lanes = pl.ds(pl.multiple_of(c * LANES, LANES), LANES)
        sums = [[jnp.zeros((cols, LANES), F32) for _ in range(rows)] for _ in range(2)]
        for j in range(7):
            for v in range(2):
                part = [wide[v, r, pl.ds(j, cols), lanes] for r in range(rows)]
                for i in range(7):
                    weight = taps[pl.ds(7 * i + (6 - j if v else j), 1), lanes]
                    for r in range(rows):
                        if 0 <= r + i - 3 < rows:
                            sums[v][r] = sums[v][r] + weight * part[r + i - 3]
        for v in range(2):
            for r in range(rows):
                conv[v, r, :, lanes] = sums[v][r]
        return carry

    lax.fori_loop(0, channels // LANES, tile, 0)
    for v in range(2):
        value = conv[v].reshape(rows * cols, channels)
        centred = value - jnp.mean(value, axis=-1, keepdims=True)
        inverse = lax.rsqrt(jnp.mean(centred * centred, axis=-1, keepdims=True) + 1e-06)
        value = centred * inverse
        nhat[v] = value
        inv[v] = jnp.broadcast_to(inverse, (rows * cols, LANES))
        normed[v] = (value * gain[...].reshape(1, channels)).astype(BF16)


def conv_norm(features, table, mirror, low, high, dw, gain):
    rows, cols, channels = features.shape
    pixels = rows * cols
    return call(
        conv_body,
        "conv_norm",
        4 * 10**9,
        [
            ((2, pixels, channels), BF16),
            ((2, pixels, channels), F32),
            ((2, pixels, LANES), F32),
            ((2, rows, 16, channels), F32),
        ],
        [((49, channels), F32), ((2, rows, cols, channels), F32)],
        features,
        table,
        mirror,
        low,
        high,
        dw,
        gain,
    )


def blocks(total):
    return [slice(at, at + BLOCK) for at in range(0, total, BLOCK)]


def forward_body(
    scale, normed, expand, reduce, wide, ls, slope, diff, disagreement, dbranch, gscale, hidden
):
    pixels, channels = normed.shape
    half = pixels // 2
    rows, cols, _ = disagreement.shape
    for here in blocks(expand.shape[1]):
        pre = dot(normed[...], expand[:, here], ((1,), (0,)))
        cdf, density = phi_parts(pre)
        slope[:, here] = (cdf + pre * density).astype(BF16)
        act = (pre * cdf).astype(BF16)
        hidden[:, here] = act
        act = act.astype(F32)
        diff[:, here] = (act[:half] - act[half:]).astype(BF16)
    branch = dot(hidden[...], reduce[...], ((1,), (0,)))
    factor = ls[...].reshape(1, channels)
    outs = []
    for v in range(2):
        own = wide[v, :, 3 : 3 + cols, :].reshape(half, channels)
        outs.append((own + factor * branch[v * half : (v + 1) * half]).astype(BF16).astype(F32))
    difference = outs[0] - outs[1]
    disagreement[...] = difference.astype(BF16).reshape(rows, cols, channels)
    residual = (difference * scale).astype(BF16).astype(F32)
    gscale[...] = jnp.sum((branch[:half] - branch[half:]) * residual, axis=0, keepdims=True)
    dbranch[...] = (factor * residual).astype(BF16)


def forward(scale, normed, expand, reduce, wide, ls, shape):
    pixels, channels = normed.shape
    hid = expand.shape[1]
    return call(
        functools.partial(forward_body, scale),
        "forward",
        6 * 10**9,
        [
            ((pixels, hid), BF16),
            ((pixels // 2, hid), BF16),
            (shape, BF16),
            ((pixels // 2, channels), BF16),
            ((1, channels), F32),
        ],
        [((pixels, hid), BF16)],
        normed,
        expand,
        reduce,
        wide,
        ls,
    )


def backward_body(
    dbranch, slope, expand, reduce, nhat, inv, gain, gscale, wide, out, dpre, grad, taps, small
):
    half, channels = dbranch.shape
    _, rows, _, _ = wide.shape
    cols = half // rows
    for here in blocks(expand.shape[1]):
        dhidden = dot(dbranch[...], reduce[here, :], ((1,), (1,)))
        dpre[:half, here] = (dhidden * slope[:half, here].astype(F32)).astype(BF16)
        dpre[half:, here] = (-dhidden * slope[half:, here].astype(F32)).astype(BF16)
    dnormed = dot(dpre[...], expand[...], ((1,), (1,)))
    factor = gain[...].reshape(1, channels)
    ggain = jnp.zeros((1, channels), F32)
    for v in range(2):
        here = slice(v * half, (v + 1) * half)
        ggain = ggain + jnp.sum(dnormed[here] * nhat[v], axis=0, keepdims=True)
        scaled = dnormed[here] * factor
        gm = jnp.mean(scaled, axis=-1, keepdims=True)
        gn = jnp.mean(scaled * nhat[v], axis=-1, keepdims=True)
        grad[here, :] = inv[v][:, :1] * (scaled - gm - nhat[v] * gn)

    def tile(c, carry):
        lanes = pl.ds(pl.multiple_of(c * LANES, LANES), LANES)
        dconv = [
            [grad[pl.ds(v * half + r * cols, cols), lanes] for r in range(rows)] for v in range(2)
        ]
        for j in range(7):
            part = [
                [wide[v, r, pl.ds(6 - j if v else j, cols), lanes] for r in range(rows)]
                for v in range(2)
            ]
            for i in range(7):
                sums = []
                for v in range(2):
                    total = None
                    for r in range(rows):
                        if 0 <= r + i - 3 < rows:
                            term = part[v][r + i - 3] * dconv[v][r]
                            total = term if total is None else total + term
                    sums.append(total)
                at = 8 * (7 * i + j)
                taps[at : at + 8, :] = sums[0] + sums[1]
        rolled = taps[pl.ds(0, 49, stride=8), :]
        for s in range(1, 8):
            rolled = rolled + taps[pl.ds(s, 49, stride=8), :]
        small[:49, lanes] = rolled
        return carry

    small[...] = jnp.zeros(small.shape, F32)
    lax.fori_loop(0, channels // LANES, tile, 0)
    small[49:50, :] = ggain
    small[50:51, :] = gscale[...]
    out[...] = small[...].astype(BF16)


def backward(dbranch, slope, expand, reduce, nhat, inv, gain, gscale, wide):
    half, channels = dbranch.shape
    hid = expand.shape[1]
    return call(
        backward_body,
        "backward",
        9 * 10**9,
        [((64, channels), BF16)],
        [
            ((2 * half, hid), BF16),
            ((2 * half, channels), F32),
            ((8 * 49, LANES), F32),
            ((64, channels), F32),
        ],
        dbranch,
        slope,
        expand,
        reduce,
        nhat,
        inv,
        gain,
        gscale,
        wide,
    )[0]


def remote_body(normed_1, normed_2, normed_3, expand, slope, diff):
    _, half, channels = normed_1.shape
    every = [ref[...].reshape(2 * half, channels) for ref in (normed_1, normed_2, normed_3)]
    for here in blocks(expand.shape[1]):
        for p in range(3):
            pre = dot(every[p], expand[:, here], ((1,), (0,)))
            cdf, density = phi_parts(pre)
            slope[p, :, here] = (cdf + pre * density).astype(BF16)
            act = (pre * cdf).astype(BF16).astype(F32)
            diff[p * half : (p + 1) * half, here] = (act[:half] - act[half:]).astype(BF16)


def remote_slopes(others, expand):
    _, half, channels = others[0].shape
    hid = expand.shape[1]
    return call(
        remote_body,
        "remote_slopes",
        7 * 10**9,
        [((3, 2 * half, hid), BF16), ((3 * half, hid), BF16)],
        [],
        *others,
        expand,
    )


def reduce_grad_body(
    where, d_0, d_1, d_2, d_3, diff_0, diff_rest, small, keep, send, total
):
    units = total.shape[0]
    parts, rows, _ = keep.shape
    lanes = pl.ds(pl.multiple_of(where[0] * units, LANES), units)
    diff = jnp.concatenate([diff_0[:, lanes], diff_rest[:, lanes]])
    every = jnp.concatenate([d_0[...], d_1[...], d_2[...], d_3[...]])
    total[...] = dot(diff, every, ((0,), (0,)))
    for x in range(parts):
        mine = pl.multiple_of((2 * x + where[1]) * rows, 16)
        theirs = pl.multiple_of((2 * x + 1 - where[1]) * rows, 16)
        keep[x] = total[pl.ds(mine, rows), :]
        send[x * rows : (x + 1) * rows, :] = total[pl.ds(theirs, rows), :].astype(BF16)
    send[parts * rows :, :] = small[...]


def reduce_grad(where, dbranch, diff_0, diff_rest, small, line, inner):
    _, channels = dbranch[0].shape
    units = diff_0.shape[1] // line
    parts, rows = inner // 2, units // inner
    return call(
        reduce_grad_body,
        "reduce_grad",
        2 * 10**9,
        [
            ((parts, rows, channels), F32),
            ((parts * rows + small.shape[0], channels), BF16),
        ],
        [((units, channels), F32)],
        where,
        *dbranch,
        diff_0,
        diff_rest,
        small,
        scalars=1,
    )


def expand_slopes_body(
    where, d_0, d_1, d_2, d_3, slope_0, slope_rest, reduce, n_0, n_1, n_2, n_3, turned, dpre
):
    half, channels = d_0.shape
    width = turned.shape[0]
    start = where[0] * (channels // 4) // LANES * LANES
    lanes = pl.ds(pl.multiple_of(start, LANES), width)
    for p, ref in enumerate((n_0, n_1, n_2, n_3)):
        for v in range(2):
            at = (2 * p + v) * half
            turned[:, at : at + half] = ref[v, :, lanes].astype(F32).T.astype(BF16)
    every = jnp.concatenate([d_0[...], d_1[...], d_2[...], d_3[...]])
    for here in blocks(reduce.shape[0]):
        dhidden = dot(every, reduce[here, :], ((1,), (1,)))
        for p in range(4):
            part = dhidden[p * half : (p + 1) * half]
            slope = (slope_rest[p - 1, :, here] if p else slope_0[:, here]).astype(F32)
            at = 2 * p * half
            dpre[at : at + half, here] = (part * slope[:half]).astype(BF16)
            dpre[at + half : at + 2 * half, here] = (-part * slope[half:]).astype(BF16)


def expand_slopes(where, dbranch, slope_0, slope_rest, reduce, normed):
    half, _ = dbranch[0].shape
    hid = reduce.shape[0]
    return call(
        expand_slopes_body,
        "expand_slopes",
        4 * 10**9,
        [((2 * LANES, 8 * half), BF16), ((8 * half, hid), BF16)],
        [],
        where,
        *dbranch,
        slope_0,
        slope_rest,
        reduce,
        *normed,
        scalars=1,
    )


def expand_grad_body(
    where, turned, dpre, kept, got, small, keep, send, keep_r, send_r, small_sum, total
):
    own, hid = total.shape
    parts, rows, _ = keep.shape
    high = kept.shape[1]
    first = where[0] * own
    lhs = turned[pl.ds(pl.multiple_of(first - first // LANES * LANES, 16), own), :]
    for here in blocks(hid):
        total[:, here] = dot(lhs, dpre[:, here], ((1,), (0,)))
    for x in range(parts):
        mine = pl.multiple_of((2 * x + where[1]) * rows, 16)
        theirs = pl.multiple_of((2 * x + 1 - where[1]) * rows, 16)
        keep[x] = total[pl.ds(mine, rows), :]
        send[x] = total[pl.ds(theirs, rows), :].astype(BF16)
    mine, theirs = where[2], 1 - where[2]
    here = lambda x: pl.ds(pl.multiple_of(x * high, 16), high)
    keep_r[...] = kept[mine] + got[here(mine), :].astype(F32)
    send_r[:high, :] = (kept[theirs] + got[here(theirs), :].astype(F32)).astype(BF16)
    value = (small[...].astype(F32) + got[parts * high :, :].astype(F32)).astype(BF16)
    small_sum[...] = value
    send_r[high:, :] = value


def expand_grad(where, turned, dpre, kept, got, small, own, inner):
    hid = dpre.shape[1]
    _, high, channels = kept.shape
    shape = (inner // 2, own // inner, hid)
    return call(
        expand_grad_body,
        "expand_grad",
        3 * 10**9,
        [
            (shape, F32),
            (shape, BF16),
            ((high, channels), F32),
            ((high + small.shape[0], channels), BF16),
            (small.shape, BF16),
        ],
        [((own, hid), F32)],
        where,
        turned,
        dpre,
        kept,
        got,
        small,
        scalars=1,
    )


def grads_plain(every, dbranch_all, expand_weight, reduce_weight, my_line, my_inner, line, inner):
    channels, hid = expand_weight.shape
    units, own = hid // line, channels // line
    every = every.reshape(-1, channels)
    pre = dot(every, expand_weight, ((1,), (0,)))
    cdf, density = phi_parts(pre)
    slope = (cdf + pre * density).reshape(line, 2, -1, hid)
    hidden = (pre * cdf).astype(BF16).astype(F32).reshape(line, 2, -1, hid)
    diff = (hidden[:, 0] - hidden[:, 1]).astype(BF16).reshape(-1, hid)
    diff = lax.dynamic_slice_in_dim(diff, my_line * units, units, 1)
    dhidden = dot(dbranch_all, reduce_weight, ((1,), (1,))).reshape(line, -1, hid)
    dpre = jnp.stack([dhidden * slope[:, 0], -dhidden * slope[:, 1]], axis=1)
    dpre = dpre.astype(BF16).reshape(-1, hid)
    normed_own = lax.dynamic_slice_in_dim(every, my_line * own, own, 1)
    expand = dot(normed_own, dpre, ((0,), (0,))).reshape(inner, own // inner, hid)
    reduce = dot(diff, dbranch_all, ((0,), (0,))).reshape(inner, units // inner, channels)
    return halves(expand, my_inner & 1), halves(reduce, my_inner & 1)


def halves(part, side):
    part = part.reshape((part.shape[0] // 2, 2) + part.shape[1:])
    keep = lax.dynamic_index_in_dim(part, side, 1, keepdims=False)
    send = lax.dynamic_index_in_dim(part, 1 - side, 1, keepdims=False)
    return keep, send.astype(BF16)


def on_device(
    features, column_table, dw_kernel, norm_gain, expand_weight, reduce_weight, layer_scale
):
    rows, cols, channels = features.shape
    hid = expand_weight.shape[1]
    count = lax.axis_size("col")
    bits = count.bit_length() - 1
    line = 1 << ((bits + 1) // 2)
    inner = count // line
    inner_bits = inner.bit_length() - 1
    me = lax.axis_index("col")
    my_line, my_inner = me // inner, me % inner
    units, own = hid // line, channels // line
    total_cols = cols * count

    def swapped(block, mask):
        return lax.ppermute(block, "col", [(d, d ^ mask) for d in range(count)])

    mirror = lax.ppermute(column_table, "col", [(d, count - 1 - d) for d in range(count)])

    def edge(here, there):
        pair = jnp.stack([column_table[here], mirror[there][::-1]]).astype(F32)
        return (features[:, here].astype(F32) + pair[:, None]).astype(BF16)

    low = lax.ppermute(
        edge(slice(cols - 3, cols), slice(0, 3)), "col", [(d, d + 1) for d in range(count - 1)]
    )
    high = lax.ppermute(
        edge(slice(0, 3), slice(cols - 3, cols)), "col", [(d + 1, d) for d in range(count - 1)]
    )
    normed, nhat, inv, wide = conv_norm(
        features, column_table, mirror, low, high, dw_kernel, norm_gain
    )
    others = [swapped(normed, p * inner) for p in range(1, line)]
    slope, diff, disagreement, dbranch, gscale = forward(
        1.0 / math.sqrt(rows * total_cols),
        normed.reshape(-1, channels),
        expand_weight,
        reduce_weight,
        wide,
        layer_scale,
        features.shape,
    )
    small = backward(
        dbranch, slope, expand_weight, reduce_weight, nhat, inv, norm_gain, gscale, wide
    )
    dbranch_all = [dbranch] + [swapped(dbranch, p * inner) for p in range(1, line)]

    normed_all = [normed] + others

    def line_sum(small):
        sums = [small] + [swapped(small, p * inner) for p in range(1, line)]
        sums = [part.astype(F32) for part in sums]
        while len(sums) > 1:
            sums = [low + high for low, high in zip(sums[::2], sums[1::2])]
        return sums[0]

    if line == 4 and inner == 4 and units % LANES == 0 and own % 64 == 0:
        side = (my_inner >> 1) & 1
        where = jnp.stack([my_line, my_inner & 1, side]).astype(jnp.int32)
        slope_rest, diff_rest = remote_slopes(others, expand_weight)
        keep_r, send_r = reduce_grad(where, dbranch_all, diff, diff_rest, small, line, inner)
        got_r = swapped(send_r, 1)
        turned, dpre = expand_slopes(
            where, dbranch_all, slope, slope_rest, reduce_weight, normed_all
        )
        keep_e, send_e, keep_r, send_r, small = expand_grad(
            where, turned, dpre, keep_r, got_r, small, own, inner
        )
        got_r = swapped(send_r, 2)
        sum_e = keep_e + swapped(send_e, 1).astype(F32)
        keep_e = lax.dynamic_index_in_dim(sum_e, side, 0, keepdims=False)
        send_e = lax.dynamic_index_in_dim(sum_e, 1 - side, 0, keepdims=False)
        got_e = swapped(send_e.astype(BF16), 2)
        sum_r = keep_r + got_r[: keep_r.shape[0]].astype(F32)
        small = small.astype(F32) + got_r[keep_r.shape[0] :].astype(F32)
        small = line_sum(small.astype(BF16))
        sum_e = keep_e + got_e.astype(F32)
    else:
        (keep_e, send_e), (keep_r, send_r) = grads_plain(
            jnp.stack(normed_all),
            jnp.concatenate(dbranch_all),
            expand_weight,
            reduce_weight,
            my_line,
            my_inner,
            line,
            inner,
        )
        small = line_sum(small)
        for bit in range(inner_bits):
            sum_r = keep_r + swapped(send_r, 1 << bit).astype(F32)
            sum_e = keep_e + swapped(send_e, 1 << bit).astype(F32)
            small = small.astype(BF16)
            small = small.astype(F32) + swapped(small, 1 << bit).astype(F32)
            if bit < inner_bits - 1:
                side = (my_inner >> (bit + 1)) & 1
                keep_r, send_r = halves(sum_r, side)
                keep_e, send_e = halves(sum_e, side)
    grad_kernel = small[:49].reshape(7, 7, channels)
    return (
        disagreement,
        sum_e.reshape(own // inner, hid),
        sum_r.reshape(units // inner, channels),
        grad_kernel,
        small[49],
        small[50],
    )


def solution(mesh):
    in_specs = (P("groups", "col", None), P("col", None), P(), P(), P(), P(), P())
    out_specs = (
        P("groups", "col", None),
        P(("groups", "col"), None),
        P(("groups", "col"), None),
        P("groups", None, None),
        P("groups"),
        P("groups"),
    )
    return jax.shard_map(
        on_device, mesh=mesh, in_specs=in_specs, out_specs=out_specs, check_vma=False
    )
```

```python
import functools
import math

import jax
import jax.numpy as jnp
from jax import lax
from jax.experimental import pallas as pl
from jax.experimental.pallas import tpu as pltpu
from jax.sharding import PartitionSpec as P

BF16 = jnp.bfloat16
F32 = jnp.float32
LANES = 128
VMEM_GRANT = 16 << 20
BLOCK = 512


def phi_parts(pre):
    decay = jnp.exp(-0.5 * pre * pre)
    t = 1.0 / (1.0 + 0.23164189 * jnp.abs(pre))
    poly = 0.5307027145 * t - 0.7265760135
    poly = poly * t + 0.7107068705
    poly = poly * t - 0.142248368
    poly = poly * t + 0.127414796
    tail = poly * t * decay
    return jnp.where(pre < 0.0, tail, 1.0 - tail), decay * 0.3989422804014327


def call(body, name, flops, out_shape, scratch, *operands, scalars=0):
    spaces = [pltpu.SMEM] * scalars + [pltpu.VMEM] * (len(operands) - scalars)
    return pl.pallas_call(
        body,
        in_specs=[pl.BlockSpec(memory_space=space) for space in spaces],
        out_specs=[pl.BlockSpec(memory_space=pltpu.VMEM) for _ in out_shape],
        out_shape=[jax.ShapeDtypeStruct(shape, dtype) for shape, dtype in out_shape],
        scratch_shapes=[pltpu.VMEM(shape, dtype) for shape, dtype in scratch],
        compiler_params=pltpu.CompilerParams(vmem_limit_bytes=VMEM_GRANT),
        cost_estimate=pl.CostEstimate(flops=flops, bytes_accessed=10**8, transcendentals=0),
        name=name,
    )(*operands)


def dot(lhs, rhs, contract):
    return lax.dot_general(lhs, rhs, (contract, ((), ())), preferred_element_type=F32)


def flipped(value):
    rows = value.shape[0]
    return jnp.concatenate([value[r : r + 1] for r in reversed(range(rows))], axis=0)


def edges_body(feat, table, mirror, gain, last, first, turned, factor):
    _, cols, channels = feat.shape
    other = flipped(mirror[...].astype(F32))
    for v, add in enumerate((table[...], other)):
        own = (feat[...] + add[None]).astype(BF16)
        last[v] = own[:, cols - 3 :]
        first[v] = own[:, :3]
    turned[...] = other
    factor[...] = gain[...].reshape(1, channels)


def edges(features, table, mirror, gain):
    rows, _, channels = features.shape
    return call(
        edges_body,
        "edges",
        10**8,
        [
            ((2, rows, 3, channels), BF16),
            ((2, rows, 3, channels), BF16),
            (table.shape, F32),
            ((1, channels), F32),
        ],
        [],
        features,
        table,
        mirror,
        gain,
    )


def conv_body(feat, table, turned, low, high, dw, gain, normed, nhat, inv, wide, conv):
    rows, cols, channels = feat.shape
    for v, add in enumerate((table, turned)):
        wide[v, :, 3 : 3 + cols, :] = (feat[...] + add[...][None]).astype(BF16).astype(F32)
        wide[v, :, 0:3, :] = low[v].astype(F32)
        wide[v, :, 3 + cols : 6 + cols, :] = high[v].astype(F32)

    def tile(c, carry):
        lanes = pl.ds(pl.multiple_of(c * LANES, LANES), LANES)
        sums = [[jnp.zeros((cols, LANES), F32) for _ in range(rows)] for _ in range(2)]
        for j in range(7):
            for v in range(2):
                part = [wide[v, r, pl.ds(j, cols), lanes] for r in range(rows)]
                for i in range(7):
                    weight = dw[i, pl.ds(6 - j if v else j, 1), lanes]
                    for r in range(rows):
                        if 0 <= r + i - 3 < rows:
                            sums[v][r] = sums[v][r] + weight * part[r + i - 3]
        for v in range(2):
            for r in range(rows):
                conv[v, r, :, lanes] = sums[v][r]
        return carry

    lax.fori_loop(0, channels // LANES, tile, 0)
    for v in range(2):
        value = conv[v].reshape(rows * cols, channels)
        centred = value - jnp.mean(value, axis=-1, keepdims=True)
        inverse = lax.rsqrt(jnp.mean(centred * centred, axis=-1, keepdims=True) + 1e-06)
        value = centred * inverse
        nhat[v] = value
        inv[v] = jnp.broadcast_to(inverse, (rows * cols, LANES))
        normed[v] = (value * gain[...]).astype(BF16)


def conv_norm(features, table, turned, low, high, dw, gain):
    rows, cols, channels = features.shape
    pixels = rows * cols
    return call(
        conv_body,
        "conv_norm",
        4 * 10**9,
        [
            ((2, pixels, channels), BF16),
            ((2, pixels, channels), F32),
            ((2, pixels, LANES), F32),
            ((2, rows, 16, channels), F32),
        ],
        [((2, rows, cols, channels), F32)],
        features,
        table,
        turned,
        low,
        high,
        dw,
        gain,
    )


def blocks(total):
    return [slice(at, at + BLOCK) for at in range(0, total, BLOCK)]


def forward_body(
    scale, normed, expand, reduce, wide, ls, slope, diff, disagreement, dbranch, gscale, hidden
):
    pixels, channels = normed.shape
    half = pixels // 2
    rows, cols, _ = disagreement.shape
    for here in blocks(expand.shape[1]):
        pre = dot(normed[...], expand[:, here], ((1,), (0,)))
        cdf, density = phi_parts(pre)
        slope[:, here] = (cdf + pre * density).astype(BF16)
        act = (pre * cdf).astype(BF16)
        hidden[:, here] = act
        act = act.astype(F32)
        diff[:, here] = (act[:half] - act[half:]).astype(BF16)
    branch = dot(hidden[...], reduce[...], ((1,), (0,)))
    factor = ls[...].reshape(1, channels)
    outs = []
    for v in range(2):
        own = wide[v, :, 3 : 3 + cols, :].reshape(half, channels)
        outs.append((own + factor * branch[v * half : (v + 1) * half]).astype(BF16).astype(F32))
    difference = outs[0] - outs[1]
    disagreement[...] = difference.astype(BF16).reshape(rows, cols, channels)
    residual = (difference * scale).astype(BF16).astype(F32)
    gscale[...] = jnp.sum((branch[:half] - branch[half:]) * residual, axis=0, keepdims=True)
    dbranch[...] = (factor * residual).astype(BF16)


def forward(scale, normed, expand, reduce, wide, ls, shape):
    pixels, channels = normed.shape
    hid = expand.shape[1]
    return call(
        functools.partial(forward_body, scale),
        "forward",
        6 * 10**9,
        [
            ((pixels, hid), BF16),
            ((pixels // 2, hid), BF16),
            (shape, BF16),
            ((pixels // 2, channels), BF16),
            ((1, channels), F32),
        ],
        [((pixels, hid), BF16)],
        normed,
        expand,
        reduce,
        wide,
        ls,
    )


def backward_body(
    dbranch, slope, expand, reduce, nhat, inv, gain, gscale, wide, out, passed, dpre, grad, taps, small
):
    half, channels = dbranch.shape
    _, rows, _, _ = wide.shape
    cols = half // rows
    for here in blocks(expand.shape[1]):
        dhidden = dot(dbranch[...], reduce[here, :], ((1,), (1,)))
        dpre[:half, here] = (dhidden * slope[:half, here].astype(F32)).astype(BF16)
        dpre[half:, here] = (-dhidden * slope[half:, here].astype(F32)).astype(BF16)
    dnormed = dot(dpre[...], expand[...], ((1,), (1,)))
    factor = gain[...]
    ggain = jnp.zeros((1, channels), F32)
    for v in range(2):
        here = slice(v * half, (v + 1) * half)
        ggain = ggain + jnp.sum(dnormed[here] * nhat[v], axis=0, keepdims=True)
        scaled = dnormed[here] * factor
        gm = jnp.mean(scaled, axis=-1, keepdims=True)
        gn = jnp.mean(scaled * nhat[v], axis=-1, keepdims=True)
        grad[here, :] = inv[v][:, :1] * (scaled - gm - nhat[v] * gn)

    def tile(c, carry):
        lanes = pl.ds(pl.multiple_of(c * LANES, LANES), LANES)
        dconv = [
            [grad[pl.ds(v * half + r * cols, cols), lanes] for r in range(rows)] for v in range(2)
        ]
        for j in range(7):
            part = [
                [wide[v, r, pl.ds(6 - j if v else j, cols), lanes] for r in range(rows)]
                for v in range(2)
            ]
            for i in range(7):
                sums = []
                for v in range(2):
                    total = None
                    for r in range(rows):
                        if 0 <= r + i - 3 < rows:
                            term = part[v][r + i - 3] * dconv[v][r]
                            total = term if total is None else total + term
                    sums.append(total)
                at = 8 * (7 * i + j)
                taps[at : at + 8, :] = sums[0] + sums[1]
        rolled = taps[pl.ds(0, 49, stride=8), :]
        for s in range(1, 8):
            rolled = rolled + taps[pl.ds(s, 49, stride=8), :]
        small[:49, lanes] = rolled
        return carry

    small[...] = jnp.zeros(small.shape, F32)
    lax.fori_loop(0, channels // LANES, tile, 0)
    small[49:50, :] = ggain
    small[50:51, :] = gscale[...]
    out[...] = small[...].astype(BF16)
    passed[...] = dbranch[...]


def backward(dbranch, slope, expand, reduce, nhat, inv, gain, gscale, wide):
    half, channels = dbranch.shape
    hid = expand.shape[1]
    return call(
        backward_body,
        "backward",
        9 * 10**9,
        [((64, channels), BF16), (dbranch.shape, BF16)],
        [
            ((2 * half, hid), BF16),
            ((2 * half, channels), F32),
            ((8 * 49, LANES), F32),
            ((64, channels), F32),
        ],
        dbranch,
        slope,
        expand,
        reduce,
        nhat,
        inv,
        gain,
        gscale,
        wide,
    )


def remote_body(normed_1, normed_2, normed_3, expand, slope, diff):
    _, half, channels = normed_1.shape
    every = [ref[...].reshape(2 * half, channels) for ref in (normed_1, normed_2, normed_3)]
    for here in blocks(expand.shape[1]):
        for p in range(3):
            pre = dot(every[p], expand[:, here], ((1,), (0,)))
            cdf, density = phi_parts(pre)
            slope[p, :, here] = (cdf + pre * density).astype(BF16)
            act = (pre * cdf).astype(BF16).astype(F32)
            diff[p * half : (p + 1) * half, here] = (act[:half] - act[half:]).astype(BF16)


def remote_slopes(others, expand):
    _, half, channels = others[0].shape
    hid = expand.shape[1]
    return call(
        remote_body,
        "remote_slopes",
        7 * 10**9,
        [((3, 2 * half, hid), BF16), ((3 * half, hid), BF16)],
        [],
        *others,
        expand,
    )


def split(total, side, keep, send):
    parts, rows, _ = keep.shape
    for x in range(parts):
        mine = pl.multiple_of((2 * x + side) * rows, 16)
        theirs = pl.multiple_of((2 * x + 1 - side) * rows, 16)
        keep[x] = total[pl.ds(mine, rows), :]
        send[x] = total[pl.ds(theirs, rows), :].astype(BF16)


def added(small, more):
    return (small[...].astype(F32) + more[...].astype(F32)).astype(BF16)


def reduce_grad_body(
    where, d_0, d_1, d_2, d_3, diff_0, diff_rest, small, more, keep, send, sums, total
):
    units = total.shape[0]
    parts, rows, _ = keep.shape
    lanes = pl.ds(pl.multiple_of(where[0] * units, LANES), units)
    diff = jnp.concatenate([diff_0[:, lanes], diff_rest[:, lanes]])
    every = jnp.concatenate([d_0[...], d_1[...], d_2[...], d_3[...]])
    total[...] = dot(diff, every, ((0,), (0,)))
    split(total, where[1], keep, send)
    sums[...] = added(small, more)


def reduce_grad(where, dbranch, diff_0, diff_rest, small, more, line, inner):
    _, channels = dbranch[0].shape
    units = diff_0.shape[1] // line
    parts, rows = inner // 2, units // inner
    return call(
        reduce_grad_body,
        "reduce_grad",
        2 * 10**9,
        [
            ((parts, rows, channels), F32),
            ((parts, rows, channels), BF16),
            (small.shape, BF16),
        ],
        [((units, channels), F32)],
        where,
        *dbranch,
        diff_0,
        diff_rest,
        small,
        more,
        scalars=1,
    )


def expand_slopes_body(
    where, d_0, d_1, d_2, d_3, slope_0, slope_rest, reduce, n_0, n_1, n_2, n_3, turned, dpre
):
    half, channels = d_0.shape
    width = turned.shape[0]
    start = where[0] * (channels // 4) // LANES * LANES
    lanes = pl.ds(pl.multiple_of(start, LANES), width)
    for p, ref in enumerate((n_0, n_1, n_2, n_3)):
        for v in range(2):
            at = (2 * p + v) * half
            turned[:, at : at + half] = ref[v, :, lanes].astype(F32).T.astype(BF16)
    every = jnp.concatenate([d_0[...], d_1[...], d_2[...], d_3[...]])
    for here in blocks(reduce.shape[0]):
        dhidden = dot(every, reduce[here, :], ((1,), (1,)))
        for p in range(4):
            part = dhidden[p * half : (p + 1) * half]
            slope = (slope_rest[p - 1, :, here] if p else slope_0[:, here]).astype(F32)
            at = 2 * p * half
            dpre[at : at + half, here] = (part * slope[:half]).astype(BF16)
            dpre[at + half : at + 2 * half, here] = (-part * slope[half:]).astype(BF16)


def expand_slopes(where, dbranch, slope_0, slope_rest, reduce, normed):
    half, _ = dbranch[0].shape
    hid = reduce.shape[0]
    return call(
        expand_slopes_body,
        "expand_slopes",
        4 * 10**9,
        [((2 * LANES, 8 * half), BF16), ((8 * half, hid), BF16)],
        [],
        where,
        *dbranch,
        slope_0,
        slope_rest,
        reduce,
        *normed,
        scalars=1,
    )


def expand_grad_body(
    where, turned, dpre, kept, got, small, more, keep, send, keep_r, send_r, sums, total
):
    own, hid = total.shape
    first = where[0] * own
    lhs = turned[pl.ds(pl.multiple_of(first - first // LANES * LANES, 16), own), :]
    for here in blocks(hid):
        total[:, here] = dot(lhs, dpre[:, here], ((1,), (0,)))
    split(total, where[1], keep, send)
    mine, theirs = where[2], 1 - where[2]
    keep_r[...] = kept[mine] + got[mine].astype(F32)
    send_r[...] = (kept[theirs] + got[theirs].astype(F32)).astype(BF16)
    sums[...] = added(small, more)


def expand_grad(where, turned, dpre, kept, got, small, more, own, inner):
    hid = dpre.shape[1]
    _, high, channels = kept.shape
    shape = (inner // 2, own // inner, hid)
    return call(
        expand_grad_body,
        "expand_grad",
        3 * 10**9,
        [
            (shape, F32),
            (shape, BF16),
            ((high, channels), F32),
            ((high, channels), BF16),
            (small.shape, BF16),
        ],
        [((own, hid), F32)],
        where,
        turned,
        dpre,
        kept,
        got,
        small,
        more,
        scalars=1,
    )


def merge_body(where, kept, got, small, more, keep, send, sums):
    mine, theirs = where[2], 1 - where[2]
    keep[...] = kept[mine] + got[mine].astype(F32)
    send[...] = (kept[theirs] + got[theirs].astype(F32)).astype(BF16)
    sums[...] = added(small, more)


def merge(where, kept, got, small, more):
    shape = kept.shape[1:]
    return call(
        merge_body,
        "merge",
        10**8,
        [(shape, F32), (shape, BF16), (small.shape, BF16)],
        [],
        where,
        kept,
        got,
        small,
        more,
        scalars=1,
    )


def grads_plain(every, dbranch_all, expand_weight, reduce_weight, my_line, my_inner, line, inner):
    channels, hid = expand_weight.shape
    units, own = hid // line, channels // line
    every = every.reshape(-1, channels)
    pre = dot(every, expand_weight, ((1,), (0,)))
    cdf, density = phi_parts(pre)
    slope = (cdf + pre * density).reshape(line, 2, -1, hid)
    hidden = (pre * cdf).astype(BF16).astype(F32).reshape(line, 2, -1, hid)
    diff = (hidden[:, 0] - hidden[:, 1]).astype(BF16).reshape(-1, hid)
    diff = lax.dynamic_slice_in_dim(diff, my_line * units, units, 1)
    dhidden = dot(dbranch_all, reduce_weight, ((1,), (1,))).reshape(line, -1, hid)
    dpre = jnp.stack([dhidden * slope[:, 0], -dhidden * slope[:, 1]], axis=1)
    dpre = dpre.astype(BF16).reshape(-1, hid)
    normed_own = lax.dynamic_slice_in_dim(every, my_line * own, own, 1)
    expand = dot(normed_own, dpre, ((0,), (0,))).reshape(inner, own // inner, hid)
    reduce = dot(diff, dbranch_all, ((0,), (0,))).reshape(inner, units // inner, channels)
    return halves(expand, my_inner & 1), halves(reduce, my_inner & 1)


def halves(part, side):
    part = part.reshape((part.shape[0] // 2, 2) + part.shape[1:])
    keep = lax.dynamic_index_in_dim(part, side, 1, keepdims=False)
    send = lax.dynamic_index_in_dim(part, 1 - side, 1, keepdims=False)
    return keep, send.astype(BF16)


def on_device(
    features, column_table, dw_kernel, norm_gain, expand_weight, reduce_weight, layer_scale
):
    rows, cols, channels = features.shape
    hid = expand_weight.shape[1]
    count = lax.axis_size("col")
    bits = count.bit_length() - 1
    line = 1 << ((bits + 1) // 2)
    inner = count // line
    inner_bits = inner.bit_length() - 1
    me = lax.axis_index("col")
    my_line, my_inner = me // inner, me % inner
    units, own = hid // line, channels // line
    total_cols = cols * count

    def swapped(block, mask):
        return lax.ppermute(block, "col", [(d, d ^ mask) for d in range(count)])

    mirror = lax.ppermute(column_table, "col", [(d, count - 1 - d) for d in range(count)])

    features_f, table_f = features.astype(F32), column_table.astype(F32)
    last, first, turned, gain = edges(features_f, table_f, mirror, norm_gain)
    low = lax.ppermute(last, "col", [(d, d + 1) for d in range(count - 1)])
    high = lax.ppermute(first, "col", [(d + 1, d) for d in range(count - 1)])
    normed, nhat, inv, wide = conv_norm(
        features_f, table_f, turned, low, high, dw_kernel.astype(F32), gain
    )
    others = [swapped(normed, p * inner) for p in range(1, line)]
    slope, diff, disagreement, dbranch, gscale = forward(
        1.0 / math.sqrt(rows * total_cols),
        normed.reshape(-1, channels),
        expand_weight,
        reduce_weight,
        wide,
        layer_scale,
        features.shape,
    )
    small, dbranch = backward(
        dbranch, slope, expand_weight, reduce_weight, nhat, inv, gain, gscale, wide
    )
    dbranch_all = [dbranch] + [swapped(dbranch, p * inner) for p in range(1, line)]

    normed_all = [normed] + others

    def line_sum(small):
        sums = [small] + [swapped(small, p * inner) for p in range(1, line)]
        sums = [part.astype(F32) for part in sums]
        while len(sums) > 1:
            sums = [low + high for low, high in zip(sums[::2], sums[1::2])]
        return sums[0]

    if line == 4 and inner == 4 and units % LANES == 0 and own % 64 == 0:
        side = (my_inner >> 1) & 1
        where = jnp.stack([my_line, my_inner & 1, side]).astype(jnp.int32)
        more = swapped(small, 2)
        slope_rest, diff_rest = remote_slopes(others, expand_weight)
        keep_r, send_r, small = reduce_grad(
            where, dbranch_all, diff, diff_rest, small, more, line, inner
        )
        got_r, more = swapped(send_r, 1), swapped(small, inner)
        turned, dpre = expand_slopes(
            where, dbranch_all, slope, slope_rest, reduce_weight, normed_all
        )
        keep_e, send_e, keep_r, send_r, small = expand_grad(
            where, turned, dpre, keep_r, got_r, small, more, own, inner
        )
        got_r, more = swapped(send_r, 2), swapped(small, 1)
        keep_e, send_e, small = merge(where, keep_e, swapped(send_e, 1), small, more)
        got_e, more = swapped(send_e, 2), swapped(small, 2 * inner)
        small = small.astype(F32) + more.astype(F32)
        sum_r = keep_r + got_r.astype(F32)
        sum_e = keep_e + got_e.astype(F32)
    else:
        (keep_e, send_e), (keep_r, send_r) = grads_plain(
            jnp.stack(normed_all),
            jnp.concatenate(dbranch_all),
            expand_weight,
            reduce_weight,
            my_line,
            my_inner,
            line,
            inner,
        )
        small = line_sum(small)
        for bit in range(inner_bits):
            sum_r = keep_r + swapped(send_r, 1 << bit).astype(F32)
            sum_e = keep_e + swapped(send_e, 1 << bit).astype(F32)
            small = small.astype(BF16)
            small = small.astype(F32) + swapped(small, 1 << bit).astype(F32)
            if bit < inner_bits - 1:
                side = (my_inner >> (bit + 1)) & 1
                keep_r, send_r = halves(sum_r, side)
                keep_e, send_e = halves(sum_e, side)
    grad_kernel = small[:49].reshape(7, 7, channels)
    return (
        disagreement,
        sum_e.reshape(own // inner, hid),
        sum_r.reshape(units // inner, channels),
        grad_kernel,
        small[49],
        small[50],
    )


def solution(mesh):
    in_specs = (P("groups", "col", None), P("col", None), P(), P(), P(), P(), P())
    out_specs = (
        P("groups", "col", None),
        P(("groups", "col"), None),
        P(("groups", "col"), None),
        P("groups", None, None),
        P("groups"),
        P("groups"),
    )
    return jax.shard_map(
        on_device, mesh=mesh, in_specs=in_specs, out_specs=out_specs, check_vma=False
    )
```

```python
import functools
import math

import jax
import jax.numpy as jnp
from jax import lax
from jax.experimental import pallas as pl
from jax.experimental.pallas import tpu as pltpu
from jax.sharding import PartitionSpec as P

BF16 = jnp.bfloat16
F32 = jnp.float32
LANES = 128
VMEM_GRANT = 16 << 20
BLOCK = 512


def phi_parts(pre):
    decay = jnp.exp(-0.5 * pre * pre)
    t = 1.0 / (1.0 + 0.23164189 * jnp.abs(pre))
    poly = 0.5307027145 * t - 0.7265760135
    poly = poly * t + 0.7107068705
    poly = poly * t - 0.142248368
    poly = poly * t + 0.127414796
    tail = poly * t * decay
    return jnp.where(pre < 0.0, tail, 1.0 - tail), decay * 0.3989422804014327


def call(body, name, flops, out_shape, scratch, *operands, scalars=0):
    spaces = [pltpu.SMEM] * scalars + [pltpu.VMEM] * (len(operands) - scalars)
    return pl.pallas_call(
        body,
        in_specs=[pl.BlockSpec(memory_space=space) for space in spaces],
        out_specs=[pl.BlockSpec(memory_space=pltpu.VMEM) for _ in out_shape],
        out_shape=[jax.ShapeDtypeStruct(shape, dtype) for shape, dtype in out_shape],
        scratch_shapes=[pltpu.VMEM(shape, dtype) for shape, dtype in scratch],
        compiler_params=pltpu.CompilerParams(vmem_limit_bytes=VMEM_GRANT),
        cost_estimate=pl.CostEstimate(flops=flops, bytes_accessed=10**8, transcendentals=0),
        name=name,
    )(*operands)


def dot(lhs, rhs, contract):
    return lax.dot_general(lhs, rhs, (contract, ((), ())), preferred_element_type=F32)


def flipped(value):
    rows = value.shape[0]
    return jnp.concatenate([value[r : r + 1] for r in reversed(range(rows))], axis=0)


def edges_body(feat, table, mirror, last, first, turned):
    _, cols, _ = feat.shape
    other = flipped(mirror[...].astype(F32))
    for v, add in enumerate((table[...], other)):
        own = (feat[...] + add[None]).astype(BF16)
        last[v] = own[:, cols - 3 :]
        first[v] = own[:, :3]
    turned[...] = other


def edges(features, table, mirror):
    rows, _, channels = features.shape
    return call(
        edges_body,
        "edges",
        10**8,
        [
            ((2, rows, 3, channels), BF16),
            ((2, rows, 3, channels), BF16),
            (table.shape, F32),
        ],
        [],
        features,
        table,
        mirror,
    )


def conv_body(feat, table, turned, low, high, dw, gain, normed, nhat, inv, wide, conv):
    rows, cols, channels = feat.shape
    for v, add in enumerate((table, turned)):
        wide[v, :, 3 : 3 + cols, :] = (feat[...] + add[...][None]).astype(BF16).astype(F32)
        wide[v, :, 0:3, :] = low[v].astype(F32)
        wide[v, :, 3 + cols : 6 + cols, :] = high[v].astype(F32)

    def tile(c, carry):
        lanes = pl.ds(pl.multiple_of(c * LANES, LANES), LANES)
        sums = [[jnp.zeros((cols, LANES), F32) for _ in range(rows)] for _ in range(2)]
        for j in range(7):
            for v in range(2):
                part = [wide[v, r, pl.ds(j, cols), lanes] for r in range(rows)]
                for i in range(7):
                    weight = dw[i, pl.ds(6 - j if v else j, 1), lanes]
                    for r in range(rows):
                        if 0 <= r + i - 3 < rows:
                            sums[v][r] = sums[v][r] + weight * part[r + i - 3]
        for v in range(2):
            for r in range(rows):
                conv[v, r, :, lanes] = sums[v][r]
        return carry

    lax.fori_loop(0, channels // LANES, tile, 0)
    for v in range(2):
        value = conv[v].reshape(rows * cols, channels)
        centred = value - jnp.mean(value, axis=-1, keepdims=True)
        inverse = lax.rsqrt(jnp.mean(centred * centred, axis=-1, keepdims=True) + 1e-06)
        value = centred * inverse
        nhat[v] = value
        inv[v] = jnp.broadcast_to(inverse, (rows * cols, LANES))
        normed[v] = (value * gain[...].reshape(1, channels)).astype(BF16)


def conv_norm(features, table, turned, low, high, dw, gain):
    rows, cols, channels = features.shape
    pixels = rows * cols
    return call(
        conv_body,
        "conv_norm",
        4 * 10**9,
        [
            ((2, pixels, channels), BF16),
            ((2, pixels, channels), F32),
            ((2, pixels, LANES), F32),
            ((2, rows, 16, channels), F32),
        ],
        [((2, rows, cols, channels), F32)],
        features,
        table,
        turned,
        low,
        high,
        dw,
        gain,
    )


def blocks(total):
    return [slice(at, at + BLOCK) for at in range(0, total, BLOCK)]


def forward_body(
    scale, normed, expand, reduce, wide, ls, slope, diff, disagreement, dbranch, gscale, hidden
):
    pixels, channels = normed.shape
    half = pixels // 2
    rows, cols, _ = disagreement.shape
    for here in blocks(expand.shape[1]):
        pre = dot(normed[...], expand[:, here], ((1,), (0,)))
        cdf, density = phi_parts(pre)
        slope[:, here] = (cdf + pre * density).astype(BF16)
        act = (pre * cdf).astype(BF16)
        hidden[:, here] = act
        act = act.astype(F32)
        diff[:, here] = (act[:half] - act[half:]).astype(BF16)
    branch = dot(hidden[...], reduce[...], ((1,), (0,)))
    factor = ls[...].reshape(1, channels)
    outs = []
    for v in range(2):
        own = wide[v, :, 3 : 3 + cols, :].reshape(half, channels)
        outs.append((own + factor * branch[v * half : (v + 1) * half]).astype(BF16).astype(F32))
    difference = outs[0] - outs[1]
    disagreement[...] = difference.astype(BF16).reshape(rows, cols, channels)
    residual = (difference * scale).astype(BF16).astype(F32)
    gscale[...] = jnp.sum((branch[:half] - branch[half:]) * residual, axis=0, keepdims=True)
    dbranch[...] = (factor * residual).astype(BF16)


def forward(scale, normed, expand, reduce, wide, ls, shape):
    pixels, channels = normed.shape
    hid = expand.shape[1]
    return call(
        functools.partial(forward_body, scale),
        "forward",
        6 * 10**9,
        [
            ((pixels, hid), BF16),
            ((pixels // 2, hid), BF16),
            (shape, BF16),
            ((pixels // 2, channels), BF16),
            ((1, channels), F32),
        ],
        [((pixels, hid), BF16)],
        normed,
        expand,
        reduce,
        wide,
        ls,
    )


def backward_body(
    dbranch, slope, expand, reduce, nhat, inv, gain, gscale, wide, out, dpre, grad, taps, small
):
    half, channels = dbranch.shape
    _, rows, _, _ = wide.shape
    cols = half // rows
    for here in blocks(expand.shape[1]):
        dhidden = dot(dbranch[...], reduce[here, :], ((1,), (1,)))
        dpre[:half, here] = (dhidden * slope[:half, here].astype(F32)).astype(BF16)
        dpre[half:, here] = (-dhidden * slope[half:, here].astype(F32)).astype(BF16)
    dnormed = dot(dpre[...], expand[...], ((1,), (1,)))
    factor = gain[...].reshape(1, channels)
    ggain = jnp.zeros((1, channels), F32)
    for v in range(2):
        here = slice(v * half, (v + 1) * half)
        ggain = ggain + jnp.sum(dnormed[here] * nhat[v], axis=0, keepdims=True)
        scaled = dnormed[here] * factor
        gm = jnp.mean(scaled, axis=-1, keepdims=True)
        gn = jnp.mean(scaled * nhat[v], axis=-1, keepdims=True)
        grad[here, :] = inv[v][:, :1] * (scaled - gm - nhat[v] * gn)

    def tile(c, carry):
        lanes = pl.ds(pl.multiple_of(c * LANES, LANES), LANES)
        dconv = [
            [grad[pl.ds(v * half + r * cols, cols), lanes] for r in range(rows)] for v in range(2)
        ]
        for j in range(7):
            part = [
                [wide[v, r, pl.ds(6 - j if v else j, cols), lanes] for r in range(rows)]
                for v in range(2)
            ]
            for i in range(7):
                sums = []
                for v in range(2):
                    total = None
                    for r in range(rows):
                        if 0 <= r + i - 3 < rows:
                            term = part[v][r + i - 3] * dconv[v][r]
                            total = term if total is None else total + term
                    sums.append(total)
                at = 8 * (7 * i + j)
                taps[at : at + 8, :] = sums[0] + sums[1]
        rolled = taps[pl.ds(0, 49, stride=8), :]
        for s in range(1, 8):
            rolled = rolled + taps[pl.ds(s, 49, stride=8), :]
        small[:49, lanes] = rolled
        return carry

    small[...] = jnp.zeros(small.shape, F32)
    lax.fori_loop(0, channels // LANES, tile, 0)
    small[49:50, :] = ggain
    small[50:51, :] = gscale[...]
    out[...] = small[...].astype(BF16)


def backward(dbranch, slope, expand, reduce, nhat, inv, gain, gscale, wide):
    half, channels = dbranch.shape
    hid = expand.shape[1]
    return call(
        backward_body,
        "backward",
        9 * 10**9,
        [((64, channels), BF16)],
        [
            ((2 * half, hid), BF16),
            ((2 * half, channels), F32),
            ((8 * 49, LANES), F32),
            ((64, channels), F32),
        ],
        dbranch,
        slope,
        expand,
        reduce,
        nhat,
        inv,
        gain,
        gscale,
        wide,
    )[0]


def gate_body(block, other, after, block_out, other_out):
    block_out[...] = block[...]
    other_out[...] = other[...]


def gate(block, other, after):
    shapes = [(a.shape, a.dtype) for a in (block, other)]
    return call(gate_body, "gate", 10**7, shapes, [], block, other, after)


def remote_body(count, *refs):
    normed, (expand, small, more, slope, diff, sums) = refs[:count], refs[count:]
    _, half, channels = normed[0].shape
    for here in blocks(expand.shape[1]):
        for p in range(count):
            pre = dot(normed[p][...].reshape(2 * half, channels), expand[:, here], ((1,), (0,)))
            cdf, density = phi_parts(pre)
            slope[p, :, here] = (cdf + pre * density).astype(BF16)
            act = (pre * cdf).astype(BF16).astype(F32)
            diff[p * half : (p + 1) * half, here] = (act[:half] - act[half:]).astype(BF16)
    sums[...] = added(small, more) if more is not None else small[...]


def remote_slopes(normed, expand, small, more=None):
    count = len(normed)
    _, half, _ = normed[0].shape
    hid = expand.shape[1]
    body = functools.partial(remote_body, count)
    if more is None:
        body = lambda *refs: remote_body(count, *refs[: count + 2], None, *refs[count + 2 :])
    return call(
        body,
        "remote_slopes",
        2 * count * 10**9,
        [((count, 2 * half, hid), BF16), ((count * half, hid), BF16), (small.shape, BF16)],
        [],
        *normed,
        expand,
        small,
        *(() if more is None else (more,)),
    )


def split(total, side, keep, send):
    parts, rows, _ = keep.shape
    for x in range(parts):
        mine = pl.multiple_of((2 * x + side) * rows, 16)
        theirs = pl.multiple_of((2 * x + 1 - side) * rows, 16)
        keep[x] = total[pl.ds(mine, rows), :]
        send[x] = total[pl.ds(theirs, rows), :].astype(BF16)


def added(small, more):
    return (small[...].astype(F32) + more[...].astype(F32)).astype(BF16)


def reduce_grad_body(
    where, d_0, d_1, d_2, d_3, diff_0, diff_12, diff_3, keep, send, total
):
    units = total.shape[0]
    parts, rows, _ = keep.shape
    lanes = pl.ds(pl.multiple_of(where[0] * units, LANES), units)
    diff = jnp.concatenate([diff_0[:, lanes], diff_12[:, lanes], diff_3[:, lanes]])
    every = jnp.concatenate([d_0[...], d_1[...], d_2[...], d_3[...]])
    total[...] = dot(diff, every, ((0,), (0,)))
    split(total, where[1], keep, send)


def reduce_grad(where, dbranch, diffs, line, inner):
    _, channels = dbranch[0].shape
    units = diffs[0].shape[1] // line
    parts, rows = inner // 2, units // inner
    return call(
        reduce_grad_body,
        "reduce_grad",
        2 * 10**9,
        [
            ((parts, rows, channels), F32),
            ((parts, rows, channels), BF16),
        ],
        [((units, channels), F32)],
        where,
        *dbranch,
        *diffs,
        scalars=1,
    )


def expand_slopes_body(
    where, d_0, d_1, d_2, d_3, slope_0, slope_12, slope_3, reduce, n_0, n_1, n_2, n_3,
    turned, dpre,
):
    half, channels = d_0.shape
    width = turned.shape[0]
    start = where[0] * (channels // 4) // LANES * LANES
    lanes = pl.ds(pl.multiple_of(start, LANES), width)
    for p, ref in enumerate((n_0, n_1, n_2, n_3)):
        for v in range(2):
            at = (2 * p + v) * half
            turned[:, at : at + half] = ref[v, :, lanes].astype(F32).T.astype(BF16)
    every = jnp.concatenate([d_0[...], d_1[...], d_2[...], d_3[...]])
    slopes = [slope_0, slope_12.at[0], slope_12.at[1], slope_3.at[0]]
    for here in blocks(reduce.shape[0]):
        dhidden = dot(every, reduce[here, :], ((1,), (1,)))
        for p in range(4):
            part = dhidden[p * half : (p + 1) * half]
            slope = slopes[p][:, here].astype(F32)
            at = 2 * p * half
            dpre[at : at + half, here] = (part * slope[:half]).astype(BF16)
            dpre[at + half : at + 2 * half, here] = (-part * slope[half:]).astype(BF16)


def expand_slopes(where, dbranch, slopes, reduce, normed):
    half, _ = dbranch[0].shape
    hid = reduce.shape[0]
    return call(
        expand_slopes_body,
        "expand_slopes",
        4 * 10**9,
        [((2 * LANES, 8 * half), BF16), ((8 * half, hid), BF16)],
        [],
        where,
        *dbranch,
        *slopes,
        reduce,
        *normed,
        scalars=1,
    )


def expand_grad_body(
    where, turned, dpre, kept, got, small, more, keep, send, keep_r, send_r, sums, total
):
    own, hid = total.shape
    first = where[0] * own
    lhs = turned[pl.ds(pl.multiple_of(first - first // LANES * LANES, 16), own), :]
    for here in blocks(hid):
        total[:, here] = dot(lhs, dpre[:, here], ((1,), (0,)))
    split(total, where[1], keep, send)
    mine, theirs = where[2], 1 - where[2]
    keep_r[...] = kept[mine] + got[mine].astype(F32)
    send_r[...] = (kept[theirs] + got[theirs].astype(F32)).astype(BF16)
    sums[...] = added(small, more)


def expand_grad(where, turned, dpre, kept, got, small, more, own, inner):
    hid = dpre.shape[1]
    _, high, channels = kept.shape
    shape = (inner // 2, own // inner, hid)
    return call(
        expand_grad_body,
        "expand_grad",
        3 * 10**9,
        [
            (shape, F32),
            (shape, BF16),
            ((high, channels), F32),
            ((high, channels), BF16),
            (small.shape, BF16),
        ],
        [((own, hid), F32)],
        where,
        turned,
        dpre,
        kept,
        got,
        small,
        more,
        scalars=1,
    )


def merge_body(where, kept, got, small, keep, send, passed):
    mine, theirs = where[2], 1 - where[2]
    keep[...] = kept[mine] + got[mine].astype(F32)
    send[...] = (kept[theirs] + got[theirs].astype(F32)).astype(BF16)
    passed[...] = small[...]


def merge(where, kept, got, small):
    shape = kept.shape[1:]
    return call(
        merge_body,
        "merge",
        10**8,
        [(shape, F32), (shape, BF16), (small.shape, BF16)],
        [],
        where,
        kept,
        got,
        small,
        scalars=1,
    )


def finish_body(keep_e, got_e, keep_r, got_r, small, more_1, more_2, more_3, out_e, out_r, kernel, gain, scale):
    out_e[...] = keep_e[...] + got_e[...].astype(F32)
    out_r[...] = keep_r[...] + got_r[...].astype(F32)
    low = small[...].astype(F32) + more_1[...].astype(F32)
    sums = low + (more_2[...].astype(F32) + more_3[...].astype(F32))
    for i in range(7):
        kernel[i] = sums[7 * i : 7 * i + 7]
    gain[...] = sums[49:50].reshape(gain.shape)
    scale[...] = sums[50:51].reshape(scale.shape)


def finish(keep_e, got_e, keep_r, got_r, small, more):
    channels = small.shape[1]
    return call(
        finish_body,
        "finish",
        10**8,
        [
            (keep_e.shape, F32),
            (keep_r.shape, F32),
            ((7, 7, channels), F32),
            ((channels,), F32),
            ((channels,), F32),
        ],
        [],
        keep_e,
        got_e,
        keep_r,
        got_r,
        small,
        *more,
    )


def grads_plain(every, dbranch_all, expand_weight, reduce_weight, my_line, my_inner, line, inner):
    channels, hid = expand_weight.shape
    units, own = hid // line, channels // line
    every = every.reshape(-1, channels)
    pre = dot(every, expand_weight, ((1,), (0,)))
    cdf, density = phi_parts(pre)
    slope = (cdf + pre * density).reshape(line, 2, -1, hid)
    hidden = (pre * cdf).astype(BF16).astype(F32).reshape(line, 2, -1, hid)
    diff = (hidden[:, 0] - hidden[:, 1]).astype(BF16).reshape(-1, hid)
    diff = lax.dynamic_slice_in_dim(diff, my_line * units, units, 1)
    dhidden = dot(dbranch_all, reduce_weight, ((1,), (1,))).reshape(line, -1, hid)
    dpre = jnp.stack([dhidden * slope[:, 0], -dhidden * slope[:, 1]], axis=1)
    dpre = dpre.astype(BF16).reshape(-1, hid)
    normed_own = lax.dynamic_slice_in_dim(every, my_line * own, own, 1)
    expand = dot(normed_own, dpre, ((0,), (0,))).reshape(inner, own // inner, hid)
    reduce = dot(diff, dbranch_all, ((0,), (0,))).reshape(inner, units // inner, channels)
    return halves(expand, my_inner & 1), halves(reduce, my_inner & 1)


def halves(part, side):
    part = part.reshape((part.shape[0] // 2, 2) + part.shape[1:])
    keep = lax.dynamic_index_in_dim(part, side, 1, keepdims=False)
    send = lax.dynamic_index_in_dim(part, 1 - side, 1, keepdims=False)
    return keep, send.astype(BF16)


def on_device(
    features, column_table, dw_kernel, norm_gain, expand_weight, reduce_weight, layer_scale
):
    rows, cols, channels = features.shape
    hid = expand_weight.shape[1]
    count = lax.axis_size("col")
    bits = count.bit_length() - 1
    line = 1 << ((bits + 1) // 2)
    inner = count // line
    inner_bits = inner.bit_length() - 1
    me = lax.axis_index("col")
    my_line, my_inner = me // inner, me % inner
    units, own = hid // line, channels // line
    total_cols = cols * count

    def swapped(block, mask):
        return lax.ppermute(block, "col", [(d, d ^ mask) for d in range(count)])

    mirror = lax.ppermute(column_table, "col", [(d, count - 1 - d) for d in range(count)])

    features_f, table_f = features.astype(F32), column_table.astype(F32)
    last, first, turned = edges(features_f, table_f, mirror)
    low = lax.ppermute(last, "col", [(d, d + 1) for d in range(count - 1)])
    high = lax.ppermute(first, "col", [(d + 1, d) for d in range(count - 1)])
    normed, nhat, inv, wide = conv_norm(
        features_f, table_f, turned, low, high, dw_kernel.astype(F32), norm_gain
    )
    fast = line == 4 and inner == 4 and units % LANES == 0 and own % 64 == 0
    if fast:
        normed_2, normed_1 = swapped(normed, 2 * inner), swapped(normed, inner)
    else:
        others = [swapped(normed, p * inner) for p in range(1, line)]
    slope, diff, disagreement, dbranch, gscale = forward(
        1.0 / math.sqrt(rows * total_cols),
        normed.reshape(-1, channels),
        expand_weight,
        reduce_weight,
        wide,
        layer_scale,
        features.shape,
    )
    small = backward(
        dbranch, slope, expand_weight, reduce_weight, nhat, inv, norm_gain, gscale, wide
    )
    if fast:
        block, dbranch = gate(normed_2, dbranch, small)
        normed_3 = swapped(block, inner)
    dbranch_all = [dbranch] + [swapped(dbranch, p * inner) for p in range(1, line)]

    if fast:
        side = (my_inner >> 1) & 1
        where = jnp.stack([my_line, my_inner & 1, side]).astype(jnp.int32)
        more = swapped(small, 2)
        slope_12, diff_12, small = remote_slopes([normed_1, normed_2], expand_weight, small)
        slope_3, diff_3, small = remote_slopes([normed_3], expand_weight, small, more)
        more = swapped(small, 1)
        keep_r, send_r = reduce_grad(where, dbranch_all, [diff, diff_12, diff_3], line, inner)
        got_r = swapped(send_r, 1)
        turned, dpre = expand_slopes(
            where,
            dbranch_all,
            [slope, slope_12, slope_3],
            reduce_weight,
            [normed, normed_1, normed_2, normed_3],
        )
        keep_e, send_e, keep_r, send_r, small = expand_grad(
            where, turned, dpre, keep_r, got_r, small, more, own, inner
        )
        got_r = swapped(send_r, 2)
        keep_e, send_e, small = merge(where, keep_e, swapped(send_e, 1), small)
        got_e = swapped(send_e, 2)
        more = [swapped(small, p * inner) for p in range(1, line)]
        sums = finish(keep_e, got_e, keep_r, got_r, small, more)
        return (disagreement, *sums)

    def line_sum(small):
        sums = [small] + [swapped(small, p * inner) for p in range(1, line)]
        sums = [part.astype(F32) for part in sums]
        while len(sums) > 1:
            sums = [low + high for low, high in zip(sums[::2], sums[1::2])]
        return sums[0]

    (keep_e, send_e), (keep_r, send_r) = grads_plain(
        jnp.stack([normed] + others),
        jnp.concatenate(dbranch_all),
        expand_weight,
        reduce_weight,
        my_line,
        my_inner,
        line,
        inner,
    )
    small = line_sum(small)
    for bit in range(inner_bits):
        sum_r = keep_r + swapped(send_r, 1 << bit).astype(F32)
        sum_e = keep_e + swapped(send_e, 1 << bit).astype(F32)
        small = small.astype(BF16)
        small = small.astype(F32) + swapped(small, 1 << bit).astype(F32)
        if bit < inner_bits - 1:
            side = (my_inner >> (bit + 1)) & 1
            keep_r, send_r = halves(sum_r, side)
            keep_e, send_e = halves(sum_e, side)
    grad_kernel = small[:49].reshape(7, 7, channels)
    return (
        disagreement,
        sum_e.reshape(own // inner, hid),
        sum_r.reshape(units // inner, channels),
        grad_kernel,
        small[49],
        small[50],
    )


def solution(mesh):
    in_specs = (P("groups", "col", None), P("col", None), P(), P(), P(), P(), P())
    out_specs = (
        P("groups", "col", None),
        P(("groups", "col"), None),
        P(("groups", "col"), None),
        P("groups", None, None),
        P("groups"),
        P("groups"),
    )
    return jax.shard_map(
        on_device, mesh=mesh, in_specs=in_specs, out_specs=out_specs, check_vma=False
    )
```

```python
import functools
import math

import jax
import jax.numpy as jnp
from jax import lax
from jax.experimental import pallas as pl
from jax.experimental.pallas import tpu as pltpu
from jax.sharding import PartitionSpec as P

BF16 = jnp.bfloat16
F32 = jnp.float32
LANES = 128
VMEM_GRANT = 16 << 20
BLOCK = 512


def phi_parts(pre):
    decay = jnp.exp(-0.5 * pre * pre)
    t = 1.0 / (1.0 + 0.23164189 * jnp.abs(pre))
    poly = 0.5307027145 * t - 0.7265760135
    poly = poly * t + 0.7107068705
    poly = poly * t - 0.142248368
    poly = poly * t + 0.127414796
    tail = poly * t * decay
    return jnp.where(pre < 0.0, tail, 1.0 - tail), decay * 0.3989422804014327


def call(body, name, flops, out_shape, scratch, *operands, read=10**8):
    return pl.pallas_call(
        body,
        in_specs=[pl.BlockSpec(memory_space=pltpu.VMEM) for _ in operands],
        out_specs=[pl.BlockSpec(memory_space=pltpu.VMEM) for _ in out_shape],
        out_shape=[jax.ShapeDtypeStruct(shape, dtype) for shape, dtype in out_shape],
        scratch_shapes=[pltpu.VMEM(shape, dtype) for shape, dtype in scratch],
        compiler_params=pltpu.CompilerParams(vmem_limit_bytes=VMEM_GRANT),
        cost_estimate=pl.CostEstimate(flops=flops, bytes_accessed=read, transcendentals=0),
        name=name,
    )(*operands)


def position(inner):
    me = lax.axis_index("col")
    return me // inner, me & 1, (me >> 1) & 1


def dot(lhs, rhs, contract):
    return lax.dot_general(lhs, rhs, (contract, ((), ())), preferred_element_type=F32)


def flipped(value):
    rows = value.shape[0]
    return jnp.concatenate([value[r : r + 1] for r in reversed(range(rows))], axis=0)


def edges_body(feat, given, mirror, inside, across, turned):
    _, cols, channels = feat.shape
    other = flipped(mirror[...].astype(F32))
    odd = (lax.axis_index("col") & 1) == 1
    for v, add in enumerate((given[:cols, :], other)):
        own = (feat[...] + add[None]).astype(BF16).astype(F32)
        first, last = own[:, :3], own[:, cols - 3 :]
        inside[v] = jnp.where(odd, first, last).astype(BF16)
        across[v] = jnp.where(odd, last, first).astype(BF16)
    turned[...] = other


def edges(features, given, mirror):
    rows, cols, channels = features.shape
    return call(
        edges_body,
        "edges",
        10**8,
        [
            ((2, rows, 3, channels), BF16),
            ((2, rows, 3, channels), BF16),
            ((cols, channels), F32),
        ],
        [],
        features,
        given,
        mirror,
    )


def conv_body(feat, given, turned, inside, across, dw, normed, nhat, inv, wide, conv):
    rows, cols, channels = feat.shape
    odd = (lax.axis_index("col") & 1) == 1
    gain = given[cols : cols + 1, :]
    for v, add in enumerate((given[:cols, :], turned[...])):
        wide[v, :, 3 : 3 + cols, :] = (feat[...] + add[None]).astype(BF16).astype(F32)
        one, two = inside[v].astype(F32), across[v].astype(F32)
        wide[v, :, 0:3, :] = jnp.where(odd, one, two)
        wide[v, :, 3 + cols : 6 + cols, :] = jnp.where(odd, two, one)

    def tile(c, carry):
        lanes = pl.ds(pl.multiple_of(c * LANES, LANES), LANES)
        sums = [[jnp.zeros((cols, LANES), F32) for _ in range(rows)] for _ in range(2)]
        for j in range(7):
            for v in range(2):
                part = [wide[v, r, pl.ds(j, cols), lanes] for r in range(rows)]
                for i in range(7):
                    weight = dw[i, pl.ds(6 - j if v else j, 1), lanes]
                    for r in range(rows):
                        if 0 <= r + i - 3 < rows:
                            sums[v][r] = sums[v][r] + weight * part[r + i - 3]
        for v in range(2):
            for r in range(rows):
                conv[v, r, :, lanes] = sums[v][r]
        return carry

    lax.fori_loop(0, channels // LANES, tile, 0)
    for v in range(2):
        value = conv[v].reshape(rows * cols, channels)
        centred = value - jnp.mean(value, axis=-1, keepdims=True)
        inverse = lax.rsqrt(jnp.mean(centred * centred, axis=-1, keepdims=True) + 1e-06)
        value = centred * inverse
        nhat[v] = value
        inv[v] = jnp.broadcast_to(inverse, (rows * cols, LANES))
        normed[v] = (value * gain).astype(BF16)


def conv_norm(features, given, turned, inside, across, dw):
    rows, cols, channels = features.shape
    pixels = rows * cols
    return call(
        conv_body,
        "conv_norm",
        4 * 10**9,
        [
            ((2, pixels, channels), BF16),
            ((2, pixels, channels), F32),
            ((2, pixels, LANES), F32),
            ((2, rows, 16, channels), F32),
        ],
        [((2, rows, cols, channels), F32)],
        features,
        given,
        turned,
        inside,
        across,
        dw,
    )


def blocks(total):
    return [slice(at, at + BLOCK) for at in range(0, total, BLOCK)]


def forward_body(
    scale, normed, expand, reduce, wide, given, slope, diff, disagreement, dbranch, gscale, hidden
):
    pixels, channels = normed.shape
    half = pixels // 2
    rows, cols, _ = disagreement.shape
    for here in blocks(expand.shape[1]):
        pre = dot(normed[...], expand[:, here], ((1,), (0,)))
        cdf, density = phi_parts(pre)
        slope[:, here] = (cdf + pre * density).astype(BF16)
        act = (pre * cdf).astype(BF16)
        hidden[:, here] = act
        act = act.astype(F32)
        diff[:, here] = (act[:half] - act[half:]).astype(BF16)
    branch = dot(hidden[...], reduce[...], ((1,), (0,)))
    factor = given[cols + 1 : cols + 2, :]
    outs = []
    for v in range(2):
        own = wide[v, :, 3 : 3 + cols, :].reshape(half, channels)
        outs.append((own + factor * branch[v * half : (v + 1) * half]).astype(BF16).astype(F32))
    difference = outs[0] - outs[1]
    disagreement[...] = difference.astype(BF16).reshape(rows, cols, channels)
    residual = (difference * scale).astype(BF16).astype(F32)
    gscale[...] = jnp.sum((branch[:half] - branch[half:]) * residual, axis=0, keepdims=True)
    dbranch[...] = (factor * residual).astype(BF16)


def forward(scale, normed, expand, reduce, wide, given, shape):
    pixels, channels = normed.shape
    hid = expand.shape[1]
    return call(
        functools.partial(forward_body, scale),
        "forward",
        6 * 10**9,
        [
            ((pixels, hid), BF16),
            ((pixels // 2, hid), BF16),
            (shape, BF16),
            ((pixels // 2, channels), BF16),
            ((1, channels), F32),
        ],
        [((pixels, hid), BF16)],
        normed,
        expand,
        reduce,
        wide,
        given,
    )


def backward_body(
    dbranch, slope, expand, reduce, nhat, inv, given, gscale, wide, out, dpre, grad, taps, small
):
    half, channels = dbranch.shape
    _, rows, _, _ = wide.shape
    cols = half // rows
    for here in blocks(expand.shape[1]):
        dhidden = dot(dbranch[...], reduce[here, :], ((1,), (1,)))
        dpre[:half, here] = (dhidden * slope[:half, here].astype(F32)).astype(BF16)
        dpre[half:, here] = (-dhidden * slope[half:, here].astype(F32)).astype(BF16)
    dnormed = dot(dpre[...], expand[...], ((1,), (1,)))
    factor = given[cols : cols + 1, :]
    ggain = jnp.zeros((1, channels), F32)
    for v in range(2):
        here = slice(v * half, (v + 1) * half)
        ggain = ggain + jnp.sum(dnormed[here] * nhat[v], axis=0, keepdims=True)
        scaled = dnormed[here] * factor
        gm = jnp.mean(scaled, axis=-1, keepdims=True)
        gn = jnp.mean(scaled * nhat[v], axis=-1, keepdims=True)
        grad[here, :] = inv[v][:, :1] * (scaled - gm - nhat[v] * gn)

    def tile(c, carry):
        lanes = pl.ds(pl.multiple_of(c * LANES, LANES), LANES)
        dconv = [
            [grad[pl.ds(v * half + r * cols, cols), lanes] for r in range(rows)] for v in range(2)
        ]
        for j in range(7):
            part = [
                [wide[v, r, pl.ds(6 - j if v else j, cols), lanes] for r in range(rows)]
                for v in range(2)
            ]
            for i in range(7):
                sums = []
                for v in range(2):
                    total = None
                    for r in range(rows):
                        if 0 <= r + i - 3 < rows:
                            term = part[v][r + i - 3] * dconv[v][r]
                            total = term if total is None else total + term
                    sums.append(total)
                at = 8 * (7 * i + j)
                taps[at : at + 8, :] = sums[0] + sums[1]
        rolled = taps[pl.ds(0, 49, stride=8), :]
        for s in range(1, 8):
            rolled = rolled + taps[pl.ds(s, 49, stride=8), :]
        small[:49, lanes] = rolled
        return carry

    small[...] = jnp.zeros(small.shape, F32)
    lax.fori_loop(0, channels // LANES, tile, 0)
    small[49:50, :] = ggain
    small[50:51, :] = gscale[...]
    out[...] = small[...].astype(BF16)


def backward(dbranch, slope, expand, reduce, nhat, inv, given, gscale, wide):
    half, channels = dbranch.shape
    hid = expand.shape[1]
    return call(
        backward_body,
        "backward",
        9 * 10**9,
        [((64, channels), BF16)],
        [
            ((2 * half, hid), BF16),
            ((2 * half, channels), F32),
            ((8 * 49, LANES), F32),
            ((64, channels), F32),
        ],
        dbranch,
        slope,
        expand,
        reduce,
        nhat,
        inv,
        given,
        gscale,
        wide,
    )[0]


def gate_body(block, after, out):
    out[...] = block[...]


def gate(block, after):
    return call(gate_body, "gate", 10**6, [(block.shape, block.dtype)], [], block, after, read=10**5)[0]


def remote_body(count, *refs):
    normed, expand, small, (slope, diff, passed) = refs[:count], refs[count], refs[count + 1], refs[-3:]
    _, half, channels = normed[0].shape
    for here in blocks(expand.shape[1]):
        for p in range(count):
            pre = dot(normed[p][...].reshape(2 * half, channels), expand[:, here], ((1,), (0,)))
            cdf, density = phi_parts(pre)
            slope[p, :, here] = (cdf + pre * density).astype(BF16)
            act = (pre * cdf).astype(BF16).astype(F32)
            diff[p * half : (p + 1) * half, here] = (act[:half] - act[half:]).astype(BF16)
    passed[...] = small[...]


def remote_slopes(normed, expand, small, *after):
    count = len(normed)
    _, half, _ = normed[0].shape
    hid = expand.shape[1]
    return call(
        functools.partial(remote_body, count),
        "remote_slopes",
        10**6,
        [((count, 2 * half, hid), BF16), ((count * half, hid), BF16), (small.shape, BF16)],
        [],
        *normed,
        expand,
        small,
        *after,
        read=10**5,
    )


def split(total, side, keep, send):
    parts, rows, _ = keep.shape
    for x in range(parts):
        mine = pl.multiple_of((2 * x + side) * rows, 16)
        theirs = pl.multiple_of((2 * x + 1 - side) * rows, 16)
        keep[x] = total[pl.ds(mine, rows), :]
        send[x] = total[pl.ds(theirs, rows), :].astype(BF16)


def added(small, more):
    return (small[...].astype(F32) + more[...].astype(F32)).astype(BF16)


def reduce_grad_body(
    d_0, d_1, d_2, d_3, diff_0, diff_12, diff_3, small, more, keep, send, sums, total
):
    units = total.shape[0]
    parts, _, _ = keep.shape
    line, core, _ = position(2 * parts)
    lanes = pl.ds(pl.multiple_of(line * units, LANES), units)
    diff = jnp.concatenate([diff_0[:, lanes], diff_12[:, lanes], diff_3[:, lanes]])
    every = jnp.concatenate([d_0[...], d_1[...], d_2[...], d_3[...]])
    total[...] = dot(diff, every, ((0,), (0,)))
    split(total, core, keep, send)
    sums[...] = added(small, more)


def reduce_grad(dbranch, diffs, small, more, line, inner):
    _, channels = dbranch[0].shape
    units = diffs[0].shape[1] // line
    parts, rows = inner // 2, units // inner
    return call(
        reduce_grad_body,
        "reduce_grad",
        2 * 10**9,
        [
            ((parts, rows, channels), F32),
            ((parts, rows, channels), BF16),
            (small.shape, BF16),
        ],
        [((units, channels), F32)],
        *dbranch,
        *diffs,
        small,
        more,
    )


def expand_slopes_body(
    d_0, d_1, d_2, d_3, slope_0, slope_12, slope_3, reduce, n_0, n_1, n_2, n_3,
    turned, dpre,
):
    half, channels = d_0.shape
    width = turned.shape[0]
    start = position(4)[0] * (channels // 4) // LANES * LANES
    lanes = pl.ds(pl.multiple_of(start, LANES), width)
    for p, ref in enumerate((n_0, n_1, n_2, n_3)):
        for v in range(2):
            at = (2 * p + v) * half
            turned[:, at : at + half] = ref[v, :, lanes].astype(F32).T.astype(BF16)
    every = jnp.concatenate([d_0[...], d_1[...], d_2[...], d_3[...]])
    slopes = [slope_0, slope_12.at[0], slope_12.at[1], slope_3.at[0]]
    for here in blocks(reduce.shape[0]):
        dhidden = dot(every, reduce[here, :], ((1,), (1,)))
        for p in range(4):
            part = dhidden[p * half : (p + 1) * half]
            slope = slopes[p][:, here].astype(F32)
            at = 2 * p * half
            dpre[at : at + half, here] = (part * slope[:half]).astype(BF16)
            dpre[at + half : at + 2 * half, here] = (-part * slope[half:]).astype(BF16)


def expand_slopes(dbranch, slopes, reduce, normed):
    half, _ = dbranch[0].shape
    hid = reduce.shape[0]
    return call(
        expand_slopes_body,
        "expand_slopes",
        4 * 10**9,
        [((2 * LANES, 8 * half), BF16), ((8 * half, hid), BF16)],
        [],
        *dbranch,
        *slopes,
        reduce,
        *normed,
    )


def expand_grad_body(turned, dpre, after, keep, send, total):
    own, hid = total.shape
    parts, _, _ = keep.shape
    line, core, _ = position(2 * parts)
    first = line * own
    lhs = turned[pl.ds(pl.multiple_of(first - first // LANES * LANES, 16), own), :]
    for here in blocks(hid):
        total[:, here] = dot(lhs, dpre[:, here], ((1,), (0,)))
    split(total, core, keep, send)


def expand_grad(turned, dpre, after, own, inner):
    hid = dpre.shape[1]
    shape = (inner // 2, own // inner, hid)
    return call(
        expand_grad_body,
        "expand_grad",
        10**6,
        [(shape, F32), (shape, BF16)],
        [((own, hid), F32)],
        turned,
        dpre,
        after,
        read=10**5,
    )


def merge_body(kept, got, small, more, keep, send, sums):
    _, _, mine = position(4)
    theirs = 1 - mine
    keep[...] = kept[mine] + got[mine].astype(F32)
    send[...] = (kept[theirs] + got[theirs].astype(F32)).astype(BF16)
    sums[...] = added(small, more) if more is not None else small[...]


def merge(kept, got, small, more=None):
    shape = kept.shape[1:]
    body = merge_body
    if more is None:
        body = lambda kept, got, small, *outs: merge_body(kept, got, small, None, *outs)
    return call(
        body,
        "merge",
        10**6,
        [(shape, F32), (shape, BF16), (small.shape, BF16)],
        [],
        kept,
        got,
        small,
        *(() if more is None else (more,)),
        read=10**5,
    )


def finish_body(keep_e, got_e, keep_r, got_r, small, more_1, more_2, more_3, out_e, out_r, kernel, gain, scale):
    out_e[...] = keep_e[...] + got_e[...].astype(F32)
    out_r[...] = keep_r[...] + got_r[...].astype(F32)
    low = small[...].astype(F32) + more_1[...].astype(F32)
    sums = low + (more_2[...].astype(F32) + more_3[...].astype(F32))
    for i in range(7):
        kernel[i] = sums[7 * i : 7 * i + 7]
    gain[...] = sums[49:50].reshape(gain.shape)
    scale[...] = sums[50:51].reshape(scale.shape)


def finish(keep_e, got_e, keep_r, got_r, small, more):
    channels = small.shape[1]
    return call(
        finish_body,
        "finish",
        10**8,
        [
            (keep_e.shape, F32),
            (keep_r.shape, F32),
            ((7, 7, channels), F32),
            ((channels,), F32),
            ((channels,), F32),
        ],
        [],
        keep_e,
        got_e,
        keep_r,
        got_r,
        small,
        *more,
    )


def grads_plain(every, dbranch_all, expand_weight, reduce_weight, my_line, my_inner, line, inner):
    channels, hid = expand_weight.shape
    units, own = hid // line, channels // line
    every = every.reshape(-1, channels)
    pre = dot(every, expand_weight, ((1,), (0,)))
    cdf, density = phi_parts(pre)
    slope = (cdf + pre * density).reshape(line, 2, -1, hid)
    hidden = (pre * cdf).astype(BF16).astype(F32).reshape(line, 2, -1, hid)
    diff = (hidden[:, 0] - hidden[:, 1]).astype(BF16).reshape(-1, hid)
    diff = lax.dynamic_slice_in_dim(diff, my_line * units, units, 1)
    dhidden = dot(dbranch_all, reduce_weight, ((1,), (1,))).reshape(line, -1, hid)
    dpre = jnp.stack([dhidden * slope[:, 0], -dhidden * slope[:, 1]], axis=1)
    dpre = dpre.astype(BF16).reshape(-1, hid)
    normed_own = lax.dynamic_slice_in_dim(every, my_line * own, own, 1)
    expand = dot(normed_own, dpre, ((0,), (0,))).reshape(inner, own // inner, hid)
    reduce = dot(diff, dbranch_all, ((0,), (0,))).reshape(inner, units // inner, channels)
    return halves(expand, my_inner & 1), halves(reduce, my_inner & 1)


def halves(part, side):
    part = part.reshape((part.shape[0] // 2, 2) + part.shape[1:])
    keep = lax.dynamic_index_in_dim(part, side, 1, keepdims=False)
    send = lax.dynamic_index_in_dim(part, 1 - side, 1, keepdims=False)
    return keep, send.astype(BF16)


def on_device(
    features, column_table, dw_kernel, norm_gain, expand_weight, reduce_weight, layer_scale
):
    rows, cols, channels = features.shape
    hid = expand_weight.shape[1]
    count = lax.axis_size("col")
    bits = count.bit_length() - 1
    line = 1 << ((bits + 1) // 2)
    inner = count // line
    inner_bits = inner.bit_length() - 1
    me = lax.axis_index("col")
    my_line, my_inner = me // inner, me % inner
    units, own = hid // line, channels // line
    total_cols = cols * count

    def swapped(block, mask):
        return lax.ppermute(block, "col", [(d, d ^ mask) for d in range(count)])

    mirror = lax.ppermute(column_table, "col", [(d, count - 1 - d) for d in range(count)])

    features_f = features.astype(F32)
    given = jnp.concatenate([column_table.astype(F32), norm_gain[None], layer_scale[None]])
    inside, across, turned = edges(features_f, given, mirror)
    inside = swapped(inside, 1)
    pairs = [(d, d + 1) for d in range(1, count - 1, 2)]
    across = lax.ppermute(across, "col", pairs + [(high, low) for low, high in pairs])
    normed, nhat, inv, wide = conv_norm(
        features_f, given, turned, inside, across, dw_kernel.astype(F32)
    )
    fast = line == 4 and inner == 4 and units % LANES == 0 and own % 64 == 0
    if fast:
        normed_2, normed_1 = swapped(normed, 2 * inner), swapped(normed, inner)
    else:
        others = [swapped(normed, p * inner) for p in range(1, line)]
    slope, diff, disagreement, dbranch, gscale = forward(
        1.0 / math.sqrt(rows * total_cols),
        normed.reshape(-1, channels),
        expand_weight,
        reduce_weight,
        wide,
        given,
        features.shape,
    )
    small = backward(
        dbranch, slope, expand_weight, reduce_weight, nhat, inv, given, gscale, wide
    )
    if fast:
        normed_3 = swapped(gate(normed_2, small), inner)
    dbranch_all = [dbranch] + [swapped(dbranch, p * inner) for p in range(1, line)]

    if fast:
        slope_12, diff_12, small = remote_slopes(
            [normed_1, normed_2], expand_weight, small, *dbranch_all[1:]
        )
        more = swapped(small, 2)
        slope_3, diff_3, small = remote_slopes([normed_3], expand_weight, small)
        keep_r, send_r, small = reduce_grad(
            dbranch_all, [diff, diff_12, diff_3], small, more, line, inner
        )
        more = swapped(small, 1)
        got_r = swapped(send_r, 1)
        turned, dpre = expand_slopes(
            dbranch_all,
            [slope, slope_12, slope_3],
            reduce_weight,
            [normed, normed_1, normed_2, normed_3],
        )
        keep_r, send_r, small = merge(keep_r, got_r, small, more)
        got_r = swapped(send_r, 2)
        keep_e, send_e = expand_grad(turned, dpre, small, own, inner)
        keep_e, send_e, small = merge(keep_e, swapped(send_e, 1), small)
        got_e = swapped(send_e, 2)
        more = [swapped(small, p * inner) for p in range(1, line)]
        sums = finish(keep_e, got_e, keep_r, got_r, small, more)
        return (disagreement, *sums)

    def line_sum(small):
        sums = [small] + [swapped(small, p * inner) for p in range(1, line)]
        sums = [part.astype(F32) for part in sums]
        while len(sums) > 1:
            sums = [low + high for low, high in zip(sums[::2], sums[1::2])]
        return sums[0]

    (keep_e, send_e), (keep_r, send_r) = grads_plain(
        jnp.stack([normed] + others),
        jnp.concatenate(dbranch_all),
        expand_weight,
        reduce_weight,
        my_line,
        my_inner,
        line,
        inner,
    )
    small = line_sum(small)
    for bit in range(inner_bits):
        sum_r = keep_r + swapped(send_r, 1 << bit).astype(F32)
        sum_e = keep_e + swapped(send_e, 1 << bit).astype(F32)
        small = small.astype(BF16)
        small = small.astype(F32) + swapped(small, 1 << bit).astype(F32)
        if bit < inner_bits - 1:
            side = (my_inner >> (bit + 1)) & 1
            keep_r, send_r = halves(sum_r, side)
            keep_e, send_e = halves(sum_e, side)
    grad_kernel = small[:49].reshape(7, 7, channels)
    return (
        disagreement,
        sum_e.reshape(own // inner, hid),
        sum_r.reshape(units // inner, channels),
        grad_kernel,
        small[49],
        small[50],
    )


def solution(mesh):
    in_specs = (P("groups", "col", None), P("col", None), P(), P(), P(), P(), P())
    out_specs = (
        P("groups", "col", None),
        P(("groups", "col"), None),
        P(("groups", "col"), None),
        P("groups", None, None),
        P("groups"),
        P("groups"),
    )
    return jax.shard_map(
        on_device, mesh=mesh, in_specs=in_specs, out_specs=out_specs, check_vma=False
    )
```

```python
import functools
import math

import jax
import jax.numpy as jnp
from jax import lax
from jax.experimental import pallas as pl
from jax.experimental.pallas import tpu as pltpu
from jax.sharding import PartitionSpec as P

BF16 = jnp.bfloat16
F32 = jnp.float32
LANES = 128
VMEM_GRANT = 16 << 20
BLOCK = 512


def phi_parts(pre):
    decay = jnp.exp(-0.5 * pre * pre)
    t = 1.0 / (1.0 + 0.23164189 * jnp.abs(pre))
    poly = 0.5307027145 * t - 0.7265760135
    poly = poly * t + 0.7107068705
    poly = poly * t - 0.142248368
    poly = poly * t + 0.127414796
    tail = poly * t * decay
    return jnp.where(pre < 0.0, tail, 1.0 - tail), decay * 0.3989422804014327


def call(body, name, flops, out_shape, scratch, *operands, read=10**8):
    return pl.pallas_call(
        body,
        in_specs=[pl.BlockSpec(memory_space=pltpu.VMEM) for _ in operands],
        out_specs=[pl.BlockSpec(memory_space=pltpu.VMEM) for _ in out_shape],
        out_shape=[jax.ShapeDtypeStruct(shape, dtype) for shape, dtype in out_shape],
        scratch_shapes=[pltpu.VMEM(shape, dtype) for shape, dtype in scratch],
        compiler_params=pltpu.CompilerParams(vmem_limit_bytes=VMEM_GRANT),
        cost_estimate=pl.CostEstimate(flops=flops, bytes_accessed=read, transcendentals=0),
        name=name,
    )(*operands)


def position(inner):
    me = lax.axis_index("col")
    return me // inner, me & 1, (me >> 1) & 1


def dot(lhs, rhs, contract):
    return lax.dot_general(lhs, rhs, (contract, ((), ())), preferred_element_type=F32)


def flipped(value):
    rows = value.shape[0]
    return jnp.concatenate([value[r : r + 1] for r in reversed(range(rows))], axis=0)


def edges_body(feat, table, mirror, inside, across, turned):
    _, cols, channels = feat.shape
    other = flipped(mirror[...].astype(F32))
    odd = (lax.axis_index("col") & 1) == 1
    for v, add in enumerate((table[...], other)):
        own = (feat[...] + add[None]).astype(BF16).astype(F32)
        first, last = own[:, :3], own[:, cols - 3 :]
        inside[v] = jnp.where(odd, first, last).astype(BF16)
        across[v] = jnp.where(odd, last, first).astype(BF16)
    turned[...] = other


def edges(features, table, mirror):
    rows, cols, channels = features.shape
    return call(
        edges_body,
        "edges",
        10**8,
        [
            ((2, rows, 3, channels), BF16),
            ((2, rows, 3, channels), BF16),
            ((cols, channels), F32),
        ],
        [],
        features,
        table,
        mirror,
    )


def conv_body(feat, table, turned, inside, across, dw, gain, normed, nhat, inv, wide, conv):
    rows, cols, channels = feat.shape
    odd = (lax.axis_index("col") & 1) == 1
    for v, add in enumerate((table[...], turned[...])):
        wide[v, :, 3 : 3 + cols, :] = (feat[...] + add[None]).astype(BF16).astype(F32)
        one, two = inside[v].astype(F32), across[v].astype(F32)
        wide[v, :, 0:3, :] = jnp.where(odd, one, two)
        wide[v, :, 3 + cols : 6 + cols, :] = jnp.where(odd, two, one)

    def tile(c, carry):
        lanes = pl.ds(pl.multiple_of(c * LANES, LANES), LANES)
        sums = [[jnp.zeros((cols, LANES), F32) for _ in range(rows)] for _ in range(2)]
        for j in range(7):
            for v in range(2):
                part = [wide[v, r, pl.ds(j, cols), lanes] for r in range(rows)]
                for i in range(7):
                    weight = dw[i, pl.ds(6 - j if v else j, 1), lanes]
                    for r in range(rows):
                        if 0 <= r + i - 3 < rows:
                            sums[v][r] = sums[v][r] + weight * part[r + i - 3]
        for v in range(2):
            for r in range(rows):
                conv[v, r, :, lanes] = sums[v][r]
        return carry

    lax.fori_loop(0, channels // LANES, tile, 0)
    for v in range(2):
        value = conv[v].reshape(rows * cols, channels)
        centred = value - jnp.mean(value, axis=-1, keepdims=True)
        inverse = lax.rsqrt(jnp.mean(centred * centred, axis=-1, keepdims=True) + 1e-06)
        value = centred * inverse
        nhat[v] = value
        inv[v] = jnp.broadcast_to(inverse, (rows * cols, LANES))
        normed[v] = (value * gain[...]).astype(BF16)


def conv_norm(features, table, turned, inside, across, dw, gain):
    rows, cols, channels = features.shape
    pixels = rows * cols
    return call(
        conv_body,
        "conv_norm",
        4 * 10**9,
        [
            ((2, pixels, channels), BF16),
            ((2, pixels, channels), F32),
            ((2, pixels, LANES), F32),
            ((2, rows, 16, channels), F32),
        ],
        [((2, rows, cols, channels), F32)],
        features,
        table,
        turned,
        inside,
        across,
        dw,
        gain,
    )


def blocks(total):
    return [slice(at, at + BLOCK) for at in range(0, total, BLOCK)]


def forward_body(
    scale, normed, expand, reduce, wide, ls, slope, diff, disagreement, dbranch, gscale, hidden
):
    pixels, channels = normed.shape
    half = pixels // 2
    rows, cols, _ = disagreement.shape
    for here in blocks(expand.shape[1]):
        pre = dot(normed[...], expand[:, here], ((1,), (0,)))
        cdf, density = phi_parts(pre)
        slope[:, here] = (cdf + pre * density).astype(BF16)
        act = (pre * cdf).astype(BF16)
        hidden[:, here] = act
        act = act.astype(F32)
        diff[:, here] = (act[:half] - act[half:]).astype(BF16)
    branch = dot(hidden[...], reduce[...], ((1,), (0,)))
    factor = ls[...].reshape(1, channels)
    outs = []
    for v in range(2):
        own = wide[v, :, 3 : 3 + cols, :].reshape(half, channels)
        outs.append((own + factor * branch[v * half : (v + 1) * half]).astype(BF16).astype(F32))
    difference = outs[0] - outs[1]
    disagreement[...] = difference.astype(BF16).reshape(rows, cols, channels)
    residual = (difference * scale).astype(BF16).astype(F32)
    gscale[...] = jnp.sum((branch[:half] - branch[half:]) * residual, axis=0, keepdims=True)
    dbranch[...] = (factor * residual).astype(BF16)


def forward(scale, normed, expand, reduce, wide, ls, shape):
    pixels, channels = normed.shape
    hid = expand.shape[1]
    return call(
        functools.partial(forward_body, scale),
        "forward",
        10**9,
        [
            ((pixels, hid), BF16),
            ((pixels // 2, hid), BF16),
            (shape, BF16),
            ((pixels // 2, channels), BF16),
            ((1, channels), F32),
        ],
        [((pixels, hid), BF16)],
        normed,
        expand,
        reduce,
        wide,
        ls,
        read=10**6,
    )


def backward_body(
    dbranch, slope, expand, reduce, nhat, inv, gain, gscale, wide, out, dpre, grad, taps, small
):
    half, channels = dbranch.shape
    _, rows, _, _ = wide.shape
    cols = half // rows
    for here in blocks(expand.shape[1]):
        dhidden = dot(dbranch[...], reduce[here, :], ((1,), (1,)))
        dpre[:half, here] = (dhidden * slope[:half, here].astype(F32)).astype(BF16)
        dpre[half:, here] = (-dhidden * slope[half:, here].astype(F32)).astype(BF16)
    dnormed = dot(dpre[...], expand[...], ((1,), (1,)))
    factor = gain[...]
    ggain = jnp.zeros((1, channels), F32)
    for v in range(2):
        here = slice(v * half, (v + 1) * half)
        ggain = ggain + jnp.sum(dnormed[here] * nhat[v], axis=0, keepdims=True)
        scaled = dnormed[here] * factor
        gm = jnp.mean(scaled, axis=-1, keepdims=True)
        gn = jnp.mean(scaled * nhat[v], axis=-1, keepdims=True)
        grad[here, :] = inv[v][:, :1] * (scaled - gm - nhat[v] * gn)

    def tile(c, carry):
        lanes = pl.ds(pl.multiple_of(c * LANES, LANES), LANES)
        dconv = [
            [grad[pl.ds(v * half + r * cols, cols), lanes] for r in range(rows)] for v in range(2)
        ]
        for j in range(7):
            part = [
                [wide[v, r, pl.ds(6 - j if v else j, cols), lanes] for r in range(rows)]
                for v in range(2)
            ]
            for i in range(7):
                sums = []
                for v in range(2):
                    total = None
                    for r in range(rows):
                        if 0 <= r + i - 3 < rows:
                            term = part[v][r + i - 3] * dconv[v][r]
                            total = term if total is None else total + term
                    sums.append(total)
                at = 8 * (7 * i + j)
                taps[at : at + 8, :] = sums[0] + sums[1]
        rolled = taps[pl.ds(0, 49, stride=8), :]
        for s in range(1, 8):
            rolled = rolled + taps[pl.ds(s, 49, stride=8), :]
        small[:49, lanes] = rolled
        return carry

    small[...] = jnp.zeros(small.shape, F32)
    lax.fori_loop(0, channels // LANES, tile, 0)
    small[49:50, :] = ggain
    small[50:51, :] = gscale[...]
    out[...] = small[...].astype(BF16)


def backward(dbranch, slope, expand, reduce, nhat, inv, gain, gscale, wide):
    half, channels = dbranch.shape
    hid = expand.shape[1]
    return call(
        backward_body,
        "backward",
        10**9,
        [((64, channels), BF16)],
        [
            ((2 * half, hid), BF16),
            ((2 * half, channels), F32),
            ((8 * 49, LANES), F32),
            ((64, channels), F32),
        ],
        dbranch,
        slope,
        expand,
        reduce,
        nhat,
        inv,
        gain,
        gscale,
        wide,
        read=10**6,
    )[0]


def gate_body(normed, dbranch, *rest):
    out = rest[-1]
    cut = normed.shape[0]
    out[:cut, :] = normed[...]
    out[cut:, :] = dbranch[...]


def gate(normed, dbranch, *after):
    rows, channels = normed.shape[0] + dbranch.shape[0], normed.shape[1]
    shapes = [((rows, channels), BF16)]
    return call(gate_body, "gate", 10**6, shapes, [], normed, dbranch, *after, read=10**5)[0]


def remote_body(count, *refs):
    normed, expand, slope, diff = refs[:count], refs[count], refs[count + 1], refs[count + 2]
    half = slope.shape[1] // 2
    for here in blocks(expand.shape[1]):
        for p in range(count):
            pre = dot(normed[p][: 2 * half, :], expand[:, here], ((1,), (0,)))
            cdf, density = phi_parts(pre)
            slope[p, :, here] = (cdf + pre * density).astype(BF16)
            act = (pre * cdf).astype(BF16).astype(F32)
            diff[p * half : (p + 1) * half, here] = (act[:half] - act[half:]).astype(BF16)


def remote_last_body(normed, expand, small, more, slope, diff, sums):
    remote_body(1, normed, expand, slope, diff)
    sums[...] = added(small, more)


def remote_slopes(normed, expand, half, *small):
    count = len(normed)
    hid = expand.shape[1]
    return call(
        remote_last_body if small else functools.partial(remote_body, count),
        "remote_slopes",
        10**6,
        [((count, 2 * half, hid), BF16), ((count * half, hid), BF16)]
        + [(part.shape, BF16) for part in small[:1]],
        [],
        *normed,
        expand,
        *small,
        read=10**5,
    )


def split(total, side, keep, send):
    parts, rows, _ = keep.shape
    for x in range(parts):
        mine = pl.multiple_of((2 * x + side) * rows, 16)
        theirs = pl.multiple_of((2 * x + 1 - side) * rows, 16)
        keep[x] = total[pl.ds(mine, rows), :]
        send[x] = total[pl.ds(theirs, rows), :].astype(BF16)


def added(small, more):
    return (small[...].astype(F32) + more[...].astype(F32)).astype(BF16)


def reduce_grad_body(
    d_0, d_1, d_2, packed, diff_0, diff_12, diff_3, keep, send, total
):
    units = total.shape[0]
    parts, _, _ = keep.shape
    line, core, _ = position(2 * parts)
    lanes = pl.ds(pl.multiple_of(line * units, LANES), units)
    diff = jnp.concatenate([diff_0[:, lanes], diff_12[:, lanes], diff_3[:, lanes]])
    every = jnp.concatenate([d_0[...], d_1[...], d_2[...], packed[2 * d_0.shape[0] :, :]])
    total[...] = dot(diff, every, ((0,), (0,)))
    split(total, core, keep, send)


def reduce_grad(dbranch, diffs, line, inner):
    _, channels = dbranch[0].shape
    units = diffs[0].shape[1] // line
    parts, rows = inner // 2, units // inner
    return call(
        reduce_grad_body,
        "reduce_grad",
        2 * 10**9,
        [
            ((parts, rows, channels), F32),
            ((parts, rows, channels), BF16),
        ],
        [((units, channels), F32)],
        *dbranch,
        *diffs,
    )


def expand_slopes_body(
    d_0, d_1, d_2, packed, slope_0, slope_12, slope_3, reduce, n_0, n_1, n_2, turned, dpre
):
    half, channels = d_0.shape
    width = turned.shape[0]
    start = position(4)[0] * (channels // 4) // LANES * LANES
    lanes = pl.ds(pl.multiple_of(start, LANES), width)
    for p, ref in enumerate((n_0, n_1, n_2, packed)):
        at = 2 * p * half
        turned[:, at : at + 2 * half] = ref[: 2 * half, lanes].astype(F32).T.astype(BF16)
    every = jnp.concatenate([d_0[...], d_1[...], d_2[...], packed[2 * d_0.shape[0] :, :]])
    slopes = [slope_0, slope_12.at[0], slope_12.at[1], slope_3.at[0]]
    for here in blocks(reduce.shape[0]):
        dhidden = dot(every, reduce[here, :], ((1,), (1,)))
        for p in range(4):
            part = dhidden[p * half : (p + 1) * half]
            slope = slopes[p][:, here].astype(F32)
            at = 2 * p * half
            dpre[at : at + half, here] = (part * slope[:half]).astype(BF16)
            dpre[at + half : at + 2 * half, here] = (-part * slope[half:]).astype(BF16)


def expand_slopes(dbranch, slopes, reduce, normed):
    half, _ = dbranch[0].shape
    hid = reduce.shape[0]
    return call(
        expand_slopes_body,
        "expand_slopes",
        4 * 10**9,
        [((2 * LANES, 8 * half), BF16), ((8 * half, hid), BF16)],
        [],
        *dbranch,
        *slopes,
        reduce,
        *normed,
    )


def expand_grad_body(turned, dpre, after, keep, send, total):
    own, hid = total.shape
    parts, _, _ = keep.shape
    line, core, _ = position(2 * parts)
    first = line * own
    lhs = turned[pl.ds(pl.multiple_of(first - first // LANES * LANES, 16), own), :]
    for here in blocks(hid):
        total[:, here] = dot(lhs, dpre[:, here], ((1,), (0,)))
    split(total, core, keep, send)


def expand_grad(turned, dpre, after, own, inner):
    hid = dpre.shape[1]
    shape = (inner // 2, own // inner, hid)
    return call(
        expand_grad_body,
        "expand_grad",
        10**6,
        [(shape, F32), (shape, BF16)],
        [((own, hid), F32)],
        turned,
        dpre,
        after,
        read=10**5,
    )


def merge_body(kept, got, small, more, keep, send, sums):
    _, _, mine = position(4)
    theirs = 1 - mine
    keep[...] = kept[mine] + got[mine].astype(F32)
    send[...] = (kept[theirs] + got[theirs].astype(F32)).astype(BF16)
    sums[...] = added(small, more) if more is not None else small[...]


def merge(kept, got, small, more=None):
    shape = kept.shape[1:]
    body = merge_body
    if more is None:
        body = lambda kept, got, small, *outs: merge_body(kept, got, small, None, *outs)
    return call(
        body,
        "merge",
        10**6,
        [(shape, F32), (shape, BF16), (small.shape, BF16)],
        [],
        kept,
        got,
        small,
        *(() if more is None else (more,)),
        read=10**5,
    )


def finish_body(keep_e, got_e, keep_r, got_r, small, more, out_e, out_r, kernel, gain, scale):
    out_e[...] = keep_e[...] + got_e[...].astype(F32)
    out_r[...] = keep_r[...] + got_r[...].astype(F32)
    sums = small[...].astype(F32) + more[...].astype(F32)
    for i in range(7):
        kernel[i] = sums[7 * i : 7 * i + 7]
    gain[...] = sums[49:50].reshape(gain.shape)
    scale[...] = sums[50:51].reshape(scale.shape)


def finish(keep_e, got_e, keep_r, got_r, small, more):
    channels = small.shape[1]
    return call(
        finish_body,
        "finish",
        10**8,
        [
            (keep_e.shape, F32),
            (keep_r.shape, F32),
            ((7, 7, channels), F32),
            ((channels,), F32),
            ((channels,), F32),
        ],
        [],
        keep_e,
        got_e,
        keep_r,
        got_r,
        small,
        more,
    )


def grads_plain(every, dbranch_all, expand_weight, reduce_weight, my_line, my_inner, line, inner):
    channels, hid = expand_weight.shape
    units, own = hid // line, channels // line
    every = every.reshape(-1, channels)
    pre = dot(every, expand_weight, ((1,), (0,)))
    cdf, density = phi_parts(pre)
    slope = (cdf + pre * density).reshape(line, 2, -1, hid)
    hidden = (pre * cdf).astype(BF16).astype(F32).reshape(line, 2, -1, hid)
    diff = (hidden[:, 0] - hidden[:, 1]).astype(BF16).reshape(-1, hid)
    diff = lax.dynamic_slice_in_dim(diff, my_line * units, units, 1)
    dhidden = dot(dbranch_all, reduce_weight, ((1,), (1,))).reshape(line, -1, hid)
    dpre = jnp.stack([dhidden * slope[:, 0], -dhidden * slope[:, 1]], axis=1)
    dpre = dpre.astype(BF16).reshape(-1, hid)
    normed_own = lax.dynamic_slice_in_dim(every, my_line * own, own, 1)
    expand = dot(normed_own, dpre, ((0,), (0,))).reshape(inner, own // inner, hid)
    reduce = dot(diff, dbranch_all, ((0,), (0,))).reshape(inner, units // inner, channels)
    return halves(expand, my_inner & 1), halves(reduce, my_inner & 1)


def halves(part, side):
    part = part.reshape((part.shape[0] // 2, 2) + part.shape[1:])
    keep = lax.dynamic_index_in_dim(part, side, 1, keepdims=False)
    send = lax.dynamic_index_in_dim(part, 1 - side, 1, keepdims=False)
    return keep, send.astype(BF16)


def on_device(
    features, column_table, dw_kernel, norm_gain, expand_weight, reduce_weight, layer_scale
):
    rows, cols, channels = features.shape
    hid = expand_weight.shape[1]
    count = lax.axis_size("col")
    bits = count.bit_length() - 1
    line = 1 << ((bits + 1) // 2)
    inner = count // line
    inner_bits = inner.bit_length() - 1
    me = lax.axis_index("col")
    my_line, my_inner = me // inner, me % inner
    units, own = hid // line, channels // line
    total_cols = cols * count

    def swapped(block, mask):
        return lax.ppermute(block, "col", [(d, d ^ mask) for d in range(count)])

    def line_sum(small):
        sums = [small] + [swapped(small, p * inner) for p in range(1, line)]
        sums = [part.astype(F32) for part in sums]
        while len(sums) > 1:
            sums = [low + high for low, high in zip(sums[::2], sums[1::2])]
        return sums[0]

    mirror = lax.ppermute(column_table, "col", [(d, count - 1 - d) for d in range(count)])

    features_f = features.astype(F32)
    table_f = column_table.astype(F32)
    gain = norm_gain[None]
    inside, across, turned = edges(features_f, table_f, mirror)
    inside = swapped(inside, 1)
    pairs = [(d, d + 1) for d in range(1, count - 1, 2)]
    across = lax.ppermute(across, "col", pairs + [(high, low) for low, high in pairs])
    normed, nhat, inv, wide = conv_norm(
        features_f, table_f, turned, inside, across, dw_kernel.astype(F32), gain
    )
    fast = line == 4 and inner == 4 and units % LANES == 0 and own % 64 == 0
    if fast:
        flat = normed.reshape(-1, channels)
        normed_2, normed_1 = swapped(flat, 2 * inner), swapped(flat, inner)
    else:
        others = [swapped(normed, p * inner) for p in range(1, line)]
    slope, diff, disagreement, dbranch, gscale = forward(
        1.0 / math.sqrt(rows * total_cols),
        normed.reshape(-1, channels),
        expand_weight,
        reduce_weight,
        wide,
        layer_scale,
        features.shape,
    )
    small = backward(
        dbranch, slope, expand_weight, reduce_weight, nhat, inv, gain, gscale, wide
    )
    if fast:
        dbranch_2, dbranch_1 = swapped(dbranch, 2 * inner), swapped(dbranch, inner)
        packed = swapped(gate(normed_2, dbranch_2, small, normed_1, dbranch_1), inner)
        dbranch_all = [dbranch, dbranch_1, dbranch_2, packed]
        half = dbranch.shape[0]
        more = swapped(small, 2)
        slope_12, diff_12 = remote_slopes([normed_1, normed_2], expand_weight, half)
        slope_3, diff_3, small = remote_slopes([packed], expand_weight, half, small, more)
        more = swapped(small, 1)
        keep_r, send_r = reduce_grad(dbranch_all, [diff, diff_12, diff_3], line, inner)
        got_r = swapped(send_r, 1)
        turned, dpre = expand_slopes(
            dbranch_all,
            [slope, slope_12, slope_3],
            reduce_weight,
            [flat, normed_1, normed_2],
        )
        keep_r, send_r, small = merge(keep_r, got_r, small, more)
        got_r = swapped(send_r, 2)
        keep_e, send_e = expand_grad(turned, dpre, small, own, inner)
        more = swapped(small, inner)
        keep_e, send_e, small = merge(keep_e, swapped(send_e, 1), small, more)
        got_e, more = swapped(send_e, 2), swapped(small, 2 * inner)
        sums = finish(keep_e, got_e, keep_r, got_r, small, more)
        return (disagreement, *sums)

    dbranch_all = [dbranch] + [swapped(dbranch, p * inner) for p in range(1, line)]
    (keep_e, send_e), (keep_r, send_r) = grads_plain(
        jnp.stack([normed] + others),
        jnp.concatenate(dbranch_all),
        expand_weight,
        reduce_weight,
        my_line,
        my_inner,
        line,
        inner,
    )
    small = line_sum(small)
    for bit in range(inner_bits):
        sum_r = keep_r + swapped(send_r, 1 << bit).astype(F32)
        sum_e = keep_e + swapped(send_e, 1 << bit).astype(F32)
        small = small.astype(BF16)
        small = small.astype(F32) + swapped(small, 1 << bit).astype(F32)
        if bit < inner_bits - 1:
            side = (my_inner >> (bit + 1)) & 1
            keep_r, send_r = halves(sum_r, side)
            keep_e, send_e = halves(sum_e, side)
    grad_kernel = small[:49].reshape(7, 7, channels)
    return (
        disagreement,
        sum_e.reshape(own // inner, hid),
        sum_r.reshape(units // inner, channels),
        grad_kernel,
        small[49],
        small[50],
    )


def solution(mesh):
    in_specs = (P("groups", "col", None), P("col", None), P(), P(), P(), P(), P())
    out_specs = (
        P("groups", "col", None),
        P(("groups", "col"), None),
        P(("groups", "col"), None),
        P("groups", None, None),
        P("groups"),
        P("groups"),
    )
    return jax.shard_map(
        on_device, mesh=mesh, in_specs=in_specs, out_specs=out_specs, check_vma=False
    )
```

```python
import functools
import math

import jax
import jax.numpy as jnp
from jax import lax
from jax.experimental import pallas as pl
from jax.experimental.pallas import tpu as pltpu
from jax.sharding import PartitionSpec as P

BF16 = jnp.bfloat16
F32 = jnp.float32
LANES = 128
VMEM_GRANT = 16 << 20
BLOCK = 512


def phi_parts(pre):
    decay = jnp.exp(-0.5 * pre * pre)
    t = 1.0 / (1.0 + 0.23164189 * jnp.abs(pre))
    poly = 0.5307027145 * t - 0.7265760135
    poly = poly * t + 0.7107068705
    poly = poly * t - 0.142248368
    poly = poly * t + 0.127414796
    tail = poly * t * decay
    return jnp.where(pre < 0.0, tail, 1.0 - tail), decay * 0.3989422804014327


def call(body, name, flops, out_shape, scratch, *operands, read=10**8):
    return pl.pallas_call(
        body,
        in_specs=[pl.BlockSpec(memory_space=pltpu.VMEM) for _ in operands],
        out_specs=[pl.BlockSpec(memory_space=pltpu.VMEM) for _ in out_shape],
        out_shape=[jax.ShapeDtypeStruct(shape, dtype) for shape, dtype in out_shape],
        scratch_shapes=[pltpu.VMEM(shape, dtype) for shape, dtype in scratch],
        compiler_params=pltpu.CompilerParams(vmem_limit_bytes=VMEM_GRANT),
        cost_estimate=pl.CostEstimate(flops=flops, bytes_accessed=read, transcendentals=0),
        name=name,
    )(*operands)


def position(inner):
    me = lax.axis_index("col")
    return me // inner, me & 1, (me >> 1) & 1


def dot(lhs, rhs, contract):
    return lax.dot_general(lhs, rhs, (contract, ((), ())), preferred_element_type=F32)


def flipped(value):
    rows = value.shape[0]
    return jnp.concatenate([value[r : r + 1] for r in reversed(range(rows))], axis=0)


def edges_body(feat, table, mirror, inside, across, turned):
    _, cols, channels = feat.shape
    other = flipped(mirror[...].astype(F32))
    odd = (lax.axis_index("col") & 1) == 1
    for v, add in enumerate((table[...], other)):
        own = (feat[...] + add[None]).astype(BF16).astype(F32)
        first, last = own[:, :3], own[:, cols - 3 :]
        inside[v] = jnp.where(odd, first, last).astype(BF16)
        across[v] = jnp.where(odd, last, first).astype(BF16)
    turned[...] = other


def edges(features, table, mirror):
    rows, cols, channels = features.shape
    return call(
        edges_body,
        "edges",
        10**8,
        [
            ((2, rows, 3, channels), BF16),
            ((2, rows, 3, channels), BF16),
            ((cols, channels), F32),
        ],
        [],
        features,
        table,
        mirror,
    )


def conv_body(feat, table, turned, inside, across, dw, gain, normed, nhat, inv, wide, conv):
    rows, cols, channels = feat.shape
    odd = (lax.axis_index("col") & 1) == 1
    for v, add in enumerate((table[...], turned[...])):
        wide[v, :, 3 : 3 + cols, :] = (feat[...] + add[None]).astype(BF16).astype(F32)
        one, two = inside[v].astype(F32), across[v].astype(F32)
        wide[v, :, 0:3, :] = jnp.where(odd, one, two)
        wide[v, :, 3 + cols : 6 + cols, :] = jnp.where(odd, two, one)

    def tile(c, carry):
        lanes = pl.ds(pl.multiple_of(c * LANES, LANES), LANES)
        sums = [[jnp.zeros((cols, LANES), F32) for _ in range(rows)] for _ in range(2)]
        for j in range(7):
            for v in range(2):
                part = [wide[v, r, pl.ds(j, cols), lanes] for r in range(rows)]
                for i in range(7):
                    weight = dw[i, pl.ds(6 - j if v else j, 1), lanes]
                    for r in range(rows):
                        if 0 <= r + i - 3 < rows:
                            sums[v][r] = sums[v][r] + weight * part[r + i - 3]
        for v in range(2):
            for r in range(rows):
                conv[v, r, :, lanes] = sums[v][r]
        return carry

    lax.fori_loop(0, channels // LANES, tile, 0)
    for v in range(2):
        value = conv[v].reshape(rows * cols, channels)
        centred = value - jnp.mean(value, axis=-1, keepdims=True)
        inverse = lax.rsqrt(jnp.mean(centred * centred, axis=-1, keepdims=True) + 1e-06)
        value = centred * inverse
        nhat[v] = value
        inv[v] = jnp.broadcast_to(inverse, (rows * cols, LANES))
        normed[v] = (value * gain[...]).astype(BF16)


def conv_norm(features, table, turned, inside, across, dw, gain):
    rows, cols, channels = features.shape
    pixels = rows * cols
    return call(
        conv_body,
        "conv_norm",
        4 * 10**9,
        [
            ((2, pixels, channels), BF16),
            ((2, pixels, channels), F32),
            ((2, pixels, LANES), F32),
            ((2, rows, 16, channels), F32),
        ],
        [((2, rows, cols, channels), F32)],
        features,
        table,
        turned,
        inside,
        across,
        dw,
        gain,
    )


def blocks(total):
    return [slice(at, at + BLOCK) for at in range(0, total, BLOCK)]


def forward_body(
    scale, normed, expand, reduce, wide, ls, slope, diff, disagreement, dbranch, gscale, hidden
):
    pixels, channels = normed.shape
    half = pixels // 2
    rows, cols, _ = disagreement.shape
    for here in blocks(expand.shape[1]):
        pre = dot(normed[...], expand[:, here], ((1,), (0,)))
        cdf, density = phi_parts(pre)
        slope[:, here] = (cdf + pre * density).astype(BF16)
        act = (pre * cdf).astype(BF16)
        hidden[:, here] = act
        act = act.astype(F32)
        diff[:, here] = (act[:half] - act[half:]).astype(BF16)
    branch = dot(hidden[...], reduce[...], ((1,), (0,)))
    factor = ls[...].reshape(1, channels)
    outs = []
    for v in range(2):
        own = wide[v, :, 3 : 3 + cols, :].reshape(half, channels)
        outs.append((own + factor * branch[v * half : (v + 1) * half]).astype(BF16).astype(F32))
    difference = outs[0] - outs[1]
    disagreement[...] = difference.astype(BF16).reshape(rows, cols, channels)
    residual = (difference * scale).astype(BF16).astype(F32)
    gscale[...] = jnp.sum((branch[:half] - branch[half:]) * residual, axis=0, keepdims=True)
    dbranch[...] = (factor * residual).astype(BF16)


def forward(scale, normed, expand, reduce, wide, ls, shape):
    pixels, channels = normed.shape
    hid = expand.shape[1]
    return call(
        functools.partial(forward_body, scale),
        "forward",
        10**9,
        [
            ((pixels, hid), BF16),
            ((pixels // 2, hid), BF16),
            (shape, BF16),
            ((pixels // 2, channels), BF16),
            ((1, channels), F32),
        ],
        [((pixels, hid), BF16)],
        normed,
        expand,
        reduce,
        wide,
        ls,
        read=10**6,
    )


def backward_body(dbranch, slope, expand, reduce, dnormed, dpre):
    half = dbranch.shape[0]
    for here in blocks(expand.shape[1]):
        dhidden = dot(dbranch[...], reduce[here, :], ((1,), (1,)))
        dpre[:, here] = dpre_of(dhidden, slope[:, here].astype(F32))
    dnormed[...] = dot(dpre[...], expand[...], ((1,), (1,)))


def backward(dbranch, slope, expand, reduce):
    half, channels = dbranch.shape
    hid = expand.shape[1]
    return call(
        backward_body,
        "backward",
        10**9,
        [((2 * half, channels), F32)],
        [((2 * half, hid), BF16)],
        dbranch,
        slope,
        expand,
        reduce,
        read=10**6,
    )[0]


def small_body(dnormed, nhat, inv, gain, gscale, wide, out, grad, taps, small):
    half, channels = dnormed.shape[0] // 2, dnormed.shape[1]
    _, rows, _, _ = wide.shape
    cols = half // rows
    factor = gain[...]
    ggain = jnp.zeros((1, channels), F32)
    for v in range(2):
        here = slice(v * half, (v + 1) * half)
        value = dnormed[here, :]
        ggain = ggain + jnp.sum(value * nhat[v], axis=0, keepdims=True)
        scaled = value * factor
        gm = jnp.mean(scaled, axis=-1, keepdims=True)
        gn = jnp.mean(scaled * nhat[v], axis=-1, keepdims=True)
        grad[here, :] = inv[v][:, :1] * (scaled - gm - nhat[v] * gn)

    def tile(c, carry):
        lanes = pl.ds(pl.multiple_of(c * LANES, LANES), LANES)
        dconv = [
            [grad[pl.ds(v * half + r * cols, cols), lanes] for r in range(rows)] for v in range(2)
        ]
        for j in range(7):
            part = [
                [wide[v, r, pl.ds(6 - j if v else j, cols), lanes] for r in range(rows)]
                for v in range(2)
            ]
            for i in range(7):
                sums = []
                for v in range(2):
                    total = None
                    for r in range(rows):
                        if 0 <= r + i - 3 < rows:
                            term = part[v][r + i - 3] * dconv[v][r]
                            total = term if total is None else total + term
                    sums.append(total)
                at = 8 * (7 * i + j)
                taps[at : at + 8, :] = sums[0] + sums[1]
        rolled = taps[pl.ds(0, 49, stride=8), :]
        for s in range(1, 8):
            rolled = rolled + taps[pl.ds(s, 49, stride=8), :]
        small[:49, lanes] = rolled
        return carry

    small[...] = jnp.zeros(small.shape, F32)
    lax.fori_loop(0, channels // LANES, tile, 0)
    small[49:50, :] = ggain
    small[50:51, :] = gscale[...]
    out[...] = small[...].astype(BF16)


def small_grads(dnormed, nhat, inv, gain, gscale, wide):
    channels = dnormed.shape[1]
    return call(
        small_body,
        "small_grads",
        10**6,
        [((64, channels), BF16)],
        [(dnormed.shape, F32), ((8 * 49, LANES), F32), ((64, channels), F32)],
        dnormed,
        nhat,
        inv,
        gain,
        gscale,
        wide,
        read=10**5,
    )[0]


def gate_body(block, *rest):
    rest[-1][...] = block[...]


def gate(block, *after):
    shapes = [(block.shape, block.dtype)]
    return call(gate_body, "gate", 10**6, shapes, [], block, *after, read=10**5)[0]


def split(total, side, keep, send):
    parts, rows, _ = keep.shape
    for x in range(parts):
        mine = pl.multiple_of((2 * x + side) * rows, 16)
        theirs = pl.multiple_of((2 * x + 1 - side) * rows, 16)
        keep[x] = total[pl.ds(mine, rows), :]
        send[x] = total[pl.ds(theirs, rows), :].astype(BF16)


def added(small, more):
    return (small[...].astype(F32) + more[...].astype(F32)).astype(BF16)


def slope_and_act(normed, expand):
    pre = dot(normed, expand, ((1,), (0,)))
    cdf, density = phi_parts(pre)
    return cdf + pre * density, (pre * cdf).astype(BF16)


def views_apart(act):
    half = act.shape[0] // 2
    return (act[:half].astype(F32) - act[half:].astype(F32)).astype(BF16)


def dpre_of(dhidden, slope):
    half = dhidden.shape[0]
    return jnp.concatenate([dhidden * slope[:half], -dhidden * slope[half:]]).astype(BF16)


def own_lanes(own, width):
    first = position(4)[0] * own
    start = first // LANES * LANES
    return pl.ds(pl.multiple_of(start, LANES), width), first - start


def near_body(
    n_0, n_1, n_2, d_0, d_1, d_2, slope_0, diff_0, expand, reduce, turned, dpre, total, diff
):
    half, channels = d_0.shape
    units = total.shape[0]
    lanes, _ = own_lanes(channels // 4, turned.shape[0])
    for p, ref in enumerate((n_0, n_1, n_2)):
        at = 2 * p * half
        turned[:, at : at + 2 * half] = ref[:, lanes].astype(F32).T.astype(BF16)
    every = jnp.concatenate([d_0[...], d_1[...], d_2[...]])
    diff[:half, :] = diff_0[...]
    both = jnp.concatenate([n_1[...], n_2[...]])
    for here in blocks(reduce.shape[0]):
        slope, act = slope_and_act(both, expand[:, here])
        slopes = [slope_0[:, here].astype(F32), slope[: 2 * half], slope[2 * half :]]
        diff[half : 2 * half, here] = views_apart(act[: 2 * half])
        diff[2 * half :, here] = views_apart(act[2 * half :])
        dhidden = dot(every, reduce[here, :], ((1,), (1,)))
        for p in range(3):
            part = dpre_of(dhidden[p * half : (p + 1) * half], slopes[p])
            dpre[2 * p * half : 2 * (p + 1) * half, here] = part
    lanes = pl.ds(pl.multiple_of(position(4)[0] * units, LANES), units)
    total[...] = dot(diff[:, lanes], every, ((0,), (0,)))


def near(normed, dbranch, slope, diff, expand, reduce, line):
    half, channels = dbranch[0].shape
    hid = expand.shape[1]
    return call(
        near_body,
        "near",
        10**6,
        [
            ((2 * LANES, 6 * half), BF16),
            ((6 * half, hid), BF16),
            ((hid // line, channels), F32),
        ],
        [((3 * half, hid), BF16)],
        *normed,
        *dbranch,
        slope,
        diff,
        expand,
        reduce,
        read=10**5,
    )


def far_reduce_body(n_3, d_3, expand, part, small, more, keep, send, sums, total):
    units = total.shape[0]
    line, core, _ = position(4)
    lanes = pl.ds(pl.multiple_of(line * units, LANES), units)
    _, act = slope_and_act(n_3[...], expand[:, lanes])
    total[...] = part[...] + dot(views_apart(act), d_3[...], ((0,), (0,)))
    split(total, core, keep, send)
    sums[...] = added(small, more)


def far_reduce(n_3, d_3, expand, part, small, more, inner):
    units, channels = part.shape
    shape = (inner // 2, units // inner, channels)
    return call(
        far_reduce_body,
        "far_reduce",
        10**6,
        [(shape, F32), (shape, BF16), (small.shape, BF16)],
        [((units, channels), F32)],
        n_3,
        d_3,
        expand,
        part,
        small,
        more,
        read=10**5,
    )


def far_expand_body(n_3, d_3, expand, reduce, after, turned, dpre):
    lanes, _ = own_lanes(n_3.shape[1] // 4, turned.shape[0])
    turned[...] = n_3[:, lanes].astype(F32).T.astype(BF16)
    for here in blocks(reduce.shape[0]):
        slope, _ = slope_and_act(n_3[...], expand[:, here])
        dpre[:, here] = dpre_of(dot(d_3[...], reduce[here, :], ((1,), (1,))), slope)


def far_expand(n_3, d_3, expand, reduce, after):
    rows = n_3.shape[0]
    hid = expand.shape[1]
    return call(
        far_expand_body,
        "far_expand",
        10**9,
        [((2 * LANES, rows), BF16), ((rows, hid), BF16)],
        [],
        n_3,
        d_3,
        expand,
        reduce,
        after,
        read=10**6,
    )


def expand_grad_body(turned, turned_3, dpre, dpre_3, after, keep, send, total):
    own, hid = total.shape
    _, core, _ = position(4)
    _, first = own_lanes(own, turned.shape[0])
    rows = pl.ds(pl.multiple_of(first, 16), own)
    for here in blocks(hid):
        part = dot(turned[rows, :], dpre[:, here], ((1,), (0,)))
        total[:, here] = part + dot(turned_3[rows, :], dpre_3[:, here], ((1,), (0,)))
    split(total, core, keep, send)


def expand_grad(turned, turned_3, dpre, dpre_3, after, own, inner):
    hid = dpre.shape[1]
    shape = (inner // 2, own // inner, hid)
    return call(
        expand_grad_body,
        "expand_grad",
        10**6,
        [(shape, F32), (shape, BF16)],
        [((own, hid), F32)],
        turned,
        turned_3,
        dpre,
        dpre_3,
        after,
        read=10**5,
    )


def merge_body(kept, got, keep, send):
    _, _, mine = position(4)
    theirs = 1 - mine
    keep[...] = kept[mine] + got[mine].astype(F32)
    send[...] = (kept[theirs] + got[theirs].astype(F32)).astype(BF16)


def merge_small_body(kept, got, small, more, keep, send, sums):
    merge_body(kept, got, keep, send)
    sums[...] = added(small, more)


def merge(kept, got, *small):
    shape = kept.shape[1:]
    return call(
        merge_small_body if small else merge_body,
        "merge",
        10**6,
        [(shape, F32), (shape, BF16)] + [(part.shape, BF16) for part in small[:1]],
        [],
        kept,
        got,
        *small,
        read=10**5,
    )


def finish_body(
    keep_e, got_e, keep_r, got_r, small, more, out_e, out_r, kernel, gain, scale
):
    out_e[...] = keep_e[...] + got_e[...].astype(F32)
    out_r[...] = keep_r[...] + got_r[...].astype(F32)
    sums = small[...].astype(F32) + more[...].astype(F32)
    for i in range(7):
        kernel[i] = sums[7 * i : 7 * i + 7]
    gain[...] = sums[49:50].reshape(gain.shape)
    scale[...] = sums[50:51].reshape(scale.shape)


def finish(keep_e, got_e, keep_r, got_r, small, more):
    channels = small.shape[1]
    return call(
        finish_body,
        "finish",
        10**8,
        [
            (keep_e.shape, F32),
            (keep_r.shape, F32),
            ((7, 7, channels), F32),
            ((channels,), F32),
            ((channels,), F32),
        ],
        [],
        keep_e,
        got_e,
        keep_r,
        got_r,
        small,
        more,
    )


def grads_plain(every, dbranch_all, expand_weight, reduce_weight, my_line, my_inner, line, inner):
    channels, hid = expand_weight.shape
    units, own = hid // line, channels // line
    every = every.reshape(-1, channels)
    pre = dot(every, expand_weight, ((1,), (0,)))
    cdf, density = phi_parts(pre)
    slope = (cdf + pre * density).reshape(line, 2, -1, hid)
    hidden = (pre * cdf).astype(BF16).astype(F32).reshape(line, 2, -1, hid)
    diff = (hidden[:, 0] - hidden[:, 1]).astype(BF16).reshape(-1, hid)
    diff = lax.dynamic_slice_in_dim(diff, my_line * units, units, 1)
    dhidden = dot(dbranch_all, reduce_weight, ((1,), (1,))).reshape(line, -1, hid)
    dpre = jnp.stack([dhidden * slope[:, 0], -dhidden * slope[:, 1]], axis=1)
    dpre = dpre.astype(BF16).reshape(-1, hid)
    normed_own = lax.dynamic_slice_in_dim(every, my_line * own, own, 1)
    expand = dot(normed_own, dpre, ((0,), (0,))).reshape(inner, own // inner, hid)
    reduce = dot(diff, dbranch_all, ((0,), (0,))).reshape(inner, units // inner, channels)
    return halves(expand, my_inner & 1), halves(reduce, my_inner & 1)


def halves(part, side):
    part = part.reshape((part.shape[0] // 2, 2) + part.shape[1:])
    keep = lax.dynamic_index_in_dim(part, side, 1, keepdims=False)
    send = lax.dynamic_index_in_dim(part, 1 - side, 1, keepdims=False)
    return keep, send.astype(BF16)


def on_device(
    features, column_table, dw_kernel, norm_gain, expand_weight, reduce_weight, layer_scale
):
    rows, cols, channels = features.shape
    hid = expand_weight.shape[1]
    count = lax.axis_size("col")
    bits = count.bit_length() - 1
    line = 1 << ((bits + 1) // 2)
    inner = count // line
    inner_bits = inner.bit_length() - 1
    me = lax.axis_index("col")
    my_line, my_inner = me // inner, me % inner
    units, own = hid // line, channels // line
    total_cols = cols * count

    def swapped(block, mask):
        return lax.ppermute(block, "col", [(d, d ^ mask) for d in range(count)])

    def line_sum(small):
        sums = [small] + [swapped(small, p * inner) for p in range(1, line)]
        sums = [part.astype(F32) for part in sums]
        while len(sums) > 1:
            sums = [low + high for low, high in zip(sums[::2], sums[1::2])]
        return sums[0]

    mirror = lax.ppermute(column_table, "col", [(d, count - 1 - d) for d in range(count)])

    features_f = features.astype(F32)
    table_f = column_table.astype(F32)
    gain = norm_gain[None]
    inside, across, turned = edges(features_f, table_f, mirror)
    inside = swapped(inside, 1)
    pairs = [(d, d + 1) for d in range(1, count - 1, 2)]
    across = lax.ppermute(across, "col", pairs + [(high, low) for low, high in pairs])
    normed, nhat, inv, wide = conv_norm(
        features_f, table_f, turned, inside, across, dw_kernel.astype(F32), gain
    )
    fast = line == 4 and inner == 4 and units % LANES == 0 and own % 64 == 0
    if fast:
        flat = normed.reshape(-1, channels)
        normed_2, normed_1 = swapped(flat, 2 * inner), swapped(flat, inner)
    else:
        others = [swapped(normed, p * inner) for p in range(1, line)]
    slope, diff, disagreement, dbranch, gscale = forward(
        1.0 / math.sqrt(rows * total_cols),
        normed.reshape(-1, channels),
        expand_weight,
        reduce_weight,
        wide,
        layer_scale,
        features.shape,
    )
    dnormed = backward(dbranch, slope, expand_weight, reduce_weight)
    small = small_grads(dnormed, nhat, inv, gain, gscale, wide)
    if fast:
        dbranch_2, dbranch_1 = swapped(dbranch, 2 * inner), swapped(dbranch, inner)
        normed_3 = swapped(gate(normed_2, dnormed, normed_1), inner)
        dbranch_3 = swapped(gate(dbranch_2, small, dbranch_1), inner)
        more = swapped(small, 2)
        turned, dpre, part = near(
            [flat, normed_1, normed_2],
            [dbranch, dbranch_1, dbranch_2],
            slope,
            diff,
            expand_weight,
            reduce_weight,
            line,
        )
        keep_r, send_r, small = far_reduce(
            normed_3, dbranch_3, expand_weight, part, small, more, inner
        )
        got_r, more = swapped(send_r, 1), swapped(small, 1)
        turned_3, dpre_3 = far_expand(normed_3, dbranch_3, expand_weight, reduce_weight, small)
        keep_r, send_r, small = merge(keep_r, got_r, small, more)
        got_r, more = swapped(send_r, 2), swapped(small, inner)
        keep_e, send_e = expand_grad(turned, turned_3, dpre, dpre_3, small, own, inner)
        keep_e, send_e, small = merge(keep_e, swapped(send_e, 1), small, more)
        got_e, more = swapped(send_e, 2), swapped(small, 2 * inner)
        sums = finish(keep_e, got_e, keep_r, got_r, small, more)
        return (disagreement, *sums)

    dbranch_all = [dbranch] + [swapped(dbranch, p * inner) for p in range(1, line)]
    (keep_e, send_e), (keep_r, send_r) = grads_plain(
        jnp.stack([normed] + others),
        jnp.concatenate(dbranch_all),
        expand_weight,
        reduce_weight,
        my_line,
        my_inner,
        line,
        inner,
    )
    small = line_sum(small)
    for bit in range(inner_bits):
        sum_r = keep_r + swapped(send_r, 1 << bit).astype(F32)
        sum_e = keep_e + swapped(send_e, 1 << bit).astype(F32)
        small = small.astype(BF16)
        small = small.astype(F32) + swapped(small, 1 << bit).astype(F32)
        if bit < inner_bits - 1:
            side = (my_inner >> (bit + 1)) & 1
            keep_r, send_r = halves(sum_r, side)
            keep_e, send_e = halves(sum_e, side)
    grad_kernel = small[:49].reshape(7, 7, channels)
    return (
        disagreement,
        sum_e.reshape(own // inner, hid),
        sum_r.reshape(units // inner, channels),
        grad_kernel,
        small[49],
        small[50],
    )


def solution(mesh):
    in_specs = (P("groups", "col", None), P("col", None), P(), P(), P(), P(), P())
    out_specs = (
        P("groups", "col", None),
        P(("groups", "col"), None),
        P(("groups", "col"), None),
        P("groups", None, None),
        P("groups"),
        P("groups"),
    )
    return jax.shard_map(
        on_device, mesh=mesh, in_specs=in_specs, out_specs=out_specs, check_vma=False
    )
```

```python
import functools
import math

import jax
import jax.numpy as jnp
from jax import lax
from jax.experimental import pallas as pl
from jax.experimental.pallas import tpu as pltpu
from jax.sharding import PartitionSpec as P

BF16 = jnp.bfloat16
F32 = jnp.float32
LANES = 128
VMEM_GRANT = 16 << 20
BLOCK = 512


def phi_parts(pre):
    decay = jnp.exp(-0.5 * pre * pre)
    t = 1.0 / (1.0 + 0.23164189 * jnp.abs(pre))
    poly = 0.5307027145 * t - 0.7265760135
    poly = poly * t + 0.7107068705
    poly = poly * t - 0.142248368
    poly = poly * t + 0.127414796
    tail = poly * t * decay
    return jnp.where(pre < 0.0, tail, 1.0 - tail), decay * 0.3989422804014327


def call(body, name, flops, out_shape, scratch, *operands, read=10**8):
    return pl.pallas_call(
        body,
        in_specs=[pl.BlockSpec(memory_space=pltpu.VMEM) for _ in operands],
        out_specs=[pl.BlockSpec(memory_space=pltpu.VMEM) for _ in out_shape],
        out_shape=[jax.ShapeDtypeStruct(shape, dtype) for shape, dtype in out_shape],
        scratch_shapes=[pltpu.VMEM(shape, dtype) for shape, dtype in scratch],
        compiler_params=pltpu.CompilerParams(vmem_limit_bytes=VMEM_GRANT),
        cost_estimate=pl.CostEstimate(flops=flops, bytes_accessed=read, transcendentals=0),
        name=name,
    )(*operands)


def position(inner):
    me = lax.axis_index("col")
    return me // inner, me & 1, (me >> 1) & 1


def dot(lhs, rhs, contract):
    return lax.dot_general(lhs, rhs, (contract, ((), ())), preferred_element_type=F32)


def flipped(value):
    rows = value.shape[0]
    return jnp.concatenate([value[r : r + 1] for r in reversed(range(rows))], axis=0)


def edges_body(feat, table, mirror, inside, across, turned):
    _, cols, channels = feat.shape
    other = flipped(mirror[...].astype(F32))
    odd = (lax.axis_index("col") & 1) == 1
    for v, add in enumerate((table[...], other)):
        own = (feat[...] + add[None]).astype(BF16).astype(F32)
        first, last = own[:, :3], own[:, cols - 3 :]
        inside[v] = jnp.where(odd, first, last).astype(BF16)
        across[v] = jnp.where(odd, last, first).astype(BF16)
    turned[...] = other


def edges(features, table, mirror):
    rows, cols, channels = features.shape
    return call(
        edges_body,
        "edges",
        10**8,
        [
            ((2, rows, 3, channels), BF16),
            ((2, rows, 3, channels), BF16),
            ((cols, channels), F32),
        ],
        [],
        features,
        table,
        mirror,
    )


def conv_body(feat, table, turned, inside, across, dw, gain, normed, nhat, inv, wide, conv):
    rows, cols, channels = feat.shape
    odd = (lax.axis_index("col") & 1) == 1
    for v, add in enumerate((table[...], turned[...])):
        wide[v, :, 3 : 3 + cols, :] = (feat[...] + add[None]).astype(BF16).astype(F32)
        one, two = inside[v].astype(F32), across[v].astype(F32)
        wide[v, :, 0:3, :] = jnp.where(odd, one, two)
        wide[v, :, 3 + cols : 6 + cols, :] = jnp.where(odd, two, one)

    def tile(c, carry):
        lanes = pl.ds(pl.multiple_of(c * LANES, LANES), LANES)
        sums = [[jnp.zeros((cols, LANES), F32) for _ in range(rows)] for _ in range(2)]
        for j in range(7):
            for v in range(2):
                part = [wide[v, r, pl.ds(j, cols), lanes] for r in range(rows)]
                for i in range(7):
                    weight = dw[i, pl.ds(6 - j if v else j, 1), lanes]
                    for r in range(rows):
                        if 0 <= r + i - 3 < rows:
                            sums[v][r] = sums[v][r] + weight * part[r + i - 3]
        for v in range(2):
            for r in range(rows):
                conv[v, r, :, lanes] = sums[v][r]
        return carry

    lax.fori_loop(0, channels // LANES, tile, 0)
    for v in range(2):
        value = conv[v].reshape(rows * cols, channels)
        centred = value - jnp.mean(value, axis=-1, keepdims=True)
        inverse = lax.rsqrt(jnp.mean(centred * centred, axis=-1, keepdims=True) + 1e-06)
        value = centred * inverse
        nhat[v] = value
        inv[v] = jnp.broadcast_to(inverse, (rows * cols, LANES))
        normed[v] = (value * gain[...]).astype(BF16)


def conv_norm(features, table, turned, inside, across, dw, gain):
    rows, cols, channels = features.shape
    pixels = rows * cols
    return call(
        conv_body,
        "conv_norm",
        4 * 10**9,
        [
            ((2, pixels, channels), BF16),
            ((2, pixels, channels), F32),
            ((2, pixels, LANES), F32),
            ((2, rows, 16, channels), F32),
        ],
        [((2, rows, cols, channels), F32)],
        features,
        table,
        turned,
        inside,
        across,
        dw,
        gain,
    )


def blocks(total):
    return [slice(at, at + BLOCK) for at in range(0, total, BLOCK)]


def forward_body(
    scale, normed, expand, reduce, wide, ls, slope, diff, disagreement, dbranch, gscale, hidden
):
    pixels, channels = normed.shape
    half = pixels // 2
    rows, cols, _ = disagreement.shape
    for here in blocks(expand.shape[1]):
        pre = dot(normed[...], expand[:, here], ((1,), (0,)))
        cdf, density = phi_parts(pre)
        slope[:, here] = (cdf + pre * density).astype(BF16)
        act = (pre * cdf).astype(BF16)
        hidden[:, here] = act
        act = act.astype(F32)
        diff[:, here] = (act[:half] - act[half:]).astype(BF16)
    branch = dot(hidden[...], reduce[...], ((1,), (0,)))
    factor = ls[...].reshape(1, channels)
    outs = []
    for v in range(2):
        own = wide[v, :, 3 : 3 + cols, :].reshape(half, channels)
        outs.append((own + factor * branch[v * half : (v + 1) * half]).astype(BF16).astype(F32))
    difference = outs[0] - outs[1]
    disagreement[...] = difference.astype(BF16).reshape(rows, cols, channels)
    residual = (difference * scale).astype(BF16).astype(F32)
    gscale[...] = jnp.sum((branch[:half] - branch[half:]) * residual, axis=0, keepdims=True)
    dbranch[...] = (factor * residual).astype(BF16)


def forward(scale, normed, expand, reduce, wide, ls, shape):
    pixels, channels = normed.shape
    hid = expand.shape[1]
    return call(
        functools.partial(forward_body, scale),
        "forward",
        10**9,
        [
            ((pixels, hid), BF16),
            ((pixels // 2, hid), BF16),
            (shape, BF16),
            ((pixels // 2, channels), BF16),
            ((1, channels), F32),
        ],
        [((pixels, hid), BF16)],
        normed,
        expand,
        reduce,
        wide,
        ls,
        read=10**6,
    )


def backward_body(dbranch, slope, expand, reduce, dnormed, dpre):
    half = dbranch.shape[0]
    for here in blocks(expand.shape[1]):
        dhidden = dot(dbranch[...], reduce[here, :], ((1,), (1,)))
        dpre[:, here] = dpre_of(dhidden, slope[:, here].astype(F32))
    dnormed[...] = dot(dpre[...], expand[...], ((1,), (1,)))


def backward(dbranch, slope, expand, reduce):
    half, channels = dbranch.shape
    hid = expand.shape[1]
    return call(
        backward_body,
        "backward",
        10**9,
        [((2 * half, channels), F32)],
        [((2 * half, hid), BF16)],
        dbranch,
        slope,
        expand,
        reduce,
        read=10**6,
    )[0]


def small_body(dnormed, nhat, inv, gain, gscale, wide, *rest):
    out, grad, taps, small = rest[-4:]
    half, channels = dnormed.shape[0] // 2, dnormed.shape[1]
    _, rows, _, _ = wide.shape
    cols = half // rows
    factor = gain[...]
    ggain = jnp.zeros((1, channels), F32)
    for v in range(2):
        here = slice(v * half, (v + 1) * half)
        value = dnormed[here, :]
        ggain = ggain + jnp.sum(value * nhat[v], axis=0, keepdims=True)
        scaled = value * factor
        gm = jnp.mean(scaled, axis=-1, keepdims=True)
        gn = jnp.mean(scaled * nhat[v], axis=-1, keepdims=True)
        grad[here, :] = inv[v][:, :1] * (scaled - gm - nhat[v] * gn)

    def tile(c, carry):
        lanes = pl.ds(pl.multiple_of(c * LANES, LANES), LANES)
        dconv = [
            [grad[pl.ds(v * half + r * cols, cols), lanes] for r in range(rows)] for v in range(2)
        ]
        for j in range(7):
            part = [
                [wide[v, r, pl.ds(6 - j if v else j, cols), lanes] for r in range(rows)]
                for v in range(2)
            ]
            for i in range(7):
                sums = []
                for v in range(2):
                    total = None
                    for r in range(rows):
                        if 0 <= r + i - 3 < rows:
                            term = part[v][r + i - 3] * dconv[v][r]
                            total = term if total is None else total + term
                    sums.append(total)
                at = 8 * (7 * i + j)
                taps[at : at + 8, :] = sums[0] + sums[1]
        rolled = taps[pl.ds(0, 49, stride=8), :]
        for s in range(1, 8):
            rolled = rolled + taps[pl.ds(s, 49, stride=8), :]
        small[:49, lanes] = rolled
        return carry

    small[...] = jnp.zeros(small.shape, F32)
    lax.fori_loop(0, channels // LANES, tile, 0)
    small[49:50, :] = ggain
    small[50:51, :] = gscale[...]
    out[...] = small[...].astype(BF16)


def small_grads(dnormed, nhat, inv, gain, gscale, wide, *after):
    channels = dnormed.shape[1]
    return call(
        small_body,
        "small_grads",
        10**6,
        [((64, channels), BF16)],
        [(dnormed.shape, F32), ((8 * 49, LANES), F32), ((64, channels), F32)],
        dnormed,
        nhat,
        inv,
        gain,
        gscale,
        wide,
        *after,
        read=10**5,
    )[0]


def gate_body(block, *rest):
    rest[-1][...] = block[...]


def gate(block, *after):
    shapes = [(block.shape, block.dtype)]
    return call(gate_body, "gate", 10**6, shapes, [], block, *after, read=10**5)[0]


def split(total, side, keep, send):
    parts, rows, _ = keep.shape
    for x in range(parts):
        mine = pl.multiple_of((2 * x + side) * rows, 16)
        theirs = pl.multiple_of((2 * x + 1 - side) * rows, 16)
        keep[x] = total[pl.ds(mine, rows), :]
        send[x] = total[pl.ds(theirs, rows), :].astype(BF16)


def added(small, more):
    return (small[...].astype(F32) + more[...].astype(F32)).astype(BF16)


def slope_and_act(normed, expand):
    pre = dot(normed, expand, ((1,), (0,)))
    cdf, density = phi_parts(pre)
    return cdf + pre * density, (pre * cdf).astype(BF16)


def views_apart(act):
    half = act.shape[0] // 2
    return (act[:half].astype(F32) - act[half:].astype(F32)).astype(BF16)


def dpre_of(dhidden, slope):
    half = dhidden.shape[0]
    return jnp.concatenate([dhidden * slope[:half], -dhidden * slope[half:]]).astype(BF16)


def own_lanes(own, width):
    first = position(4)[0] * own
    start = first // LANES * LANES
    return pl.ds(pl.multiple_of(start, LANES), width), first - start


def near_reduce_body(n_1, n_2, d_0, d_1, d_2, diff_0, expand, total):
    half = d_0.shape[0]
    units = total.shape[0]
    lanes = pl.ds(pl.multiple_of(position(4)[0] * units, LANES), units)
    both = jnp.concatenate([n_1[...], n_2[...]])
    _, act = slope_and_act(both, expand[:, lanes])
    diffs = [diff_0[:, lanes], views_apart(act[: 2 * half]), views_apart(act[2 * half :])]
    every = jnp.concatenate([d_0[...], d_1[...], d_2[...]])
    total[...] = dot(jnp.concatenate(diffs), every, ((0,), (0,)))


def near_reduce(normed, dbranch, diff, expand, line):
    channels, hid = expand.shape
    return call(
        near_reduce_body,
        "near_reduce",
        10**6,
        [((hid // line, channels), F32)],
        [],
        *normed,
        *dbranch,
        diff,
        expand,
        read=10**5,
    )[0]


def near_expand_body(n_0, n_1, n_2, d_0, d_1, d_2, slope_0, expand, reduce, after, turned, dpre):
    half, channels = d_0.shape
    lanes, _ = own_lanes(channels // 4, turned.shape[0])
    for p, ref in enumerate((n_0, n_1, n_2)):
        at = 2 * p * half
        turned[:, at : at + 2 * half] = ref[:, lanes].astype(F32).T.astype(BF16)
    every = jnp.concatenate([d_0[...], d_1[...], d_2[...]])
    both = jnp.concatenate([n_1[...], n_2[...]])
    for here in blocks(reduce.shape[0]):
        slope, _ = slope_and_act(both, expand[:, here])
        slopes = [slope_0[:, here].astype(F32), slope[: 2 * half], slope[2 * half :]]
        dhidden = dot(every, reduce[here, :], ((1,), (1,)))
        for p in range(3):
            part = dpre_of(dhidden[p * half : (p + 1) * half], slopes[p])
            dpre[2 * p * half : 2 * (p + 1) * half, here] = part


def near_expand(normed, dbranch, slope, expand, reduce, after):
    half, _ = dbranch[0].shape
    hid = expand.shape[1]
    return call(
        near_expand_body,
        "near_expand",
        10**9,
        [((2 * LANES, 6 * half), BF16), ((6 * half, hid), BF16)],
        [],
        *normed,
        *dbranch,
        slope,
        expand,
        reduce,
        after,
        read=10**6,
    )


def far_reduce_body(n_3, d_3, expand, part, small, more, keep, send, sums, total):
    units = total.shape[0]
    line, core, _ = position(4)
    lanes = pl.ds(pl.multiple_of(line * units, LANES), units)
    _, act = slope_and_act(n_3[...], expand[:, lanes])
    total[...] = part[...] + dot(views_apart(act), d_3[...], ((0,), (0,)))
    split(total, core, keep, send)
    sums[...] = added(small, more)


def far_reduce(n_3, d_3, expand, part, small, more, inner):
    units, channels = part.shape
    shape = (inner // 2, units // inner, channels)
    return call(
        far_reduce_body,
        "far_reduce",
        10**6,
        [(shape, F32), (shape, BF16), (small.shape, BF16)],
        [((units, channels), F32)],
        n_3,
        d_3,
        expand,
        part,
        small,
        more,
        read=10**5,
    )


def far_expand_body(n_3, d_3, expand, reduce, after, turned, dpre):
    lanes, _ = own_lanes(n_3.shape[1] // 4, turned.shape[0])
    turned[...] = n_3[:, lanes].astype(F32).T.astype(BF16)
    for here in blocks(reduce.shape[0]):
        slope, _ = slope_and_act(n_3[...], expand[:, here])
        dpre[:, here] = dpre_of(dot(d_3[...], reduce[here, :], ((1,), (1,))), slope)


def far_expand(n_3, d_3, expand, reduce, after):
    rows = n_3.shape[0]
    hid = expand.shape[1]
    return call(
        far_expand_body,
        "far_expand",
        10**6,
        [((2 * LANES, rows), BF16), ((rows, hid), BF16)],
        [],
        n_3,
        d_3,
        expand,
        reduce,
        after,
        read=10**5,
    )


def expand_grad_body(turned, turned_3, dpre, dpre_3, keep, send, total):
    own, hid = total.shape
    _, core, _ = position(4)
    _, first = own_lanes(own, turned.shape[0])
    rows = pl.ds(pl.multiple_of(first, 16), own)
    for here in blocks(hid):
        part = dot(turned[rows, :], dpre[:, here], ((1,), (0,)))
        total[:, here] = part + dot(turned_3[rows, :], dpre_3[:, here], ((1,), (0,)))
    split(total, core, keep, send)


def expand_grad(turned, turned_3, dpre, dpre_3, own, inner):
    hid = dpre.shape[1]
    shape = (inner // 2, own // inner, hid)
    return call(
        expand_grad_body,
        "expand_grad",
        10**6,
        [(shape, F32), (shape, BF16)],
        [((own, hid), F32)],
        turned,
        turned_3,
        dpre,
        dpre_3,
        read=10**5,
    )


def merge_body(kept, got, small, more, after, keep, send, sums):
    _, _, mine = position(4)
    theirs = 1 - mine
    keep[...] = kept[mine] + got[mine].astype(F32)
    send[...] = (kept[theirs] + got[theirs].astype(F32)).astype(BF16)
    sums[...] = added(small, more) if more is not None else small[...]


def merge(kept, got, small, more=None, after=None):
    shape = kept.shape[1:]
    if more is None:
        body = lambda kept, got, small, *outs: merge_body(kept, got, small, None, None, *outs)
    else:
        body = merge_body
    return call(
        body,
        "merge",
        10**6,
        [(shape, F32), (shape, BF16), (small.shape, BF16)],
        [],
        kept,
        got,
        small,
        *(() if more is None else (more, after)),
        read=10**5,
    )


def turn_body(small, more, after, sums):
    sums[...] = added(small, more)


def turn(small, more, after):
    return call(turn_body, "turn", 10**11, [(small.shape, BF16)], [], small, more, after)[0]


def finish_body(
    keep_e, got_e, keep_r, got_r, small, more, out_e, out_r, kernel, gain, scale
):
    out_e[...] = keep_e[...] + got_e[...].astype(F32)
    out_r[...] = keep_r[...] + got_r[...].astype(F32)
    sums = small[...].astype(F32) + more[...].astype(F32)
    for i in range(7):
        kernel[i] = sums[7 * i : 7 * i + 7]
    gain[...] = sums[49:50].reshape(gain.shape)
    scale[...] = sums[50:51].reshape(scale.shape)


def finish(keep_e, got_e, keep_r, got_r, small, more):
    channels = small.shape[1]
    return call(
        finish_body,
        "finish",
        10**8,
        [
            (keep_e.shape, F32),
            (keep_r.shape, F32),
            ((7, 7, channels), F32),
            ((channels,), F32),
            ((channels,), F32),
        ],
        [],
        keep_e,
        got_e,
        keep_r,
        got_r,
        small,
        more,
    )


def grads_plain(every, dbranch_all, expand_weight, reduce_weight, my_line, my_inner, line, inner):
    channels, hid = expand_weight.shape
    units, own = hid // line, channels // line
    every = every.reshape(-1, channels)
    pre = dot(every, expand_weight, ((1,), (0,)))
    cdf, density = phi_parts(pre)
    slope = (cdf + pre * density).reshape(line, 2, -1, hid)
    hidden = (pre * cdf).astype(BF16).astype(F32).reshape(line, 2, -1, hid)
    diff = (hidden[:, 0] - hidden[:, 1]).astype(BF16).reshape(-1, hid)
    diff = lax.dynamic_slice_in_dim(diff, my_line * units, units, 1)
    dhidden = dot(dbranch_all, reduce_weight, ((1,), (1,))).reshape(line, -1, hid)
    dpre = jnp.stack([dhidden * slope[:, 0], -dhidden * slope[:, 1]], axis=1)
    dpre = dpre.astype(BF16).reshape(-1, hid)
    normed_own = lax.dynamic_slice_in_dim(every, my_line * own, own, 1)
    expand = dot(normed_own, dpre, ((0,), (0,))).reshape(inner, own // inner, hid)
    reduce = dot(diff, dbranch_all, ((0,), (0,))).reshape(inner, units // inner, channels)
    return halves(expand, my_inner & 1), halves(reduce, my_inner & 1)


def halves(part, side):
    part = part.reshape((part.shape[0] // 2, 2) + part.shape[1:])
    keep = lax.dynamic_index_in_dim(part, side, 1, keepdims=False)
    send = lax.dynamic_index_in_dim(part, 1 - side, 1, keepdims=False)
    return keep, send.astype(BF16)


def on_device(
    features, column_table, dw_kernel, norm_gain, expand_weight, reduce_weight, layer_scale
):
    rows, cols, channels = features.shape
    hid = expand_weight.shape[1]
    count = lax.axis_size("col")
    bits = count.bit_length() - 1
    line = 1 << ((bits + 1) // 2)
    inner = count // line
    inner_bits = inner.bit_length() - 1
    me = lax.axis_index("col")
    my_line, my_inner = me // inner, me % inner
    units, own = hid // line, channels // line
    total_cols = cols * count

    def swapped(block, mask):
        return lax.ppermute(block, "col", [(d, d ^ mask) for d in range(count)])

    def line_sum(small):
        sums = [small] + [swapped(small, p * inner) for p in range(1, line)]
        sums = [part.astype(F32) for part in sums]
        while len(sums) > 1:
            sums = [low + high for low, high in zip(sums[::2], sums[1::2])]
        return sums[0]

    mirror = lax.ppermute(column_table, "col", [(d, count - 1 - d) for d in range(count)])

    features_f = features.astype(F32)
    table_f = column_table.astype(F32)
    gain = norm_gain[None]
    inside, across, turned = edges(features_f, table_f, mirror)
    inside = swapped(inside, 1)
    pairs = [(d, d + 1) for d in range(1, count - 1, 2)]
    across = lax.ppermute(across, "col", pairs + [(high, low) for low, high in pairs])
    normed, nhat, inv, wide = conv_norm(
        features_f, table_f, turned, inside, across, dw_kernel.astype(F32), gain
    )
    fast = line == 4 and inner == 4 and units % LANES == 0 and own % 64 == 0
    if fast:
        flat = normed.reshape(-1, channels)
        normed_2, normed_1 = swapped(flat, 2 * inner), swapped(flat, inner)
    else:
        others = [swapped(normed, p * inner) for p in range(1, line)]
    slope, diff, disagreement, dbranch, gscale = forward(
        1.0 / math.sqrt(rows * total_cols),
        normed.reshape(-1, channels),
        expand_weight,
        reduce_weight,
        wide,
        layer_scale,
        features.shape,
    )
    dnormed = backward(dbranch, slope, expand_weight, reduce_weight)
    if fast:
        dbranch_all = [dbranch, swapped(dbranch, inner), swapped(dbranch, 2 * inner)]
        dbranch_3 = swapped(dbranch, 3 * inner)
        normed_3 = swapped(gate(normed_2, dnormed, normed_1), inner)
        small = small_grads(dnormed, nhat, inv, gain, gscale, wide, *dbranch_all[1:])
        more = swapped(small, 2)
        part = near_reduce([normed_1, normed_2], dbranch_all, diff, expand_weight, line)
        keep_r, send_r, small = far_reduce(
            normed_3, dbranch_3, expand_weight, part, small, more, inner
        )
        got_r, more = swapped(send_r, 1), swapped(small, 1)
        turned, dpre = near_expand(
            [flat, normed_1, normed_2], dbranch_all, slope, expand_weight, reduce_weight, small
        )
        keep_r, send_r, small = merge(keep_r, got_r, small, more, turned)
        got_r, more = swapped(send_r, 2), swapped(small, inner)
        turned_3, dpre_3 = far_expand(normed_3, dbranch_3, expand_weight, reduce_weight, small)
        keep_e, send_e = expand_grad(turned, turned_3, dpre, dpre_3, own, inner)
        got_e = swapped(send_e, 1)
        keep_e, send_e, small = merge(keep_e, got_e, turn(small, more, got_r))
        got_e, more = swapped(send_e, 2), swapped(small, 2 * inner)
        sums = finish(keep_e, got_e, keep_r, got_r, small, more)
        return (disagreement, *sums)

    small = small_grads(dnormed, nhat, inv, gain, gscale, wide)
    dbranch_all = [dbranch] + [swapped(dbranch, p * inner) for p in range(1, line)]
    (keep_e, send_e), (keep_r, send_r) = grads_plain(
        jnp.stack([normed] + others),
        jnp.concatenate(dbranch_all),
        expand_weight,
        reduce_weight,
        my_line,
        my_inner,
        line,
        inner,
    )
    small = line_sum(small)
    for bit in range(inner_bits):
        sum_r = keep_r + swapped(send_r, 1 << bit).astype(F32)
        sum_e = keep_e + swapped(send_e, 1 << bit).astype(F32)
        small = small.astype(BF16)
        small = small.astype(F32) + swapped(small, 1 << bit).astype(F32)
        if bit < inner_bits - 1:
            side = (my_inner >> (bit + 1)) & 1
            keep_r, send_r = halves(sum_r, side)
            keep_e, send_e = halves(sum_e, side)
    grad_kernel = small[:49].reshape(7, 7, channels)
    return (
        disagreement,
        sum_e.reshape(own // inner, hid),
        sum_r.reshape(units // inner, channels),
        grad_kernel,
        small[49],
        small[50],
    )


def solution(mesh):
    in_specs = (P("groups", "col", None), P("col", None), P(), P(), P(), P(), P())
    out_specs = (
        P("groups", "col", None),
        P(("groups", "col"), None),
        P(("groups", "col"), None),
        P("groups", None, None),
        P("groups"),
        P("groups"),
    )
    return jax.shard_map(
        on_device, mesh=mesh, in_specs=in_specs, out_specs=out_specs, check_vma=False
    )
```

```python
import functools
import math

import jax
import jax.numpy as jnp
from jax import lax
from jax.experimental import pallas as pl
from jax.experimental.pallas import tpu as pltpu
from jax.sharding import PartitionSpec as P

BF16 = jnp.bfloat16
F32 = jnp.float32
LANES = 128
VMEM_GRANT = 16 << 20
BLOCK = 512


def phi_parts(pre, inverse=lambda value: 1.0 / value):
    decay = jnp.exp2(-0.7213475204444817 * (pre * pre))
    t = inverse(1.0 + 0.23164189 * jnp.abs(pre))
    poly = 0.5307027145 * t - 0.7265760135
    poly = poly * t + 0.7107068705
    poly = poly * t - 0.142248368
    poly = poly * t + 0.127414796
    tail = poly * t * decay
    return jnp.where(pre < 0.0, tail, 1.0 - tail), decay * 0.3989422804014327


def refined(value):
    guess = pl.reciprocal(value, approx=True)
    guess = guess * (2.0 - value * guess)
    return guess * (2.0 - value * guess)


def call(body, name, flops, out_shape, scratch, *operands, read=10**8):
    return pl.pallas_call(
        body,
        in_specs=[pl.BlockSpec(memory_space=pltpu.VMEM) for _ in operands],
        out_specs=[pl.BlockSpec(memory_space=pltpu.VMEM) for _ in out_shape],
        out_shape=[jax.ShapeDtypeStruct(shape, dtype) for shape, dtype in out_shape],
        scratch_shapes=[pltpu.VMEM(shape, dtype) for shape, dtype in scratch],
        compiler_params=pltpu.CompilerParams(vmem_limit_bytes=VMEM_GRANT),
        cost_estimate=pl.CostEstimate(flops=flops, bytes_accessed=read, transcendentals=0),
        name=name,
    )(*operands)


def position(inner):
    me = lax.axis_index("col")
    return me // inner, me & 1, (me >> 1) & 1


def dot(lhs, rhs, contract):
    return lax.dot_general(lhs, rhs, (contract, ((), ())), preferred_element_type=F32)


def flipped(value):
    rows = value.shape[0]
    return jnp.concatenate([value[r : r + 1] for r in reversed(range(rows))], axis=0)


def edges_body(feat, table, inside, across):
    rows, cols, _ = feat.shape
    odd = (lax.axis_index("col") & 1) == 1
    for source, place in ((feat[...], slice(0, rows)), (table[...][None], slice(rows, rows + 1))):
        first, last = source[:, :3], source[:, cols - 3 :]
        inside[place] = jnp.where(odd, first, last).astype(BF16)
        across[place] = jnp.where(odd, last, first).astype(BF16)


def edges(features, table):
    rows, _, channels = features.shape
    return call(
        edges_body,
        "edges",
        10**8,
        [((rows + 1, 3, channels), BF16), ((rows + 1, 3, channels), BF16)],
        [],
        features,
        table,
    )


def conv_body(
    feat, table, mirror, mirror_low, mirror_high, inside, across, dw, gain,
    normed, nhat, inv, wide, conv,
):
    rows, cols, channels = feat.shape
    odd = (lax.axis_index("col") & 1) == 1
    one, two = inside[...].astype(F32), across[...].astype(F32)
    low, high = jnp.where(odd, one, two), jnp.where(odd, two, one)
    low_m = flipped(mirror_low[...].astype(F32)[:3])
    high_m = flipped(mirror_high[...].astype(F32)[cols - 3 :])
    tables = (
        (table[...], low[rows], high[rows]),
        (flipped(mirror[...].astype(F32)), low_m, high_m),
    )
    for v, (own, before, after) in enumerate(tables):
        wide[v, :, 3 : 3 + cols, :] = (feat[...] + own[None]).astype(BF16).astype(F32)
        wide[v, :, 0:3, :] = (low[:rows] + before[None]).astype(BF16).astype(F32)
        wide[v, :, 3 + cols : 6 + cols, :] = (high[:rows] + after[None]).astype(BF16).astype(F32)

    def tile(c, carry):
        lanes = pl.ds(pl.multiple_of(c * LANES, LANES), LANES)
        sums = [[jnp.zeros((cols, LANES), F32) for _ in range(rows)] for _ in range(2)]
        for j in range(7):
            for v in range(2):
                part = [wide[v, r, pl.ds(j, cols), lanes] for r in range(rows)]
                for i in range(7):
                    weight = dw[i, pl.ds(6 - j if v else j, 1), lanes]
                    for r in range(rows):
                        if 0 <= r + i - 3 < rows:
                            sums[v][r] = sums[v][r] + weight * part[r + i - 3]
        for v in range(2):
            for r in range(rows):
                conv[v, r, :, lanes] = sums[v][r]
        return carry

    lax.fori_loop(0, channels // LANES, tile, 0)
    for v in range(2):
        value = conv[v].reshape(rows * cols, channels)
        centred = value - jnp.mean(value, axis=-1, keepdims=True)
        inverse = lax.rsqrt(jnp.mean(centred * centred, axis=-1, keepdims=True) + 1e-06)
        value = centred * inverse
        nhat[v] = value
        inv[v] = jnp.broadcast_to(inverse, (rows * cols, LANES))
        normed[v] = (value * gain[...]).astype(BF16)


def conv_norm(features, table, mirrors, inside, across, dw, gain):
    rows, cols, channels = features.shape
    pixels = rows * cols
    return call(
        conv_body,
        "conv_norm",
        4 * 10**9,
        [
            ((2, pixels, channels), BF16),
            ((2, pixels, channels), F32),
            ((2, pixels, LANES), F32),
            ((2, rows, 16, channels), F32),
        ],
        [((2, rows, cols, channels), F32)],
        features,
        table,
        *mirrors,
        inside,
        across,
        dw,
        gain,
    )


def blocks(total):
    return [slice(at, at + BLOCK) for at in range(0, total, BLOCK)]


def forward_body(
    scale, normed, expand, reduce, wide, ls, slope, diff, disagreement, dbranch, gscale, hidden
):
    pixels, channels = normed.shape
    half = pixels // 2
    rows, cols, _ = disagreement.shape
    for here in blocks(expand.shape[1]):
        value, act = slope_and_act(normed[...], expand[:, here])
        slope[:, here] = value.astype(BF16)
        hidden[:, here] = act
        diff[:, here] = views_apart(act)
    branch = dot(hidden[...], reduce[...], ((1,), (0,)))
    factor = ls[...].reshape(1, channels)
    outs = []
    for v in range(2):
        own = wide[v, :, 3 : 3 + cols, :].reshape(half, channels)
        outs.append((own + factor * branch[v * half : (v + 1) * half]).astype(BF16).astype(F32))
    difference = outs[0] - outs[1]
    disagreement[...] = difference.astype(BF16).reshape(rows, cols, channels)
    residual = (difference * scale).astype(BF16).astype(F32)
    gscale[...] = jnp.sum((branch[:half] - branch[half:]) * residual, axis=0, keepdims=True)
    dbranch[...] = (factor * residual).astype(BF16)


def forward(scale, normed, expand, reduce, wide, ls, shape):
    pixels, channels = normed.shape
    hid = expand.shape[1]
    return call(
        functools.partial(forward_body, scale),
        "forward",
        10**9,
        [
            ((pixels, hid), BF16),
            ((pixels // 2, hid), BF16),
            (shape, BF16),
            ((pixels // 2, channels), BF16),
            ((1, channels), F32),
        ],
        [((pixels, hid), BF16)],
        normed,
        expand,
        reduce,
        wide,
        ls,
        read=10**6,
    )


def backward_body(dbranch, slope, expand, reduce, dnormed, dpre):
    half = dbranch.shape[0]
    for here in blocks(expand.shape[1]):
        dhidden = dot(dbranch[...], reduce[here, :], ((1,), (1,)))
        dpre[:, here] = dpre_of(dhidden, slope[:, here].astype(F32))
    dnormed[...] = dot(dpre[...], expand[...], ((1,), (1,)))


def backward(dbranch, slope, expand, reduce):
    half, channels = dbranch.shape
    hid = expand.shape[1]
    return call(
        backward_body,
        "backward",
        10**9,
        [((2 * half, channels), F32)],
        [((2 * half, hid), BF16)],
        dbranch,
        slope,
        expand,
        reduce,
        read=10**6,
    )[0]


def small_body(dnormed, nhat, inv, gain, gscale, wide, out, grad, taps, small):
    half, channels = dnormed.shape[0] // 2, dnormed.shape[1]
    _, rows, _, _ = wide.shape
    cols = half // rows
    factor = gain[...]
    ggain = jnp.zeros((1, channels), F32)
    for v in range(2):
        here = slice(v * half, (v + 1) * half)
        value = dnormed[here, :]
        ggain = ggain + jnp.sum(value * nhat[v], axis=0, keepdims=True)
        scaled = value * factor
        gm = jnp.mean(scaled, axis=-1, keepdims=True)
        gn = jnp.mean(scaled * nhat[v], axis=-1, keepdims=True)
        grad[here, :] = inv[v][:, :1] * (scaled - gm - nhat[v] * gn)

    def tile(c, carry):
        lanes = pl.ds(pl.multiple_of(c * LANES, LANES), LANES)
        dconv = [
            [grad[pl.ds(v * half + r * cols, cols), lanes] for r in range(rows)] for v in range(2)
        ]
        for j in range(7):
            part = [
                [wide[v, r, pl.ds(6 - j if v else j, cols), lanes] for r in range(rows)]
                for v in range(2)
            ]
            for i in range(7):
                sums = []
                for v in range(2):
                    total = None
                    for r in range(rows):
                        if 0 <= r + i - 3 < rows:
                            term = part[v][r + i - 3] * dconv[v][r]
                            total = term if total is None else total + term
                    sums.append(total)
                at = 8 * (7 * i + j)
                taps[at : at + 8, :] = sums[0] + sums[1]
        rolled = taps[pl.ds(0, 49, stride=8), :]
        for s in range(1, 8):
            rolled = rolled + taps[pl.ds(s, 49, stride=8), :]
        small[:49, lanes] = rolled
        return carry

    small[...] = jnp.zeros(small.shape, F32)
    lax.fori_loop(0, channels // LANES, tile, 0)
    small[49:50, :] = ggain
    small[50:51, :] = gscale[...]
    out[...] = small[...].astype(BF16)


def small_grads(dnormed, nhat, inv, gain, gscale, wide):
    channels = dnormed.shape[1]
    return call(
        small_body,
        "small_grads",
        10**6,
        [((64, channels), BF16)],
        [(dnormed.shape, F32), ((8 * 49, LANES), F32), ((64, channels), F32)],
        dnormed,
        nhat,
        inv,
        gain,
        gscale,
        wide,
        read=10**5,
    )[0]


def gate_body(block, *rest):
    rest[-1][...] = block[...]


def gate(block, *after):
    shapes = [(block.shape, block.dtype)]
    return call(gate_body, "gate", 10**6, shapes, [], block, *after, read=10**5)[0]


def split(total, side, keep, send):
    parts, rows, _ = keep.shape
    for x in range(parts):
        mine = pl.multiple_of((2 * x + side) * rows, 16)
        theirs = pl.multiple_of((2 * x + 1 - side) * rows, 16)
        keep[x] = total[pl.ds(mine, rows), :]
        send[x] = total[pl.ds(theirs, rows), :].astype(BF16)


def added(small, more):
    return (small[...].astype(F32) + more[...].astype(F32)).astype(BF16)


def slope_and_act(normed, expand):
    pre = dot(normed, expand, ((1,), (0,)))
    cdf, density = phi_parts(pre, refined)
    return cdf + pre * density, (pre * cdf).astype(BF16)


def views_apart(act):
    half = act.shape[0] // 2
    return (act[:half].astype(F32) - act[half:].astype(F32)).astype(BF16)


def dpre_of(dhidden, slope):
    half = dhidden.shape[0]
    return jnp.concatenate([dhidden * slope[:half], -dhidden * slope[half:]]).astype(BF16)


def own_lanes(own, width):
    first = position(4)[0] * own
    start = first // LANES * LANES
    return pl.ds(pl.multiple_of(start, LANES), width), first - start


def near_body(
    n_0, n_1, n_2, d_0, d_1, d_2, slope_0, diff_0, expand, reduce, turned, dpre, total, diff
):
    half, channels = d_0.shape
    units = total.shape[0]
    lanes, _ = own_lanes(channels // 4, turned.shape[0])
    for p, ref in enumerate((n_0, n_1, n_2)):
        at = 2 * p * half
        turned[:, at : at + 2 * half] = ref[:, lanes].astype(F32).T.astype(BF16)
    every = jnp.concatenate([d_0[...], d_1[...], d_2[...]])
    diff[:half, :] = diff_0[...]
    both = jnp.concatenate([n_1[...], n_2[...]])
    for here in blocks(reduce.shape[0]):
        slope, act = slope_and_act(both, expand[:, here])
        slopes = [slope_0[:, here].astype(F32), slope[: 2 * half], slope[2 * half :]]
        diff[half : 2 * half, here] = views_apart(act[: 2 * half])
        diff[2 * half :, here] = views_apart(act[2 * half :])
        dhidden = dot(every, reduce[here, :], ((1,), (1,)))
        for p in range(3):
            part = dpre_of(dhidden[p * half : (p + 1) * half], slopes[p])
            dpre[2 * p * half : 2 * (p + 1) * half, here] = part
    lanes = pl.ds(pl.multiple_of(position(4)[0] * units, LANES), units)
    total[...] = dot(diff[:, lanes], every, ((0,), (0,)))


def near(normed, dbranch, slope, diff, expand, reduce, line):
    half, channels = dbranch[0].shape
    hid = expand.shape[1]
    return call(
        near_body,
        "near",
        10**6,
        [
            ((2 * LANES, 6 * half), BF16),
            ((6 * half, hid), BF16),
            ((hid // line, channels), F32),
        ],
        [((3 * half, hid), BF16)],
        *normed,
        *dbranch,
        slope,
        diff,
        expand,
        reduce,
        read=10**5,
    )


def far_reduce_body(n_3, d_3, expand, part, small, more, keep, send, sums, total):
    units = total.shape[0]
    line, core, _ = position(4)
    lanes = pl.ds(pl.multiple_of(line * units, LANES), units)
    _, act = slope_and_act(n_3[...], expand[:, lanes])
    total[...] = part[...] + dot(views_apart(act), d_3[...], ((0,), (0,)))
    split(total, core, keep, send)
    sums[...] = added(small, more)


def far_reduce(n_3, d_3, expand, part, small, more, inner):
    units, channels = part.shape
    shape = (inner // 2, units // inner, channels)
    return call(
        far_reduce_body,
        "far_reduce",
        10**6,
        [(shape, F32), (shape, BF16), (small.shape, BF16)],
        [((units, channels), F32)],
        n_3,
        d_3,
        expand,
        part,
        small,
        more,
        read=10**5,
    )


def far_expand_body(n_3, d_3, expand, reduce, after, turned, dpre):
    lanes, _ = own_lanes(n_3.shape[1] // 4, turned.shape[0])
    turned[...] = n_3[:, lanes].astype(F32).T.astype(BF16)
    for here in blocks(reduce.shape[0]):
        slope, _ = slope_and_act(n_3[...], expand[:, here])
        dpre[:, here] = dpre_of(dot(d_3[...], reduce[here, :], ((1,), (1,))), slope)


def far_expand(n_3, d_3, expand, reduce, after):
    rows = n_3.shape[0]
    hid = expand.shape[1]
    return call(
        far_expand_body,
        "far_expand",
        10**9,
        [((2 * LANES, rows), BF16), ((rows, hid), BF16)],
        [],
        n_3,
        d_3,
        expand,
        reduce,
        after,
        read=10**6,
    )


def expand_grad_body(turned, turned_3, dpre, dpre_3, after, keep, send, total):
    own, hid = total.shape
    _, core, _ = position(4)
    _, first = own_lanes(own, turned.shape[0])
    rows = pl.ds(pl.multiple_of(first, 16), own)
    for here in blocks(hid):
        part = dot(turned[rows, :], dpre[:, here], ((1,), (0,)))
        total[:, here] = part + dot(turned_3[rows, :], dpre_3[:, here], ((1,), (0,)))
    split(total, core, keep, send)


def expand_grad(turned, turned_3, dpre, dpre_3, after, own, inner):
    hid = dpre.shape[1]
    shape = (inner // 2, own // inner, hid)
    return call(
        expand_grad_body,
        "expand_grad",
        10**6,
        [(shape, F32), (shape, BF16)],
        [((own, hid), F32)],
        turned,
        turned_3,
        dpre,
        dpre_3,
        after,
        read=10**5,
    )


def merge_body(kept, got, keep, send):
    _, _, mine = position(4)
    theirs = 1 - mine
    keep[...] = kept[mine] + got[mine].astype(F32)
    send[...] = (kept[theirs] + got[theirs].astype(F32)).astype(BF16)


def merge_small_body(kept, got, small, more, keep, send, sums):
    merge_body(kept, got, keep, send)
    sums[...] = added(small, more)


def merge(kept, got, *small):
    shape = kept.shape[1:]
    return call(
        merge_small_body if small else merge_body,
        "merge",
        10**6,
        [(shape, F32), (shape, BF16)] + [(part.shape, BF16) for part in small[:1]],
        [],
        kept,
        got,
        *small,
        read=10**5,
    )


def finish_body(
    keep_e, got_e, keep_r, got_r, small, more, out_e, out_r, kernel, gain, scale
):
    out_e[...] = keep_e[...] + got_e[...].astype(F32)
    out_r[...] = keep_r[...] + got_r[...].astype(F32)
    sums = small[...].astype(F32) + more[...].astype(F32)
    for i in range(7):
        kernel[i] = sums[7 * i : 7 * i + 7]
    gain[...] = sums[49:50].reshape(gain.shape)
    scale[...] = sums[50:51].reshape(scale.shape)


def finish(keep_e, got_e, keep_r, got_r, small, more):
    channels = small.shape[1]
    return call(
        finish_body,
        "finish",
        10**8,
        [
            (keep_e.shape, F32),
            (keep_r.shape, F32),
            ((7, 7, channels), F32),
            ((channels,), F32),
            ((channels,), F32),
        ],
        [],
        keep_e,
        got_e,
        keep_r,
        got_r,
        small,
        more,
    )


def grads_plain(every, dbranch_all, expand_weight, reduce_weight, my_line, my_inner, line, inner):
    channels, hid = expand_weight.shape
    units, own = hid // line, channels // line
    every = every.reshape(-1, channels)
    pre = dot(every, expand_weight, ((1,), (0,)))
    cdf, density = phi_parts(pre)
    slope = (cdf + pre * density).reshape(line, 2, -1, hid)
    hidden = (pre * cdf).astype(BF16).astype(F32).reshape(line, 2, -1, hid)
    diff = (hidden[:, 0] - hidden[:, 1]).astype(BF16).reshape(-1, hid)
    diff = lax.dynamic_slice_in_dim(diff, my_line * units, units, 1)
    dhidden = dot(dbranch_all, reduce_weight, ((1,), (1,))).reshape(line, -1, hid)
    dpre = jnp.stack([dhidden * slope[:, 0], -dhidden * slope[:, 1]], axis=1)
    dpre = dpre.astype(BF16).reshape(-1, hid)
    normed_own = lax.dynamic_slice_in_dim(every, my_line * own, own, 1)
    expand = dot(normed_own, dpre, ((0,), (0,))).reshape(inner, own // inner, hid)
    reduce = dot(diff, dbranch_all, ((0,), (0,))).reshape(inner, units // inner, channels)
    return halves(expand, my_inner & 1), halves(reduce, my_inner & 1)


def halves(part, side):
    part = part.reshape((part.shape[0] // 2, 2) + part.shape[1:])
    keep = lax.dynamic_index_in_dim(part, side, 1, keepdims=False)
    send = lax.dynamic_index_in_dim(part, 1 - side, 1, keepdims=False)
    return keep, send.astype(BF16)


def on_device(
    features, column_table, dw_kernel, norm_gain, expand_weight, reduce_weight, layer_scale
):
    rows, cols, channels = features.shape
    hid = expand_weight.shape[1]
    count = lax.axis_size("col")
    bits = count.bit_length() - 1
    line = 1 << ((bits + 1) // 2)
    inner = count // line
    inner_bits = inner.bit_length() - 1
    me = lax.axis_index("col")
    my_line, my_inner = me // inner, me % inner
    units, own = hid // line, channels // line
    total_cols = cols * count

    def swapped(block, mask):
        return lax.ppermute(block, "col", [(d, d ^ mask) for d in range(count)])

    def line_sum(small):
        sums = [small] + [swapped(small, p * inner) for p in range(1, line)]
        sums = [part.astype(F32) for part in sums]
        while len(sums) > 1:
            sums = [low + high for low, high in zip(sums[::2], sums[1::2])]
        return sums[0]

    mirrors = [
        lax.ppermute(
            column_table, "col", [(d, total - d) for d in range(count) if 0 <= total - d < count]
        )
        for total in (count - 1, count, count - 2)
    ]
    features_f, table_f = features.astype(F32), column_table.astype(F32)
    inside, across = edges(features_f, table_f)
    inside = swapped(inside, 1)
    pairs = [(d, d + 1) for d in range(1, count - 1, 2)]
    across = lax.ppermute(across, "col", pairs + [(high, low) for low, high in pairs])
    normed, nhat, inv, wide = conv_norm(
        features_f, table_f, mirrors, inside, across, dw_kernel.astype(F32), norm_gain[None]
    )
    fast = line == 4 and inner == 4 and units % LANES == 0 and own % 64 == 0
    if fast:
        flat = normed.reshape(-1, channels)
        normed_2, normed_1 = swapped(flat, 2 * inner), swapped(flat, inner)
    else:
        others = [swapped(normed, p * inner) for p in range(1, line)]
    slope, diff, disagreement, dbranch, gscale = forward(
        1.0 / math.sqrt(rows * total_cols),
        normed.reshape(-1, channels),
        expand_weight,
        reduce_weight,
        wide,
        layer_scale,
        features.shape,
    )
    dnormed = backward(dbranch, slope, expand_weight, reduce_weight)
    small = small_grads(dnormed, nhat, inv, norm_gain[None], gscale, wide)
    if fast:
        dbranch_2, dbranch_1 = swapped(dbranch, 2 * inner), swapped(dbranch, inner)
        normed_3 = swapped(gate(normed_2, dnormed, normed_1), inner)
        dbranch_3 = swapped(gate(dbranch_2, small, dbranch_1), inner)
        more = swapped(small, 2)
        turned, dpre, part = near(
            [flat, normed_1, normed_2],
            [dbranch, dbranch_1, dbranch_2],
            slope,
            diff,
            expand_weight,
            reduce_weight,
            line,
        )
        keep_r, send_r, small = far_reduce(
            normed_3, dbranch_3, expand_weight, part, small, more, inner
        )
        got_r, more = swapped(send_r, 1), swapped(small, 1)
        turned_3, dpre_3 = far_expand(normed_3, dbranch_3, expand_weight, reduce_weight, small)
        keep_r, send_r, small = merge(keep_r, got_r, small, more)
        got_r, more = swapped(send_r, 2), swapped(small, inner)
        keep_e, send_e = expand_grad(turned, turned_3, dpre, dpre_3, small, own, inner)
        keep_e, send_e, small = merge(keep_e, swapped(send_e, 1), small, more)
        got_e, more = swapped(send_e, 2), swapped(small, 2 * inner)
        sums = finish(keep_e, got_e, keep_r, got_r, small, more)
        return (disagreement, *sums)

    dbranch_all = [dbranch] + [swapped(dbranch, p * inner) for p in range(1, line)]
    (keep_e, send_e), (keep_r, send_r) = grads_plain(
        jnp.stack([normed] + others),
        jnp.concatenate(dbranch_all),
        expand_weight,
        reduce_weight,
        my_line,
        my_inner,
        line,
        inner,
    )
    small = line_sum(small)
    for bit in range(inner_bits):
        sum_r = keep_r + swapped(send_r, 1 << bit).astype(F32)
        sum_e = keep_e + swapped(send_e, 1 << bit).astype(F32)
        small = small.astype(BF16)
        small = small.astype(F32) + swapped(small, 1 << bit).astype(F32)
        if bit < inner_bits - 1:
            side = (my_inner >> (bit + 1)) & 1
            keep_r, send_r = halves(sum_r, side)
            keep_e, send_e = halves(sum_e, side)
    grad_kernel = small[:49].reshape(7, 7, channels)
    return (
        disagreement,
        sum_e.reshape(own // inner, hid),
        sum_r.reshape(units // inner, channels),
        grad_kernel,
        small[49],
        small[50],
    )


def solution(mesh):
    in_specs = (P("groups", "col", None), P("col", None), P(), P(), P(), P(), P())
    out_specs = (
        P("groups", "col", None),
        P(("groups", "col"), None),
        P(("groups", "col"), None),
        P("groups", None, None),
        P("groups"),
        P("groups"),
    )
    return jax.shard_map(
        on_device, mesh=mesh, in_specs=in_specs, out_specs=out_specs, check_vma=False
    )
```

```python
import functools
import math

import jax
import jax.numpy as jnp
from jax import lax
from jax.experimental import pallas as pl
from jax.experimental.pallas import tpu as pltpu
from jax.sharding import PartitionSpec as P

BF16 = jnp.bfloat16
F32 = jnp.float32
LANES = 128
VMEM_GRANT = 16 << 20
BLOCK = 256


def phi_parts(pre):
    decay = jnp.exp(-0.5 * pre * pre)
    t = 1.0 / (1.0 + 0.23164189 * jnp.abs(pre))
    poly = 0.5307027145 * t - 0.7265760135
    poly = poly * t + 0.7107068705
    poly = poly * t - 0.142248368
    poly = poly * t + 0.127414796
    tail = poly * t * decay
    return jnp.where(pre < 0.0, tail, 1.0 - tail), decay * 0.3989422804014327


def call(body, name, flops, out_shape, scratch, *operands, read=10**8):
    return pl.pallas_call(
        body,
        in_specs=[pl.BlockSpec(memory_space=pltpu.VMEM) for _ in operands],
        out_specs=[pl.BlockSpec(memory_space=pltpu.VMEM) for _ in out_shape],
        out_shape=[jax.ShapeDtypeStruct(shape, dtype) for shape, dtype in out_shape],
        scratch_shapes=[pltpu.VMEM(shape, dtype) for shape, dtype in scratch],
        compiler_params=pltpu.CompilerParams(vmem_limit_bytes=VMEM_GRANT),
        cost_estimate=pl.CostEstimate(flops=flops, bytes_accessed=read, transcendentals=0),
        name=name,
    )(*operands)


def position(inner):
    me = lax.axis_index("col")
    return me // inner, me & 1, (me >> 1) & 1


def dot(lhs, rhs, contract):
    return lax.dot_general(lhs, rhs, (contract, ((), ())), preferred_element_type=F32)


def flipped(value):
    rows = value.shape[0]
    return jnp.concatenate([value[r : r + 1] for r in reversed(range(rows))], axis=0)


def edges_body(feat, table, mirror, inside, across, turned):
    _, cols, channels = feat.shape
    other = flipped(mirror[...].astype(F32))
    odd = (lax.axis_index("col") & 1) == 1
    for v, add in enumerate((table[...], other)):
        own = (feat[...] + add[None]).astype(BF16).astype(F32)
        first, last = own[:, :3], own[:, cols - 3 :]
        inside[v] = jnp.where(odd, first, last).astype(BF16)
        across[v] = jnp.where(odd, last, first).astype(BF16)
    turned[...] = other


def edges(features, table, mirror):
    rows, cols, channels = features.shape
    return call(
        edges_body,
        "edges",
        10**8,
        [
            ((2, rows, 3, channels), BF16),
            ((2, rows, 3, channels), BF16),
            ((cols, channels), F32),
        ],
        [],
        features,
        table,
        mirror,
    )


def conv_body(feat, table, turned, inside, across, dw, gain, normed, nhat, inv, wide, conv):
    rows, cols, channels = feat.shape
    odd = (lax.axis_index("col") & 1) == 1
    for v, add in enumerate((table[...], turned[...])):
        wide[v, :, 3 : 3 + cols, :] = (feat[...] + add[None]).astype(BF16).astype(F32)
        one, two = inside[v].astype(F32), across[v].astype(F32)
        wide[v, :, 0:3, :] = jnp.where(odd, one, two)
        wide[v, :, 3 + cols : 6 + cols, :] = jnp.where(odd, two, one)

    def tile(c, carry):
        lanes = pl.ds(pl.multiple_of(c * LANES, LANES), LANES)
        sums = [[jnp.zeros((cols, LANES), F32) for _ in range(rows)] for _ in range(2)]
        for j in range(7):
            for v in range(2):
                part = [wide[v, r, pl.ds(j, cols), lanes] for r in range(rows)]
                for i in range(7):
                    weight = dw[i, pl.ds(6 - j if v else j, 1), lanes]
                    for r in range(rows):
                        if 0 <= r + i - 3 < rows:
                            sums[v][r] = sums[v][r] + weight * part[r + i - 3]
        for v in range(2):
            for r in range(rows):
                conv[v, r, :, lanes] = sums[v][r]
        return carry

    lax.fori_loop(0, channels // LANES, tile, 0)
    for v in range(2):
        value = conv[v].reshape(rows * cols, channels)
        centred = value - jnp.mean(value, axis=-1, keepdims=True)
        inverse = lax.rsqrt(jnp.mean(centred * centred, axis=-1, keepdims=True) + 1e-06)
        value = centred * inverse
        nhat[v] = value
        inv[v] = jnp.broadcast_to(inverse, (rows * cols, LANES))
        normed[v] = (value * gain[...]).astype(BF16)


def conv_norm(features, table, turned, inside, across, dw, gain):
    rows, cols, channels = features.shape
    pixels = rows * cols
    return call(
        conv_body,
        "conv_norm",
        4 * 10**9,
        [
            ((2, pixels, channels), BF16),
            ((2, pixels, channels), F32),
            ((2, pixels, LANES), F32),
            ((2, rows, 16, channels), F32),
        ],
        [((2, rows, cols, channels), F32)],
        features,
        table,
        turned,
        inside,
        across,
        dw,
        gain,
    )


def blocks(total):
    return [slice(at, at + BLOCK) for at in range(0, total, BLOCK)]


def forward_body(
    scale, normed, expand, reduce, wide, ls, slope, hidden, disagreement, dbranch, gscale
):
    pixels, channels = normed.shape
    half = pixels // 2
    rows, cols, _ = disagreement.shape
    for here in blocks(expand.shape[1]):
        pre = dot(normed[...], expand[:, here], ((1,), (0,)))
        cdf, density = phi_parts(pre)
        slope[:, here] = (cdf + pre * density).astype(BF16)
        hidden[:, here] = (pre * cdf).astype(BF16)
    branch = dot(hidden[...], reduce[...], ((1,), (0,)))
    factor = ls[...].reshape(1, channels)
    outs = []
    for v in range(2):
        own = wide[v, :, 3 : 3 + cols, :].reshape(half, channels)
        outs.append((own + factor * branch[v * half : (v + 1) * half]).astype(BF16).astype(F32))
    difference = outs[0] - outs[1]
    disagreement[...] = difference.astype(BF16).reshape(rows, cols, channels)
    residual = (difference * scale).astype(BF16).astype(F32)
    gscale[...] = jnp.sum((branch[:half] - branch[half:]) * residual, axis=0, keepdims=True)
    dbranch[...] = (factor * residual).astype(BF16)


def forward(scale, normed, expand, reduce, wide, ls, shape):
    pixels, channels = normed.shape
    hid = expand.shape[1]
    return call(
        functools.partial(forward_body, scale),
        "forward",
        10**9,
        [
            ((pixels, hid), BF16),
            ((pixels, hid), BF16),
            (shape, BF16),
            ((pixels // 2, channels), BF16),
            ((1, channels), F32),
        ],
        [],
        normed,
        expand,
        reduce,
        wide,
        ls,
        read=10**6,
    )


def backward_body(dbranch, slope, expand, reduce, dnormed, dpre):
    half = dbranch.shape[0]
    for here in blocks(expand.shape[1]):
        dhidden = dot(dbranch[...], reduce[here, :], ((1,), (1,)))
        dpre[:, here] = dpre_of(dhidden, slope[:, here].astype(F32))
    dnormed[...] = dot(dpre[...], expand[...], ((1,), (1,)))


def backward(dbranch, slope, expand, reduce):
    half, channels = dbranch.shape
    hid = expand.shape[1]
    return call(
        backward_body,
        "backward",
        10**9,
        [((2 * half, channels), F32)],
        [((2 * half, hid), BF16)],
        dbranch,
        slope,
        expand,
        reduce,
        read=10**6,
    )[0]


def small_body(dnormed, nhat, inv, gain, gscale, wide, out, grad, taps, small):
    half, channels = dnormed.shape[0] // 2, dnormed.shape[1]
    _, rows, _, _ = wide.shape
    cols = half // rows
    factor = gain[...]
    ggain = jnp.zeros((1, channels), F32)
    for v in range(2):
        here = slice(v * half, (v + 1) * half)
        value = dnormed[here, :]
        ggain = ggain + jnp.sum(value * nhat[v], axis=0, keepdims=True)
        scaled = value * factor
        gm = jnp.mean(scaled, axis=-1, keepdims=True)
        gn = jnp.mean(scaled * nhat[v], axis=-1, keepdims=True)
        grad[here, :] = inv[v][:, :1] * (scaled - gm - nhat[v] * gn)

    def tile(c, carry):
        lanes = pl.ds(pl.multiple_of(c * LANES, LANES), LANES)
        dconv = [
            [grad[pl.ds(v * half + r * cols, cols), lanes] for r in range(rows)] for v in range(2)
        ]
        for j in range(7):
            part = [
                [wide[v, r, pl.ds(6 - j if v else j, cols), lanes] for r in range(rows)]
                for v in range(2)
            ]
            for i in range(7):
                sums = []
                for v in range(2):
                    total = None
                    for r in range(rows):
                        if 0 <= r + i - 3 < rows:
                            term = part[v][r + i - 3] * dconv[v][r]
                            total = term if total is None else total + term
                    sums.append(total)
                at = 8 * (7 * i + j)
                taps[at : at + 8, :] = sums[0] + sums[1]
        rolled = taps[pl.ds(0, 49, stride=8), :]
        for s in range(1, 8):
            rolled = rolled + taps[pl.ds(s, 49, stride=8), :]
        small[:49, lanes] = rolled
        return carry

    small[...] = jnp.zeros(small.shape, F32)
    lax.fori_loop(0, channels // LANES, tile, 0)
    small[49:50, :] = ggain
    small[50:51, :] = gscale[...]
    out[...] = small[...].astype(BF16)


def small_grads(dnormed, nhat, inv, gain, gscale, wide):
    channels = dnormed.shape[1]
    return call(
        small_body,
        "small_grads",
        10**6,
        [((64, channels), BF16)],
        [(dnormed.shape, F32), ((8 * 49, LANES), F32), ((64, channels), F32)],
        dnormed,
        nhat,
        inv,
        gain,
        gscale,
        wide,
        read=10**5,
    )[0]


def gate_body(block, *rest):
    rest[-1][...] = block[...]


def gate(block, *after):
    shapes = [(block.shape, block.dtype)]
    return call(gate_body, "gate", 10**6, shapes, [], block, *after, read=10**5)[0]


def split(total, side, keep, send):
    parts, rows, _ = keep.shape
    for x in range(parts):
        mine = pl.multiple_of((2 * x + side) * rows, 16)
        theirs = pl.multiple_of((2 * x + 1 - side) * rows, 16)
        keep[x] = total[pl.ds(mine, rows), :]
        send[x] = total[pl.ds(theirs, rows), :].astype(BF16)


def added(small, more):
    return (small[...].astype(F32) + more[...].astype(F32)).astype(BF16)


def slope_and_act(normed, expand):
    pre = dot(normed, expand, ((1,), (0,)))
    cdf, density = phi_parts(pre)
    return cdf + pre * density, (pre * cdf).astype(BF16)


def views_apart(act):
    half = act.shape[0] // 2
    return (act[:half].astype(F32) - act[half:].astype(F32)).astype(BF16)


def dpre_of(dhidden, slope):
    half = dhidden.shape[0]
    return jnp.concatenate([dhidden * slope[:half], -dhidden * slope[half:]]).astype(BF16)


def own_lanes(own, width):
    first = position(4)[0] * own
    start = first // LANES * LANES
    return pl.ds(pl.multiple_of(start, LANES), width), first - start


def near_body(
    n_0, n_1, n_2, d_0, d_1, d_2, slope_0, hidden_0, expand, reduce, turned, dpre, total, hidden
):
    half, channels = d_0.shape
    units = total.shape[0]
    lanes, _ = own_lanes(channels // 4, turned.shape[0])
    for p, ref in enumerate((n_0, n_1, n_2)):
        at = 2 * p * half
        turned[:, at : at + 2 * half] = ref[:, lanes].astype(F32).T.astype(BF16)
    every = jnp.concatenate([d_0[...], d_1[...], d_2[...]])
    both = jnp.concatenate([n_1[...], n_2[...]])
    for here in blocks(reduce.shape[0]):
        slope, act = slope_and_act(both, expand[:, here])
        slopes = [slope_0[:, here].astype(F32), slope[: 2 * half], slope[2 * half :]]
        hidden[:, here] = act
        dhidden = dot(every, reduce[here, :], ((1,), (1,)))
        for p in range(3):
            part = dpre_of(dhidden[p * half : (p + 1) * half], slopes[p])
            dpre[2 * p * half : 2 * (p + 1) * half, here] = part
    lanes = pl.ds(pl.multiple_of(position(4)[0] * units, LANES), units)
    acts = (hidden_0[:, lanes], hidden[: 2 * half, lanes], hidden[2 * half :, lanes])
    total[...] = dot(jnp.concatenate([views_apart(act) for act in acts]), every, ((0,), (0,)))


def near(normed, dbranch, slope, hidden, expand, reduce, line):
    half, channels = dbranch[0].shape
    hid = expand.shape[1]
    return call(
        near_body,
        "near",
        10**6,
        [
            ((2 * LANES, 6 * half), BF16),
            ((6 * half, hid), BF16),
            ((hid // line, channels), F32),
        ],
        [((4 * half, hid), BF16)],
        *normed,
        *dbranch,
        slope,
        hidden,
        expand,
        reduce,
        read=10**5,
    )


def far_reduce_body(n_3, d_3, expand, part, small, more, keep, send, sums, total):
    units = total.shape[0]
    line, core, _ = position(4)
    lanes = pl.ds(pl.multiple_of(line * units, LANES), units)
    _, act = slope_and_act(n_3[...], expand[:, lanes])
    total[...] = part[...] + dot(views_apart(act), d_3[...], ((0,), (0,)))
    split(total, core, keep, send)
    sums[...] = added(small, more)


def far_reduce(n_3, d_3, expand, part, small, more, inner):
    units, channels = part.shape
    shape = (inner // 2, units // inner, channels)
    return call(
        far_reduce_body,
        "far_reduce",
        10**6,
        [(shape, F32), (shape, BF16), (small.shape, BF16)],
        [((units, channels), F32)],
        n_3,
        d_3,
        expand,
        part,
        small,
        more,
        read=10**5,
    )


def far_expand_body(n_3, d_3, expand, reduce, after, turned, dpre):
    lanes, _ = own_lanes(n_3.shape[1] // 4, turned.shape[0])
    turned[...] = n_3[:, lanes].astype(F32).T.astype(BF16)
    for here in blocks(reduce.shape[0]):
        slope, _ = slope_and_act(n_3[...], expand[:, here])
        dpre[:, here] = dpre_of(dot(d_3[...], reduce[here, :], ((1,), (1,))), slope)


def far_expand(n_3, d_3, expand, reduce, after):
    rows = n_3.shape[0]
    hid = expand.shape[1]
    return call(
        far_expand_body,
        "far_expand",
        10**9,
        [((2 * LANES, rows), BF16), ((rows, hid), BF16)],
        [],
        n_3,
        d_3,
        expand,
        reduce,
        after,
        read=10**6,
    )


def expand_grad_body(turned, turned_3, dpre, dpre_3, after, keep, send, total):
    own, hid = total.shape
    _, core, _ = position(4)
    _, first = own_lanes(own, turned.shape[0])
    rows = pl.ds(pl.multiple_of(first, 16), own)
    for here in blocks(hid):
        part = dot(turned[rows, :], dpre[:, here], ((1,), (0,)))
        total[:, here] = part + dot(turned_3[rows, :], dpre_3[:, here], ((1,), (0,)))
    split(total, core, keep, send)


def expand_grad(turned, turned_3, dpre, dpre_3, after, own, inner):
    hid = dpre.shape[1]
    shape = (inner // 2, own // inner, hid)
    return call(
        expand_grad_body,
        "expand_grad",
        10**6,
        [(shape, F32), (shape, BF16)],
        [((own, hid), F32)],
        turned,
        turned_3,
        dpre,
        dpre_3,
        after,
        read=10**5,
    )


def merge_body(kept, got, keep, send):
    _, _, mine = position(4)
    theirs = 1 - mine
    keep[...] = kept[mine] + got[mine].astype(F32)
    send[...] = (kept[theirs] + got[theirs].astype(F32)).astype(BF16)


def merge_small_body(kept, got, small, more, keep, send, sums):
    merge_body(kept, got, keep, send)
    sums[...] = added(small, more)


def merge(kept, got, *small):
    shape = kept.shape[1:]
    return call(
        merge_small_body if small else merge_body,
        "merge",
        10**6,
        [(shape, F32), (shape, BF16)] + [(part.shape, BF16) for part in small[:1]],
        [],
        kept,
        got,
        *small,
        read=10**5,
    )


def finish_body(
    keep_e, got_e, keep_r, got_r, small, more, out_e, out_r, kernel, gain, scale
):
    out_e[...] = keep_e[...] + got_e[...].astype(F32)
    out_r[...] = keep_r[...] + got_r[...].astype(F32)
    sums = small[...].astype(F32) + more[...].astype(F32)
    for i in range(7):
        kernel[i] = sums[7 * i : 7 * i + 7]
    gain[...] = sums[49:50].reshape(gain.shape)
    scale[...] = sums[50:51].reshape(scale.shape)


def finish(keep_e, got_e, keep_r, got_r, small, more):
    channels = small.shape[1]
    return call(
        finish_body,
        "finish",
        10**8,
        [
            (keep_e.shape, F32),
            (keep_r.shape, F32),
            ((7, 7, channels), F32),
            ((channels,), F32),
            ((channels,), F32),
        ],
        [],
        keep_e,
        got_e,
        keep_r,
        got_r,
        small,
        more,
    )


def grads_plain(every, dbranch_all, expand_weight, reduce_weight, my_line, my_inner, line, inner):
    channels, hid = expand_weight.shape
    units, own = hid // line, channels // line
    every = every.reshape(-1, channels)
    pre = dot(every, expand_weight, ((1,), (0,)))
    cdf, density = phi_parts(pre)
    slope = (cdf + pre * density).reshape(line, 2, -1, hid)
    hidden = (pre * cdf).astype(BF16).astype(F32).reshape(line, 2, -1, hid)
    diff = (hidden[:, 0] - hidden[:, 1]).astype(BF16).reshape(-1, hid)
    diff = lax.dynamic_slice_in_dim(diff, my_line * units, units, 1)
    dhidden = dot(dbranch_all, reduce_weight, ((1,), (1,))).reshape(line, -1, hid)
    dpre = jnp.stack([dhidden * slope[:, 0], -dhidden * slope[:, 1]], axis=1)
    dpre = dpre.astype(BF16).reshape(-1, hid)
    normed_own = lax.dynamic_slice_in_dim(every, my_line * own, own, 1)
    expand = dot(normed_own, dpre, ((0,), (0,))).reshape(inner, own // inner, hid)
    reduce = dot(diff, dbranch_all, ((0,), (0,))).reshape(inner, units // inner, channels)
    return halves(expand, my_inner & 1), halves(reduce, my_inner & 1)


def halves(part, side):
    part = part.reshape((part.shape[0] // 2, 2) + part.shape[1:])
    keep = lax.dynamic_index_in_dim(part, side, 1, keepdims=False)
    send = lax.dynamic_index_in_dim(part, 1 - side, 1, keepdims=False)
    return keep, send.astype(BF16)


def on_device(
    features, column_table, dw_kernel, norm_gain, expand_weight, reduce_weight, layer_scale
):
    rows, cols, channels = features.shape
    hid = expand_weight.shape[1]
    count = lax.axis_size("col")
    bits = count.bit_length() - 1
    line = 1 << ((bits + 1) // 2)
    inner = count // line
    inner_bits = inner.bit_length() - 1
    me = lax.axis_index("col")
    my_line, my_inner = me // inner, me % inner
    units, own = hid // line, channels // line
    total_cols = cols * count

    def swapped(block, mask):
        return lax.ppermute(block, "col", [(d, d ^ mask) for d in range(count)])

    def line_sum(small):
        sums = [small] + [swapped(small, p * inner) for p in range(1, line)]
        sums = [part.astype(F32) for part in sums]
        while len(sums) > 1:
            sums = [low + high for low, high in zip(sums[::2], sums[1::2])]
        return sums[0]

    mirror = lax.ppermute(column_table, "col", [(d, count - 1 - d) for d in range(count)])

    features_f = features.astype(F32)
    table_f = column_table.astype(F32)
    gain = norm_gain[None]
    inside, across, turned = edges(features_f, table_f, mirror)
    inside = swapped(inside, 1)
    pairs = [(d, d + 1) for d in range(1, count - 1, 2)]
    across = lax.ppermute(across, "col", pairs + [(high, low) for low, high in pairs])
    normed, nhat, inv, wide = conv_norm(
        features_f, table_f, turned, inside, across, dw_kernel.astype(F32), gain
    )
    fast = line == 4 and inner == 4 and units % LANES == 0 and own % 64 == 0
    if fast:
        flat = normed.reshape(-1, channels)
        normed_2, normed_1 = swapped(flat, 2 * inner), swapped(flat, inner)
    else:
        others = [swapped(normed, p * inner) for p in range(1, line)]
    slope, hidden, disagreement, dbranch, gscale = forward(
        1.0 / math.sqrt(rows * total_cols),
        normed.reshape(-1, channels),
        expand_weight,
        reduce_weight,
        wide,
        layer_scale,
        features.shape,
    )
    dnormed = backward(dbranch, slope, expand_weight, reduce_weight)
    small = small_grads(dnormed, nhat, inv, gain, gscale, wide)
    if fast:
        dbranch_2, dbranch_1 = swapped(dbranch, 2 * inner), swapped(dbranch, inner)
        normed_3 = swapped(gate(normed_2, dnormed, normed_1), inner)
        dbranch_3 = swapped(gate(dbranch_2, small, dbranch_1), inner)
        more = swapped(small, 2)
        turned, dpre, part = near(
            [flat, normed_1, normed_2],
            [dbranch, dbranch_1, dbranch_2],
            slope,
            hidden,
            expand_weight,
            reduce_weight,
            line,
        )
        keep_r, send_r, small = far_reduce(
            normed_3, dbranch_3, expand_weight, part, small, more, inner
        )
        got_r, more = swapped(send_r, 1), swapped(small, 1)
        turned_3, dpre_3 = far_expand(normed_3, dbranch_3, expand_weight, reduce_weight, small)
        keep_r, send_r, small = merge(keep_r, got_r, small, more)
        got_r, more = swapped(send_r, 2), swapped(small, inner)
        keep_e, send_e = expand_grad(turned, turned_3, dpre, dpre_3, small, own, inner)
        keep_e, send_e, small = merge(keep_e, swapped(send_e, 1), small, more)
        got_e, more = swapped(send_e, 2), swapped(small, 2 * inner)
        sums = finish(keep_e, got_e, keep_r, got_r, small, more)
        return (disagreement, *sums)

    dbranch_all = [dbranch] + [swapped(dbranch, p * inner) for p in range(1, line)]
    (keep_e, send_e), (keep_r, send_r) = grads_plain(
        jnp.stack([normed] + others),
        jnp.concatenate(dbranch_all),
        expand_weight,
        reduce_weight,
        my_line,
        my_inner,
        line,
        inner,
    )
    small = line_sum(small)
    for bit in range(inner_bits):
        sum_r = keep_r + swapped(send_r, 1 << bit).astype(F32)
        sum_e = keep_e + swapped(send_e, 1 << bit).astype(F32)
        small = small.astype(BF16)
        small = small.astype(F32) + swapped(small, 1 << bit).astype(F32)
        if bit < inner_bits - 1:
            side = (my_inner >> (bit + 1)) & 1
            keep_r, send_r = halves(sum_r, side)
            keep_e, send_e = halves(sum_e, side)
    grad_kernel = small[:49].reshape(7, 7, channels)
    return (
        disagreement,
        sum_e.reshape(own // inner, hid),
        sum_r.reshape(units // inner, channels),
        grad_kernel,
        small[49],
        small[50],
    )


def solution(mesh):
    in_specs = (P("groups", "col", None), P("col", None), P(), P(), P(), P(), P())
    out_specs = (
        P("groups", "col", None),
        P(("groups", "col"), None),
        P(("groups", "col"), None),
        P("groups", None, None),
        P("groups"),
        P("groups"),
    )
    return jax.shard_map(
        on_device, mesh=mesh, in_specs=in_specs, out_specs=out_specs, check_vma=False
    )
```

```python
import functools
import math

import jax
import jax.numpy as jnp
from jax import lax
from jax.experimental import pallas as pl
from jax.experimental.pallas import tpu as pltpu
from jax.sharding import PartitionSpec as P

BF16 = jnp.bfloat16
F32 = jnp.float32
LANES = 128
VMEM_GRANT = 16 << 20
BLOCK = 256


def phi_parts(pre):
    decay = jnp.exp(-0.5 * pre * pre)
    t = 1.0 / (1.0 + 0.23164189 * jnp.abs(pre))
    poly = 0.5307027145 * t - 0.7265760135
    poly = poly * t + 0.7107068705
    poly = poly * t - 0.142248368
    poly = poly * t + 0.127414796
    tail = poly * t * decay
    return jnp.where(pre < 0.0, tail, 1.0 - tail), decay * 0.3989422804014327


def call(body, name, flops, out_shape, scratch, *operands, read=10**8):
    return pl.pallas_call(
        body,
        in_specs=[pl.BlockSpec(memory_space=pltpu.VMEM) for _ in operands],
        out_specs=[pl.BlockSpec(memory_space=pltpu.VMEM) for _ in out_shape],
        out_shape=[jax.ShapeDtypeStruct(shape, dtype) for shape, dtype in out_shape],
        scratch_shapes=[pltpu.VMEM(shape, dtype) for shape, dtype in scratch],
        compiler_params=pltpu.CompilerParams(vmem_limit_bytes=VMEM_GRANT),
        cost_estimate=pl.CostEstimate(flops=flops, bytes_accessed=read, transcendentals=0),
        name=name,
    )(*operands)


def position(inner):
    me = lax.axis_index("col")
    return me // inner, me & 1, (me >> 1) & 1


def dot(lhs, rhs, contract):
    return lax.dot_general(lhs, rhs, (contract, ((), ())), preferred_element_type=F32)


def flipped(value):
    rows = value.shape[0]
    return jnp.concatenate([value[r : r + 1] for r in reversed(range(rows))], axis=0)


def edges_body(feat, table, mirror, inside, across, turned):
    _, cols, channels = feat.shape
    other = flipped(mirror[...].astype(F32))
    odd = (lax.axis_index("col") & 1) == 1
    for v, add in enumerate((table[...], other)):
        own = (feat[...] + add[None]).astype(BF16).astype(F32)
        first, last = own[:, :3], own[:, cols - 3 :]
        inside[v] = jnp.where(odd, first, last).astype(BF16)
        across[v] = jnp.where(odd, last, first).astype(BF16)
    turned[...] = other


def edges(features, table, mirror):
    rows, cols, channels = features.shape
    return call(
        edges_body,
        "edges",
        10**8,
        [
            ((2, rows, 3, channels), BF16),
            ((2, rows, 3, channels), BF16),
            ((cols, channels), F32),
        ],
        [],
        features,
        table,
        mirror,
    )


def conv_body(feat, table, turned, inside, across, dw, gain, normed, nhat, inv, wide, conv):
    rows, cols, channels = feat.shape
    odd = (lax.axis_index("col") & 1) == 1
    for v, add in enumerate((table[...], turned[...])):
        wide[v, :, 3 : 3 + cols, :] = (feat[...] + add[None]).astype(BF16).astype(F32)
        one, two = inside[v].astype(F32), across[v].astype(F32)
        wide[v, :, 0:3, :] = jnp.where(odd, one, two)
        wide[v, :, 3 + cols : 6 + cols, :] = jnp.where(odd, two, one)

    def tile(c, carry):
        lanes = pl.ds(pl.multiple_of(c * LANES, LANES), LANES)
        sums = [[jnp.zeros((cols, LANES), F32) for _ in range(rows)] for _ in range(2)]
        for j in range(7):
            for v in range(2):
                part = [wide[v, r, pl.ds(j, cols), lanes] for r in range(rows)]
                for i in range(7):
                    weight = dw[i, pl.ds(6 - j if v else j, 1), lanes]
                    for r in range(rows):
                        if 0 <= r + i - 3 < rows:
                            sums[v][r] = sums[v][r] + weight * part[r + i - 3]
        for v in range(2):
            for r in range(rows):
                conv[v, r, :, lanes] = sums[v][r]
        return carry

    lax.fori_loop(0, channels // LANES, tile, 0)
    for v in range(2):
        value = conv[v].reshape(rows * cols, channels)
        centred = value - jnp.mean(value, axis=-1, keepdims=True)
        inverse = lax.rsqrt(jnp.mean(centred * centred, axis=-1, keepdims=True) + 1e-06)
        value = centred * inverse
        nhat[v] = value
        inv[v] = jnp.broadcast_to(inverse, (rows * cols, LANES))
        normed[v] = (value * gain[...]).astype(BF16)


def conv_norm(features, table, turned, inside, across, dw, gain):
    rows, cols, channels = features.shape
    pixels = rows * cols
    return call(
        conv_body,
        "conv_norm",
        4 * 10**9,
        [
            ((2, pixels, channels), BF16),
            ((2, pixels, channels), F32),
            ((2, pixels, LANES), F32),
            ((2, rows, 16, channels), F32),
        ],
        [((2, rows, cols, channels), F32)],
        features,
        table,
        turned,
        inside,
        across,
        dw,
        gain,
    )


def blocks(total):
    return [slice(at, at + BLOCK) for at in range(0, total, BLOCK)]


def forward_body(
    scale, normed, expand, reduce, wide, ls, slope, hidden, disagreement, dbranch, gscale
):
    pixels, channels = normed.shape
    half = pixels // 2
    rows, cols, _ = disagreement.shape
    for here in blocks(expand.shape[1]):
        pre = dot(normed[...], expand[:, here], ((1,), (0,)))
        cdf, density = phi_parts(pre)
        slope[:, here] = (cdf + pre * density).astype(BF16)
        hidden[:, here] = (pre * cdf).astype(BF16)
    branch = dot(hidden[...], reduce[...], ((1,), (0,)))
    factor = ls[...].reshape(1, channels)
    outs = []
    for v in range(2):
        own = wide[v, :, 3 : 3 + cols, :].reshape(half, channels)
        outs.append((own + factor * branch[v * half : (v + 1) * half]).astype(BF16).astype(F32))
    difference = outs[0] - outs[1]
    disagreement[...] = difference.astype(BF16).reshape(rows, cols, channels)
    residual = (difference * scale).astype(BF16).astype(F32)
    gscale[...] = jnp.sum((branch[:half] - branch[half:]) * residual, axis=0, keepdims=True)
    dbranch[...] = (factor * residual).astype(BF16)


def forward(scale, normed, expand, reduce, wide, ls, shape):
    pixels, channels = normed.shape
    hid = expand.shape[1]
    return call(
        functools.partial(forward_body, scale),
        "forward",
        10**9,
        [
            ((pixels, hid), BF16),
            ((pixels, hid), BF16),
            (shape, BF16),
            ((pixels // 2, channels), BF16),
            ((1, channels), F32),
        ],
        [],
        normed,
        expand,
        reduce,
        wide,
        ls,
        read=10**6,
    )


def backward_body(dbranch, slope, expand, reduce, dnormed, dpre):
    half = dbranch.shape[0]
    for here in blocks(expand.shape[1]):
        dhidden = dot(dbranch[...], reduce[here, :], ((1,), (1,)))
        dpre[:, here] = dpre_of(dhidden, slope[:, here].astype(F32))
    dnormed[...] = dot(dpre[...], expand[...], ((1,), (1,)))


def backward(dbranch, slope, expand, reduce):
    half, channels = dbranch.shape
    hid = expand.shape[1]
    return call(
        backward_body,
        "backward",
        10**9,
        [((2 * half, channels), F32), ((2 * half, hid), BF16)],
        [],
        dbranch,
        slope,
        expand,
        reduce,
        read=10**6,
    )


def small_body(dnormed, nhat, inv, gain, gscale, wide, *rest):
    out, grad, taps, small = rest[-4:]
    half, channels = dnormed.shape[0] // 2, dnormed.shape[1]
    _, rows, _, _ = wide.shape
    cols = half // rows
    factor = gain[...]
    ggain = jnp.zeros((1, channels), F32)
    for v in range(2):
        here = slice(v * half, (v + 1) * half)
        value = dnormed[here, :]
        ggain = ggain + jnp.sum(value * nhat[v], axis=0, keepdims=True)
        scaled = value * factor
        gm = jnp.mean(scaled, axis=-1, keepdims=True)
        gn = jnp.mean(scaled * nhat[v], axis=-1, keepdims=True)
        grad[here, :] = inv[v][:, :1] * (scaled - gm - nhat[v] * gn)

    def tile(c, carry):
        lanes = pl.ds(pl.multiple_of(c * LANES, LANES), LANES)
        dconv = [
            [grad[pl.ds(v * half + r * cols, cols), lanes] for r in range(rows)] for v in range(2)
        ]
        for j in range(7):
            part = [
                [wide[v, r, pl.ds(6 - j if v else j, cols), lanes] for r in range(rows)]
                for v in range(2)
            ]
            for i in range(7):
                sums = []
                for v in range(2):
                    total = None
                    for r in range(rows):
                        if 0 <= r + i - 3 < rows:
                            term = part[v][r + i - 3] * dconv[v][r]
                            total = term if total is None else total + term
                    sums.append(total)
                at = 8 * (7 * i + j)
                taps[at : at + 8, :] = sums[0] + sums[1]
        rolled = taps[pl.ds(0, 49, stride=8), :]
        for s in range(1, 8):
            rolled = rolled + taps[pl.ds(s, 49, stride=8), :]
        small[:49, lanes] = rolled
        return carry

    small[...] = jnp.zeros(small.shape, F32)
    lax.fori_loop(0, channels // LANES, tile, 0)
    small[49:50, :] = ggain
    small[50:51, :] = gscale[...]
    out[...] = small[...].astype(BF16)


def small_grads(dnormed, nhat, inv, gain, gscale, wide, *after):
    channels = dnormed.shape[1]
    return call(
        small_body,
        "small_grads",
        10**6,
        [((64, channels), BF16)],
        [(dnormed.shape, F32), ((8 * 49, LANES), F32), ((64, channels), F32)],
        dnormed,
        nhat,
        inv,
        gain,
        gscale,
        wide,
        *after,
        read=10**5,
    )[0]


def gate_body(block, *rest):
    rest[-1][...] = block[...]


def gate(block, *after):
    shapes = [(block.shape, block.dtype)]
    return call(gate_body, "gate", 10**6, shapes, [], block, *after, read=10**5)[0]


def split(total, side, keep, send):
    parts, rows, _ = keep.shape
    for x in range(parts):
        mine = pl.multiple_of((2 * x + side) * rows, 16)
        theirs = pl.multiple_of((2 * x + 1 - side) * rows, 16)
        keep[x] = total[pl.ds(mine, rows), :]
        send[x] = total[pl.ds(theirs, rows), :].astype(BF16)


def added(small, more):
    return (small[...].astype(F32) + more[...].astype(F32)).astype(BF16)


def slope_and_act(normed, expand):
    pre = dot(normed, expand, ((1,), (0,)))
    cdf, density = phi_parts(pre)
    return cdf + pre * density, (pre * cdf).astype(BF16)


def views_apart(act):
    half = act.shape[0] // 2
    return (act[:half].astype(F32) - act[half:].astype(F32)).astype(BF16)


def dpre_of(dhidden, slope):
    half = dhidden.shape[0]
    return jnp.concatenate([dhidden * slope[:half], -dhidden * slope[half:]]).astype(BF16)


def own_lanes(own, width):
    first = position(4)[0] * own
    start = first // LANES * LANES
    return pl.ds(pl.multiple_of(start, LANES), width), first - start


def near_body(
    n_0, n_1, n_2, d_0, d_1, d_2, hidden_0, expand, reduce, turned, dpre, total, hidden
):
    half, channels = d_0.shape
    units = total.shape[0]
    lanes, _ = own_lanes(channels // 4, turned.shape[0])
    for p, ref in enumerate((n_0, n_1, n_2)):
        at = 2 * p * half
        turned[:, at : at + 2 * half] = ref[:, lanes].astype(F32).T.astype(BF16)
    others = jnp.concatenate([d_1[...], d_2[...]])
    both = jnp.concatenate([n_1[...], n_2[...]])
    for here in blocks(reduce.shape[0]):
        slope, act = slope_and_act(both, expand[:, here])
        hidden[:, here] = act
        dhidden = dot(others, reduce[here, :], ((1,), (1,)))
        dpre[: 2 * half, here] = dpre_of(dhidden[:half], slope[: 2 * half])
        dpre[2 * half :, here] = dpre_of(dhidden[half:], slope[2 * half :])
    lanes = pl.ds(pl.multiple_of(position(4)[0] * units, LANES), units)
    every = jnp.concatenate([d_0[...], others])
    acts = (hidden_0[:, lanes], hidden[: 2 * half, lanes], hidden[2 * half :, lanes])
    total[...] = dot(jnp.concatenate([views_apart(act) for act in acts]), every, ((0,), (0,)))


def near(normed, dbranch, hidden, expand, reduce, line):
    half, channels = dbranch[0].shape
    hid = expand.shape[1]
    return call(
        near_body,
        "near",
        10**6,
        [
            ((2 * LANES, 6 * half), BF16),
            ((4 * half, hid), BF16),
            ((hid // line, channels), F32),
        ],
        [((4 * half, hid), BF16)],
        *normed,
        *dbranch,
        hidden,
        expand,
        reduce,
        read=10**5,
    )


def far_reduce_body(n_3, d_3, expand, part, small, more, keep, send, sums, total):
    units = total.shape[0]
    line, core, _ = position(4)
    lanes = pl.ds(pl.multiple_of(line * units, LANES), units)
    _, act = slope_and_act(n_3[...], expand[:, lanes])
    total[...] = part[...] + dot(views_apart(act), d_3[...], ((0,), (0,)))
    split(total, core, keep, send)
    sums[...] = added(small, more)


def far_reduce(n_3, d_3, expand, part, small, more, inner):
    units, channels = part.shape
    shape = (inner // 2, units // inner, channels)
    return call(
        far_reduce_body,
        "far_reduce",
        10**6,
        [(shape, F32), (shape, BF16), (small.shape, BF16)],
        [((units, channels), F32)],
        n_3,
        d_3,
        expand,
        part,
        small,
        more,
        read=10**5,
    )


def far_expand_body(n_3, d_3, expand, reduce, after, turned, dpre):
    lanes, _ = own_lanes(n_3.shape[1] // 4, turned.shape[0])
    turned[...] = n_3[:, lanes].astype(F32).T.astype(BF16)
    for here in blocks(reduce.shape[0]):
        slope, _ = slope_and_act(n_3[...], expand[:, here])
        dpre[:, here] = dpre_of(dot(d_3[...], reduce[here, :], ((1,), (1,))), slope)


def far_expand(n_3, d_3, expand, reduce, after):
    rows = n_3.shape[0]
    hid = expand.shape[1]
    return call(
        far_expand_body,
        "far_expand",
        10**9,
        [((2 * LANES, rows), BF16), ((rows, hid), BF16)],
        [],
        n_3,
        d_3,
        expand,
        reduce,
        after,
        read=10**6,
    )


def expand_grad_body(turned, turned_3, dpre_0, dpre, dpre_3, after, keep, send, total):
    own, hid = total.shape
    _, core, _ = position(4)
    _, first = own_lanes(own, turned.shape[0])
    rows = pl.ds(pl.multiple_of(first, 16), own)
    lhs = jnp.concatenate([turned[rows, :], turned_3[rows, :]], axis=1)
    for here in blocks(hid):
        every = jnp.concatenate([dpre_0[:, here], dpre[:, here], dpre_3[:, here]])
        total[:, here] = dot(lhs, every, ((1,), (0,)))
    split(total, core, keep, send)


def expand_grad(turned, turned_3, dpre_0, dpre, dpre_3, after, own, inner):
    hid = dpre.shape[1]
    shape = (inner // 2, own // inner, hid)
    return call(
        expand_grad_body,
        "expand_grad",
        10**6,
        [(shape, F32), (shape, BF16)],
        [((own, hid), F32)],
        turned,
        turned_3,
        dpre_0,
        dpre,
        dpre_3,
        after,
        read=10**5,
    )


def merge_body(kept, got, keep, send):
    _, _, mine = position(4)
    theirs = 1 - mine
    keep[...] = kept[mine] + got[mine].astype(F32)
    send[...] = (kept[theirs] + got[theirs].astype(F32)).astype(BF16)


def merge_small_body(kept, got, small, more, keep, send, sums):
    merge_body(kept, got, keep, send)
    sums[...] = added(small, more)


def merge(kept, got, *small):
    shape = kept.shape[1:]
    return call(
        merge_small_body if small else merge_body,
        "merge",
        10**6,
        [(shape, F32), (shape, BF16)] + [(part.shape, BF16) for part in small[:1]],
        [],
        kept,
        got,
        *small,
        read=10**5,
    )


def finish_body(
    keep_e, got_e, keep_r, got_r, small, more, out_e, out_r, kernel, gain, scale
):
    out_e[...] = keep_e[...] + got_e[...].astype(F32)
    out_r[...] = keep_r[...] + got_r[...].astype(F32)
    sums = small[...].astype(F32) + more[...].astype(F32)
    for i in range(7):
        kernel[i] = sums[7 * i : 7 * i + 7]
    gain[...] = sums[49:50].reshape(gain.shape)
    scale[...] = sums[50:51].reshape(scale.shape)


def finish(keep_e, got_e, keep_r, got_r, small, more):
    channels = small.shape[1]
    return call(
        finish_body,
        "finish",
        10**8,
        [
            (keep_e.shape, F32),
            (keep_r.shape, F32),
            ((7, 7, channels), F32),
            ((channels,), F32),
            ((channels,), F32),
        ],
        [],
        keep_e,
        got_e,
        keep_r,
        got_r,
        small,
        more,
    )


def grads_plain(every, dbranch_all, expand_weight, reduce_weight, my_line, my_inner, line, inner):
    channels, hid = expand_weight.shape
    units, own = hid // line, channels // line
    every = every.reshape(-1, channels)
    pre = dot(every, expand_weight, ((1,), (0,)))
    cdf, density = phi_parts(pre)
    slope = (cdf + pre * density).reshape(line, 2, -1, hid)
    hidden = (pre * cdf).astype(BF16).astype(F32).reshape(line, 2, -1, hid)
    diff = (hidden[:, 0] - hidden[:, 1]).astype(BF16).reshape(-1, hid)
    diff = lax.dynamic_slice_in_dim(diff, my_line * units, units, 1)
    dhidden = dot(dbranch_all, reduce_weight, ((1,), (1,))).reshape(line, -1, hid)
    dpre = jnp.stack([dhidden * slope[:, 0], -dhidden * slope[:, 1]], axis=1)
    dpre = dpre.astype(BF16).reshape(-1, hid)
    normed_own = lax.dynamic_slice_in_dim(every, my_line * own, own, 1)
    expand = dot(normed_own, dpre, ((0,), (0,))).reshape(inner, own // inner, hid)
    reduce = dot(diff, dbranch_all, ((0,), (0,))).reshape(inner, units // inner, channels)
    return halves(expand, my_inner & 1), halves(reduce, my_inner & 1)


def halves(part, side):
    part = part.reshape((part.shape[0] // 2, 2) + part.shape[1:])
    keep = lax.dynamic_index_in_dim(part, side, 1, keepdims=False)
    send = lax.dynamic_index_in_dim(part, 1 - side, 1, keepdims=False)
    return keep, send.astype(BF16)


def on_device(
    features, column_table, dw_kernel, norm_gain, expand_weight, reduce_weight, layer_scale
):
    rows, cols, channels = features.shape
    hid = expand_weight.shape[1]
    count = lax.axis_size("col")
    bits = count.bit_length() - 1
    line = 1 << ((bits + 1) // 2)
    inner = count // line
    inner_bits = inner.bit_length() - 1
    me = lax.axis_index("col")
    my_line, my_inner = me // inner, me % inner
    units, own = hid // line, channels // line
    total_cols = cols * count

    def swapped(block, mask):
        return lax.ppermute(block, "col", [(d, d ^ mask) for d in range(count)])

    def line_sum(small):
        sums = [small] + [swapped(small, p * inner) for p in range(1, line)]
        sums = [part.astype(F32) for part in sums]
        while len(sums) > 1:
            sums = [low + high for low, high in zip(sums[::2], sums[1::2])]
        return sums[0]

    mirror = lax.ppermute(column_table, "col", [(d, count - 1 - d) for d in range(count)])

    features_f = features.astype(F32)
    table_f = column_table.astype(F32)
    gain = norm_gain[None]
    inside, across, turned = edges(features_f, table_f, mirror)
    inside = swapped(inside, 1)
    pairs = [(d, d + 1) for d in range(1, count - 1, 2)]
    across = lax.ppermute(across, "col", pairs + [(high, low) for low, high in pairs])
    normed, nhat, inv, wide = conv_norm(
        features_f, table_f, turned, inside, across, dw_kernel.astype(F32), gain
    )
    fast = line == 4 and inner == 4 and units % LANES == 0 and own % 64 == 0
    if fast:
        flat = normed.reshape(-1, channels)
        normed_2, normed_1 = swapped(flat, 2 * inner), swapped(flat, inner)
    else:
        others = [swapped(normed, p * inner) for p in range(1, line)]
    slope, hidden, disagreement, dbranch, gscale = forward(
        1.0 / math.sqrt(rows * total_cols),
        normed.reshape(-1, channels),
        expand_weight,
        reduce_weight,
        wide,
        layer_scale,
        features.shape,
    )
    dnormed, dpre_0 = backward(dbranch, slope, expand_weight, reduce_weight)
    if fast:
        dbranch_2, dbranch_1 = swapped(dbranch, 2 * inner), swapped(dbranch, inner)
        small = small_grads(dnormed, nhat, inv, gain, gscale, wide, dbranch_1, dbranch_2)
    else:
        small = small_grads(dnormed, nhat, inv, gain, gscale, wide)
    if fast:
        normed_3 = swapped(gate(normed_2, dnormed, normed_1), inner)
        dbranch_3 = swapped(dbranch, 3 * inner)
        more = swapped(small, 2)
        turned, dpre, part = near(
            [flat, normed_1, normed_2],
            [dbranch, dbranch_1, dbranch_2],
            hidden,
            expand_weight,
            reduce_weight,
            line,
        )
        keep_r, send_r, small = far_reduce(
            normed_3, dbranch_3, expand_weight, part, small, more, inner
        )
        got_r, more = swapped(send_r, 1), swapped(small, 1)
        turned_3, dpre_3 = far_expand(normed_3, dbranch_3, expand_weight, reduce_weight, small)
        keep_r, send_r, small = merge(keep_r, got_r, small, more)
        got_r, more = swapped(send_r, 2), swapped(small, inner)
        keep_e, send_e = expand_grad(
            turned, turned_3, dpre_0, dpre, dpre_3, small, own, inner
        )
        keep_e, send_e, small = merge(keep_e, swapped(send_e, 1), small, more)
        got_e, more = swapped(send_e, 2), swapped(small, 2 * inner)
        sums = finish(keep_e, got_e, keep_r, got_r, small, more)
        return (disagreement, *sums)

    dbranch_all = [dbranch] + [swapped(dbranch, p * inner) for p in range(1, line)]
    (keep_e, send_e), (keep_r, send_r) = grads_plain(
        jnp.stack([normed] + others),
        jnp.concatenate(dbranch_all),
        expand_weight,
        reduce_weight,
        my_line,
        my_inner,
        line,
        inner,
    )
    small = line_sum(small)
    for bit in range(inner_bits):
        sum_r = keep_r + swapped(send_r, 1 << bit).astype(F32)
        sum_e = keep_e + swapped(send_e, 1 << bit).astype(F32)
        small = small.astype(BF16)
        small = small.astype(F32) + swapped(small, 1 << bit).astype(F32)
        if bit < inner_bits - 1:
            side = (my_inner >> (bit + 1)) & 1
            keep_r, send_r = halves(sum_r, side)
            keep_e, send_e = halves(sum_e, side)
    grad_kernel = small[:49].reshape(7, 7, channels)
    return (
        disagreement,
        sum_e.reshape(own // inner, hid),
        sum_r.reshape(units // inner, channels),
        grad_kernel,
        small[49],
        small[50],
    )


def solution(mesh):
    in_specs = (P("groups", "col", None), P("col", None), P(), P(), P(), P(), P())
    out_specs = (
        P("groups", "col", None),
        P(("groups", "col"), None),
        P(("groups", "col"), None),
        P("groups", None, None),
        P("groups"),
        P("groups"),
    )
    return jax.shard_map(
        on_device, mesh=mesh, in_specs=in_specs, out_specs=out_specs, check_vma=False
    )
```

```python
import functools
import math

import jax
import jax.numpy as jnp
from jax import lax
from jax.experimental import pallas as pl
from jax.experimental.pallas import tpu as pltpu
from jax.sharding import PartitionSpec as P

BF16 = jnp.bfloat16
F32 = jnp.float32
LANES = 128
VMEM_GRANT = 16 << 20
BLOCK = 256


def phi_parts(pre):
    decay = jnp.exp(-0.5 * pre * pre)
    t = 1.0 / (1.0 + 0.23164189 * jnp.abs(pre))
    poly = 0.5307027145 * t - 0.7265760135
    poly = poly * t + 0.7107068705
    poly = poly * t - 0.142248368
    poly = poly * t + 0.127414796
    tail = poly * t * decay
    return jnp.where(pre < 0.0, tail, 1.0 - tail), decay * 0.3989422804014327


def call(body, name, flops, out_shape, scratch, *operands, read=10**8):
    return pl.pallas_call(
        body,
        in_specs=[pl.BlockSpec(memory_space=pltpu.VMEM) for _ in operands],
        out_specs=[pl.BlockSpec(memory_space=pltpu.VMEM) for _ in out_shape],
        out_shape=[jax.ShapeDtypeStruct(shape, dtype) for shape, dtype in out_shape],
        scratch_shapes=[pltpu.VMEM(shape, dtype) for shape, dtype in scratch],
        compiler_params=pltpu.CompilerParams(vmem_limit_bytes=VMEM_GRANT),
        cost_estimate=pl.CostEstimate(flops=flops, bytes_accessed=read, transcendentals=0),
        name=name,
    )(*operands)


def position(inner):
    me = lax.axis_index("col")
    return me // inner, me & 1, (me >> 1) & 1


def dot(lhs, rhs, contract):
    return lax.dot_general(lhs, rhs, (contract, ((), ())), preferred_element_type=F32)


def flipped(value):
    rows = value.shape[0]
    return jnp.concatenate([value[r : r + 1] for r in reversed(range(rows))], axis=0)


def edges_body(feat, table, mirror, inside, across, turned):
    _, cols, channels = feat.shape
    other = flipped(mirror[...].astype(F32))
    odd = (lax.axis_index("col") & 1) == 1
    for v, add in enumerate((table[...], other)):
        own = (feat[...] + add[None]).astype(BF16).astype(F32)
        first, last = own[:, :3], own[:, cols - 3 :]
        inside[v] = jnp.where(odd, first, last).astype(BF16)
        across[v] = jnp.where(odd, last, first).astype(BF16)
    turned[...] = other


def edges(features, table, mirror):
    rows, cols, channels = features.shape
    return call(
        edges_body,
        "edges",
        10**8,
        [
            ((2, rows, 3, channels), BF16),
            ((2, rows, 3, channels), BF16),
            ((cols, channels), F32),
        ],
        [],
        features,
        table,
        mirror,
    )


def conv_body(feat, table, turned, inside, across, dw, gain, normed, nhat, inv, wide, conv):
    rows, cols, channels = feat.shape
    odd = (lax.axis_index("col") & 1) == 1
    for v, add in enumerate((table[...], turned[...])):
        wide[v, :, 3 : 3 + cols, :] = (feat[...] + add[None]).astype(BF16).astype(F32)
        one, two = inside[v].astype(F32), across[v].astype(F32)
        wide[v, :, 0:3, :] = jnp.where(odd, one, two)
        wide[v, :, 3 + cols : 6 + cols, :] = jnp.where(odd, two, one)

    def tile(c, carry):
        lanes = pl.ds(pl.multiple_of(c * LANES, LANES), LANES)
        sums = [[jnp.zeros((cols, LANES), F32) for _ in range(rows)] for _ in range(2)]
        for j in range(7):
            for v in range(2):
                part = [wide[v, r, pl.ds(j, cols), lanes] for r in range(rows)]
                for i in range(7):
                    weight = dw[i, pl.ds(6 - j if v else j, 1), lanes]
                    for r in range(rows):
                        if 0 <= r + i - 3 < rows:
                            sums[v][r] = sums[v][r] + weight * part[r + i - 3]
        for v in range(2):
            for r in range(rows):
                conv[v, r, :, lanes] = sums[v][r]
        return carry

    lax.fori_loop(0, channels // LANES, tile, 0)
    for v in range(2):
        value = conv[v].reshape(rows * cols, channels)
        centred = value - jnp.mean(value, axis=-1, keepdims=True)
        inverse = lax.rsqrt(jnp.mean(centred * centred, axis=-1, keepdims=True) + 1e-06)
        value = centred * inverse
        nhat[v] = value
        inv[v] = jnp.broadcast_to(inverse, (rows * cols, LANES))
        normed[v] = (value * gain[...]).astype(BF16)


def conv_norm(features, table, turned, inside, across, dw, gain):
    rows, cols, channels = features.shape
    pixels = rows * cols
    return call(
        conv_body,
        "conv_norm",
        4 * 10**9,
        [
            ((2, pixels, channels), BF16),
            ((2, pixels, channels), F32),
            ((2, pixels, LANES), F32),
            ((2, rows, 16, channels), F32),
        ],
        [((2, rows, cols, channels), F32)],
        features,
        table,
        turned,
        inside,
        across,
        dw,
        gain,
    )


def blocks(total):
    return [slice(at, at + BLOCK) for at in range(0, total, BLOCK)]


def forward_body(
    scale, normed, expand, reduce, wide, ls, slope, hidden, disagreement, dbranch, gscale
):
    pixels, channels = normed.shape
    half = pixels // 2
    rows, cols, _ = disagreement.shape
    for here in blocks(expand.shape[1]):
        pre = dot(normed[...], expand[:, here], ((1,), (0,)))
        cdf, density = phi_parts(pre)
        slope[:, here] = (cdf + pre * density).astype(BF16)
        hidden[:, here] = (pre * cdf).astype(BF16)
    branch = dot(hidden[...], reduce[...], ((1,), (0,)))
    factor = ls[...].reshape(1, channels)
    outs = []
    for v in range(2):
        own = wide[v, :, 3 : 3 + cols, :].reshape(half, channels)
        outs.append((own + factor * branch[v * half : (v + 1) * half]).astype(BF16).astype(F32))
    difference = outs[0] - outs[1]
    disagreement[...] = difference.astype(BF16).reshape(rows, cols, channels)
    residual = (difference * scale).astype(BF16).astype(F32)
    gscale[...] = jnp.sum((branch[:half] - branch[half:]) * residual, axis=0, keepdims=True)
    dbranch[...] = (factor * residual).astype(BF16)


def forward(scale, normed, expand, reduce, wide, ls, shape):
    pixels, channels = normed.shape
    hid = expand.shape[1]
    return call(
        functools.partial(forward_body, scale),
        "forward",
        10**9,
        [
            ((pixels, hid), BF16),
            ((pixels, hid), BF16),
            (shape, BF16),
            ((pixels // 2, channels), BF16),
            ((1, channels), F32),
        ],
        [],
        normed,
        expand,
        reduce,
        wide,
        ls,
        read=10**6,
    )


def backward_body(dbranch, slope, expand, reduce, dnormed, dpre):
    half = dbranch.shape[0]
    for here in blocks(expand.shape[1]):
        dhidden = dot(dbranch[...], reduce[here, :], ((1,), (1,)))
        dpre[:, here] = dpre_of(dhidden, slope[:, here].astype(F32))
    dnormed[...] = dot(dpre[...], expand[...], ((1,), (1,)))


def backward(dbranch, slope, expand, reduce):
    half, channels = dbranch.shape
    hid = expand.shape[1]
    return call(
        backward_body,
        "backward",
        10**9,
        [((2 * half, channels), F32), ((2 * half, hid), BF16)],
        [],
        dbranch,
        slope,
        expand,
        reduce,
        read=10**6,
    )


def small_body(dnormed, nhat, inv, gain, gscale, wide, *rest):
    out, grad, taps, small = rest[-4:]
    half, channels = dnormed.shape[0] // 2, dnormed.shape[1]
    _, rows, _, _ = wide.shape
    cols = half // rows
    factor = gain[...]
    ggain = jnp.zeros((1, channels), F32)
    for v in range(2):
        here = slice(v * half, (v + 1) * half)
        value = dnormed[here, :]
        ggain = ggain + jnp.sum(value * nhat[v], axis=0, keepdims=True)
        scaled = value * factor
        gm = jnp.mean(scaled, axis=-1, keepdims=True)
        gn = jnp.mean(scaled * nhat[v], axis=-1, keepdims=True)
        grad[here, :] = inv[v][:, :1] * (scaled - gm - nhat[v] * gn)

    def tile(c, carry):
        lanes = pl.ds(pl.multiple_of(c * LANES, LANES), LANES)
        dconv = [
            [grad[pl.ds(v * half + r * cols, cols), lanes] for r in range(rows)] for v in range(2)
        ]
        for j in range(7):
            part = [
                [wide[v, r, pl.ds(6 - j if v else j, cols), lanes] for r in range(rows)]
                for v in range(2)
            ]
            for i in range(7):
                sums = []
                for v in range(2):
                    total = None
                    for r in range(rows):
                        if 0 <= r + i - 3 < rows:
                            term = part[v][r + i - 3] * dconv[v][r]
                            total = term if total is None else total + term
                    sums.append(total)
                at = 8 * (7 * i + j)
                taps[at : at + 8, :] = sums[0] + sums[1]
        rolled = taps[pl.ds(0, 49, stride=8), :]
        for s in range(1, 8):
            rolled = rolled + taps[pl.ds(s, 49, stride=8), :]
        small[:49, lanes] = rolled
        return carry

    small[...] = jnp.zeros(small.shape, F32)
    lax.fori_loop(0, channels // LANES, tile, 0)
    small[49:50, :] = ggain
    small[50:51, :] = gscale[...]
    out[...] = small[...].astype(BF16)


def small_grads(dnormed, nhat, inv, gain, gscale, wide, *after):
    channels = dnormed.shape[1]
    return call(
        small_body,
        "small_grads",
        10**6,
        [((64, channels), BF16)],
        [(dnormed.shape, F32), ((8 * 49, LANES), F32), ((64, channels), F32)],
        dnormed,
        nhat,
        inv,
        gain,
        gscale,
        wide,
        *after,
        read=10**5,
    )[0]


def gate_body(block, *rest):
    rest[-1][...] = block[...]


def gate(block, *after):
    shapes = [(block.shape, block.dtype)]
    return call(gate_body, "gate", 10**6, shapes, [], block, *after, read=10**5)[0]


def split(total, side, keep, send):
    parts, rows, _ = keep.shape
    for x in range(parts):
        mine = pl.multiple_of((2 * x + side) * rows, 16)
        theirs = pl.multiple_of((2 * x + 1 - side) * rows, 16)
        keep[x] = total[pl.ds(mine, rows), :]
        send[x] = total[pl.ds(theirs, rows), :].astype(BF16)


def added(small, more):
    return (small[...].astype(F32) + more[...].astype(F32)).astype(BF16)


def slope_and_act(normed, expand):
    pre = dot(normed, expand, ((1,), (0,)))
    cdf, density = phi_parts(pre)
    return cdf + pre * density, (pre * cdf).astype(BF16)


def views_apart(act):
    half = act.shape[0] // 2
    return (act[:half].astype(F32) - act[half:].astype(F32)).astype(BF16)


def dpre_of(dhidden, slope):
    half = dhidden.shape[0]
    return jnp.concatenate([dhidden * slope[:half], -dhidden * slope[half:]]).astype(BF16)


def own_lanes(own, width):
    first = position(4)[0] * own
    start = first // LANES * LANES
    return pl.ds(pl.multiple_of(start, LANES), width), first - start


def near_body(
    n_0, n_1, n_2, d_0, d_1, d_2, hidden_0, expand, reduce, turned, dpre, total, hidden
):
    half, channels = d_0.shape
    units = total.shape[0]
    lanes, _ = own_lanes(channels // 4, turned.shape[0])
    for p, ref in enumerate((n_0, n_1, n_2)):
        at = 2 * p * half
        turned[:, at : at + 2 * half] = ref[:, lanes].astype(F32).T.astype(BF16)
    others = jnp.concatenate([d_1[...], d_2[...]])
    both = jnp.concatenate([n_1[...], n_2[...]])
    for here in blocks(reduce.shape[0]):
        slope, act = slope_and_act(both, expand[:, here])
        hidden[:, here] = act
        dhidden = dot(others, reduce[here, :], ((1,), (1,)))
        dpre[: 2 * half, here] = dpre_of(dhidden[:half], slope[: 2 * half])
        dpre[2 * half :, here] = dpre_of(dhidden[half:], slope[2 * half :])
    lanes = pl.ds(pl.multiple_of(position(4)[0] * units, LANES), units)
    every = jnp.concatenate([d_0[...], others])
    acts = (hidden_0[:, lanes], hidden[: 2 * half, lanes], hidden[2 * half :, lanes])
    total[...] = dot(jnp.concatenate([views_apart(act) for act in acts]), every, ((0,), (0,)))


def near(normed, dbranch, hidden, expand, reduce, line):
    half, channels = dbranch[0].shape
    hid = expand.shape[1]
    return call(
        near_body,
        "near",
        10**6,
        [
            ((2 * LANES, 6 * half), BF16),
            ((4 * half, hid), BF16),
            ((hid // line, channels), F32),
        ],
        [((4 * half, hid), BF16)],
        *normed,
        *dbranch,
        hidden,
        expand,
        reduce,
        read=10**5,
    )


def far_reduce_body(n_3, d_3, expand, part, small, more, keep, send, sums, total):
    units = total.shape[0]
    line, core, _ = position(4)
    lanes = pl.ds(pl.multiple_of(line * units, LANES), units)
    _, act = slope_and_act(n_3[...], expand[:, lanes])
    total[...] = part[...] + dot(views_apart(act), d_3[...], ((0,), (0,)))
    split(total, core, keep, send)
    sums[...] = added(small, more)


def far_reduce(n_3, d_3, expand, part, small, more, inner):
    units, channels = part.shape
    shape = (inner // 2, units // inner, channels)
    return call(
        far_reduce_body,
        "far_reduce",
        10**6,
        [(shape, F32), (shape, BF16), (small.shape, BF16)],
        [((units, channels), F32)],
        n_3,
        d_3,
        expand,
        part,
        small,
        more,
        read=10**5,
    )


def far_expand_body(n_3, d_3, expand, reduce, after, turned, dpre):
    lanes, _ = own_lanes(n_3.shape[1] // 4, turned.shape[0])
    turned[...] = n_3[:, lanes].astype(F32).T.astype(BF16)
    for here in blocks(reduce.shape[0]):
        slope, _ = slope_and_act(n_3[...], expand[:, here])
        dpre[:, here] = dpre_of(dot(d_3[...], reduce[here, :], ((1,), (1,))), slope)


def far_expand(n_3, d_3, expand, reduce, after):
    rows = n_3.shape[0]
    hid = expand.shape[1]
    return call(
        far_expand_body,
        "far_expand",
        10**9,
        [((2 * LANES, rows), BF16), ((rows, hid), BF16)],
        [],
        n_3,
        d_3,
        expand,
        reduce,
        after,
        read=10**6,
    )


def expand_grad_body(turned, turned_3, dpre_0, dpre, dpre_3, after, keep, send, total):
    own, hid = total.shape
    _, core, _ = position(4)
    _, first = own_lanes(own, turned.shape[0])
    rows = pl.ds(pl.multiple_of(first, 16), own)
    lhs = jnp.concatenate([turned[rows, :], turned_3[rows, :]], axis=1)
    for here in blocks(hid):
        every = jnp.concatenate([dpre_0[:, here], dpre[:, here], dpre_3[:, here]])
        total[:, here] = dot(lhs, every, ((1,), (0,)))
    split(total, core, keep, send)


def expand_grad(turned, turned_3, dpre_0, dpre, dpre_3, after, own, inner):
    hid = dpre.shape[1]
    shape = (inner // 2, own // inner, hid)
    return call(
        expand_grad_body,
        "expand_grad",
        10**6,
        [(shape, F32), (shape, BF16)],
        [((own, hid), F32)],
        turned,
        turned_3,
        dpre_0,
        dpre,
        dpre_3,
        after,
        read=10**5,
    )


def merge_body(kept, got, keep, send):
    _, _, mine = position(4)
    theirs = 1 - mine
    keep[...] = kept[mine] + got[mine].astype(F32)
    send[...] = (kept[theirs] + got[theirs].astype(F32)).astype(BF16)


def merge_small_body(kept, got, small, more, keep, send, sums):
    merge_body(kept, got, keep, send)
    sums[...] = added(small, more)


def merge(kept, got, *small):
    shape = kept.shape[1:]
    return call(
        merge_small_body if small else merge_body,
        "merge",
        10**6,
        [(shape, F32), (shape, BF16)] + [(part.shape, BF16) for part in small[:1]],
        [],
        kept,
        got,
        *small,
        read=10**5,
    )


def finish_reduce_body(keep, got, small, more, out, kernel, gain, scale):
    out[...] = keep[...] + got[...].astype(F32)
    sums = small[...].astype(F32) + more[...].astype(F32)
    for i in range(7):
        kernel[i] = sums[7 * i : 7 * i + 7]
    gain[...] = sums[49:50].reshape(gain.shape)
    scale[...] = sums[50:51].reshape(scale.shape)


def finish_reduce(keep, got, small, more):
    channels = small.shape[1]
    return call(
        finish_reduce_body,
        "finish_reduce",
        10**9,
        [
            (keep.shape, F32),
            ((7, 7, channels), F32),
            ((channels,), F32),
            ((channels,), F32),
        ],
        [],
        keep,
        got,
        small,
        more,
        read=10**6,
    )


def finish_expand_body(keep, got, after, out):
    out[...] = keep[...] + got[...].astype(F32)


def finish_expand(keep, got, after):
    return call(
        finish_expand_body, "finish_expand", 10**6, [(keep.shape, F32)], [], keep, got, after, read=10**5
    )[0]


def grads_plain(every, dbranch_all, expand_weight, reduce_weight, my_line, my_inner, line, inner):
    channels, hid = expand_weight.shape
    units, own = hid // line, channels // line
    every = every.reshape(-1, channels)
    pre = dot(every, expand_weight, ((1,), (0,)))
    cdf, density = phi_parts(pre)
    slope = (cdf + pre * density).reshape(line, 2, -1, hid)
    hidden = (pre * cdf).astype(BF16).astype(F32).reshape(line, 2, -1, hid)
    diff = (hidden[:, 0] - hidden[:, 1]).astype(BF16).reshape(-1, hid)
    diff = lax.dynamic_slice_in_dim(diff, my_line * units, units, 1)
    dhidden = dot(dbranch_all, reduce_weight, ((1,), (1,))).reshape(line, -1, hid)
    dpre = jnp.stack([dhidden * slope[:, 0], -dhidden * slope[:, 1]], axis=1)
    dpre = dpre.astype(BF16).reshape(-1, hid)
    normed_own = lax.dynamic_slice_in_dim(every, my_line * own, own, 1)
    expand = dot(normed_own, dpre, ((0,), (0,))).reshape(inner, own // inner, hid)
    reduce = dot(diff, dbranch_all, ((0,), (0,))).reshape(inner, units // inner, channels)
    return halves(expand, my_inner & 1), halves(reduce, my_inner & 1)


def halves(part, side):
    part = part.reshape((part.shape[0] // 2, 2) + part.shape[1:])
    keep = lax.dynamic_index_in_dim(part, side, 1, keepdims=False)
    send = lax.dynamic_index_in_dim(part, 1 - side, 1, keepdims=False)
    return keep, send.astype(BF16)


def on_device(
    features, column_table, dw_kernel, norm_gain, expand_weight, reduce_weight, layer_scale
):
    rows, cols, channels = features.shape
    hid = expand_weight.shape[1]
    count = lax.axis_size("col")
    bits = count.bit_length() - 1
    line = 1 << ((bits + 1) // 2)
    inner = count // line
    inner_bits = inner.bit_length() - 1
    me = lax.axis_index("col")
    my_line, my_inner = me // inner, me % inner
    units, own = hid // line, channels // line
    total_cols = cols * count

    def swapped(block, mask):
        return lax.ppermute(block, "col", [(d, d ^ mask) for d in range(count)])

    def line_sum(small):
        sums = [small] + [swapped(small, p * inner) for p in range(1, line)]
        sums = [part.astype(F32) for part in sums]
        while len(sums) > 1:
            sums = [low + high for low, high in zip(sums[::2], sums[1::2])]
        return sums[0]

    mirror = lax.ppermute(column_table, "col", [(d, count - 1 - d) for d in range(count)])

    features_f = features.astype(F32)
    table_f = column_table.astype(F32)
    gain = norm_gain[None]
    inside, across, turned = edges(features_f, table_f, mirror)
    inside = swapped(inside, 1)
    pairs = [(d, d + 1) for d in range(1, count - 1, 2)]
    across = lax.ppermute(across, "col", pairs + [(high, low) for low, high in pairs])
    normed, nhat, inv, wide = conv_norm(
        features_f, table_f, turned, inside, across, dw_kernel.astype(F32), gain
    )
    fast = line == 4 and inner == 4 and units % LANES == 0 and own % 64 == 0
    if fast:
        flat = normed.reshape(-1, channels)
        normed_2, normed_1 = swapped(flat, 2 * inner), swapped(flat, inner)
    else:
        others = [swapped(normed, p * inner) for p in range(1, line)]
    slope, hidden, disagreement, dbranch, gscale = forward(
        1.0 / math.sqrt(rows * total_cols),
        normed.reshape(-1, channels),
        expand_weight,
        reduce_weight,
        wide,
        layer_scale,
        features.shape,
    )
    dnormed, dpre_0 = backward(dbranch, slope, expand_weight, reduce_weight)
    small = small_grads(dnormed, nhat, inv, gain, gscale, wide)
    if fast:
        dbranch_2, dbranch_1 = swapped(dbranch, 2 * inner), swapped(dbranch, inner)
        normed_3 = swapped(gate(normed_2, dnormed, normed_1), inner)
        dbranch_3 = swapped(gate(dbranch_2, small, dbranch_1), inner)
        more = swapped(small, 2)
        turned, dpre, part = near(
            [flat, normed_1, normed_2],
            [dbranch, dbranch_1, dbranch_2],
            hidden,
            expand_weight,
            reduce_weight,
            line,
        )
        keep_r, send_r, small = far_reduce(
            normed_3, dbranch_3, expand_weight, part, small, more, inner
        )
        got_r, more = swapped(send_r, 1), swapped(small, 1)
        turned_3, dpre_3 = far_expand(normed_3, dbranch_3, expand_weight, reduce_weight, small)
        keep_r, send_r, small = merge(keep_r, got_r, small, more)
        got_r, more = swapped(send_r, 2), swapped(small, inner)
        keep_e, send_e = expand_grad(
            turned, turned_3, dpre_0, dpre, dpre_3, small, own, inner
        )
        small = (small.astype(F32) + more.astype(F32)).astype(BF16)
        more = swapped(small, 2 * inner)
        keep_e, send_e = merge(keep_e, swapped(send_e, 1))
        got_e = swapped(send_e, 2)
        sum_r, *sums = finish_reduce(keep_r, got_r, small, more)
        sum_e = finish_expand(keep_e, got_e, sums[-1])
        return (disagreement, sum_e, sum_r, *sums)

    dbranch_all = [dbranch] + [swapped(dbranch, p * inner) for p in range(1, line)]
    (keep_e, send_e), (keep_r, send_r) = grads_plain(
        jnp.stack([normed] + others),
        jnp.concatenate(dbranch_all),
        expand_weight,
        reduce_weight,
        my_line,
        my_inner,
        line,
        inner,
    )
    small = line_sum(small)
    for bit in range(inner_bits):
        sum_r = keep_r + swapped(send_r, 1 << bit).astype(F32)
        sum_e = keep_e + swapped(send_e, 1 << bit).astype(F32)
        small = small.astype(BF16)
        small = small.astype(F32) + swapped(small, 1 << bit).astype(F32)
        if bit < inner_bits - 1:
            side = (my_inner >> (bit + 1)) & 1
            keep_r, send_r = halves(sum_r, side)
            keep_e, send_e = halves(sum_e, side)
    grad_kernel = small[:49].reshape(7, 7, channels)
    return (
        disagreement,
        sum_e.reshape(own // inner, hid),
        sum_r.reshape(units // inner, channels),
        grad_kernel,
        small[49],
        small[50],
    )


def solution(mesh):
    in_specs = (P("groups", "col", None), P("col", None), P(), P(), P(), P(), P())
    out_specs = (
        P("groups", "col", None),
        P(("groups", "col"), None),
        P(("groups", "col"), None),
        P("groups", None, None),
        P("groups"),
        P("groups"),
    )
    return jax.shard_map(
        on_device, mesh=mesh, in_specs=in_specs, out_specs=out_specs, check_vma=False
    )
```

```python
import functools
import math

import jax
import jax.numpy as jnp
from jax import lax
from jax.experimental import pallas as pl
from jax.experimental.pallas import tpu as pltpu
from jax.sharding import PartitionSpec as P

BF16 = jnp.bfloat16
F32 = jnp.float32
LANES = 128
VMEM_GRANT = 16 << 20
BLOCK = 256


def phi_parts(pre):
    decay = jnp.exp(-0.5 * pre * pre)
    t = 1.0 / (1.0 + 0.23164189 * jnp.abs(pre))
    poly = 0.5307027145 * t - 0.7265760135
    poly = poly * t + 0.7107068705
    poly = poly * t - 0.142248368
    poly = poly * t + 0.127414796
    tail = poly * t * decay
    return jnp.where(pre < 0.0, tail, 1.0 - tail), decay * 0.3989422804014327


def call(body, name, flops, out_shape, scratch, *operands, read=10**8):
    return pl.pallas_call(
        body,
        in_specs=[pl.BlockSpec(memory_space=pltpu.VMEM) for _ in operands],
        out_specs=[pl.BlockSpec(memory_space=pltpu.VMEM) for _ in out_shape],
        out_shape=[jax.ShapeDtypeStruct(shape, dtype) for shape, dtype in out_shape],
        scratch_shapes=[pltpu.VMEM(shape, dtype) for shape, dtype in scratch],
        compiler_params=pltpu.CompilerParams(vmem_limit_bytes=VMEM_GRANT),
        cost_estimate=pl.CostEstimate(flops=flops, bytes_accessed=read, transcendentals=0),
        name=name,
    )(*operands)


def position(inner):
    me = lax.axis_index("col")
    return me // inner, me & 1, (me >> 1) & 1


def dot(lhs, rhs, contract):
    return lax.dot_general(lhs, rhs, (contract, ((), ())), preferred_element_type=F32)


def flipped(value):
    rows = value.shape[0]
    return jnp.concatenate([value[r : r + 1] for r in reversed(range(rows))], axis=0)


def edges_body(feat, table, mirror, inside, across, turned):
    _, cols, channels = feat.shape
    other = flipped(mirror[...].astype(F32))
    odd = (lax.axis_index("col") & 1) == 1
    for v, add in enumerate((table[...], other)):
        own = (feat[...] + add[None]).astype(BF16).astype(F32)
        first, last = own[:, :3], own[:, cols - 3 :]
        inside[v] = jnp.where(odd, first, last).astype(BF16)
        across[v] = jnp.where(odd, last, first).astype(BF16)
    turned[...] = other


def edges(features, table, mirror):
    rows, cols, channels = features.shape
    return call(
        edges_body,
        "edges",
        10**8,
        [
            ((2, rows, 3, channels), BF16),
            ((2, rows, 3, channels), BF16),
            ((cols, channels), F32),
        ],
        [],
        features,
        table,
        mirror,
    )


def conv_body(feat, table, turned, inside, across, dw, gain, normed, nhat, inv, wide, conv):
    rows, cols, channels = feat.shape
    odd = (lax.axis_index("col") & 1) == 1
    for v, add in enumerate((table[...], turned[...])):
        wide[v, :, 3 : 3 + cols, :] = (feat[...] + add[None]).astype(BF16).astype(F32)
        one, two = inside[v].astype(F32), across[v].astype(F32)
        wide[v, :, 0:3, :] = jnp.where(odd, one, two)
        wide[v, :, 3 + cols : 6 + cols, :] = jnp.where(odd, two, one)

    def tile(c, carry):
        lanes = pl.ds(pl.multiple_of(c * LANES, LANES), LANES)
        sums = [[jnp.zeros((cols, LANES), F32) for _ in range(rows)] for _ in range(2)]
        for j in range(7):
            for v in range(2):
                part = [wide[v, r, pl.ds(j, cols), lanes] for r in range(rows)]
                for i in range(7):
                    weight = dw[i, pl.ds(6 - j if v else j, 1), lanes]
                    for r in range(rows):
                        if 0 <= r + i - 3 < rows:
                            sums[v][r] = sums[v][r] + weight * part[r + i - 3]
        for v in range(2):
            for r in range(rows):
                conv[v, r, :, lanes] = sums[v][r]
        return carry

    lax.fori_loop(0, channels // LANES, tile, 0)
    for v in range(2):
        value = conv[v].reshape(rows * cols, channels)
        centred = value - jnp.mean(value, axis=-1, keepdims=True)
        inverse = lax.rsqrt(jnp.mean(centred * centred, axis=-1, keepdims=True) + 1e-06)
        value = centred * inverse
        nhat[v] = value
        inv[v] = jnp.broadcast_to(inverse, (rows * cols, LANES))
        normed[v] = (value * gain[...]).astype(BF16)


def conv_norm(features, table, turned, inside, across, dw, gain):
    rows, cols, channels = features.shape
    pixels = rows * cols
    return call(
        conv_body,
        "conv_norm",
        4 * 10**9,
        [
            ((2, pixels, channels), BF16),
            ((2, pixels, channels), F32),
            ((2, pixels, LANES), F32),
            ((2, rows, 16, channels), F32),
        ],
        [((2, rows, cols, channels), F32)],
        features,
        table,
        turned,
        inside,
        across,
        dw,
        gain,
    )


def blocks(total):
    return [slice(at, at + BLOCK) for at in range(0, total, BLOCK)]


def forward_body(
    scale, normed, expand, reduce, wide, ls, slope, hidden, disagreement, dbranch, gscale
):
    pixels, channels = normed.shape
    half = pixels // 2
    rows, cols, _ = disagreement.shape
    for here in blocks(expand.shape[1]):
        pre = dot(normed[...], expand[:, here], ((1,), (0,)))
        cdf, density = phi_parts(pre)
        slope[:, here] = (cdf + pre * density).astype(BF16)
        hidden[:, here] = (pre * cdf).astype(BF16)
    branch = dot(hidden[...], reduce[...], ((1,), (0,)))
    factor = ls[...].reshape(1, channels)
    outs = []
    for v in range(2):
        own = wide[v, :, 3 : 3 + cols, :].reshape(half, channels)
        outs.append((own + factor * branch[v * half : (v + 1) * half]).astype(BF16).astype(F32))
    difference = outs[0] - outs[1]
    disagreement[...] = difference.astype(BF16).reshape(rows, cols, channels)
    residual = (difference * scale).astype(BF16).astype(F32)
    gscale[...] = jnp.sum((branch[:half] - branch[half:]) * residual, axis=0, keepdims=True)
    dbranch[...] = (factor * residual).astype(BF16)


def forward(scale, normed, expand, reduce, wide, ls, shape):
    pixels, channels = normed.shape
    hid = expand.shape[1]
    return call(
        functools.partial(forward_body, scale),
        "forward",
        10**9,
        [
            ((pixels, hid), BF16),
            ((pixels, hid), BF16),
            (shape, BF16),
            ((pixels // 2, channels), BF16),
            ((1, channels), F32),
        ],
        [],
        normed,
        expand,
        reduce,
        wide,
        ls,
        read=10**6,
    )


def backward_body(dbranch, slope, expand, reduce, dnormed, dpre):
    half = dbranch.shape[0]
    for here in blocks(expand.shape[1]):
        dhidden = dot(dbranch[...], reduce[here, :], ((1,), (1,)))
        dpre[:, here] = dpre_of(dhidden, slope[:, here].astype(F32))
    dnormed[...] = dot(dpre[...], expand[...], ((1,), (1,)))


def backward(dbranch, slope, expand, reduce):
    half, channels = dbranch.shape
    hid = expand.shape[1]
    return call(
        backward_body,
        "backward",
        10**9,
        [((2 * half, channels), F32), ((2 * half, hid), BF16)],
        [],
        dbranch,
        slope,
        expand,
        reduce,
        read=10**6,
    )


def small_body(dnormed, nhat, inv, gain, gscale, wide, *rest):
    out, grad, taps, small = rest[-4:]
    half, channels = dnormed.shape[0] // 2, dnormed.shape[1]
    _, rows, _, _ = wide.shape
    cols = half // rows
    factor = gain[...]
    ggain = jnp.zeros((1, channels), F32)
    for v in range(2):
        here = slice(v * half, (v + 1) * half)
        value = dnormed[here, :]
        ggain = ggain + jnp.sum(value * nhat[v], axis=0, keepdims=True)
        scaled = value * factor
        gm = jnp.mean(scaled, axis=-1, keepdims=True)
        gn = jnp.mean(scaled * nhat[v], axis=-1, keepdims=True)
        grad[here, :] = inv[v][:, :1] * (scaled - gm - nhat[v] * gn)

    def tile(c, carry):
        lanes = pl.ds(pl.multiple_of(c * LANES, LANES), LANES)
        dconv = [
            [grad[pl.ds(v * half + r * cols, cols), lanes] for r in range(rows)] for v in range(2)
        ]
        for j in range(7):
            part = [
                [wide[v, r, pl.ds(6 - j if v else j, cols), lanes] for r in range(rows)]
                for v in range(2)
            ]
            for i in range(7):
                sums = []
                for v in range(2):
                    total = None
                    for r in range(rows):
                        if 0 <= r + i - 3 < rows:
                            term = part[v][r + i - 3] * dconv[v][r]
                            total = term if total is None else total + term
                    sums.append(total)
                at = 8 * (7 * i + j)
                taps[at : at + 8, :] = sums[0] + sums[1]
        rolled = taps[pl.ds(0, 49, stride=8), :]
        for s in range(1, 8):
            rolled = rolled + taps[pl.ds(s, 49, stride=8), :]
        small[:49, lanes] = rolled
        return carry

    small[...] = jnp.zeros(small.shape, F32)
    lax.fori_loop(0, channels // LANES, tile, 0)
    small[49:50, :] = ggain
    small[50:51, :] = gscale[...]
    out[...] = small[...].astype(BF16)


def small_grads(dnormed, nhat, inv, gain, gscale, wide, *after):
    channels = dnormed.shape[1]
    return call(
        small_body,
        "small_grads",
        10**6,
        [((64, channels), BF16)],
        [(dnormed.shape, F32), ((8 * 49, LANES), F32), ((64, channels), F32)],
        dnormed,
        nhat,
        inv,
        gain,
        gscale,
        wide,
        *after,
        read=10**5,
    )[0]


def gate_body(block, *rest):
    rest[-1][...] = block[...]


def gate(block, *after):
    shapes = [(block.shape, block.dtype)]
    return call(gate_body, "gate", 10**6, shapes, [], block, *after, read=10**5)[0]


def split(total, side, keep, send):
    parts, rows, _ = keep.shape
    for x in range(parts):
        mine = pl.multiple_of((2 * x + side) * rows, 16)
        theirs = pl.multiple_of((2 * x + 1 - side) * rows, 16)
        keep[x] = total[pl.ds(mine, rows), :]
        send[x] = total[pl.ds(theirs, rows), :].astype(BF16)


def added(small, more):
    return (small[...].astype(F32) + more[...].astype(F32)).astype(BF16)


def slope_and_act(normed, expand):
    pre = dot(normed, expand, ((1,), (0,)))
    cdf, density = phi_parts(pre)
    return cdf + pre * density, (pre * cdf).astype(BF16)


def views_apart(act):
    half = act.shape[0] // 2
    return (act[:half].astype(F32) - act[half:].astype(F32)).astype(BF16)


def dpre_of(dhidden, slope):
    half = dhidden.shape[0]
    return jnp.concatenate([dhidden * slope[:half], -dhidden * slope[half:]]).astype(BF16)


def own_lanes(own, width):
    first = position(4)[0] * own
    start = first // LANES * LANES
    return pl.ds(pl.multiple_of(start, LANES), width), first - start


def near_body(
    n_0, n_1, n_2, d_0, d_1, d_2, hidden_0, expand, reduce, turned, dpre, total, hidden
):
    half, channels = d_0.shape
    units = total.shape[0]
    lanes, _ = own_lanes(channels // 4, turned.shape[0])
    for p, ref in enumerate((n_0, n_1, n_2)):
        at = 2 * p * half
        turned[:, at : at + 2 * half] = ref[:, lanes].astype(F32).T.astype(BF16)
    others = jnp.concatenate([d_1[...], d_2[...]])
    both = jnp.concatenate([n_1[...], n_2[...]])
    for here in blocks(reduce.shape[0]):
        slope, act = slope_and_act(both, expand[:, here])
        hidden[:, here] = act
        dhidden = dot(others, reduce[here, :], ((1,), (1,)))
        dpre[: 2 * half, here] = dpre_of(dhidden[:half], slope[: 2 * half])
        dpre[2 * half :, here] = dpre_of(dhidden[half:], slope[2 * half :])
    lanes = pl.ds(pl.multiple_of(position(4)[0] * units, LANES), units)
    every = jnp.concatenate([d_0[...], others])
    acts = (hidden_0[:, lanes], hidden[: 2 * half, lanes], hidden[2 * half :, lanes])
    total[...] = dot(jnp.concatenate([views_apart(act) for act in acts]), every, ((0,), (0,)))


def near(normed, dbranch, hidden, expand, reduce, line):
    half, channels = dbranch[0].shape
    hid = expand.shape[1]
    return call(
        near_body,
        "near",
        10**6,
        [
            ((2 * LANES, 6 * half), BF16),
            ((4 * half, hid), BF16),
            ((hid // line, channels), F32),
        ],
        [((4 * half, hid), BF16)],
        *normed,
        *dbranch,
        hidden,
        expand,
        reduce,
        read=10**5,
    )


def far_reduce_body(n_3, d_3, expand, part, small, more, keep, send, sums, total):
    units = total.shape[0]
    line, core, _ = position(4)
    lanes = pl.ds(pl.multiple_of(line * units, LANES), units)
    _, act = slope_and_act(n_3[...], expand[:, lanes])
    total[...] = part[...] + dot(views_apart(act), d_3[...], ((0,), (0,)))
    split(total, core, keep, send)
    sums[...] = added(small, more)


def far_reduce(n_3, d_3, expand, part, small, more, inner):
    units, channels = part.shape
    shape = (inner // 2, units // inner, channels)
    return call(
        far_reduce_body,
        "far_reduce",
        10**6,
        [(shape, F32), (shape, BF16), (small.shape, BF16)],
        [((units, channels), F32)],
        n_3,
        d_3,
        expand,
        part,
        small,
        more,
        read=10**5,
    )


def far_expand_body(n_3, d_3, expand, reduce, after, turned, dpre):
    lanes, _ = own_lanes(n_3.shape[1] // 4, turned.shape[0])
    turned[...] = n_3[:, lanes].astype(F32).T.astype(BF16)
    for here in blocks(reduce.shape[0]):
        slope, _ = slope_and_act(n_3[...], expand[:, here])
        dpre[:, here] = dpre_of(dot(d_3[...], reduce[here, :], ((1,), (1,))), slope)


def far_expand(n_3, d_3, expand, reduce, after):
    rows = n_3.shape[0]
    hid = expand.shape[1]
    return call(
        far_expand_body,
        "far_expand",
        10**9,
        [((2 * LANES, rows), BF16), ((rows, hid), BF16)],
        [],
        n_3,
        d_3,
        expand,
        reduce,
        after,
        read=10**6,
    )


def expand_grad_body(turned, turned_3, dpre_0, dpre, dpre_3, after, keep, send, total):
    own, hid = total.shape
    _, core, _ = position(4)
    _, first = own_lanes(own, turned.shape[0])
    rows = pl.ds(pl.multiple_of(first, 16), own)
    lhs = jnp.concatenate([turned[rows, :], turned_3[rows, :]], axis=1)
    for here in blocks(hid):
        every = jnp.concatenate([dpre_0[:, here], dpre[:, here], dpre_3[:, here]])
        total[:, here] = dot(lhs, every, ((1,), (0,)))
    split(total, core, keep, send)


def expand_grad(turned, turned_3, dpre_0, dpre, dpre_3, after, own, inner):
    hid = dpre.shape[1]
    shape = (inner // 2, own // inner, hid)
    return call(
        expand_grad_body,
        "expand_grad",
        10**6,
        [(shape, F32), (shape, BF16)],
        [((own, hid), F32)],
        turned,
        turned_3,
        dpre_0,
        dpre,
        dpre_3,
        after,
        read=10**5,
    )


def merge_body(kept, got, keep, send):
    _, _, mine = position(4)
    theirs = 1 - mine
    keep[...] = kept[mine] + got[mine].astype(F32)
    send[...] = (kept[theirs] + got[theirs].astype(F32)).astype(BF16)


def merge_small_body(kept, got, small, more, keep, send, sums):
    merge_body(kept, got, keep, send)
    sums[...] = added(small, more)


def merge(kept, got, *small):
    shape = kept.shape[1:]
    return call(
        merge_small_body if small else merge_body,
        "merge",
        10**6,
        [(shape, F32), (shape, BF16)] + [(part.shape, BF16) for part in small[:1]],
        [],
        kept,
        got,
        *small,
        read=10**5,
    )


def finish_reduce_body(keep, got, small, more, out, kernel, gain, scale, done):
    out[...] = keep[...] + got[...].astype(F32)
    sums = small[...].astype(F32) + more[...].astype(F32)
    for i in range(7):
        kernel[i] = sums[7 * i : 7 * i + 7]
    gain[...] = sums[49:50].reshape(gain.shape)
    scale[...] = sums[50:51].reshape(scale.shape)
    done[...] = jnp.zeros(done.shape, F32)


def finish_reduce(keep, got, small, more):
    channels = small.shape[1]
    return call(
        finish_reduce_body,
        "finish_reduce",
        10**9,
        [
            (keep.shape, F32),
            ((7, 7, channels), F32),
            ((channels,), F32),
            ((channels,), F32),
            ((8, LANES), F32),
        ],
        [],
        keep,
        got,
        small,
        more,
        read=10**6,
    )


def finish_expand_body(keep, got, after, out):
    out[...] = keep[...] + got[...].astype(F32)


def finish_expand(keep, got, after):
    return call(
        finish_expand_body, "finish_expand", 10**6, [(keep.shape, F32)], [], keep, got, after, read=10**5
    )[0]


def grads_plain(every, dbranch_all, expand_weight, reduce_weight, my_line, my_inner, line, inner):
    channels, hid = expand_weight.shape
    units, own = hid // line, channels // line
    every = every.reshape(-1, channels)
    pre = dot(every, expand_weight, ((1,), (0,)))
    cdf, density = phi_parts(pre)
    slope = (cdf + pre * density).reshape(line, 2, -1, hid)
    hidden = (pre * cdf).astype(BF16).astype(F32).reshape(line, 2, -1, hid)
    diff = (hidden[:, 0] - hidden[:, 1]).astype(BF16).reshape(-1, hid)
    diff = lax.dynamic_slice_in_dim(diff, my_line * units, units, 1)
    dhidden = dot(dbranch_all, reduce_weight, ((1,), (1,))).reshape(line, -1, hid)
    dpre = jnp.stack([dhidden * slope[:, 0], -dhidden * slope[:, 1]], axis=1)
    dpre = dpre.astype(BF16).reshape(-1, hid)
    normed_own = lax.dynamic_slice_in_dim(every, my_line * own, own, 1)
    expand = dot(normed_own, dpre, ((0,), (0,))).reshape(inner, own // inner, hid)
    reduce = dot(diff, dbranch_all, ((0,), (0,))).reshape(inner, units // inner, channels)
    return halves(expand, my_inner & 1), halves(reduce, my_inner & 1)


def halves(part, side):
    part = part.reshape((part.shape[0] // 2, 2) + part.shape[1:])
    keep = lax.dynamic_index_in_dim(part, side, 1, keepdims=False)
    send = lax.dynamic_index_in_dim(part, 1 - side, 1, keepdims=False)
    return keep, send.astype(BF16)


def on_device(
    features, column_table, dw_kernel, norm_gain, expand_weight, reduce_weight, layer_scale
):
    rows, cols, channels = features.shape
    hid = expand_weight.shape[1]
    count = lax.axis_size("col")
    bits = count.bit_length() - 1
    line = 1 << ((bits + 1) // 2)
    inner = count // line
    inner_bits = inner.bit_length() - 1
    me = lax.axis_index("col")
    my_line, my_inner = me // inner, me % inner
    units, own = hid // line, channels // line
    total_cols = cols * count

    def swapped(block, mask):
        return lax.ppermute(block, "col", [(d, d ^ mask) for d in range(count)])

    def line_sum(small):
        sums = [small] + [swapped(small, p * inner) for p in range(1, line)]
        sums = [part.astype(F32) for part in sums]
        while len(sums) > 1:
            sums = [low + high for low, high in zip(sums[::2], sums[1::2])]
        return sums[0]

    mirror = lax.ppermute(column_table, "col", [(d, count - 1 - d) for d in range(count)])

    features_f = features.astype(F32)
    table_f = column_table.astype(F32)
    gain = norm_gain[None]
    inside, across, turned = edges(features_f, table_f, mirror)
    inside = swapped(inside, 1)
    pairs = [(d, d + 1) for d in range(1, count - 1, 2)]
    across = lax.ppermute(across, "col", pairs + [(high, low) for low, high in pairs])
    normed, nhat, inv, wide = conv_norm(
        features_f, table_f, turned, inside, across, dw_kernel.astype(F32), gain
    )
    fast = line == 4 and inner == 4 and units % LANES == 0 and own % 64 == 0
    if fast:
        flat = normed.reshape(-1, channels)
        normed_2, normed_1 = swapped(flat, 2 * inner), swapped(flat, inner)
    else:
        others = [swapped(normed, p * inner) for p in range(1, line)]
    slope, hidden, disagreement, dbranch, gscale = forward(
        1.0 / math.sqrt(rows * total_cols),
        normed.reshape(-1, channels),
        expand_weight,
        reduce_weight,
        wide,
        layer_scale,
        features.shape,
    )
    dnormed, dpre_0 = backward(dbranch, slope, expand_weight, reduce_weight)
    small = small_grads(dnormed, nhat, inv, gain, gscale, wide)
    if fast:
        dbranch_2, dbranch_1 = swapped(dbranch, 2 * inner), swapped(dbranch, inner)
        normed_3 = swapped(gate(normed_2, dnormed, normed_1), inner)
        dbranch_3 = swapped(gate(dbranch_2, small, dbranch_1), inner)
        more = swapped(small, 2)
        turned, dpre, part = near(
            [flat, normed_1, normed_2],
            [dbranch, dbranch_1, dbranch_2],
            hidden,
            expand_weight,
            reduce_weight,
            line,
        )
        keep_r, send_r, small = far_reduce(
            normed_3, dbranch_3, expand_weight, part, small, more, inner
        )
        got_r, more = swapped(send_r, 1), swapped(small, 1)
        turned_3, dpre_3 = far_expand(normed_3, dbranch_3, expand_weight, reduce_weight, small)
        keep_r, send_r, small = merge(keep_r, got_r, small, more)
        got_r, more = swapped(send_r, 2), swapped(small, inner)
        keep_e, send_e = expand_grad(
            turned, turned_3, dpre_0, dpre, dpre_3, small, own, inner
        )
        small = (small.astype(F32) + more.astype(F32)).astype(BF16)
        more = swapped(small, 2 * inner)
        keep_e, send_e = merge(keep_e, swapped(send_e, 1))
        got_e = swapped(send_e, 2)
        sum_r, *sums, done = finish_reduce(keep_r, got_r, small, more)
        sum_e = finish_expand(keep_e, got_e, done)
        return (disagreement, sum_e, sum_r, *sums)

    dbranch_all = [dbranch] + [swapped(dbranch, p * inner) for p in range(1, line)]
    (keep_e, send_e), (keep_r, send_r) = grads_plain(
        jnp.stack([normed] + others),
        jnp.concatenate(dbranch_all),
        expand_weight,
        reduce_weight,
        my_line,
        my_inner,
        line,
        inner,
    )
    small = line_sum(small)
    for bit in range(inner_bits):
        sum_r = keep_r + swapped(send_r, 1 << bit).astype(F32)
        sum_e = keep_e + swapped(send_e, 1 << bit).astype(F32)
        small = small.astype(BF16)
        small = small.astype(F32) + swapped(small, 1 << bit).astype(F32)
        if bit < inner_bits - 1:
            side = (my_inner >> (bit + 1)) & 1
            keep_r, send_r = halves(sum_r, side)
            keep_e, send_e = halves(sum_e, side)
    grad_kernel = small[:49].reshape(7, 7, channels)
    return (
        disagreement,
        sum_e.reshape(own // inner, hid),
        sum_r.reshape(units // inner, channels),
        grad_kernel,
        small[49],
        small[50],
    )


def solution(mesh):
    in_specs = (P("groups", "col", None), P("col", None), P(), P(), P(), P(), P())
    out_specs = (
        P("groups", "col", None),
        P(("groups", "col"), None),
        P(("groups", "col"), None),
        P("groups", None, None),
        P("groups"),
        P("groups"),
    )
    return jax.shard_map(
        on_device, mesh=mesh, in_specs=in_specs, out_specs=out_specs, check_vma=False
    )
```

```python
import functools
import math

import jax
import jax.numpy as jnp
from jax import lax
from jax.experimental import pallas as pl
from jax.experimental.pallas import tpu as pltpu
from jax.sharding import PartitionSpec as P

BF16 = jnp.bfloat16
F32 = jnp.float32
LANES = 128
VMEM_GRANT = 16 << 20
BLOCK = 256


def phi_parts(pre):
    decay = jnp.exp(-0.5 * pre * pre)
    t = 1.0 / (1.0 + 0.23164189 * jnp.abs(pre))
    poly = 0.5307027145 * t - 0.7265760135
    poly = poly * t + 0.7107068705
    poly = poly * t - 0.142248368
    poly = poly * t + 0.127414796
    tail = poly * t * decay
    return jnp.where(pre < 0.0, tail, 1.0 - tail), decay * 0.3989422804014327


def call(body, name, flops, out_shape, scratch, *operands, read=10**8):
    return pl.pallas_call(
        body,
        in_specs=[pl.BlockSpec(memory_space=pltpu.VMEM) for _ in operands],
        out_specs=[pl.BlockSpec(memory_space=pltpu.VMEM) for _ in out_shape],
        out_shape=[jax.ShapeDtypeStruct(shape, dtype) for shape, dtype in out_shape],
        scratch_shapes=[pltpu.VMEM(shape, dtype) for shape, dtype in scratch],
        compiler_params=pltpu.CompilerParams(vmem_limit_bytes=VMEM_GRANT),
        cost_estimate=pl.CostEstimate(flops=flops, bytes_accessed=read, transcendentals=0),
        name=name,
    )(*operands)


def position(inner):
    me = lax.axis_index("col")
    return me // inner, me & 1, (me >> 1) & 1


def dot(lhs, rhs, contract):
    return lax.dot_general(lhs, rhs, (contract, ((), ())), preferred_element_type=F32)


def flipped(value):
    rows = value.shape[0]
    return jnp.concatenate([value[r : r + 1] for r in reversed(range(rows))], axis=0)


def edges_body(feat, table, mirror, inside, across, turned):
    _, cols, channels = feat.shape
    other = flipped(mirror[...].astype(F32))
    odd = (lax.axis_index("col") & 1) == 1
    for v, add in enumerate((table[...], other)):
        own = (feat[...] + add[None]).astype(BF16).astype(F32)
        first, last = own[:, :3], own[:, cols - 3 :]
        inside[v] = jnp.where(odd, first, last).astype(BF16)
        across[v] = jnp.where(odd, last, first).astype(BF16)
    turned[...] = other


def edges(features, table, mirror):
    rows, cols, channels = features.shape
    return call(
        edges_body,
        "edges",
        10**8,
        [
            ((2, rows, 3, channels), BF16),
            ((2, rows, 3, channels), BF16),
            ((cols, channels), F32),
        ],
        [],
        features,
        table,
        mirror,
    )


def conv_body(feat, table, turned, inside, across, dw, gain, normed, nhat, inv, wide, conv):
    rows, cols, channels = feat.shape
    odd = (lax.axis_index("col") & 1) == 1
    for v, add in enumerate((table[...], turned[...])):
        wide[v, :, 3 : 3 + cols, :] = (feat[...] + add[None]).astype(BF16).astype(F32)
        one, two = inside[v].astype(F32), across[v].astype(F32)
        wide[v, :, 0:3, :] = jnp.where(odd, one, two)
        wide[v, :, 3 + cols : 6 + cols, :] = jnp.where(odd, two, one)

    def tile(c, carry):
        lanes = pl.ds(pl.multiple_of(c * LANES, LANES), LANES)
        sums = [[jnp.zeros((cols, LANES), F32) for _ in range(rows)] for _ in range(2)]
        for j in range(7):
            for v in range(2):
                part = [wide[v, r, pl.ds(j, cols), lanes] for r in range(rows)]
                for i in range(7):
                    weight = dw[i, pl.ds(6 - j if v else j, 1), lanes]
                    for r in range(rows):
                        if 0 <= r + i - 3 < rows:
                            sums[v][r] = sums[v][r] + weight * part[r + i - 3]
        for v in range(2):
            for r in range(rows):
                conv[v, r, :, lanes] = sums[v][r]
        return carry

    lax.fori_loop(0, channels // LANES, tile, 0)
    for v in range(2):
        value = conv[v].reshape(rows * cols, channels)
        centred = value - jnp.mean(value, axis=-1, keepdims=True)
        inverse = lax.rsqrt(jnp.mean(centred * centred, axis=-1, keepdims=True) + 1e-06)
        value = centred * inverse
        nhat[v] = value
        inv[v] = jnp.broadcast_to(inverse, (rows * cols, LANES))
        normed[v] = (value * gain[...]).astype(BF16)


def conv_norm(features, table, turned, inside, across, dw, gain):
    rows, cols, channels = features.shape
    pixels = rows * cols
    return call(
        conv_body,
        "conv_norm",
        4 * 10**9,
        [
            ((2, pixels, channels), BF16),
            ((2, pixels, channels), F32),
            ((2, pixels, LANES), F32),
            ((2, rows, 16, channels), F32),
        ],
        [((2, rows, cols, channels), F32)],
        features,
        table,
        turned,
        inside,
        across,
        dw,
        gain,
    )


def blocks(total):
    return [slice(at, at + BLOCK) for at in range(0, total, BLOCK)]


def forward_body(
    scale, normed, expand, reduce, wide, ls, slope, hidden, disagreement, dbranch, gscale
):
    pixels, channels = normed.shape
    half = pixels // 2
    rows, cols, _ = disagreement.shape
    for here in blocks(expand.shape[1]):
        pre = dot(normed[...], expand[:, here], ((1,), (0,)))
        cdf, density = phi_parts(pre)
        slope[:, here] = (cdf + pre * density).astype(BF16)
        hidden[:, here] = (pre * cdf).astype(BF16)
    branch = dot(hidden[...], reduce[...], ((1,), (0,)))
    factor = ls[...].reshape(1, channels)
    outs = []
    for v in range(2):
        own = wide[v, :, 3 : 3 + cols, :].reshape(half, channels)
        outs.append((own + factor * branch[v * half : (v + 1) * half]).astype(BF16).astype(F32))
    difference = outs[0] - outs[1]
    disagreement[...] = difference.astype(BF16).reshape(rows, cols, channels)
    residual = (difference * scale).astype(BF16).astype(F32)
    gscale[...] = jnp.sum((branch[:half] - branch[half:]) * residual, axis=0, keepdims=True)
    dbranch[...] = (factor * residual).astype(BF16)


def forward(scale, normed, expand, reduce, wide, ls, shape):
    pixels, channels = normed.shape
    hid = expand.shape[1]
    return call(
        functools.partial(forward_body, scale),
        "forward",
        10**9,
        [
            ((pixels, hid), BF16),
            ((pixels, hid), BF16),
            (shape, BF16),
            ((pixels // 2, channels), BF16),
            ((1, channels), F32),
        ],
        [],
        normed,
        expand,
        reduce,
        wide,
        ls,
        read=10**6,
    )


def backward_body(dbranch, slope, expand, reduce, dnormed, dpre):
    half = dbranch.shape[0]
    for here in blocks(expand.shape[1]):
        dhidden = dot(dbranch[...], reduce[here, :], ((1,), (1,)))
        dpre[:, here] = dpre_of(dhidden, slope[:, here].astype(F32))
    dnormed[...] = dot(dpre[...], expand[...], ((1,), (1,)))


def backward(dbranch, slope, expand, reduce):
    half, channels = dbranch.shape
    hid = expand.shape[1]
    return call(
        backward_body,
        "backward",
        10**9,
        [((2 * half, channels), F32), ((2 * half, hid), BF16)],
        [],
        dbranch,
        slope,
        expand,
        reduce,
        read=10**6,
    )


def small_body(dnormed, nhat, inv, gain, gscale, wide, *rest):
    out, grad, taps, small = rest[-4:]
    half, channels = dnormed.shape[0] // 2, dnormed.shape[1]
    _, rows, _, _ = wide.shape
    cols = half // rows
    factor = gain[...]
    ggain = jnp.zeros((1, channels), F32)
    for v in range(2):
        here = slice(v * half, (v + 1) * half)
        value = dnormed[here, :]
        ggain = ggain + jnp.sum(value * nhat[v], axis=0, keepdims=True)
        scaled = value * factor
        gm = jnp.mean(scaled, axis=-1, keepdims=True)
        gn = jnp.mean(scaled * nhat[v], axis=-1, keepdims=True)
        grad[here, :] = inv[v][:, :1] * (scaled - gm - nhat[v] * gn)

    def tile(c, carry):
        lanes = pl.ds(pl.multiple_of(c * LANES, LANES), LANES)
        dconv = [
            [grad[pl.ds(v * half + r * cols, cols), lanes] for r in range(rows)] for v in range(2)
        ]
        for j in range(7):
            part = [
                [wide[v, r, pl.ds(6 - j if v else j, cols), lanes] for r in range(rows)]
                for v in range(2)
            ]
            for i in range(7):
                sums = []
                for v in range(2):
                    total = None
                    for r in range(rows):
                        if 0 <= r + i - 3 < rows:
                            term = part[v][r + i - 3] * dconv[v][r]
                            total = term if total is None else total + term
                    sums.append(total)
                at = 8 * (7 * i + j)
                taps[at : at + 8, :] = sums[0] + sums[1]
        rolled = taps[pl.ds(0, 49, stride=8), :]
        for s in range(1, 8):
            rolled = rolled + taps[pl.ds(s, 49, stride=8), :]
        small[:49, lanes] = rolled
        return carry

    small[...] = jnp.zeros(small.shape, F32)
    lax.fori_loop(0, channels // LANES, tile, 0)
    small[49:50, :] = ggain
    small[50:51, :] = gscale[...]
    out[...] = small[...].astype(BF16)


def small_grads(dnormed, nhat, inv, gain, gscale, wide, *after):
    channels = dnormed.shape[1]
    return call(
        small_body,
        "small_grads",
        10**6,
        [((64, channels), BF16)],
        [(dnormed.shape, F32), ((8 * 49, LANES), F32), ((64, channels), F32)],
        dnormed,
        nhat,
        inv,
        gain,
        gscale,
        wide,
        *after,
        read=10**5,
    )[0]


def gate_body(block, *rest):
    rest[-1][...] = block[...]


def gate(block, *after):
    shapes = [(block.shape, block.dtype)]
    return call(gate_body, "gate", 10**6, shapes, [], block, *after, read=10**5)[0]


def kept_first(ref):
    rows = ref.shape[0] // 4
    _, core, _ = position(4)
    blocks_of = lambda side: [
        ref[pl.ds(pl.multiple_of((2 * x + side) * rows, 16), rows), :] for x in range(2)
    ]
    return jnp.concatenate(blocks_of(core) + blocks_of(1 - core))


def added(small, more):
    return (small[...].astype(F32) + more[...].astype(F32)).astype(BF16)


def slope_and_act(normed, expand):
    pre = dot(normed, expand, ((1,), (0,)))
    cdf, density = phi_parts(pre)
    return cdf + pre * density, (pre * cdf).astype(BF16)


def views_apart(act):
    half = act.shape[0] // 2
    return (act[:half].astype(F32) - act[half:].astype(F32)).astype(BF16)


def dpre_of(dhidden, slope):
    half = dhidden.shape[0]
    return jnp.concatenate([dhidden * slope[:half], -dhidden * slope[half:]]).astype(BF16)


def own_lanes(own, width):
    first = position(4)[0] * own
    start = first // LANES * LANES
    return pl.ds(pl.multiple_of(start, LANES), width), first - start


def near_body(
    n_0, n_1, n_2, d_0, d_1, d_2, hidden_0, expand, reduce, turned, dpre, total, hidden, apart
):
    half, channels = d_0.shape
    units = total.shape[0]
    lanes, _ = own_lanes(channels // 4, turned.shape[0])
    for p, ref in enumerate((n_0, n_1, n_2)):
        at = 2 * p * half
        turned[:, at : at + 2 * half] = ref[:, lanes].astype(F32).T.astype(BF16)
    others = jnp.concatenate([d_1[...], d_2[...]])
    both = jnp.concatenate([n_1[...], n_2[...]])
    for here in blocks(reduce.shape[0]):
        slope, act = slope_and_act(both, expand[:, here])
        hidden[:, here] = act
        dhidden = dot(others, reduce[here, :], ((1,), (1,)))
        dpre[: 2 * half, here] = dpre_of(dhidden[:half], slope[: 2 * half])
        dpre[2 * half :, here] = dpre_of(dhidden[half:], slope[2 * half :])
    lanes = pl.ds(pl.multiple_of(position(4)[0] * units, LANES), units)
    every = jnp.concatenate([d_0[...], others])
    acts = (hidden_0[:, lanes], hidden[: 2 * half, lanes], hidden[2 * half :, lanes])
    for p, act in enumerate(acts):
        apart[:, p * half : (p + 1) * half] = views_apart(act).astype(F32).T.astype(BF16)
    total[...] = dot(kept_first(apart), every, ((1,), (0,)))


def near(normed, dbranch, hidden, expand, reduce, line):
    half, channels = dbranch[0].shape
    hid = expand.shape[1]
    return call(
        near_body,
        "near",
        10**6,
        [
            ((2 * LANES, 6 * half), BF16),
            ((4 * half, hid), BF16),
            ((hid // line, channels), F32),
        ],
        [((4 * half, hid), BF16), ((hid // line, 3 * half), BF16)],
        *normed,
        *dbranch,
        hidden,
        expand,
        reduce,
        read=10**5,
    )


def far_reduce_body(n_3, d_3, expand, part, small, more, keep, send, sums, apart):
    parts, rows, channels = keep.shape
    units, cut = apart.shape[0], parts * rows
    lanes = pl.ds(pl.multiple_of(position(4)[0] * units, LANES), units)
    _, act = slope_and_act(n_3[...], expand[:, lanes])
    apart[...] = views_apart(act).astype(F32).T.astype(BF16)
    total = dot(kept_first(apart), d_3[...], ((1,), (0,)))
    keep[...] = (part[:cut, :] + total[:cut]).reshape(parts, rows, channels)
    send[...] = (part[cut:, :] + total[cut:]).astype(BF16).reshape(parts, rows, channels)
    sums[...] = added(small, more)


def far_reduce(n_3, d_3, expand, part, small, more, inner):
    units, channels = part.shape
    shape = (inner // 2, units // inner, channels)
    return call(
        far_reduce_body,
        "far_reduce",
        10**6,
        [(shape, F32), (shape, BF16), (small.shape, BF16)],
        [((units, d_3.shape[0]), BF16)],
        n_3,
        d_3,
        expand,
        part,
        small,
        more,
        read=10**5,
    )


def far_expand_body(n_3, d_3, expand, reduce, after, turned, dpre):
    lanes, _ = own_lanes(n_3.shape[1] // 4, turned.shape[0])
    turned[...] = n_3[:, lanes].astype(F32).T.astype(BF16)
    for here in blocks(reduce.shape[0]):
        slope, _ = slope_and_act(n_3[...], expand[:, here])
        dpre[:, here] = dpre_of(dot(d_3[...], reduce[here, :], ((1,), (1,))), slope)


def far_expand(n_3, d_3, expand, reduce, after):
    rows = n_3.shape[0]
    hid = expand.shape[1]
    return call(
        far_expand_body,
        "far_expand",
        10**9,
        [((2 * LANES, rows), BF16), ((rows, hid), BF16)],
        [],
        n_3,
        d_3,
        expand,
        reduce,
        after,
        read=10**6,
    )


def expand_grad_body(turned, turned_3, dpre_0, dpre, dpre_3, after, keep, send, lhs):
    own, near_width = lhs.shape[0], turned.shape[1]
    parts, rows, hid = keep.shape
    _, first = own_lanes(own, turned.shape[0])
    here = pl.ds(pl.multiple_of(first, 16), own)
    lhs[:, :near_width] = turned[here, :]
    lhs[:, near_width:] = turned_3[here, :]
    ordered = kept_first(lhs)
    cut = parts * rows
    for here in blocks(hid):
        every = jnp.concatenate([dpre_0[:, here], dpre[:, here], dpre_3[:, here]])
        total = dot(ordered, every, ((1,), (0,)))
        for x in range(parts):
            at = x * rows
            keep[x, :, here] = total[at : at + rows]
            send[x, :, here] = total[cut + at : cut + at + rows].astype(BF16)


def expand_grad(turned, turned_3, dpre_0, dpre, dpre_3, after, own, inner):
    hid = dpre.shape[1]
    shape = (inner // 2, own // inner, hid)
    return call(
        expand_grad_body,
        "expand_grad",
        10**6,
        [(shape, F32), (shape, BF16)],
        [((own, turned.shape[1] + turned_3.shape[1]), BF16)],
        turned,
        turned_3,
        dpre_0,
        dpre,
        dpre_3,
        after,
        read=10**5,
    )


def merge_body(kept, got, keep, send):
    _, _, mine = position(4)
    theirs = 1 - mine
    keep[...] = kept[mine] + got[mine].astype(F32)
    send[...] = (kept[theirs] + got[theirs].astype(F32)).astype(BF16)


def merge_small_body(kept, got, small, more, keep, send, sums):
    merge_body(kept, got, keep, send)
    sums[...] = added(small, more)


def merge(kept, got, *small):
    shape = kept.shape[1:]
    return call(
        merge_small_body if small else merge_body,
        "merge",
        10**6,
        [(shape, F32), (shape, BF16)] + [(part.shape, BF16) for part in small[:1]],
        [],
        kept,
        got,
        *small,
        read=10**5,
    )


def finish_reduce_body(keep, got, small, more, out, kernel, gain, scale, done):
    out[...] = keep[...] + got[...].astype(F32)
    sums = small[...].astype(F32) + more[...].astype(F32)
    for i in range(7):
        kernel[i] = sums[7 * i : 7 * i + 7]
    gain[...] = sums[49:50].reshape(gain.shape)
    scale[...] = sums[50:51].reshape(scale.shape)
    done[...] = jnp.zeros(done.shape, F32)


def finish_reduce(keep, got, small, more):
    channels = small.shape[1]
    return call(
        finish_reduce_body,
        "finish_reduce",
        10**9,
        [
            (keep.shape, F32),
            ((7, 7, channels), F32),
            ((channels,), F32),
            ((channels,), F32),
            ((8, LANES), F32),
        ],
        [],
        keep,
        got,
        small,
        more,
        read=10**6,
    )


def finish_expand_body(keep, got, after, out):
    out[...] = keep[...] + got[...].astype(F32)


def finish_expand(keep, got, after):
    return call(
        finish_expand_body, "finish_expand", 10**6, [(keep.shape, F32)], [], keep, got, after, read=10**5
    )[0]


def grads_plain(every, dbranch_all, expand_weight, reduce_weight, my_line, my_inner, line, inner):
    channels, hid = expand_weight.shape
    units, own = hid // line, channels // line
    every = every.reshape(-1, channels)
    pre = dot(every, expand_weight, ((1,), (0,)))
    cdf, density = phi_parts(pre)
    slope = (cdf + pre * density).reshape(line, 2, -1, hid)
    hidden = (pre * cdf).astype(BF16).astype(F32).reshape(line, 2, -1, hid)
    diff = (hidden[:, 0] - hidden[:, 1]).astype(BF16).reshape(-1, hid)
    diff = lax.dynamic_slice_in_dim(diff, my_line * units, units, 1)
    dhidden = dot(dbranch_all, reduce_weight, ((1,), (1,))).reshape(line, -1, hid)
    dpre = jnp.stack([dhidden * slope[:, 0], -dhidden * slope[:, 1]], axis=1)
    dpre = dpre.astype(BF16).reshape(-1, hid)
    normed_own = lax.dynamic_slice_in_dim(every, my_line * own, own, 1)
    expand = dot(normed_own, dpre, ((0,), (0,))).reshape(inner, own // inner, hid)
    reduce = dot(diff, dbranch_all, ((0,), (0,))).reshape(inner, units // inner, channels)
    return halves(expand, my_inner & 1), halves(reduce, my_inner & 1)


def halves(part, side):
    part = part.reshape((part.shape[0] // 2, 2) + part.shape[1:])
    keep = lax.dynamic_index_in_dim(part, side, 1, keepdims=False)
    send = lax.dynamic_index_in_dim(part, 1 - side, 1, keepdims=False)
    return keep, send.astype(BF16)


def on_device(
    features, column_table, dw_kernel, norm_gain, expand_weight, reduce_weight, layer_scale
):
    rows, cols, channels = features.shape
    hid = expand_weight.shape[1]
    count = lax.axis_size("col")
    bits = count.bit_length() - 1
    line = 1 << ((bits + 1) // 2)
    inner = count // line
    inner_bits = inner.bit_length() - 1
    me = lax.axis_index("col")
    my_line, my_inner = me // inner, me % inner
    units, own = hid // line, channels // line
    total_cols = cols * count

    def swapped(block, mask):
        return lax.ppermute(block, "col", [(d, d ^ mask) for d in range(count)])

    def line_sum(small):
        sums = [small] + [swapped(small, p * inner) for p in range(1, line)]
        sums = [part.astype(F32) for part in sums]
        while len(sums) > 1:
            sums = [low + high for low, high in zip(sums[::2], sums[1::2])]
        return sums[0]

    mirror = lax.ppermute(column_table, "col", [(d, count - 1 - d) for d in range(count)])

    features_f = features.astype(F32)
    table_f = column_table.astype(F32)
    gain = norm_gain[None]
    inside, across, turned = edges(features_f, table_f, mirror)
    inside = swapped(inside, 1)
    pairs = [(d, d + 1) for d in range(1, count - 1, 2)]
    across = lax.ppermute(across, "col", pairs + [(high, low) for low, high in pairs])
    normed, nhat, inv, wide = conv_norm(
        features_f, table_f, turned, inside, across, dw_kernel.astype(F32), gain
    )
    fast = line == 4 and inner == 4 and units % LANES == 0 and own % 64 == 0
    if fast:
        flat = normed.reshape(-1, channels)
        normed_2, normed_1 = swapped(flat, 2 * inner), swapped(flat, inner)
    else:
        others = [swapped(normed, p * inner) for p in range(1, line)]
    slope, hidden, disagreement, dbranch, gscale = forward(
        1.0 / math.sqrt(rows * total_cols),
        normed.reshape(-1, channels),
        expand_weight,
        reduce_weight,
        wide,
        layer_scale,
        features.shape,
    )
    dnormed, dpre_0 = backward(dbranch, slope, expand_weight, reduce_weight)
    small = small_grads(dnormed, nhat, inv, gain, gscale, wide)
    if fast:
        dbranch_2, dbranch_1 = swapped(dbranch, 2 * inner), swapped(dbranch, inner)
        normed_3 = swapped(gate(normed_2, dnormed, normed_1), inner)
        dbranch_3 = swapped(gate(dbranch_2, small, dbranch_1), inner)
        more = swapped(small, 2)
        turned, dpre, part = near(
            [flat, normed_1, normed_2],
            [dbranch, dbranch_1, dbranch_2],
            hidden,
            expand_weight,
            reduce_weight,
            line,
        )
        keep_r, send_r, small = far_reduce(
            normed_3, dbranch_3, expand_weight, part, small, more, inner
        )
        got_r, more = swapped(send_r, 1), swapped(small, 1)
        turned_3, dpre_3 = far_expand(normed_3, dbranch_3, expand_weight, reduce_weight, small)
        keep_r, send_r, small = merge(keep_r, got_r, small, more)
        got_r, more = swapped(send_r, 2), swapped(small, inner)
        keep_e, send_e = expand_grad(
            turned, turned_3, dpre_0, dpre, dpre_3, small, own, inner
        )
        small = (small.astype(F32) + more.astype(F32)).astype(BF16)
        more = swapped(small, 2 * inner)
        keep_e, send_e = merge(keep_e, swapped(send_e, 1))
        got_e = swapped(send_e, 2)
        sum_r, *sums, done = finish_reduce(keep_r, got_r, small, more)
        sum_e = finish_expand(keep_e, got_e, done)
        return (disagreement, sum_e, sum_r, *sums)

    dbranch_all = [dbranch] + [swapped(dbranch, p * inner) for p in range(1, line)]
    (keep_e, send_e), (keep_r, send_r) = grads_plain(
        jnp.stack([normed] + others),
        jnp.concatenate(dbranch_all),
        expand_weight,
        reduce_weight,
        my_line,
        my_inner,
        line,
        inner,
    )
    small = line_sum(small)
    for bit in range(inner_bits):
        sum_r = keep_r + swapped(send_r, 1 << bit).astype(F32)
        sum_e = keep_e + swapped(send_e, 1 << bit).astype(F32)
        small = small.astype(BF16)
        small = small.astype(F32) + swapped(small, 1 << bit).astype(F32)
        if bit < inner_bits - 1:
            side = (my_inner >> (bit + 1)) & 1
            keep_r, send_r = halves(sum_r, side)
            keep_e, send_e = halves(sum_e, side)
    grad_kernel = small[:49].reshape(7, 7, channels)
    return (
        disagreement,
        sum_e.reshape(own // inner, hid),
        sum_r.reshape(units // inner, channels),
        grad_kernel,
        small[49],
        small[50],
    )


def solution(mesh):
    in_specs = (P("groups", "col", None), P("col", None), P(), P(), P(), P(), P())
    out_specs = (
        P("groups", "col", None),
        P(("groups", "col"), None),
        P(("groups", "col"), None),
        P("groups", None, None),
        P("groups"),
        P("groups"),
    )
    return jax.shard_map(
        on_device, mesh=mesh, in_specs=in_specs, out_specs=out_specs, check_vma=False
    )
```

```python
import functools
import math

import jax
import jax.numpy as jnp
from jax import lax
from jax.experimental import pallas as pl
from jax.experimental.pallas import tpu as pltpu
from jax.sharding import PartitionSpec as P

BF16 = jnp.bfloat16
F32 = jnp.float32
LANES = 128
VMEM_GRANT = 16 << 20
BLOCK = 256


def phi_parts(pre):
    decay = jnp.exp(-0.5 * pre * pre)
    t = 1.0 / (1.0 + 0.23164189 * jnp.abs(pre))
    poly = 0.5307027145 * t - 0.7265760135
    poly = poly * t + 0.7107068705
    poly = poly * t - 0.142248368
    poly = poly * t + 0.127414796
    tail = poly * t * decay
    return jnp.where(pre < 0.0, tail, 1.0 - tail), decay * 0.3989422804014327


def call(body, name, flops, out_shape, scratch, *operands, read=10**8):
    return pl.pallas_call(
        body,
        in_specs=[pl.BlockSpec(memory_space=pltpu.VMEM) for _ in operands],
        out_specs=[pl.BlockSpec(memory_space=pltpu.VMEM) for _ in out_shape],
        out_shape=[jax.ShapeDtypeStruct(shape, dtype) for shape, dtype in out_shape],
        scratch_shapes=[pltpu.VMEM(shape, dtype) for shape, dtype in scratch],
        compiler_params=pltpu.CompilerParams(vmem_limit_bytes=VMEM_GRANT),
        cost_estimate=pl.CostEstimate(flops=flops, bytes_accessed=read, transcendentals=0),
        name=name,
    )(*operands)


def position(inner):
    me = lax.axis_index("col")
    return me // inner, me & 1, (me >> 1) & 1


def dot(lhs, rhs, contract):
    return lax.dot_general(lhs, rhs, (contract, ((), ())), preferred_element_type=F32)


def flipped(value):
    rows = value.shape[0]
    return jnp.concatenate([value[r : r + 1] for r in reversed(range(rows))], axis=0)


def edges_body(feat, table, mirror, inside, across, turned):
    _, cols, channels = feat.shape
    other = flipped(mirror[...].astype(F32))
    odd = (lax.axis_index("col") & 1) == 1
    for v, add in enumerate((table[...], other)):
        own = (feat[...] + add[None]).astype(BF16).astype(F32)
        first, last = own[:, :3], own[:, cols - 3 :]
        inside[v] = jnp.where(odd, first, last).astype(BF16)
        across[v] = jnp.where(odd, last, first).astype(BF16)
    turned[...] = other


def edges(features, table, mirror):
    rows, cols, channels = features.shape
    return call(
        edges_body,
        "edges",
        10**8,
        [
            ((2, rows, 3, channels), BF16),
            ((2, rows, 3, channels), BF16),
            ((cols, channels), F32),
        ],
        [],
        features,
        table,
        mirror,
    )


def conv_body(feat, table, turned, inside, across, dw, gain, normed, nhat, inv, wide, conv):
    rows, cols, channels = feat.shape
    odd = (lax.axis_index("col") & 1) == 1
    for v, add in enumerate((table[...], turned[...])):
        wide[v, :, 3 : 3 + cols, :] = (feat[...] + add[None]).astype(BF16).astype(F32)
        one, two = inside[v].astype(F32), across[v].astype(F32)
        wide[v, :, 0:3, :] = jnp.where(odd, one, two)
        wide[v, :, 3 + cols : 6 + cols, :] = jnp.where(odd, two, one)

    def tile(c, carry):
        lanes = pl.ds(pl.multiple_of(c * LANES, LANES), LANES)
        sums = [[jnp.zeros((cols, LANES), F32) for _ in range(rows)] for _ in range(2)]
        for j in range(7):
            for v in range(2):
                part = [wide[v, r, pl.ds(j, cols), lanes] for r in range(rows)]
                for i in range(7):
                    weight = dw[i, pl.ds(6 - j if v else j, 1), lanes]
                    for r in range(rows):
                        if 0 <= r + i - 3 < rows:
                            sums[v][r] = sums[v][r] + weight * part[r + i - 3]
        for v in range(2):
            for r in range(rows):
                conv[v, r, :, lanes] = sums[v][r]
        return carry

    lax.fori_loop(0, channels // LANES, tile, 0)
    for v in range(2):
        value = conv[v].reshape(rows * cols, channels)
        centred = value - jnp.mean(value, axis=-1, keepdims=True)
        inverse = lax.rsqrt(jnp.mean(centred * centred, axis=-1, keepdims=True) + 1e-06)
        value = centred * inverse
        nhat[v] = value
        inv[v] = jnp.broadcast_to(inverse, (rows * cols, LANES))
        normed[v] = (value * gain[...]).astype(BF16)


def conv_norm(features, table, turned, inside, across, dw, gain):
    rows, cols, channels = features.shape
    pixels = rows * cols
    return call(
        conv_body,
        "conv_norm",
        4 * 10**9,
        [
            ((2, pixels, channels), BF16),
            ((2, pixels, channels), F32),
            ((2, pixels, LANES), F32),
            ((2, rows, 16, channels), F32),
        ],
        [((2, rows, cols, channels), F32)],
        features,
        table,
        turned,
        inside,
        across,
        dw,
        gain,
    )


def blocks(total):
    return [slice(at, at + BLOCK) for at in range(0, total, BLOCK)]


def forward_body(
    scale, normed, expand, reduce, wide, ls, slope, hidden, disagreement, dbranch, gscale
):
    pixels, channels = normed.shape
    half = pixels // 2
    rows, cols, _ = disagreement.shape
    for here in blocks(expand.shape[1]):
        pre = dot(normed[...], expand[:, here], ((1,), (0,)))
        cdf, density = phi_parts(pre)
        slope[:, here] = (cdf + pre * density).astype(BF16)
        hidden[:, here] = (pre * cdf).astype(BF16)
    branch = dot(hidden[...], reduce[...], ((1,), (0,)))
    factor = ls[...].reshape(1, channels)
    outs = []
    for v in range(2):
        own = wide[v, :, 3 : 3 + cols, :].reshape(half, channels)
        outs.append((own + factor * branch[v * half : (v + 1) * half]).astype(BF16).astype(F32))
    difference = outs[0] - outs[1]
    disagreement[...] = difference.astype(BF16).reshape(rows, cols, channels)
    residual = (difference * scale).astype(BF16).astype(F32)
    gscale[...] = jnp.sum((branch[:half] - branch[half:]) * residual, axis=0, keepdims=True)
    dbranch[...] = (factor * residual).astype(BF16)


def forward(scale, normed, expand, reduce, wide, ls, shape):
    pixels, channels = normed.shape
    hid = expand.shape[1]
    return call(
        functools.partial(forward_body, scale),
        "forward",
        10**9,
        [
            ((pixels, hid), BF16),
            ((pixels, hid), BF16),
            (shape, BF16),
            ((pixels // 2, channels), BF16),
            ((1, channels), F32),
        ],
        [],
        normed,
        expand,
        reduce,
        wide,
        ls,
        read=10**6,
    )


def backward_body(dbranch, slope, expand, reduce, dnormed, dpre):
    half = dbranch.shape[0]
    for here in blocks(expand.shape[1]):
        dhidden = dot(dbranch[...], reduce[here, :], ((1,), (1,)))
        dpre[:, here] = dpre_of(dhidden, slope[:, here].astype(F32))
    dnormed[...] = dot(dpre[...], expand[...], ((1,), (1,)))


def backward(dbranch, slope, expand, reduce):
    half, channels = dbranch.shape
    hid = expand.shape[1]
    return call(
        backward_body,
        "backward",
        10**9,
        [((2 * half, channels), F32), ((2 * half, hid), BF16)],
        [],
        dbranch,
        slope,
        expand,
        reduce,
        read=10**6,
    )


def small_body(dnormed, nhat, inv, gain, gscale, wide, *rest):
    out, grad, taps, small = rest[-4:]
    half, channels = dnormed.shape[0] // 2, dnormed.shape[1]
    _, rows, _, _ = wide.shape
    cols = half // rows
    factor = gain[...]
    ggain = jnp.zeros((1, channels), F32)
    for v in range(2):
        here = slice(v * half, (v + 1) * half)
        value = dnormed[here, :]
        ggain = ggain + jnp.sum(value * nhat[v], axis=0, keepdims=True)
        scaled = value * factor
        gm = jnp.mean(scaled, axis=-1, keepdims=True)
        gn = jnp.mean(scaled * nhat[v], axis=-1, keepdims=True)
        grad[here, :] = inv[v][:, :1] * (scaled - gm - nhat[v] * gn)

    def tile(c, carry):
        lanes = pl.ds(pl.multiple_of(c * LANES, LANES), LANES)
        dconv = [
            [grad[pl.ds(v * half + r * cols, cols), lanes] for r in range(rows)] for v in range(2)
        ]
        for j in range(7):
            part = [
                [wide[v, r, pl.ds(6 - j if v else j, cols), lanes] for r in range(rows)]
                for v in range(2)
            ]
            for i in range(7):
                sums = []
                for v in range(2):
                    total = None
                    for r in range(rows):
                        if 0 <= r + i - 3 < rows:
                            term = part[v][r + i - 3] * dconv[v][r]
                            total = term if total is None else total + term
                    sums.append(total)
                at = 8 * (7 * i + j)
                taps[at : at + 8, :] = sums[0] + sums[1]
        rolled = taps[pl.ds(0, 49, stride=8), :]
        for s in range(1, 8):
            rolled = rolled + taps[pl.ds(s, 49, stride=8), :]
        small[:49, lanes] = rolled
        return carry

    small[...] = jnp.zeros(small.shape, F32)
    lax.fori_loop(0, channels // LANES, tile, 0)
    small[49:50, :] = ggain
    small[50:51, :] = gscale[...]
    out[...] = small[...].astype(BF16)


def small_grads(dnormed, nhat, inv, gain, gscale, wide, *after):
    channels = dnormed.shape[1]
    return call(
        small_body,
        "small_grads",
        10**6,
        [((64, channels), BF16)],
        [(dnormed.shape, F32), ((8 * 49, LANES), F32), ((64, channels), F32)],
        dnormed,
        nhat,
        inv,
        gain,
        gscale,
        wide,
        *after,
        read=10**5,
    )[0]


def gate_body(block, *rest):
    rest[-1][...] = block[...]


def gate(block, *after):
    shapes = [(block.shape, block.dtype)]
    return call(gate_body, "gate", 10**6, shapes, [], block, *after, read=10**5)[0]


def kept_first(ref):
    rows = ref.shape[0] // 4
    _, core, _ = position(4)
    blocks_of = lambda side: [
        ref[pl.ds(pl.multiple_of((2 * x + side) * rows, 16), rows), :] for x in range(2)
    ]
    return jnp.concatenate(blocks_of(core) + blocks_of(1 - core))


def added(small, more):
    return (small[...].astype(F32) + more[...].astype(F32)).astype(BF16)


def slope_and_act(normed, expand):
    pre = dot(normed, expand, ((1,), (0,)))
    cdf, density = phi_parts(pre)
    return cdf + pre * density, (pre * cdf).astype(BF16)


def views_apart(act):
    half = act.shape[0] // 2
    return (act[:half].astype(F32) - act[half:].astype(F32)).astype(BF16)


def dpre_of(dhidden, slope):
    half = dhidden.shape[0]
    return jnp.concatenate([dhidden * slope[:half], -dhidden * slope[half:]]).astype(BF16)


def own_lanes(own, width):
    first = position(4)[0] * own
    start = first // LANES * LANES
    return pl.ds(pl.multiple_of(start, LANES), width), first - start


def near_body(
    n_0, n_1, n_2, d_0, d_1, d_2, hidden_0, expand, reduce, turned, dpre, total, hidden
):
    half, channels = d_0.shape
    units = total.shape[0]
    lanes, _ = own_lanes(channels // 4, turned.shape[0])
    for p, ref in enumerate((n_0, n_1, n_2)):
        at = 2 * p * half
        turned[:, at : at + 2 * half] = ref[:, lanes].astype(F32).T.astype(BF16)
    others = jnp.concatenate([d_1[...], d_2[...]])
    both = jnp.concatenate([n_1[...], n_2[...]])
    for here in blocks(reduce.shape[0]):
        slope, act = slope_and_act(both, expand[:, here])
        hidden[:, here] = act
        dhidden = dot(others, reduce[here, :], ((1,), (1,)))
        dpre[: 2 * half, here] = dpre_of(dhidden[:half], slope[: 2 * half])
        dpre[2 * half :, here] = dpre_of(dhidden[half:], slope[2 * half :])
    lanes = pl.ds(pl.multiple_of(position(4)[0] * units, LANES), units)
    every = jnp.concatenate([d_0[...], others])
    acts = (hidden_0[:, lanes], hidden[: 2 * half, lanes], hidden[2 * half :, lanes])
    total[...] = dot(jnp.concatenate([views_apart(act) for act in acts]), every, ((0,), (0,)))


def near(normed, dbranch, hidden, expand, reduce, line):
    half, channels = dbranch[0].shape
    hid = expand.shape[1]
    return call(
        near_body,
        "near",
        10**6,
        [
            ((2 * LANES, 6 * half), BF16),
            ((4 * half, hid), BF16),
            ((hid // line, channels), F32),
        ],
        [((4 * half, hid), BF16)],
        *normed,
        *dbranch,
        hidden,
        expand,
        reduce,
        read=10**5,
    )


def far_reduce_body(n_3, d_3, expand, part, small, more, keep, send, sums, apart):
    parts, rows, channels = keep.shape
    units, cut = apart.shape[0], parts * rows
    lanes = pl.ds(pl.multiple_of(position(4)[0] * units, LANES), units)
    _, act = slope_and_act(n_3[...], expand[:, lanes])
    apart[...] = views_apart(act).astype(F32).T.astype(BF16)
    total = kept_first(part) + dot(kept_first(apart), d_3[...], ((1,), (0,)))
    keep[...] = total[:cut].reshape(parts, rows, channels)
    send[...] = total[cut:].astype(BF16).reshape(parts, rows, channels)
    sums[...] = added(small, more)


def far_reduce(n_3, d_3, expand, part, small, more, inner):
    units, channels = part.shape
    shape = (inner // 2, units // inner, channels)
    return call(
        far_reduce_body,
        "far_reduce",
        10**6,
        [(shape, F32), (shape, BF16), (small.shape, BF16)],
        [((units, d_3.shape[0]), BF16)],
        n_3,
        d_3,
        expand,
        part,
        small,
        more,
        read=10**5,
    )


def far_expand_body(n_3, d_3, expand, reduce, after, turned, dpre):
    lanes, _ = own_lanes(n_3.shape[1] // 4, turned.shape[0])
    turned[...] = n_3[:, lanes].astype(F32).T.astype(BF16)
    for here in blocks(reduce.shape[0]):
        slope, _ = slope_and_act(n_3[...], expand[:, here])
        dpre[:, here] = dpre_of(dot(d_3[...], reduce[here, :], ((1,), (1,))), slope)


def far_expand(n_3, d_3, expand, reduce, after):
    rows = n_3.shape[0]
    hid = expand.shape[1]
    return call(
        far_expand_body,
        "far_expand",
        10**9,
        [((2 * LANES, rows), BF16), ((rows, hid), BF16)],
        [],
        n_3,
        d_3,
        expand,
        reduce,
        after,
        read=10**6,
    )


def expand_grad_body(turned, turned_3, dpre_0, dpre, dpre_3, after, keep, send, lhs):
    own, near_width = lhs.shape[0], turned.shape[1]
    parts, rows, hid = keep.shape
    _, first = own_lanes(own, turned.shape[0])
    here = pl.ds(pl.multiple_of(first, 16), own)
    lhs[:, :near_width] = turned[here, :]
    lhs[:, near_width:] = turned_3[here, :]
    ordered = kept_first(lhs)
    cut = parts * rows
    for here in blocks(hid):
        every = jnp.concatenate([dpre_0[:, here], dpre[:, here], dpre_3[:, here]])
        total = dot(ordered, every, ((1,), (0,)))
        for x in range(parts):
            at = x * rows
            keep[x, :, here] = total[at : at + rows]
            send[x, :, here] = total[cut + at : cut + at + rows].astype(BF16)


def expand_grad(turned, turned_3, dpre_0, dpre, dpre_3, after, own, inner):
    hid = dpre.shape[1]
    shape = (inner // 2, own // inner, hid)
    return call(
        expand_grad_body,
        "expand_grad",
        10**6,
        [(shape, F32), (shape, BF16)],
        [((own, turned.shape[1] + turned_3.shape[1]), BF16)],
        turned,
        turned_3,
        dpre_0,
        dpre,
        dpre_3,
        after,
        read=10**5,
    )


def merge_body(kept, got, keep, send):
    _, _, mine = position(4)
    theirs = 1 - mine
    keep[...] = kept[mine] + got[mine].astype(F32)
    send[...] = (kept[theirs] + got[theirs].astype(F32)).astype(BF16)


def merge_small_body(kept, got, small, more, keep, send, sums):
    merge_body(kept, got, keep, send)
    sums[...] = added(small, more)


def merge(kept, got, *small):
    shape = kept.shape[1:]
    return call(
        merge_small_body if small else merge_body,
        "merge",
        10**6,
        [(shape, F32), (shape, BF16)] + [(part.shape, BF16) for part in small[:1]],
        [],
        kept,
        got,
        *small,
        read=10**5,
    )


def finish_reduce_body(keep, got, small, more, out, kernel, gain, scale, done):
    out[...] = keep[...] + got[...].astype(F32)
    sums = small[...].astype(F32) + more[...].astype(F32)
    for i in range(7):
        kernel[i] = sums[7 * i : 7 * i + 7]
    gain[...] = sums[49:50].reshape(gain.shape)
    scale[...] = sums[50:51].reshape(scale.shape)
    done[...] = jnp.zeros(done.shape, F32)


def finish_reduce(keep, got, small, more):
    channels = small.shape[1]
    return call(
        finish_reduce_body,
        "finish_reduce",
        10**9,
        [
            (keep.shape, F32),
            ((7, 7, channels), F32),
            ((channels,), F32),
            ((channels,), F32),
            ((8, LANES), F32),
        ],
        [],
        keep,
        got,
        small,
        more,
        read=10**6,
    )


def finish_expand_body(keep, got, after, out):
    out[...] = keep[...] + got[...].astype(F32)


def finish_expand(keep, got, after):
    return call(
        finish_expand_body, "finish_expand", 10**6, [(keep.shape, F32)], [], keep, got, after, read=10**5
    )[0]


def grads_plain(every, dbranch_all, expand_weight, reduce_weight, my_line, my_inner, line, inner):
    channels, hid = expand_weight.shape
    units, own = hid // line, channels // line
    every = every.reshape(-1, channels)
    pre = dot(every, expand_weight, ((1,), (0,)))
    cdf, density = phi_parts(pre)
    slope = (cdf + pre * density).reshape(line, 2, -1, hid)
    hidden = (pre * cdf).astype(BF16).astype(F32).reshape(line, 2, -1, hid)
    diff = (hidden[:, 0] - hidden[:, 1]).astype(BF16).reshape(-1, hid)
    diff = lax.dynamic_slice_in_dim(diff, my_line * units, units, 1)
    dhidden = dot(dbranch_all, reduce_weight, ((1,), (1,))).reshape(line, -1, hid)
    dpre = jnp.stack([dhidden * slope[:, 0], -dhidden * slope[:, 1]], axis=1)
    dpre = dpre.astype(BF16).reshape(-1, hid)
    normed_own = lax.dynamic_slice_in_dim(every, my_line * own, own, 1)
    expand = dot(normed_own, dpre, ((0,), (0,))).reshape(inner, own // inner, hid)
    reduce = dot(diff, dbranch_all, ((0,), (0,))).reshape(inner, units // inner, channels)
    return halves(expand, my_inner & 1), halves(reduce, my_inner & 1)


def halves(part, side):
    part = part.reshape((part.shape[0] // 2, 2) + part.shape[1:])
    keep = lax.dynamic_index_in_dim(part, side, 1, keepdims=False)
    send = lax.dynamic_index_in_dim(part, 1 - side, 1, keepdims=False)
    return keep, send.astype(BF16)


def on_device(
    features, column_table, dw_kernel, norm_gain, expand_weight, reduce_weight, layer_scale
):
    rows, cols, channels = features.shape
    hid = expand_weight.shape[1]
    count = lax.axis_size("col")
    bits = count.bit_length() - 1
    line = 1 << ((bits + 1) // 2)
    inner = count // line
    inner_bits = inner.bit_length() - 1
    me = lax.axis_index("col")
    my_line, my_inner = me // inner, me % inner
    units, own = hid // line, channels // line
    total_cols = cols * count

    def swapped(block, mask):
        return lax.ppermute(block, "col", [(d, d ^ mask) for d in range(count)])

    def line_sum(small):
        sums = [small] + [swapped(small, p * inner) for p in range(1, line)]
        sums = [part.astype(F32) for part in sums]
        while len(sums) > 1:
            sums = [low + high for low, high in zip(sums[::2], sums[1::2])]
        return sums[0]

    mirror = lax.ppermute(column_table, "col", [(d, count - 1 - d) for d in range(count)])

    features_f = features.astype(F32)
    table_f = column_table.astype(F32)
    gain = norm_gain[None]
    inside, across, turned = edges(features_f, table_f, mirror)
    inside = swapped(inside, 1)
    pairs = [(d, d + 1) for d in range(1, count - 1, 2)]
    across = lax.ppermute(across, "col", pairs + [(high, low) for low, high in pairs])
    normed, nhat, inv, wide = conv_norm(
        features_f, table_f, turned, inside, across, dw_kernel.astype(F32), gain
    )
    fast = line == 4 and inner == 4 and units % LANES == 0 and own % 64 == 0
    if fast:
        flat = normed.reshape(-1, channels)
        normed_2, normed_1 = swapped(flat, 2 * inner), swapped(flat, inner)
    else:
        others = [swapped(normed, p * inner) for p in range(1, line)]
    slope, hidden, disagreement, dbranch, gscale = forward(
        1.0 / math.sqrt(rows * total_cols),
        normed.reshape(-1, channels),
        expand_weight,
        reduce_weight,
        wide,
        layer_scale,
        features.shape,
    )
    dnormed, dpre_0 = backward(dbranch, slope, expand_weight, reduce_weight)
    small = small_grads(dnormed, nhat, inv, gain, gscale, wide)
    if fast:
        dbranch_2, dbranch_1 = swapped(dbranch, 2 * inner), swapped(dbranch, inner)
        normed_3 = swapped(gate(normed_2, dnormed, normed_1), inner)
        dbranch_3 = swapped(gate(dbranch_2, small, dbranch_1), inner)
        more = swapped(small, 2)
        turned, dpre, part = near(
            [flat, normed_1, normed_2],
            [dbranch, dbranch_1, dbranch_2],
            hidden,
            expand_weight,
            reduce_weight,
            line,
        )
        keep_r, send_r, small = far_reduce(
            normed_3, dbranch_3, expand_weight, part, small, more, inner
        )
        got_r, more = swapped(send_r, 1), swapped(small, 1)
        turned_3, dpre_3 = far_expand(normed_3, dbranch_3, expand_weight, reduce_weight, small)
        keep_r, send_r, small = merge(keep_r, got_r, small, more)
        got_r, more = swapped(send_r, 2), swapped(small, inner)
        keep_e, send_e = expand_grad(
            turned, turned_3, dpre_0, dpre, dpre_3, small, own, inner
        )
        small = (small.astype(F32) + more.astype(F32)).astype(BF16)
        more = swapped(small, 2 * inner)
        keep_e, send_e = merge(keep_e, swapped(send_e, 1))
        got_e = swapped(send_e, 2)
        sum_r, *sums, done = finish_reduce(keep_r, got_r, small, more)
        sum_e = finish_expand(keep_e, got_e, done)
        return (disagreement, sum_e, sum_r, *sums)

    dbranch_all = [dbranch] + [swapped(dbranch, p * inner) for p in range(1, line)]
    (keep_e, send_e), (keep_r, send_r) = grads_plain(
        jnp.stack([normed] + others),
        jnp.concatenate(dbranch_all),
        expand_weight,
        reduce_weight,
        my_line,
        my_inner,
        line,
        inner,
    )
    small = line_sum(small)
    for bit in range(inner_bits):
        sum_r = keep_r + swapped(send_r, 1 << bit).astype(F32)
        sum_e = keep_e + swapped(send_e, 1 << bit).astype(F32)
        small = small.astype(BF16)
        small = small.astype(F32) + swapped(small, 1 << bit).astype(F32)
        if bit < inner_bits - 1:
            side = (my_inner >> (bit + 1)) & 1
            keep_r, send_r = halves(sum_r, side)
            keep_e, send_e = halves(sum_e, side)
    grad_kernel = small[:49].reshape(7, 7, channels)
    return (
        disagreement,
        sum_e.reshape(own // inner, hid),
        sum_r.reshape(units // inner, channels),
        grad_kernel,
        small[49],
        small[50],
    )


def solution(mesh):
    in_specs = (P("groups", "col", None), P("col", None), P(), P(), P(), P(), P())
    out_specs = (
        P("groups", "col", None),
        P(("groups", "col"), None),
        P(("groups", "col"), None),
        P("groups", None, None),
        P("groups"),
        P("groups"),
    )
    return jax.shard_map(
        on_device, mesh=mesh, in_specs=in_specs, out_specs=out_specs, check_vma=False
    )
```

```python
import functools
import math

import jax
import jax.numpy as jnp
from jax import lax
from jax.experimental import pallas as pl
from jax.experimental.pallas import tpu as pltpu
from jax.sharding import PartitionSpec as P

BF16 = jnp.bfloat16
F32 = jnp.float32
LANES = 128
VMEM_GRANT = 16 << 20
BLOCK = 512


def phi_parts(pre):
    decay = jnp.exp(-0.5 * pre * pre)
    t = 1.0 / (1.0 + 0.23164189 * jnp.abs(pre))
    poly = 0.5307027145 * t - 0.7265760135
    poly = poly * t + 0.7107068705
    poly = poly * t - 0.142248368
    poly = poly * t + 0.127414796
    tail = poly * t * decay
    return jnp.where(pre < 0.0, tail, 1.0 - tail), decay * 0.3989422804014327


def call(body, name, flops, out_shape, scratch, *operands, read=10**8):
    return pl.pallas_call(
        body,
        in_specs=[pl.BlockSpec(memory_space=pltpu.VMEM) for _ in operands],
        out_specs=[pl.BlockSpec(memory_space=pltpu.VMEM) for _ in out_shape],
        out_shape=[jax.ShapeDtypeStruct(shape, dtype) for shape, dtype in out_shape],
        scratch_shapes=[pltpu.VMEM(shape, dtype) for shape, dtype in scratch],
        compiler_params=pltpu.CompilerParams(vmem_limit_bytes=VMEM_GRANT),
        cost_estimate=pl.CostEstimate(flops=flops, bytes_accessed=read, transcendentals=0),
        name=name,
    )(*operands)


def position(inner):
    me = lax.axis_index("col")
    return me // inner, me & 1, (me >> 1) & 1


def dot(lhs, rhs, contract):
    return lax.dot_general(lhs, rhs, (contract, ((), ())), preferred_element_type=F32)


def flipped(value):
    rows = value.shape[0]
    return jnp.concatenate([value[r : r + 1] for r in reversed(range(rows))], axis=0)


def edges_body(feat, table, mirror, inside, across, turned):
    _, cols, channels = feat.shape
    other = flipped(mirror[...].astype(F32))
    odd = (lax.axis_index("col") & 1) == 1
    for v, add in enumerate((table[...], other)):
        own = (feat[...] + add[None]).astype(BF16).astype(F32)
        first, last = own[:, :3], own[:, cols - 3 :]
        inside[v] = jnp.where(odd, first, last).astype(BF16)
        across[v] = jnp.where(odd, last, first).astype(BF16)
    turned[...] = other


def edges(features, table, mirror):
    rows, cols, channels = features.shape
    return call(
        edges_body,
        "edges",
        10**8,
        [
            ((2, rows, 3, channels), BF16),
            ((2, rows, 3, channels), BF16),
            ((cols, channels), F32),
        ],
        [],
        features,
        table,
        mirror,
    )


def conv_body(feat, table, turned, inside, across, dw, gain, normed, nhat, inv, wide, conv):
    rows, cols, channels = feat.shape
    odd = (lax.axis_index("col") & 1) == 1
    for v, add in enumerate((table[...], turned[...])):
        wide[v, :, 3 : 3 + cols, :] = (feat[...] + add[None]).astype(BF16).astype(F32)
        one, two = inside[v].astype(F32), across[v].astype(F32)
        wide[v, :, 0:3, :] = jnp.where(odd, one, two)
        wide[v, :, 3 + cols : 6 + cols, :] = jnp.where(odd, two, one)

    def tile(c, carry):
        lanes = pl.ds(pl.multiple_of(c * LANES, LANES), LANES)
        sums = [[jnp.zeros((cols, LANES), F32) for _ in range(rows)] for _ in range(2)]
        for j in range(7):
            for v in range(2):
                part = [wide[v, r, pl.ds(j, cols), lanes] for r in range(rows)]
                for i in range(7):
                    weight = dw[i, pl.ds(6 - j if v else j, 1), lanes]
                    for r in range(rows):
                        if 0 <= r + i - 3 < rows:
                            sums[v][r] = sums[v][r] + weight * part[r + i - 3]
        for v in range(2):
            for r in range(rows):
                conv[v, r, :, lanes] = sums[v][r]
        return carry

    lax.fori_loop(0, channels // LANES, tile, 0)
    for v in range(2):
        value = conv[v].reshape(rows * cols, channels)
        centred = value - jnp.mean(value, axis=-1, keepdims=True)
        inverse = lax.rsqrt(jnp.mean(centred * centred, axis=-1, keepdims=True) + 1e-06)
        value = centred * inverse
        nhat[v] = value
        inv[v] = jnp.broadcast_to(inverse, (rows * cols, LANES))
        normed[v] = (value * gain[...]).astype(BF16)


def conv_norm(features, table, turned, inside, across, dw, gain):
    rows, cols, channels = features.shape
    pixels = rows * cols
    return call(
        conv_body,
        "conv_norm",
        4 * 10**9,
        [
            ((2, pixels, channels), BF16),
            ((2, pixels, channels), F32),
            ((2, pixels, LANES), F32),
            ((2, rows, 16, channels), F32),
        ],
        [((2, rows, cols, channels), F32)],
        features,
        table,
        turned,
        inside,
        across,
        dw,
        gain,
    )


def blocks(total):
    return [slice(at, at + BLOCK) for at in range(0, total, BLOCK)]


def forward_body(
    scale, normed, expand, reduce, wide, ls, slope, hidden, disagreement, dbranch, gscale
):
    pixels, channels = normed.shape
    half = pixels // 2
    rows, cols, _ = disagreement.shape
    for here in blocks(expand.shape[1]):
        pre = dot(normed[...], expand[:, here], ((1,), (0,)))
        cdf, density = phi_parts(pre)
        slope[:, here] = (cdf + pre * density).astype(BF16)
        hidden[:, here] = (pre * cdf).astype(BF16)
    branch = dot(hidden[...], reduce[...], ((1,), (0,)))
    factor = ls[...].reshape(1, channels)
    outs = []
    for v in range(2):
        own = wide[v, :, 3 : 3 + cols, :].reshape(half, channels)
        outs.append((own + factor * branch[v * half : (v + 1) * half]).astype(BF16).astype(F32))
    difference = outs[0] - outs[1]
    disagreement[...] = difference.astype(BF16).reshape(rows, cols, channels)
    residual = (difference * scale).astype(BF16).astype(F32)
    gscale[...] = jnp.sum((branch[:half] - branch[half:]) * residual, axis=0, keepdims=True)
    dbranch[...] = (factor * residual).astype(BF16)


def forward(scale, normed, expand, reduce, wide, ls, shape):
    pixels, channels = normed.shape
    hid = expand.shape[1]
    return call(
        functools.partial(forward_body, scale),
        "forward",
        10**9,
        [
            ((pixels, hid), BF16),
            ((pixels, hid), BF16),
            (shape, BF16),
            ((pixels // 2, channels), BF16),
            ((1, channels), F32),
        ],
        [],
        normed,
        expand,
        reduce,
        wide,
        ls,
        read=10**6,
    )


def backward_body(dbranch, slope, expand, reduce, dnormed, dpre):
    half = dbranch.shape[0]
    for here in blocks(expand.shape[1]):
        dhidden = dot(dbranch[...], reduce[here, :], ((1,), (1,)))
        dpre[:, here] = dpre_of(dhidden, slope[:, here].astype(F32))
    dnormed[...] = dot(dpre[...], expand[...], ((1,), (1,)))


def backward(dbranch, slope, expand, reduce):
    half, channels = dbranch.shape
    hid = expand.shape[1]
    return call(
        backward_body,
        "backward",
        10**9,
        [((2 * half, channels), F32), ((2 * half, hid), BF16)],
        [],
        dbranch,
        slope,
        expand,
        reduce,
        read=10**6,
    )


def small_body(dnormed, nhat, inv, gain, gscale, wide, *rest):
    out, grad, taps, small = rest[-4:]
    half, channels = dnormed.shape[0] // 2, dnormed.shape[1]
    _, rows, _, _ = wide.shape
    cols = half // rows
    factor = gain[...]
    ggain = jnp.zeros((1, channels), F32)
    for v in range(2):
        here = slice(v * half, (v + 1) * half)
        value = dnormed[here, :]
        ggain = ggain + jnp.sum(value * nhat[v], axis=0, keepdims=True)
        scaled = value * factor
        gm = jnp.mean(scaled, axis=-1, keepdims=True)
        gn = jnp.mean(scaled * nhat[v], axis=-1, keepdims=True)
        grad[here, :] = inv[v][:, :1] * (scaled - gm - nhat[v] * gn)

    def tile(c, carry):
        lanes = pl.ds(pl.multiple_of(c * LANES, LANES), LANES)
        dconv = [
            [grad[pl.ds(v * half + r * cols, cols), lanes] for r in range(rows)] for v in range(2)
        ]
        for j in range(7):
            part = [
                [wide[v, r, pl.ds(6 - j if v else j, cols), lanes] for r in range(rows)]
                for v in range(2)
            ]
            for i in range(7):
                sums = []
                for v in range(2):
                    total = None
                    for r in range(rows):
                        if 0 <= r + i - 3 < rows:
                            term = part[v][r + i - 3] * dconv[v][r]
                            total = term if total is None else total + term
                    sums.append(total)
                at = 8 * (7 * i + j)
                taps[at : at + 8, :] = sums[0] + sums[1]
        rolled = taps[pl.ds(0, 49, stride=8), :]
        for s in range(1, 8):
            rolled = rolled + taps[pl.ds(s, 49, stride=8), :]
        small[:49, lanes] = rolled
        return carry

    small[...] = jnp.zeros(small.shape, F32)
    lax.fori_loop(0, channels // LANES, tile, 0)
    small[49:50, :] = ggain
    small[50:51, :] = gscale[...]
    out[...] = small[...].astype(BF16)


def small_grads(dnormed, nhat, inv, gain, gscale, wide, *after):
    channels = dnormed.shape[1]
    return call(
        small_body,
        "small_grads",
        10**6,
        [((64, channels), BF16)],
        [(dnormed.shape, F32), ((8 * 49, LANES), F32), ((64, channels), F32)],
        dnormed,
        nhat,
        inv,
        gain,
        gscale,
        wide,
        *after,
        read=10**5,
    )[0]


def gate_body(block, *rest):
    rest[-1][...] = block[...]


def gate(block, *after):
    shapes = [(block.shape, block.dtype)]
    return call(gate_body, "gate", 10**6, shapes, [], block, *after, read=10**5)[0]


def kept_first(ref):
    rows = ref.shape[0] // 4
    _, core, _ = position(4)
    blocks_of = lambda side: [
        ref[pl.ds(pl.multiple_of((2 * x + side) * rows, 16), rows), :] for x in range(2)
    ]
    return jnp.concatenate(blocks_of(core) + blocks_of(1 - core))


def added(small, more):
    return (small[...].astype(F32) + more[...].astype(F32)).astype(BF16)


def slope_and_act(normed, expand):
    pre = dot(normed, expand, ((1,), (0,)))
    cdf, density = phi_parts(pre)
    return cdf + pre * density, (pre * cdf).astype(BF16)


def views_apart(act):
    half = act.shape[0] // 2
    return (act[:half].astype(F32) - act[half:].astype(F32)).astype(BF16)


def dpre_of(dhidden, slope):
    half = dhidden.shape[0]
    return jnp.concatenate([dhidden * slope[:half], -dhidden * slope[half:]]).astype(BF16)


def own_lanes(own, width):
    first = position(4)[0] * own
    start = first // LANES * LANES
    return pl.ds(pl.multiple_of(start, LANES), width), first - start


def near_body(
    n_0, n_1, n_2, d_0, d_1, d_2, hidden_0, expand, reduce, turned, dpre, total, hidden
):
    half, channels = d_0.shape
    units = total.shape[0]
    lanes, _ = own_lanes(channels // 4, turned.shape[0])
    for p, ref in enumerate((n_0, n_1, n_2)):
        at = 2 * p * half
        turned[:, at : at + 2 * half] = ref[:, lanes].astype(F32).T.astype(BF16)
    others = jnp.concatenate([d_1[...], d_2[...]])
    both = jnp.concatenate([n_1[...], n_2[...]])
    for here in blocks(reduce.shape[0]):
        slope, act = slope_and_act(both, expand[:, here])
        hidden[:, here] = act
        dhidden = dot(others, reduce[here, :], ((1,), (1,)))
        dpre[: 2 * half, here] = dpre_of(dhidden[:half], slope[: 2 * half])
        dpre[2 * half :, here] = dpre_of(dhidden[half:], slope[2 * half :])
    lanes = pl.ds(pl.multiple_of(position(4)[0] * units, LANES), units)
    every = jnp.concatenate([d_0[...], others])
    acts = (hidden_0[:, lanes], hidden[: 2 * half, lanes], hidden[2 * half :, lanes])
    total[...] = dot(jnp.concatenate([views_apart(act) for act in acts]), every, ((0,), (0,)))


def near(normed, dbranch, hidden, expand, reduce, line):
    half, channels = dbranch[0].shape
    hid = expand.shape[1]
    return call(
        near_body,
        "near",
        10**6,
        [
            ((2 * LANES, 6 * half), BF16),
            ((4 * half, hid), BF16),
            ((hid // line, channels), F32),
        ],
        [((4 * half, hid), BF16)],
        *normed,
        *dbranch,
        hidden,
        expand,
        reduce,
        read=10**5,
    )


def far_reduce_body(n_3, d_3, expand, part, small, more, keep, send, sums, apart):
    parts, rows, channels = keep.shape
    units, cut = apart.shape[0], parts * rows
    lanes = pl.ds(pl.multiple_of(position(4)[0] * units, LANES), units)
    _, act = slope_and_act(n_3[...], expand[:, lanes])
    apart[...] = views_apart(act).astype(F32).T.astype(BF16)
    total = kept_first(part) + dot(kept_first(apart), d_3[...], ((1,), (0,)))
    keep[...] = total[:cut].reshape(parts, rows, channels)
    send[...] = total[cut:].astype(BF16).reshape(parts, rows, channels)
    sums[...] = added(small, more)


def far_reduce(n_3, d_3, expand, part, small, more, inner):
    units, channels = part.shape
    shape = (inner // 2, units // inner, channels)
    return call(
        far_reduce_body,
        "far_reduce",
        10**6,
        [(shape, F32), (shape, BF16), (small.shape, BF16)],
        [((units, d_3.shape[0]), BF16)],
        n_3,
        d_3,
        expand,
        part,
        small,
        more,
        read=10**5,
    )


def far_expand_body(n_3, d_3, expand, reduce, after, turned, dpre):
    lanes, _ = own_lanes(n_3.shape[1] // 4, turned.shape[0])
    turned[...] = n_3[:, lanes].astype(F32).T.astype(BF16)
    for here in blocks(reduce.shape[0]):
        slope, _ = slope_and_act(n_3[...], expand[:, here])
        dpre[:, here] = dpre_of(dot(d_3[...], reduce[here, :], ((1,), (1,))), slope)


def far_expand(n_3, d_3, expand, reduce, after):
    rows = n_3.shape[0]
    hid = expand.shape[1]
    return call(
        far_expand_body,
        "far_expand",
        10**9,
        [((2 * LANES, rows), BF16), ((rows, hid), BF16)],
        [],
        n_3,
        d_3,
        expand,
        reduce,
        after,
        read=10**6,
    )


def expand_grad_body(turned, turned_3, dpre_0, dpre, dpre_3, after, keep, send, lhs):
    own, near_width = lhs.shape[0], turned.shape[1]
    parts, rows, hid = keep.shape
    _, first = own_lanes(own, turned.shape[0])
    here = pl.ds(pl.multiple_of(first, 16), own)
    lhs[:, :near_width] = turned[here, :]
    lhs[:, near_width:] = turned_3[here, :]
    ordered = kept_first(lhs)
    cut = parts * rows
    for here in blocks(hid):
        every = jnp.concatenate([dpre_0[:, here], dpre[:, here], dpre_3[:, here]])
        total = dot(ordered, every, ((1,), (0,)))
        for x in range(parts):
            at = x * rows
            keep[x, :, here] = total[at : at + rows]
            send[x, :, here] = total[cut + at : cut + at + rows].astype(BF16)


def expand_grad(turned, turned_3, dpre_0, dpre, dpre_3, after, own, inner):
    hid = dpre.shape[1]
    shape = (inner // 2, own // inner, hid)
    return call(
        expand_grad_body,
        "expand_grad",
        10**6,
        [(shape, F32), (shape, BF16)],
        [((own, turned.shape[1] + turned_3.shape[1]), BF16)],
        turned,
        turned_3,
        dpre_0,
        dpre,
        dpre_3,
        after,
        read=10**5,
    )


def merge_body(kept, got, keep, send):
    _, _, mine = position(4)
    theirs = 1 - mine
    keep[...] = kept[mine] + got[mine].astype(F32)
    send[...] = (kept[theirs] + got[theirs].astype(F32)).astype(BF16)


def merge_small_body(kept, got, small, more, keep, send, sums):
    merge_body(kept, got, keep, send)
    sums[...] = added(small, more)


def merge(kept, got, *small):
    shape = kept.shape[1:]
    return call(
        merge_small_body if small else merge_body,
        "merge",
        10**6,
        [(shape, F32), (shape, BF16)] + [(part.shape, BF16) for part in small[:1]],
        [],
        kept,
        got,
        *small,
        read=10**5,
    )


def finish_reduce_body(keep, got, small, more, out, kernel, gain, scale, done):
    out[...] = keep[...] + got[...].astype(F32)
    sums = small[...].astype(F32) + more[...].astype(F32)
    for i in range(7):
        kernel[i] = sums[7 * i : 7 * i + 7]
    gain[...] = sums[49:50].reshape(gain.shape)
    scale[...] = sums[50:51].reshape(scale.shape)
    done[...] = jnp.zeros(done.shape, F32)


def finish_reduce(keep, got, small, more):
    channels = small.shape[1]
    return call(
        finish_reduce_body,
        "finish_reduce",
        10**9,
        [
            (keep.shape, F32),
            ((7, 7, channels), F32),
            ((channels,), F32),
            ((channels,), F32),
            ((8, LANES), F32),
        ],
        [],
        keep,
        got,
        small,
        more,
        read=10**6,
    )


def finish_expand_body(keep, got, after, out):
    out[...] = keep[...] + got[...].astype(F32)


def finish_expand(keep, got, after):
    return call(
        finish_expand_body, "finish_expand", 10**6, [(keep.shape, F32)], [], keep, got, after, read=10**5
    )[0]


def grads_plain(every, dbranch_all, expand_weight, reduce_weight, my_line, my_inner, line, inner):
    channels, hid = expand_weight.shape
    units, own = hid // line, channels // line
    every = every.reshape(-1, channels)
    pre = dot(every, expand_weight, ((1,), (0,)))
    cdf, density = phi_parts(pre)
    slope = (cdf + pre * density).reshape(line, 2, -1, hid)
    hidden = (pre * cdf).astype(BF16).astype(F32).reshape(line, 2, -1, hid)
    diff = (hidden[:, 0] - hidden[:, 1]).astype(BF16).reshape(-1, hid)
    diff = lax.dynamic_slice_in_dim(diff, my_line * units, units, 1)
    dhidden = dot(dbranch_all, reduce_weight, ((1,), (1,))).reshape(line, -1, hid)
    dpre = jnp.stack([dhidden * slope[:, 0], -dhidden * slope[:, 1]], axis=1)
    dpre = dpre.astype(BF16).reshape(-1, hid)
    normed_own = lax.dynamic_slice_in_dim(every, my_line * own, own, 1)
    expand = dot(normed_own, dpre, ((0,), (0,))).reshape(inner, own // inner, hid)
    reduce = dot(diff, dbranch_all, ((0,), (0,))).reshape(inner, units // inner, channels)
    return halves(expand, my_inner & 1), halves(reduce, my_inner & 1)


def halves(part, side):
    part = part.reshape((part.shape[0] // 2, 2) + part.shape[1:])
    keep = lax.dynamic_index_in_dim(part, side, 1, keepdims=False)
    send = lax.dynamic_index_in_dim(part, 1 - side, 1, keepdims=False)
    return keep, send.astype(BF16)


def on_device(
    features, column_table, dw_kernel, norm_gain, expand_weight, reduce_weight, layer_scale
):
    rows, cols, channels = features.shape
    hid = expand_weight.shape[1]
    count = lax.axis_size("col")
    bits = count.bit_length() - 1
    line = 1 << ((bits + 1) // 2)
    inner = count // line
    inner_bits = inner.bit_length() - 1
    me = lax.axis_index("col")
    my_line, my_inner = me // inner, me % inner
    units, own = hid // line, channels // line
    total_cols = cols * count

    def swapped(block, mask):
        return lax.ppermute(block, "col", [(d, d ^ mask) for d in range(count)])

    def line_sum(small):
        sums = [small] + [swapped(small, p * inner) for p in range(1, line)]
        sums = [part.astype(F32) for part in sums]
        while len(sums) > 1:
            sums = [low + high for low, high in zip(sums[::2], sums[1::2])]
        return sums[0]

    mirror = lax.ppermute(column_table, "col", [(d, count - 1 - d) for d in range(count)])

    features_f = features.astype(F32)
    table_f = column_table.astype(F32)
    gain = norm_gain[None]
    inside, across, turned = edges(features_f, table_f, mirror)
    inside = swapped(inside, 1)
    pairs = [(d, d + 1) for d in range(1, count - 1, 2)]
    across = lax.ppermute(across, "col", pairs + [(high, low) for low, high in pairs])
    normed, nhat, inv, wide = conv_norm(
        features_f, table_f, turned, inside, across, dw_kernel.astype(F32), gain
    )
    fast = line == 4 and inner == 4 and units % LANES == 0 and own % 64 == 0
    if fast:
        flat = normed.reshape(-1, channels)
        normed_2, normed_1 = swapped(flat, 2 * inner), swapped(flat, inner)
    else:
        others = [swapped(normed, p * inner) for p in range(1, line)]
    slope, hidden, disagreement, dbranch, gscale = forward(
        1.0 / math.sqrt(rows * total_cols),
        normed.reshape(-1, channels),
        expand_weight,
        reduce_weight,
        wide,
        layer_scale,
        features.shape,
    )
    dnormed, dpre_0 = backward(dbranch, slope, expand_weight, reduce_weight)
    small = small_grads(dnormed, nhat, inv, gain, gscale, wide)
    if fast:
        dbranch_2, dbranch_1 = swapped(dbranch, 2 * inner), swapped(dbranch, inner)
        normed_3 = swapped(gate(normed_2, dnormed, normed_1), inner)
        dbranch_3 = swapped(gate(dbranch_2, small, dbranch_1), inner)
        more = swapped(small, 2)
        turned, dpre, part = near(
            [flat, normed_1, normed_2],
            [dbranch, dbranch_1, dbranch_2],
            hidden,
            expand_weight,
            reduce_weight,
            line,
        )
        keep_r, send_r, small = far_reduce(
            normed_3, dbranch_3, expand_weight, part, small, more, inner
        )
        got_r, more = swapped(send_r, 1), swapped(small, 1)
        turned_3, dpre_3 = far_expand(normed_3, dbranch_3, expand_weight, reduce_weight, small)
        keep_r, send_r, small = merge(keep_r, got_r, small, more)
        got_r, more = swapped(send_r, 2), swapped(small, inner)
        keep_e, send_e = expand_grad(
            turned, turned_3, dpre_0, dpre, dpre_3, small, own, inner
        )
        small = (small.astype(F32) + more.astype(F32)).astype(BF16)
        more = swapped(small, 2 * inner)
        keep_e, send_e = merge(keep_e, swapped(send_e, 1))
        got_e = swapped(send_e, 2)
        sum_r, *sums, done = finish_reduce(keep_r, got_r, small, more)
        sum_e = finish_expand(keep_e, got_e, done)
        return (disagreement, sum_e, sum_r, *sums)

    dbranch_all = [dbranch] + [swapped(dbranch, p * inner) for p in range(1, line)]
    (keep_e, send_e), (keep_r, send_r) = grads_plain(
        jnp.stack([normed] + others),
        jnp.concatenate(dbranch_all),
        expand_weight,
        reduce_weight,
        my_line,
        my_inner,
        line,
        inner,
    )
    small = line_sum(small)
    for bit in range(inner_bits):
        sum_r = keep_r + swapped(send_r, 1 << bit).astype(F32)
        sum_e = keep_e + swapped(send_e, 1 << bit).astype(F32)
        small = small.astype(BF16)
        small = small.astype(F32) + swapped(small, 1 << bit).astype(F32)
        if bit < inner_bits - 1:
            side = (my_inner >> (bit + 1)) & 1
            keep_r, send_r = halves(sum_r, side)
            keep_e, send_e = halves(sum_e, side)
    grad_kernel = small[:49].reshape(7, 7, channels)
    return (
        disagreement,
        sum_e.reshape(own // inner, hid),
        sum_r.reshape(units // inner, channels),
        grad_kernel,
        small[49],
        small[50],
    )


def solution(mesh):
    in_specs = (P("groups", "col", None), P("col", None), P(), P(), P(), P(), P())
    out_specs = (
        P("groups", "col", None),
        P(("groups", "col"), None),
        P(("groups", "col"), None),
        P("groups", None, None),
        P("groups"),
        P("groups"),
    )
    return jax.shard_map(
        on_device, mesh=mesh, in_specs=in_specs, out_specs=out_specs, check_vma=False
    )
```
